128 devices in a mesh: dp: 8 (over y, x_hi), ctx: 16 (over x_lo, z, core).
Axes of the slice: x: 4 (x_hi: 2, x_lo: 2; x = x_hi * 2 + x_lo), y: 4, z: 4, core: 2. Of those that a mesh axis runs over, the one named last changes fastest.
Arguments:
- tokens: bfloat16 [8, 2048, 2048], P('dp', 'ctx'), may hold values from -6 to 6
- segments: int32 [8, 2048], P('dp', 'ctx'), may hold values from 0 to 31, as said below
- cotangent: bfloat16 [8, 2048, 2048], P('dp', 'ctx'), may hold values from -6 to 6
- norm_attn: bfloat16 [2048], P('dp'), may hold values from 0.5 to 1.5
- norm_ffn: bfloat16 [2048], P('dp'), may hold values from 0.5 to 1.5
- wqkv: bfloat16 [2048, 2560], P('dp'), may hold values from -0.125 to 0.125
- wo: bfloat16 [2048, 2048], P('dp'), may hold values from -0.5 to 0.5
- w1: bfloat16 [2048, 5632], P('dp'), may hold values from -0.125 to 0.125
- w3: bfloat16 [2048, 5632], P('dp'), may hold values from -0.125 to 0.125
- w2: bfloat16 [5632, 2048], P('dp'), may hold values from -0.078125 to 0.078125
Outputs:
- output: float32 [8, 2048, 2048], P('dp', 'ctx')
- input_grad: float32 [8, 2048, 2048], P('dp', 'ctx')
- grad_norm_attn: float32 [2048], P('dp')
- grad_norm_ffn: float32 [2048], P('dp')
- grad_wqkv: float32 [2048, 2560], P('dp')
- grad_wo: float32 [2048, 2048], P('dp')
- grad_w1: float32 [2048, 5632], P('dp')
- grad_w3: float32 [2048, 5632], P('dp')
- grad_w2: float32 [5632, 2048], P('dp')
The draws below stay inside these ranges and needn't reach their ends.
Inputs may be any that keep to these rules, and one draw needn't show every extreme that they name: `segments`: document numbers start at 0 and rise by one at each new document, so a document's tokens are contiguous; every sequence holds all 32 documents.
All inputs are finite; a program needn't handle non-finite values.
Results may differ from the reference program's by a relative error of at most 0.025.
Values may be sent and summed in bfloat16 or wider, within the bound.
A program may use at most 384 MiB of HBM per device.

```python
import jax
import jax.numpy as jnp
from jax import lax

D = 2048
HEADS = 32
KV_HEADS = 4
HEAD_DIM = 64
FF = 5632
TOK_DEV = 128
COUNT = 32
QDIM = 2048
KVDIM = 256
QKV = 2560
LENGTH = 2048
SEQS = 8


def one_sequence(key):
    cut_key, order_key = jax.random.split(key)
    middle = LENGTH // TOK_DEV // 2
    cut = middle * TOK_DEV + jax.random.randint(cut_key, (), 1, TOK_DEV)
    order = jax.random.permutation(order_key, LENGTH).astype(jnp.int32)
    eligible = (order > cut).astype(jnp.int32)
    taken = eligible * (jnp.cumsum(eligible) <= COUNT - 2).astype(jnp.int32)
    marks = jnp.zeros((LENGTH,), jnp.int32).at[order].add(taken)
    marks = marks.at[cut].add(1)
    return jnp.cumsum(marks).astype(jnp.int32)


def draw_segments(key, part):
    key = jax.random.fold_in(key, 11)
    keys = jax.random.split(key, SEQS)
    return jax.vmap(one_sequence)(keys)


def steps_of(stream_key, extent, shards, smallest, largest):
    loudness, own = 1.0, jax.random.fold_in(stream_key, 6)
    for position, shards_of in shards:
        heights = jnp.exp(jax.random.uniform(jax.random.fold_in(own, position), (shards_of,), jnp.float32, smallest / len(shards), largest / len(shards)))
        loudness = loudness * jnp.repeat(heights, extent[position] // shards_of).reshape([-1 if axis == position else 1 for axis in range(len(extent))])
    return loudness


def gaussian(own_key, extent, spread, bound, cuts=(), held_as=jnp.bfloat16):
    drawn = spread * jax.random.normal(own_key, extent, jnp.float32)
    if cuts:
        drawn = drawn * steps_of(own_key, extent, cuts, -0.22, 0.18)
    return jnp.clip(drawn, -bound, bound).astype(held_as)


def setup_inputs(seed: int = 0) -> dict:
    key_list = jax.random.split(jax.random.key(seed), 11)
    tokens = gaussian(key_list[0], (SEQS, LENGTH, D), 1.0, 6.0, ((0, 8), (1, 16)))
    segments = draw_segments(jax.random.fold_in(key_list[10], 71), 0)
    cotangent = gaussian(key_list[2], (SEQS, LENGTH, D), 1.0, 6.0, ((0, 8), (1, 16)))
    norm_attn = jnp.clip(1.0 + 0.1 * jax.random.normal(key_list[3], (D,), jnp.float32), 0.5, 1.5).astype(jnp.bfloat16)
    norm_ffn = jnp.clip(1.0 + 0.1 * jax.random.normal(key_list[4], (D,), jnp.float32), 0.5, 1.5).astype(jnp.bfloat16)
    wqkv = gaussian(key_list[5], (D, QKV), D ** -0.5, 0.125, ((0, 8),))
    wo = gaussian(key_list[6], (QDIM, D), (QDIM // 16) ** -0.5, 0.5, ((0, 8),))
    w1 = gaussian(key_list[7], (D, FF), D ** -0.5, 0.125, ((0, 8),))
    w3 = gaussian(key_list[8], (D, FF), D ** -0.5, 0.125, ((0, 8),))
    w2 = gaussian(key_list[9], (FF, D), FF ** -0.5, 0.078125, ((0, 8),))
    return {"tokens": tokens, "segments": segments, "cotangent": cotangent, "norm_attn": norm_attn, "norm_ffn": norm_ffn, "wqkv": wqkv, "wo": wo, "w1": w1, "w3": w3, "w2": w2}


@jax.custom_vjp
def low(v):
    return lax.optimization_barrier(v.astype(jnp.bfloat16)).astype(jnp.float32)

@jax.custom_vjp
def low_back(v):
    return v

def low_keep(v):
    return (low(v), None)

def low_pass(kept, grad):
    return (grad,)

def back_keep(v):
    return (v, None)

def back_low(kept, grad):
    return (low(grad),)
low.defvjp(low_keep, low_pass)
low_back.defvjp(back_keep, back_low)
EPS = 1e-05
THETA = 10000.0
HIGH = lax.Precision.HIGHEST

def rms(v, gain):
    return v * lax.rsqrt(lax.optimization_barrier(jnp.mean(v * v, axis=-1, keepdims=True)) + EPS) * gain

def rotate(v, cosine, sine):
    half = v.shape[-1] // 2
    turned = jnp.concatenate([-v[..., half:], v[..., :half]], axis=-1)
    return v * cosine[:, None, :] + turned * sine[:, None, :]

def attend(query, keys, values, index, start):
    length = query.shape[0]
    rows = min(512, length)
    blocks = length // rows
    query_blocks = query.reshape((blocks, rows) + query.shape[1:])
    index_blocks = index.reshape(blocks, rows)
    start_blocks = start.reshape(blocks, rows)
    scale = 1.0 / HEAD_DIM ** 0.5

    def one_block(args):
        qq, ii, ss = args
        raw = jnp.einsum('tkgd,skd->kgts', qq, keys, precision=HIGH)
        scores = low_back(raw * scale)
        visible = (index[None, :] <= ii[:, None]) & (index[None, :] >= ss[:, None])
        scores = jnp.where(visible[None, None], scores, -1e+30)
        top = lax.optimization_barrier(jnp.max(scores, axis=-1, keepdims=True))
        weights = jnp.exp(scores - top)
        probs = low(weights / lax.optimization_barrier(jnp.sum(weights, axis=-1, keepdims=True)))
        return jnp.einsum('kgts,skd->tkgd', probs, values, precision=HIGH)
    out = lax.map(jax.checkpoint(one_block), (query_blocks, index_blocks, start_blocks))
    return out.reshape(length, QDIM)

def layer(x, segs, gain_attn, gain_ffn, wqkv, wo, w1, w3, w2):
    length = x.shape[0]
    index = jnp.arange(length, dtype=jnp.int32)
    first = lax.optimization_barrier(jnp.sum((segs[None, :] < segs[:, None]).astype(jnp.int32), axis=1))
    place = index - first
    start = index - place
    freq = THETA ** (-jnp.arange(HEAD_DIM // 2, dtype=jnp.float32) * 2.0 / HEAD_DIM)
    angle = place.astype(jnp.float32)[:, None] * freq[None, :]
    cosine = jnp.concatenate([jnp.cos(angle), jnp.cos(angle)], axis=-1)
    sine = jnp.concatenate([jnp.sin(angle), jnp.sin(angle)], axis=-1)
    norm_one = low(rms(x, gain_attn))
    mixed = low_back(jnp.dot(norm_one, wqkv, precision=HIGH))
    query = mixed[:, :QDIM].reshape(length, HEADS, HEAD_DIM)
    keys = mixed[:, QDIM:QDIM + KVDIM].reshape(length, KV_HEADS, HEAD_DIM)
    values = low(mixed[:, QDIM + KVDIM:].reshape(length, KV_HEADS, HEAD_DIM))
    query = low(rotate(query, cosine, sine))
    keys = low(rotate(keys, cosine, sine))
    group = HEADS // KV_HEADS
    query = query.reshape(length, KV_HEADS, group, HEAD_DIM)
    heads_out = low(low_back(attend(query, keys, values, index, start)))
    resid = x + low_back(jnp.dot(heads_out, wo, precision=HIGH))
    norm_two = low(rms(resid, gain_ffn))
    gate = low_back(jnp.dot(norm_two, w1, precision=HIGH))
    up = low_back(jnp.dot(norm_two, w3, precision=HIGH))
    hidden = low(jax.nn.silu(gate) * up)
    return resid + jnp.dot(hidden, w2, precision=HIGH)

def reference(tokens, segments, cotangent, norm_attn, norm_ffn, wqkv, wo, w1, w3, w2):
    params = tuple((w.astype(jnp.float32) for w in (norm_attn, norm_ffn, wqkv, wo, w1, w3, w2)))

    def step(totals, row):
        x_row, seg_row, grad_row = row

        def forward(xx, *weights):
            return layer(xx, seg_row, *weights)
        result, pull = jax.vjp(forward, x_row.astype(jnp.float32), *params)
        grads = pull(grad_row.astype(jnp.float32))
        new_totals = tuple((t + g for t, g in zip(totals, grads[1:])))
        return (new_totals, (result, grads[0]))
    zeros = tuple((jnp.zeros(w.shape, jnp.float32) for w in params))
    totals, (results, input_grads) = lax.scan(step, zeros, (tokens, segments, cotangent))
    return (results, input_grads, totals[0], totals[1], totals[2], totals[3], totals[4], totals[5], totals[6])
```

```python
import functools

import jax
import jax.numpy as jnp
from jax import lax
from jax.experimental import pallas as pl
from jax.experimental.pallas import tpu as pltpu
from jax.sharding import PartitionSpec as P

D = 2048
HEAD_DIM = 64
TOK = 128
RING = 4
QDIM = 2048
KVDIM = 256
GROUP = 8
QZ = 512
MZ = 640
FZ = 1408
SPLIT = 2048
EPS = 1e-05
THETA = 10000.0
MESH = pl.DeviceIdType.MESH
VMEM_LIMIT = 56 << 20
BF = jnp.bfloat16
F32 = jnp.float32
ANY = pl.BlockSpec(memory_space=pl.ANY)
VMEM = pl.BlockSpec(memory_space=pltpu.VMEM)


def coords():
    dp, ctx = lax.axis_index("dp"), lax.axis_index("ctx")
    y, xh = dp // 2, dp % 2
    xl, z, c = ctx // 8, (ctx // 2) % 4, ctx % 2
    return dict(y=y, x=xh * 2 + xl, xh=xh, xl=xl, z=z, c=c)


def device(q, **change):
    r = {k: change.get(k, q[k]) for k in ("y", "x", "z", "c")}
    return (r["y"] * 2 + r["x"] // 2, (r["x"] % 2) * 8 + r["z"] * 2 + r["c"])


def ring(q, axis):
    return [device(q, **{axis: (q[axis] + s) % 4}) for s in (1, 3, 2)]


def shift_pairs(axis, by):
    size = 2 if axis == "c" else 4
    pairs = []
    for y in range(4):
        for x in range(4):
            for z in range(4):
                for c in range(2):
                    q = dict(y=y, x=x, z=z, c=c)
                    pairs.append((device(q), device(q, **{axis: (q[axis] + by) % size})))
    return [(a[0] * 16 + a[1], b[0] * 16 + b[1]) for a, b in pairs]


def swap_pairs():
    pairs = []
    for y in range(4):
        for x in range(4):
            for z in range(4):
                for c in range(2):
                    q = dict(y=y, x=x, z=z, c=c)
                    pairs.append((device(q), device(q, y=z, z=y)))
    return [(a[0] * 16 + a[1], b[0] * 16 + b[1]) for a, b in pairs]


def move(v, axis, by):
    return lax.ppermute(v, ("dp", "ctx"), shift_pairs(axis, by))


class Copies:
    def __init__(self, send_sems, recv_sems):
        self.send_sems, self.recv_sems, self.n, self.open = send_sems, recv_sems, 0, []

    def send(self, src, dst, to):
        cp = pltpu.make_async_remote_copy(
            src_ref=src,
            dst_ref=dst,
            send_sem=self.send_sems.at[self.n],
            recv_sem=self.recv_sems.at[self.n],
            device_id=to,
            device_id_type=MESH,
        )
        cp.start()
        self.n += 1
        self.open.append(cp.wait_send)
        return cp

    def local(self, src, dst):
        cp = pltpu.make_async_copy(src, dst, self.send_sems.at[self.n])
        cp.start()
        self.n += 1
        return cp

    def close(self):
        for wait in self.open:
            wait()


def greet(targets):
    barrier = pltpu.get_barrier_semaphore()
    for to in targets:
        pl.semaphore_signal(barrier, inc=1, device_id=to, device_id_type=MESH)
    pl.semaphore_wait(barrier, len(targets))


def cost(us):
    return pl.CostEstimate(flops=int(us * 1e9), bytes_accessed=0, transcendentals=0)


def talk(kernel, name, cid, us, copies, ins, outs, scratch=(), near=()):
    return pl.pallas_call(
        kernel,
        name=name,
        out_shape=[jax.ShapeDtypeStruct(s, t) for s, t in outs],
        in_specs=[VMEM if i in near else ANY for i in range(len(ins))],
        out_specs=[ANY] * len(outs),
        scratch_shapes=[
            *scratch,
            pltpu.SemaphoreType.DMA((copies,)),
            pltpu.SemaphoreType.DMA((copies,)),
        ],
        cost_estimate=cost(us),
        compiler_params=pltpu.CompilerParams(
            collective_id=cid, has_side_effects=True, vmem_limit_bytes=VMEM_LIMIT
        ),
    )(*ins)


def fetch_kernel(
    x, seg, gn, wq, wo, w1, w3, w2, X, SEG, GN, WQ, WO, A1, A3, AX, AY, T2, TO, QP, P1, P3, ss, rs
):
    q = coords()
    y, xx, xh, xl, z, c = q["y"], q["x"], q["xh"], q["xl"], q["z"], q["c"]
    zs, ys, xs = ring(q, "z"), ring(q, "y"), ring(q, "x")
    mate = device(q, c=1 - c)
    other = device(q, x=xx ^ 1)
    other_mate = device(q, x=xx ^ 1, c=1 - c)
    swap = device(q, y=z, z=y)
    k = Copies(ss, rs)
    rows = pl.ds(pl.multiple_of(128 * c + 64 * xl, 64), 64)
    qcols = pl.ds(pl.multiple_of(MZ * z, 128), MZ)
    fcols = pl.ds(pl.multiple_of(FZ * z, 128), FZ)
    loads = [
        k.local(wq.at[rows, qcols], QP),
        k.local(w1.at[rows, fcols], P1),
        k.local(w3.at[rows, fcols], P3),
    ]
    barrier = pltpu.get_barrier_semaphore()
    greeted = zs + ys + xs + [mate, other_mate]
    for to in greeted:
        pl.semaphore_signal(barrier, inc=1, device_id=to, device_id_type=MESH)

    @pl.when(y != z)
    def _():
        pl.semaphore_signal(barrier, inc=1, device_id=swap, device_id_type=MESH)

    pl.semaphore_wait(barrier, len(greeted) + (y != z).astype(jnp.int32))
    piece = pl.ds(pl.multiple_of(128 * (c * 8 + z * 2 + xl), 128), 128)
    turned = []
    for src, dst in ((wo, TO), (w2, T2)):
        n = k.n
        k.n += 1
        remote = pltpu.make_async_remote_copy(
            src_ref=src.at[:, piece],
            dst_ref=dst,
            send_sem=ss.at[n],
            recv_sem=rs.at[n],
            device_id=swap,
            device_id_type=MESH,
        )
        here = pltpu.make_async_copy(src.at[:, piece], dst, ss.at[n])

        @pl.when(y != z)
        def _(remote=remote):
            remote.start()

        @pl.when(y == z)
        def _(here=here):
            here.start()

        turned.append((remote, here))
    for cp in loads:
        cp.wait()
    top, low = pl.ds(0, 32), pl.ds(32, 32)
    q_top = [k.send(QP.at[top], WQ.at[c, y, xh, xl, top], to) for to in xs]
    q_low = [k.send(QP.at[low], WQ.at[c, y, xh, xl, low], to) for to in ys]
    q_here = k.local(QP, WQ.at[c, y, xh, xl])
    seg_z = [k.send(seg, SEG.at[xl, z, c], to) for to in zs]
    seg_here = k.local(seg, SEG.at[xl, z, c])
    gn_y = [k.send(gn, GN.at[y, xh], to) for to in ys]
    gn_here = k.local(gn, GN.at[y, xh])
    x_z = [k.send(x, X.at[z], to) for to in zs]
    x_here = k.local(x, X.at[z])
    q_here.wait()
    for cp in q_top:
        cp.wait_recv()
    part = WQ.at[c, y, :, :, top]
    q2 = [k.send(part, part, to) for to in ys]
    for cp in q_low:
        cp.wait_recv()
    part = WQ.at[c, :, xh, xl, low]
    q2 += [k.send(part, part, to) for to in xs]
    for remote, here in turned:

        @pl.when(y != z)
        def _(remote=remote):
            remote.wait_recv()
            remote.wait_send()

        @pl.when(y == z)
        def _(here=here):
            here.wait()

    ocol = pl.ds(pl.multiple_of(128 * (c * 8 + y * 2 + xl), 128), 128)
    o1 = [k.send(TO, WO.at[xh, :, ocol], to) for to in xs]
    o1_here = k.local(TO, WO.at[xh, :, ocol])
    a1 = [k.send(P1, A1.at[xh, xl], to) for to in xs]
    a1_here = k.local(P1, A1.at[xh, xl])
    a3 = [k.send(P3, A3.at[y], to) for to in ys]
    a3_here = k.local(P3, A3.at[y])
    t_top, t_low = pl.ds(0, 352), pl.ds(352, 352)
    ax = [k.send(T2.at[t_top], AX.at[xh, xl], to) for to in xs]
    ax_here = k.local(T2.at[t_top], AX.at[xh, xl])
    ay = [k.send(T2.at[t_low], AY.at[y], to) for to in ys]
    ay_here = k.local(T2.at[t_low], AY.at[y])
    for cp in seg_z:
        cp.wait_recv()
    seg_here.wait()
    part = SEG.at[xl, :, c]
    seg2 = [k.send(part, part, to) for to in (mate, other, other_mate)]
    for cp in gn_y:
        cp.wait_recv()
    gn_here.wait()
    gn2 = k.send(GN.at[:, xh], GN.at[:, xh], device(q, x=3 - xx))
    for cp in o1:
        cp.wait_recv()
    o1_here.wait()
    part = WO.at[:, :, pl.ds(pl.multiple_of(128 * (c * 8 + y * 2), 256), 256)]
    o2 = [k.send(part, part, to) for to in ys]
    for cp in q2:
        cp.wait_recv()
    q3 = k.send(WQ.at[c], WQ.at[c], mate)
    for cp in o2:
        cp.wait_recv()
    part = WO.at[:, :, pl.ds(pl.multiple_of(1024 * c, 1024), 1024)]
    o3 = k.send(part, part, mate)
    for cp in x_z + a1 + a3 + ax + ay + seg2 + [gn2, q3, o3]:
        cp.wait_recv()
    for cp in (x_here, a1_here, a3_here, ax_here, ay_here):
        cp.wait()
    k.close()


def kv_kernel(kv, KV, ss, rs):
    q = coords()
    xx, xl, c = q["x"], q["xl"], q["c"]
    mate = device(q, c=1 - c)
    other = device(q, x=xx ^ 1)
    greet([mate, other])
    k = Copies(ss, rs)
    here = k.local(kv, KV.at[xl, :, c])
    near = k.send(kv, KV.at[xl, :, c], mate)
    far = pltpu.make_async_remote_copy(
        src_ref=kv,
        dst_ref=KV.at[0, :, c],
        send_sem=ss.at[2],
        recv_sem=rs.at[2],
        device_id=other,
        device_id_type=MESH,
    )
    on = pltpu.make_async_remote_copy(
        src_ref=KV.at[0, :, c],
        dst_ref=KV.at[0, :, c],
        send_sem=ss.at[3],
        recv_sem=rs.at[3],
        device_id=mate,
        device_id_type=MESH,
    )

    @pl.when(xl == 0)
    def _():
        far.start()
        far.wait_send()

    @pl.when(xl == 1)
    def _():
        far.wait_recv()
        on.start()
        on.wait_recv()
        on.wait_send()

    here.wait()
    near.wait_recv()
    k.close()


def gather_kernel(v, V, ss, rs):
    q = coords()
    zs = ring(q, "z")
    greet(zs)
    k = Copies(ss, rs)
    sent = [k.send(v, V.at[q["z"]], to) for to in zs]
    here = k.local(v, V.at[q["z"]])
    for cp in sent:
        cp.wait_recv()
    here.wait()
    k.close()


def assemble_kernel(*refs):
    n2, g = refs[0], refs[1:5]
    a1, a3, ax, ay = refs[5:9], refs[9:13], refs[13:17], refs[17:21]
    N2, G, W13, W2, gb, b1, b3, bx, by, ss, rs = refs[21:]
    q = coords()
    y, xx, z, c = q["y"], q["x"], q["z"], q["c"]
    zs = ring(q, "z")
    mate = device(q, c=1 - c)
    k = Copies(ss, rs)
    bufs = ((a1, b1), (a3, b3), (ax, bx), (ay, by), (g, gb))
    loads = [[k.local(refs[j], buf.at[j]) for refs, buf in bufs] for j in range(4)]
    greet(zs + [mate])
    sent = [k.send(n2, N2.at[z], to) for to in zs]
    heres = [k.local(n2, N2.at[z])]
    for j, step in enumerate((0, 3, 1, 2)):
        yy, x2 = (y + step) % 4, (xx + step) % 4
        xh, xl = x2 // 2, x2 % 2
        for cp in loads[j]:
            cp.wait()
        heres.append(k.local(gb.at[j], G.at[(z + step) % 4]))
        places = [
            (b1.at[j], W13.at[c, yy, :, :, :, pl.ds(0, FZ)]),
            (b3.at[j], W13.at[c, :, xh, xl, :, pl.ds(FZ, FZ)]),
        ]
        for b in range(2):
            cols = pl.ds(pl.multiple_of(128 * (c * 8 + yy * 2 + b), 128), 128)
            places.append((bx.at[j, :, b], W2.at[:, pl.ds(0, 352), cols]))
        for b in range(4):
            cols = pl.ds(pl.multiple_of(128 * (c * 8 + b * 2 + xl), 128), 128)
            places.append((by.at[j, b], W2.at[xh, pl.ds(352, 352), cols]))
        for src, dst in places:
            sent.append(k.send(src, dst, mate))
            heres.append(k.local(src, dst))
    for cp in sent:
        cp.wait_recv()
    for cp in heres:
        cp.wait()
    k.close()


def dkv_kernel(dkv, R, ss, rs):
    q = coords()
    xx, xl, c = q["x"], q["xl"], q["c"]
    mate = device(q, c=1 - c)
    other = device(q, x=xx ^ 1)
    other_mate = device(q, x=xx ^ 1, c=1 - c)
    greet([mate, other, other_mate])
    k = Copies(ss, rs)
    near = k.send(dkv.at[xl, :, 1 - c], R.at[0], mate)
    far = [
        pltpu.make_async_remote_copy(
            src_ref=dkv.at[0, :, cc],
            dst_ref=R.at[1 + i],
            send_sem=ss.at[1 + i],
            recv_sem=rs.at[1 + i],
            device_id=to,
            device_id_type=MESH,
        )
        for i, (to, cc) in enumerate(((other, c), (other_mate, 1 - c)))
    ]

    @pl.when(xl == 1)
    def _():
        for cp in far:
            cp.start()
        for cp in far:
            cp.wait_send()

    @pl.when(xl == 0)
    def _():
        for cp in far:
            cp.wait_recv()

    near.wait_recv()
    k.close()


def spread_kernel(
    fa, fb, f2, fo, fq, gain, G1, G3, G2, GO, GQ, gain_out, s0, s1, s2, s3, s4, total, ss, rs
):
    q = coords()
    y, xx, xh, xl, z, c = q["y"], q["x"], q["xh"], q["xl"], q["z"], q["c"]
    zs, ys = ring(q, "z"), ring(q, "y")
    mate, other, cross = device(q, c=1 - c), device(q, x=xx ^ 1), device(q, x=3 - xx)
    greet(zs + ys + [mate, other, cross])
    k = Copies(ss, rs)
    gain_y = [k.send(gain.at[(y + s) % 4], s0.at[y], to) for s, to in zip((1, 3, 2), ys)]
    gain_here = k.local(gain.at[y], s0.at[y])
    rows = pl.ds(pl.multiple_of(128 * c + 64 * xl, 64), 64)
    pair = pl.ds(pl.multiple_of(128 * c, 128), 128)
    fz = FZ * z
    rest = SPLIT - FZ
    wide = [
        (fa.at[:, pl.ds(0, FZ)], G1.at[rows, pl.ds(pl.multiple_of(fz, 128), FZ)]),
        (fa.at[:, pl.ds(FZ, rest)], G3.at[rows, pl.ds(pl.multiple_of(fz, 128), rest)]),
        (fb, G3.at[rows, pl.ds(pl.multiple_of(fz + rest, 128), FZ - rest)]),
    ]
    leg_z = [k.send(src, dst, to) for src, dst in wide for to in zs]
    heres = [k.local(src, dst) for src, dst in wide]
    col = pl.ds(pl.multiple_of(128 * (c * 8 + z * 2 + xl), 128), 128)
    cols = pl.ds(pl.multiple_of(128 * (c * 8 + z * 2), 256), 256)
    half = pl.ds(pl.multiple_of(1024 * c, 1024), 1024)
    mq = pl.ds(pl.multiple_of(MZ * z, 128), MZ)
    tall = [(f2, G2.at[:, col]), (fo, GO.at[:, col]), (fq, GQ.at[rows, mq])]
    leg_x = [k.send(src, dst, other) for src, dst in tall]
    tall_here = [k.local(src, dst) for src, dst in tall]
    for cp in leg_x:
        cp.wait_recv()
    for cp in tall_here:
        cp.wait()
    parts = [G2.at[:, cols], GO.at[:, cols], GQ.at[pair, mq]]
    leg_xz = [k.send(part, part, to) for part in parts for to in zs]
    for cp in gain_y:
        cp.wait_recv()
    gain_here.wait()
    s1[0] = s0[0] + s0[1] + s0[2] + s0[3]
    cp = k.send(s1.at[0, 1 - xh], s1.at[1, 0], cross)
    cp.wait_recv()
    s2[z] = s1[0, xh] + s1[1, 0]
    gain_z = [k.send(s2.at[z], s2.at[z], to) for to in zs]
    for cp in gain_z:
        cp.wait_recv()
    s3[0] = s2[0] + s2[1] + s2[2] + s2[3]
    cp = k.send(s3.at[0], s3.at[1], other)
    cp.wait_recv()
    s4[0] = s3[0] + s3[1]
    cp = k.send(s4.at[0], s4.at[1], mate)
    cp.wait_recv()
    total[...] = s4[0] + s4[1]
    gain_done = k.local(total, gain_out)
    for cp in leg_z:
        cp.wait_recv()
    for cp in heres:
        cp.wait()
    leg_zx = [k.send(ref.at[rows], ref.at[rows], other) for ref in (G1, G3)]
    for cp in leg_xz:
        cp.wait_recv()
    parts = [G2.at[:, half], GO.at[:, half], GQ.at[pair]]
    last = [k.send(part, part, mate) for part in parts]
    for cp in leg_zx:
        cp.wait_recv()
    last += [k.send(ref.at[pair], ref.at[pair], mate) for ref in (G1, G3)]
    for cp in last:
        cp.wait_recv()
    gain_done.wait()
    k.close()


PARAMS = pltpu.CompilerParams(vmem_limit_bytes=VMEM_LIMIT)


def to_pieces(v):
    return jnp.concatenate(
        [v[:, 256 * d + 128 * c : 256 * d + 128 * c + 128] for c in range(2) for d in range(8)],
        axis=1,
    )


def from_pieces(v):
    return jnp.concatenate(
        [v[:, 1024 * c + 128 * d : 1024 * c + 128 * d + 128] for d in range(8) for c in range(2)],
        axis=1,
    )


def swapped(u):
    lane = lax.broadcasted_iota(jnp.int32, u.shape, 1)
    return jnp.where(lane % 64 < 32, pltpu.roll(u, 96, 1), pltpu.roll(u, 32, 1))


def project_kernel(x, gain, w, cosine, sine, n1, query, kv):
    xv = x[0].astype(F32)
    scale = lax.rsqrt(jnp.mean(xv * xv, axis=-1, keepdims=True) + EPS)
    normed = to_pieces((xv * scale * gain[...]).astype(BF))
    n1[0] = normed
    cos, sin = cosine[0], sine[0]
    for j in range(5):
        u = jnp.dot(normed, w[:, 128 * j : 128 * j + 128], preferred_element_type=F32)
        turned = u * cos + swapped(u) * sin
        if j < 4:
            query[0, :, 128 * j : 128 * j + 128] = turned.astype(BF)
        else:
            lane = lax.broadcasted_iota(jnp.int32, u.shape, 1)
            kv[0] = jnp.where(lane < HEAD_DIM, turned, u).astype(BF)


def project(x, gain, w, cosine, sine):
    chunk = lambda cols: pl.BlockSpec((1, TOK, cols), lambda i: (i, 0, 0))
    whole = lambda shape: pl.BlockSpec(shape, lambda i: (0,) * len(shape))
    return pl.pallas_call(
        project_kernel,
        name="project",
        cost_estimate=cost(7),
        grid=(RING,),
        in_specs=[chunk(D), whole((1, D)), whole((D, MZ)), chunk(128), chunk(128)],
        out_specs=[chunk(D), chunk(QZ), chunk(128)],
        out_shape=[
            jax.ShapeDtypeStruct((RING, TOK, D), BF),
            jax.ShapeDtypeStruct((RING, TOK, QZ), BF),
            jax.ShapeDtypeStruct((RING, TOK, 128), BF),
        ],
        compiler_params=PARAMS,
    )(x, gain, w, cosine, sine)


def stacked_low(tiles):
    out = []
    for pair in range(4):
        tile = tiles[:, 128 * pair : 128 * pair + 128].astype(F32)
        lane = lax.broadcasted_iota(jnp.int32, tile.shape, 1)
        out.append(jnp.where(lane < HEAD_DIM, tile, 0.0))
        out.append(jnp.where(lane < HEAD_DIM, pltpu.roll(tile, 64, 1), 0.0))
    return jnp.concatenate(out, axis=0)


def stacked_high(tiles):
    out = []
    for pair in range(4):
        tile = tiles[:, 128 * pair : 128 * pair + 128].astype(F32)
        lane = lax.broadcasted_iota(jnp.int32, tile.shape, 1)
        out.append(jnp.where(lane >= HEAD_DIM, pltpu.roll(tile, 64, 1), 0.0))
        out.append(jnp.where(lane >= HEAD_DIM, tile, 0.0))
    return jnp.concatenate(out, axis=0)


def unstacked(v):
    tiles = []
    for pair in range(4):
        both = jnp.concatenate(
            [v[:, 256 * pair : 256 * pair + 128], v[:, 256 * pair + 128 : 256 * pair + 256]],
            axis=0,
        )
        tiles.append(both.T)
    return tiles


def nt(a, b):
    return lax.dot_general(a, b, (((1,), (1,)), ((), ())), preferred_element_type=F32)


def tn(a, b):
    return lax.dot_general(a, b, (((0,), (0,)), ((), ())), preferred_element_type=F32)


def chunk_scores(keys, stacked, kc, chunk, start):
    raw = nt(keys, stacked)
    key = kc * TOK + lax.broadcasted_iota(jnp.int32, raw.shape, 0)
    query = chunk * TOK + lax.broadcasted_iota(jnp.int32, raw.shape, 1) % TOK
    return jnp.where((key <= query) & (key >= start), raw, -1e30)


def attend_kernel(info, query, kv, start, out, logsum):
    i = pl.program_id(0)
    low, chunk = info[0, i], info[1, i]
    stacked = (stacked_low(query[0]) * (1.0 / HEAD_DIM**0.5)).astype(BF)
    starts = jnp.concatenate([start[0]] * GROUP, axis=1)

    def step(kc, carry):
        top, summed, total = carry
        keys = kv[kc]
        scores = chunk_scores(keys, stacked, kc, chunk, starts)
        new_top = jnp.maximum(top, jnp.max(scores, axis=0, keepdims=True))
        weights = jnp.exp(scores - new_top)
        fade = jnp.exp(top - new_top)
        summed = summed * fade + jnp.sum(weights, axis=0, keepdims=True)
        part = tn(keys, weights.astype(BF))
        return new_top, summed, total * fade + part[HEAD_DIM:]

    rows = GROUP * TOK
    carry = (jnp.full((1, rows), -1e30, F32), jnp.zeros((1, rows), F32), jnp.zeros((64, rows), F32))
    top, summed, total = lax.fori_loop(low, chunk + 1, step, carry)
    for pair, tile in enumerate(unstacked(total / summed)):
        out[0, :, 128 * pair : 128 * pair + 128] = tile.astype(BF)
    logsum[0] = top + jnp.log(summed)


def attend(info, query, kv, start):
    chunk = lambda r, cols: pl.BlockSpec((1, r, cols), lambda i, s: (i, 0, 0))
    return pl.pallas_call(
        attend_kernel,
        name="attend",
        cost_estimate=cost(12),
        grid_spec=pltpu.PrefetchScalarGridSpec(
            num_scalar_prefetch=1,
            grid=(RING,),
            in_specs=[
                chunk(TOK, QZ),
                pl.BlockSpec((16, TOK, 128), lambda i, s: (0, 0, 0)),
                chunk(1, TOK),
            ],
            out_specs=[chunk(TOK, QZ), chunk(1, GROUP * TOK)],
        ),
        out_shape=[
            jax.ShapeDtypeStruct((RING, TOK, QZ), BF),
            jax.ShapeDtypeStruct((RING, 1, GROUP * TOK), F32),
        ],
        compiler_params=PARAMS,
    )(info, query, kv, start)


def attend_back_kernel(
    info, query, kv, start, out, grad_out, logsum, cosine, sine, dquery, dkv, total
):
    i = pl.program_id(0)
    low, chunk = info[0, i], info[1, i]
    stacked = (stacked_low(query[0]) * (1.0 / HEAD_DIM**0.5)).astype(BF)
    grads = stacked_high(grad_out[0]).astype(BF)
    starts = jnp.concatenate([start[0]] * GROUP, axis=1)
    lse = logsum[0]
    deltas = []
    for pair in range(4):
        cols = slice(128 * pair, 128 * pair + 128)
        prod = (out[0, :, cols].astype(F32) * grad_out[0, :, cols].astype(F32)).T
        deltas.append(jnp.sum(prod[:HEAD_DIM], axis=0, keepdims=True))
        deltas.append(jnp.sum(prod[HEAD_DIM:], axis=0, keepdims=True))
    delta = jnp.concatenate(deltas, axis=1)

    @pl.when(i == 0)
    def _():
        total[...] = jnp.zeros_like(total)

    def step(kc, dq):
        keys = kv[kc]
        scores = chunk_scores(keys, stacked, kc, chunk, starts)
        probs = jnp.exp(scores - lse)
        grad_probs = nt(keys, grads)
        grad_scores = (probs * (grad_probs - delta)).astype(BF)
        total[kc] += jnp.dot(grad_scores, stacked, preferred_element_type=F32) + jnp.dot(
            probs.astype(BF), grads, preferred_element_type=F32
        )
        return dq + tn(keys, grad_scores)[:HEAD_DIM]

    dq = lax.fori_loop(low, chunk + 1, step, jnp.zeros((64, GROUP * TOK), F32))
    cos, sin = cosine[0], sine[0]
    for pair, tile in enumerate(unstacked(dq)):
        tile = tile * (1.0 / HEAD_DIM**0.5)
        dquery[0, :, 128 * pair : 128 * pair + 128] = (tile * cos - swapped(tile) * sin).astype(BF)

    @pl.when(i == RING - 1)
    def _():
        dkv[...] = total[...].astype(BF)


def attend_back(info, query, kv, start, out, grad_out, logsum, cosine, sine):
    chunk = lambda r, cols: pl.BlockSpec((1, r, cols), lambda i, s: (i, 0, 0))
    whole = pl.BlockSpec((16, TOK, 128), lambda i, s: (0, 0, 0))
    return pl.pallas_call(
        attend_back_kernel,
        name="attend_back",
        cost_estimate=cost(15),
        grid_spec=pltpu.PrefetchScalarGridSpec(
            num_scalar_prefetch=1,
            grid=(RING,),
            in_specs=[
                chunk(TOK, QZ),
                whole,
                chunk(1, TOK),
                chunk(TOK, QZ),
                chunk(TOK, QZ),
                chunk(1, GROUP * TOK),
                chunk(TOK, 128),
                chunk(TOK, 128),
            ],
            out_specs=[chunk(TOK, QZ), whole],
            scratch_shapes=[pltpu.VMEM((16, TOK, 128), F32)],
        ),
        out_shape=[
            jax.ShapeDtypeStruct((RING, TOK, QZ), BF),
            jax.ShapeDtypeStruct((16, TOK, 128), BF),
        ],
        compiler_params=PARAMS,
    )(info, query, kv, start, out, grad_out, logsum, cosine, sine)


def dmixed_kernel(xl, dkv, received, cosine, sine, out):
    t = dkv[...].astype(F32) + received[0].astype(F32)
    far = received[1].astype(F32) + received[2].astype(F32)
    t = jnp.where(xl[0] == 0, t + far, t)
    for i in range(RING):
        w = t[i]
        lane = lax.broadcasted_iota(jnp.int32, w.shape, 1)
        out[i] = jnp.where(lane < HEAD_DIM, w * cosine[i] - swapped(w) * sine[i], w).astype(BF)


def dmixed_kv(xl, dkv, received, cosine, sine):
    vmem = pl.BlockSpec(memory_space=pltpu.VMEM)
    return pl.pallas_call(
        dmixed_kernel,
        name="dmixed_kv",
        cost_estimate=cost(2),
        in_specs=[pl.BlockSpec(memory_space=pltpu.SMEM)] + [vmem] * 4,
        out_specs=vmem,
        out_shape=jax.ShapeDtypeStruct((RING, TOK, 128), BF),
        compiler_params=PARAMS,
    )(xl, dkv, received, cosine, sine)


def resid_kernel(x, a, b, c, d, gain, h, n2):
    total = x[...].astype(F32) + (
        (a[...].astype(F32) + b[...].astype(F32)) + (c[...].astype(F32) + d[...].astype(F32))
    )
    h[...] = total
    scale = lax.rsqrt(jnp.mean(total * total, axis=-1, keepdims=True) + EPS)
    n2[...] = to_pieces((total * scale * gain[...]).astype(BF))


def resid(x, parts, gain):
    return pl.pallas_call(
        resid_kernel,
        name="resid",
        cost_estimate=cost(3),
        out_shape=[jax.ShapeDtypeStruct((TOK, D), F32), jax.ShapeDtypeStruct((TOK, D), BF)],
        compiler_params=PARAMS,
    )(x, *parts, gain)


def rms_back(v, gain, grad):
    scale = lax.rsqrt(jnp.mean(v * v, axis=-1, keepdims=True) + EPS)
    unit = v * scale
    gain_grad = jnp.sum(grad * unit, axis=0, keepdims=True)
    inner = grad * gain
    return scale * (inner - unit * jnp.mean(inner * unit, axis=-1, keepdims=True)), gain_grad


def norm_back_kernel(v, base, a, b, c, d, gain, grad, *outs):
    dn = from_pieces(
        (a[...].astype(F32) + b[...].astype(F32)) + (c[...].astype(F32) + d[...].astype(F32))
    )
    back, gain_grad = rms_back(v[...].astype(F32), gain[...], dn)
    total = base[...].astype(F32) + back
    grad[...] = total
    outs[-1][...] = gain_grad
    if len(outs) == 2:
        outs[0][...] = total.astype(BF)


def norm_back(v, base, parts, gain, rounded):
    shapes = [jax.ShapeDtypeStruct((TOK, D), F32)]
    if rounded:
        shapes.append(jax.ShapeDtypeStruct((TOK, D), BF))
    shapes.append(jax.ShapeDtypeStruct((1, D), F32))
    return pl.pallas_call(
        norm_back_kernel,
        name="norm_back",
        cost_estimate=cost(4),
        out_shape=shapes,
        compiler_params=PARAMS,
    )(v, base, *parts, gain)


def pick(v, index, axis=0):
    return lax.dynamic_index_in_dim(v, index, axis, keepdims=False)


def scatter(v, q, axis, dim):
    at = q[axis]
    got = [move(pick(v, (at + s) % 4, dim), axis, s) for s in (1, 3, 2)]
    return [pick(v, at, dim)] + got


def add(parts):
    a, b, c, d = (p.astype(F32) for p in parts)
    return ((a + b) + (c + d)).astype(BF)


def scatter_cols(v, q, axis, width):
    at = q[axis]
    cut = lambda j: lax.dynamic_slice_in_dim(v, j * width, width, 1)
    return [cut(at)] + [move(cut((at + s) % 4), axis, s) for s in (1, 3, 2)]


def scatter_quarters(v, q, rows):
    cut = lambda j: lax.dynamic_slice(v, ((j // 2) * rows, (j % 2) * 128), (rows, 128))
    at = q["x"]
    return [cut(at)] + [move(cut((at + s) % 4), "x", s) for s in (1, 3, 2)]


def dot(a, b):
    return jnp.dot(a, b, preferred_element_type=F32)


def body(tokens, segments, cotangent, norm_attn, norm_ffn, wqkv, wo, w1, w3, w2):
    q = coords()
    y, xx, xl, z, c = q["y"], q["x"], q["xl"], q["z"], q["c"]
    x = tokens[0]
    g = cotangent[0]
    seg = jnp.broadcast_to(segments, (8, TOK))
    gn = jnp.concatenate(
        [jnp.broadcast_to(v[None], (16, 256)) for v in (norm_attn, norm_ffn)], axis=0
    )
    heads = wqkv[:, :QDIM].reshape(256, 4, QZ)
    kz = wqkv[:, QDIM : QDIM + KVDIM].reshape(256, 4, HEAD_DIM)
    vz = wqkv[:, QDIM + KVDIM :].reshape(256, 4, HEAD_DIM)
    wq = jnp.concatenate([heads, kz, vz], axis=2).reshape(256, 4 * MZ)

    X, SEG, GN, WQ, WO, A1, A3, AX, AY = talk(
        fetch_kernel,
        "fetch",
        1,
        30,
        80,
        (x, seg, gn, wq, wo, w1, w3, w2),
        [
            ((RING, TOK, D), BF),
            ((2, 4, 2, 8, TOK), jnp.int32),
            ((4, 2, 32, 256), BF),
            ((2, 4, 2, 2, 64, MZ), BF),
            ((2, 256, D), BF),
            ((2, 2, 64, FZ), BF),
            ((4, 64, FZ), BF),
            ((2, 2, 352, 128), BF),
            ((4, 352, 128), BF),
        ],
        scratch=[
            pltpu.VMEM((704, 128), BF),
            pltpu.VMEM((256, 128), BF),
            pltpu.VMEM((64, MZ), BF),
            pltpu.VMEM((64, FZ), BF),
            pltpu.VMEM((64, FZ), BF),
        ],
        near=(0, 1, 2),
    )
    legs = lambda v, axis: [v] + [move(v, axis, s) for s in (1, 3, 2)]
    a1, a3 = legs(A1, "y"), legs(A3, "x")
    ax, ay = legs(AX, "y"), legs(AY, "x")
    gs = legs(g, "z")

    docs = SEG[:, :, :, 0, :].reshape(16 * TOK)
    mine = pick(pick(SEG[:, :, :, 0, :], xl, 0), c, 1)
    chunks = xl * 8 + 2 * jnp.arange(4, dtype=jnp.int32) + c
    start = jnp.sum((docs[None, None, :] < mine[:, :, None]).astype(jnp.int32), axis=2)
    index = chunks[:, None] * TOK + jnp.arange(TOK, dtype=jnp.int32)[None]
    place = (index - start).astype(F32)
    lane = jnp.arange(128)
    freq = THETA ** (-(lane % 32).astype(F32) * 2.0 / HEAD_DIM)
    angle = place[:, :, None] * freq[None, None, :]
    cosine = jnp.cos(angle)
    sine = jnp.sin(angle) * jnp.where(lane % 64 < 32, -1.0, 1.0)
    info = jnp.stack([jnp.min(start, axis=1) // TOK, chunks])
    start = start[:, None, :]
    gain_attn = GN[:, :, 0, :].reshape(1, D).astype(F32)
    gain_ffn = GN[:, :, 16, :].reshape(1, D).astype(F32)

    WQ = WQ.reshape(D, MZ)
    WO = WO.reshape(QZ, D)
    n1, query, kv = project(X, gain_attn, WQ, cosine, sine)
    (KV,) = talk(
        kv_kernel, "kv", 2, 7, 4, (kv,), [((2, 4, 2, TOK, 128), BF)], near=(0,)
    )
    KV = KV.reshape(16, TOK, 128)
    heads_out, logsum = attend(info, query, KV, start)
    o = heads_out.reshape(RING * TOK, QZ)
    part = dot(o, WO).astype(BF).reshape(RING, TOK, D)
    h, n2 = resid(x, scatter(part, q, "z", 0), gain_ffn)

    N2, G, W13, W2 = talk(
        assemble_kernel,
        "assemble",
        3,
        27,
        110,
        (n2, *gs, *a1, *a3, *ax, *ay),
        [
            ((RING, TOK, D), BF),
            ((RING, TOK, D), BF),
            ((2, 4, 2, 2, 64, 2 * FZ), BF),
            ((2, 704, D), BF),
        ],
        scratch=[
            pltpu.VMEM((4, TOK, D), BF),
            pltpu.VMEM((4, 2, 2, 64, FZ), BF),
            pltpu.VMEM((4, 4, 64, FZ), BF),
            pltpu.VMEM((4, 2, 2, 352, 128), BF),
            pltpu.VMEM((4, 4, 352, 128), BF),
        ],
        near=(0,),
    )
    N2, G = N2.reshape(RING * TOK, D), G.reshape(RING * TOK, D)
    W13, W2 = W13.reshape(D, 2 * FZ), W2.reshape(FZ, D)
    gate, up = dot(N2, W13[:, :FZ]), dot(N2, W13[:, FZ:])
    hidden = (jax.nn.silu(gate) * up).astype(BF)
    out_part = dot(hidden, W2).astype(BF).reshape(RING, TOK, D)
    dhid = jnp.einsum("td,fd->tf", G, W2, preferred_element_type=F32)
    sigma = jax.nn.sigmoid(gate)
    dgate = (dhid * up * sigma * (1.0 + gate * (1.0 - sigma))).astype(BF)
    dup = (dhid * gate * sigma).astype(BF)
    both = jnp.concatenate([dgate, dup], axis=1)
    dn2 = jnp.einsum("tf,df->td", both, W13, preferred_element_type=F32)
    dn2 = dn2.astype(BF).reshape(RING, TOK, D)
    dn2_parts = scatter(dn2, q, "z", 0)

    half = lambda v, j: lax.dynamic_slice_in_dim(v, 1024 * j, 1024, 1)
    outer = lambda a, b: jnp.einsum("ta,tb->ab", a, b, preferred_element_type=F32)
    other13 = move(outer(half(N2, 1 - c), both).astype(BF), "c", 1)
    other2 = move(outer(hidden, half(G, 1 - c)).astype(BF), "c", 1)
    sum13 = (outer(half(N2, c), both) + other13.astype(F32)).astype(BF)
    sum2 = (outer(hidden, half(G, c)) + other2.astype(F32)).astype(BF)
    sum13 = sum13.reshape(4, 4, 64, 2 * FZ)
    fa = add(scatter(sum13[..., :SPLIT], q, "x", 1))
    fa = add(scatter(fa, q, "y", 0))
    fb = add(scatter(sum13[..., SPLIT:], q, "y", 0))
    fb = add(scatter(fb, q, "x", 0))
    f2 = add(scatter_cols(sum2, q, "y", 256))
    f2 = add(scatter_quarters(f2, q, 704))
    f2 = lax.ppermute(f2, ("dp", "ctx"), swap_pairs())

    dh, dhb, gain2 = norm_back(h, g, dn2_parts, gain_ffn, True)
    (DH,) = talk(
        gather_kernel, "gather", 4, 27, 4, (dhb,), [((RING, TOK, D), BF)], near=(0,)
    )
    DH = DH.reshape(RING * TOK, D)
    dheads = jnp.einsum("td,qd->tq", DH, WO, preferred_element_type=F32).astype(BF)
    dquery, dkv = attend_back(
        info, query, KV, start, heads_out, dheads.reshape(RING, TOK, QZ), logsum, cosine, sine
    )
    dkv = dkv.reshape(2, 4, 2, TOK, 128)
    (received,) = talk(
        dkv_kernel, "dkv", 5, 8, 4, (dkv,), [((3, 4, TOK, 128), BF)]
    )
    own_dkv = pick(pick(dkv, xl, 0), c, 1)
    dkv_rot = dmixed_kv(xl[None], own_dkv, received, cosine, sine)
    dmixed = jnp.concatenate([dquery, dkv_rot], axis=2).reshape(RING * TOK, MZ)
    dn1 = jnp.einsum("tc,dc->td", dmixed, WQ, preferred_element_type=F32)
    dn1 = dn1.astype(BF).reshape(RING, TOK, D)
    input_grad, gain1 = norm_back(x, dh, scatter(dn1, q, "z", 0), gain_attn, False)

    n1 = n1.reshape(RING * TOK, D)
    other_q = move(outer(half(n1, 1 - c), dmixed).astype(BF), "c", 1)
    other_o = move(outer(o, half(DH, 1 - c)).astype(BF), "c", 1)
    sum_q = (outer(half(n1, c), dmixed) + other_q.astype(F32)).astype(BF)
    sum_o = (outer(o, half(DH, c)) + other_o.astype(F32)).astype(BF)
    fq = add(scatter(sum_q.reshape(4, 4, 64, MZ), q, "x", 1))
    fq = add(scatter(fq, q, "y", 0))
    fo = add(scatter_cols(sum_o, q, "y", 256))
    fo = add(scatter_quarters(fo, q, 256))
    fo = lax.ppermute(fo, ("dp", "ctx"), swap_pairs())

    gains = jnp.concatenate([gain1, gain2], axis=0).reshape(2, 8, 256).transpose(1, 0, 2)
    gains = jnp.pad(gains, ((0, 0), (0, 6), (0, 0))).reshape(4, 2, 8, 256)
    small = (8, 256)
    G1, G3, G2, GO, GQ, gain_out = talk(
        spread_kernel,
        "spread",
        6,
        50,
        60,
        (fa, fb, f2, fo, fq, gains),
        [
            ((256, 4 * FZ), BF),
            ((256, 4 * FZ), BF),
            ((704, D), BF),
            ((256, D), BF),
            ((256, 4 * MZ), BF),
            (small, F32),
        ],
        scratch=[
            pltpu.VMEM((4, 2) + small, F32),
            pltpu.VMEM((2, 2) + small, F32),
            pltpu.VMEM((4,) + small, F32),
            pltpu.VMEM((2,) + small, F32),
            pltpu.VMEM((2,) + small, F32),
            pltpu.VMEM(small, F32),
        ],
        near=(0, 1, 2, 3, 4, 5),
    )
    GQ = GQ.astype(F32).reshape(256, 4, MZ)
    flat = lambda v: v.reshape(256, -1)
    grad_qkv = jnp.concatenate(
        [flat(GQ[:, :, :QZ]), flat(GQ[:, :, QZ : QZ + 64]), flat(GQ[:, :, QZ + 64 :])], axis=1
    )
    out_parts = [p.astype(F32) for p in scatter(out_part, q, "z", 0)]
    output = h + ((out_parts[0] + out_parts[1]) + (out_parts[2] + out_parts[3]))
    return (
        output[None],
        input_grad[None],
        gain_out[0],
        gain_out[1],
        grad_qkv,
        GO.astype(F32),
        G1.astype(F32),
        G3.astype(F32),
        G2.astype(F32),
    )


def solution(mesh):
    rows = P("dp", None)
    acts = P("dp", "ctx", None)
    return jax.shard_map(
        body,
        mesh=mesh,
        in_specs=(acts, P("dp", "ctx"), acts, P("dp"), P("dp"), rows, rows, rows, rows, rows),
        out_specs=(acts, acts, P("dp"), P("dp"), rows, rows, rows, rows, rows),
        check_vma=False,
    )
```

```python
import functools

import jax
import jax.numpy as jnp
from jax import lax
from jax.experimental import pallas as pl
from jax.experimental.pallas import tpu as pltpu
from jax.sharding import PartitionSpec as P

D = 2048
HEAD_DIM = 64
TOK = 128
RING = 4
QDIM = 2048
KVDIM = 256
GROUP = 8
QZ = 512
MZ = 640
FZ = 1408
SPLIT = 2048
EPS = 1e-05
THETA = 10000.0
MESH = pl.DeviceIdType.MESH
VMEM_LIMIT = 56 << 20
BF = jnp.bfloat16
F32 = jnp.float32
ANY = pl.BlockSpec(memory_space=pl.ANY)
VMEM = pl.BlockSpec(memory_space=pltpu.VMEM)


def coords():
    dp, ctx = lax.axis_index("dp"), lax.axis_index("ctx")
    y, xh = dp // 2, dp % 2
    xl, z, c = ctx // 8, (ctx // 2) % 4, ctx % 2
    return dict(y=y, x=xh * 2 + xl, xh=xh, xl=xl, z=z, c=c)


def device(q, **change):
    r = {k: change.get(k, q[k]) for k in ("y", "x", "z", "c")}
    return (r["y"] * 2 + r["x"] // 2, (r["x"] % 2) * 8 + r["z"] * 2 + r["c"])


def ring(q, axis):
    return [device(q, **{axis: (q[axis] + s) % 4}) for s in (1, 3, 2)]


def shift_pairs(axis, by):
    size = 2 if axis == "c" else 4
    pairs = []
    for y in range(4):
        for x in range(4):
            for z in range(4):
                for c in range(2):
                    q = dict(y=y, x=x, z=z, c=c)
                    pairs.append((device(q), device(q, **{axis: (q[axis] + by) % size})))
    return [(a[0] * 16 + a[1], b[0] * 16 + b[1]) for a, b in pairs]


def swap_pairs():
    pairs = []
    for y in range(4):
        for x in range(4):
            for z in range(4):
                for c in range(2):
                    q = dict(y=y, x=x, z=z, c=c)
                    pairs.append((device(q), device(q, y=z, z=y)))
    return [(a[0] * 16 + a[1], b[0] * 16 + b[1]) for a, b in pairs]


def move(v, axis, by):
    return lax.ppermute(v, ("dp", "ctx"), shift_pairs(axis, by))


class Copies:
    def __init__(self, send_sems, recv_sems):
        self.send_sems, self.recv_sems, self.n, self.open = send_sems, recv_sems, 0, []

    def send(self, src, dst, to):
        cp = pltpu.make_async_remote_copy(
            src_ref=src,
            dst_ref=dst,
            send_sem=self.send_sems.at[self.n],
            recv_sem=self.recv_sems.at[self.n],
            device_id=to,
            device_id_type=MESH,
        )
        cp.start()
        self.n += 1
        self.open.append(cp.wait_send)
        return cp

    def local(self, src, dst):
        cp = pltpu.make_async_copy(src, dst, self.send_sems.at[self.n])
        cp.start()
        self.n += 1
        return cp

    def close(self):
        for wait in self.open:
            wait()


def greet(targets, q=None):
    barrier = pltpu.get_barrier_semaphore()
    for to in targets:
        pl.semaphore_signal(barrier, inc=1, device_id=to, device_id_type=MESH)
    if q is None:
        pl.semaphore_wait(barrier, len(targets))
    else:
        y, z = q["y"], q["z"]

        @pl.when(y != z)
        def _():
            to = device(q, y=z, z=y)
            pl.semaphore_signal(barrier, inc=1, device_id=to, device_id_type=MESH)

        pl.semaphore_wait(barrier, len(targets) + (y != z).astype(jnp.int32))


TOP, LOW = pl.ds(0, TOK // 2), pl.ds(TOK // 2, TOK // 2)


def gather_start(k, q, src, dst):
    z = q["z"]
    up, down = device(q, z=(z + 1) % 4), device(q, z=(z + 3) % 4)
    first = k.send(src.at[TOP], dst.at[z, TOP], up)
    second = k.send(src.at[LOW], dst.at[z, LOW], down)
    rest = [
        k.send(src.at[LOW], dst.at[z, LOW], up),
        k.send(src.at[TOP], dst.at[z, TOP], down),
    ]
    return first, second, rest, k.local(src, dst.at[z])


def gather_pass(k, q, dst, state):
    z = q["z"]
    below, above = (z + 3) % 4, (z + 1) % 4
    first, second, rest, here = state
    first.wait_recv()
    rest.append(k.send(dst.at[below, TOP], dst.at[below, TOP], device(q, z=above)))
    second.wait_recv()
    rest.append(k.send(dst.at[above, LOW], dst.at[above, LOW], device(q, z=below)))


def gather_end(state):
    for cp in state[2]:
        cp.wait_recv()
    state[3].wait()


def sum_start(k, q, part, pass_top, pass_low, below, above):
    z = q["z"]
    up, down = device(q, z=(z + 1) % 4), device(q, z=(z + 3) % 4)
    far = (z + 2) % 4
    return (
        k.send(part.at[far, TOP], pass_top, up),
        k.send(part.at[far, LOW], pass_low, down),
        [
            k.send(part.at[(z + 1) % 4, LOW], below.at[LOW], up),
            k.send(part.at[(z + 3) % 4, TOP], above.at[TOP], down),
        ],
    )


def sum_pass(k, q, part, pass_top, pass_low, send_top, send_low, below, above, state):
    z = q["z"]
    up, down = device(q, z=(z + 1) % 4), device(q, z=(z + 3) % 4)
    first, second, rest = state
    first.wait_recv()
    send_top[...] = (pass_top[...].astype(F32) + part[(z + 1) % 4, TOP].astype(F32)).astype(BF)
    rest.append(k.send(send_top, below.at[TOP], up))
    second.wait_recv()
    send_low[...] = (pass_low[...].astype(F32) + part[(z + 3) % 4, LOW].astype(F32)).astype(BF)
    rest.append(k.send(send_low, above.at[LOW], down))


def sum_end(state):
    for cp in state[2]:
        cp.wait_recv()


HALF = (TOK // 2, D)


def turn(k, q, moves):
    y, z = q["y"], q["z"]
    swap = device(q, y=z, z=y)
    pairs = []
    for src, dst in moves:
        n = k.n
        k.n += 1
        remote = pltpu.make_async_remote_copy(
            src_ref=src,
            dst_ref=dst,
            send_sem=k.send_sems.at[n],
            recv_sem=k.recv_sems.at[n],
            device_id=swap,
            device_id_type=MESH,
        )
        pairs.append((remote, pltpu.make_async_copy(src, dst, k.send_sems.at[n])))

    @pl.when(y != z)
    def _():
        for remote, _ in pairs:
            remote.start()

    @pl.when(y == z)
    def _():
        for _, here in pairs:
            here.start()

    def wait():
        @pl.when(y != z)
        def _():
            for remote, _ in pairs:
                remote.wait_recv()
                remote.wait_send()

        @pl.when(y == z)
        def _():
            for _, here in pairs:
                here.wait()

    return wait


def cost(us):
    return pl.CostEstimate(flops=int(us * 1e9), bytes_accessed=0, transcendentals=0)


def talk(kernel, name, cid, us, copies, ins, outs, scratch=(), near=(), near_out=()):
    return pl.pallas_call(
        kernel,
        name=name,
        out_shape=[jax.ShapeDtypeStruct(s, t) for s, t in outs],
        in_specs=[VMEM if i in near else ANY for i in range(len(ins))],
        out_specs=[VMEM if i in near_out else ANY for i in range(len(outs))],
        scratch_shapes=[
            *scratch,
            pltpu.SemaphoreType.DMA((copies,)),
            pltpu.SemaphoreType.DMA((copies,)),
        ],
        cost_estimate=cost(us),
        compiler_params=pltpu.CompilerParams(
            collective_id=cid, has_side_effects=True, vmem_limit_bytes=VMEM_LIMIT
        ),
    )(*ins)


def fetch_kernel(
    x, seg, gn, wq, wo, w1, w3, X, SEG, GN, WQ, WO, A1, A3, TO, QP, P1, P3, ss, rs
):
    q = coords()
    y, xx, xh, xl, z, c = q["y"], q["x"], q["xh"], q["xl"], q["z"], q["c"]
    zs, ys, xs = ring(q, "z"), ring(q, "y"), ring(q, "x")
    mate = device(q, c=1 - c)
    other = device(q, x=xx ^ 1)
    other_mate = device(q, x=xx ^ 1, c=1 - c)
    k = Copies(ss, rs)
    rows = pl.ds(pl.multiple_of(128 * c + 64 * xl, 64), 64)
    qcols = pl.ds(pl.multiple_of(MZ * z, 128), MZ)
    fcols = pl.ds(pl.multiple_of(FZ * z, 128), FZ)
    loads = [
        k.local(wq.at[rows, qcols], QP),
        k.local(w1.at[rows, fcols], P1),
        k.local(w3.at[rows, fcols], P3),
    ]
    greet(zs + ys + xs + [mate, other_mate], q)
    piece = pl.ds(pl.multiple_of(128 * (c * 8 + z * 2 + xl), 128), 128)
    turned = turn(k, q, [(wo.at[:, piece], TO)])
    for cp in loads:
        cp.wait()
    top, low = pl.ds(0, 32), pl.ds(32, 32)
    q_top = [k.send(QP.at[top], WQ.at[c, y, xh, xl, top], to) for to in xs]
    q_low = [k.send(QP.at[low], WQ.at[c, y, xh, xl, low], to) for to in ys]
    q_here = k.local(QP, WQ.at[c, y, xh, xl])
    seg_z = [k.send(seg, SEG.at[xl, z, c], to) for to in zs]
    seg_here = k.local(seg, SEG.at[xl, z, c])
    gn_y = [k.send(gn, GN.at[y, xh], to) for to in ys]
    gn_here = k.local(gn, GN.at[y, xh])
    x_state = gather_start(k, q, x, X)
    turned()
    ocol = pl.ds(pl.multiple_of(128 * (c * 8 + y * 2 + xl), 128), 128)
    o1 = [k.send(TO, WO.at[xh, :, ocol], to) for to in xs]
    o1_here = k.local(TO, WO.at[xh, :, ocol])
    q_here.wait()
    for cp in q_top:
        cp.wait_recv()
    part = WQ.at[c, y, :, :, top]
    q2 = [k.send(part, part, to) for to in ys]
    for cp in q_low:
        cp.wait_recv()
    part = WQ.at[c, :, xh, xl, low]
    q2 += [k.send(part, part, to) for to in xs]
    for cp in o1:
        cp.wait_recv()
    o1_here.wait()
    part = WO.at[:, :, pl.ds(pl.multiple_of(128 * (c * 8 + y * 2), 256), 256)]
    o2 = [k.send(part, part, to) for to in ys]
    a1 = [k.send(P1, A1.at[xh, xl], to) for to in xs]
    a3 = [k.send(P3, A3.at[y], to) for to in ys]
    heres = [k.local(P1, A1.at[xh, xl]), k.local(P3, A3.at[y])]
    gather_pass(k, q, X, x_state)
    for cp in seg_z:
        cp.wait_recv()
    seg_here.wait()
    part = SEG.at[xl, :, c]
    seg2 = [k.send(part, part, to) for to in (mate, other, other_mate)]
    for cp in gn_y:
        cp.wait_recv()
    gn_here.wait()
    gn2 = k.send(GN.at[:, xh], GN.at[:, xh], device(q, x=3 - xx))
    for cp in q2:
        cp.wait_recv()
    q3 = k.send(WQ.at[c], WQ.at[c], mate)
    for cp in o2:
        cp.wait_recv()
    part = WO.at[:, :, pl.ds(pl.multiple_of(1024 * c, 1024), 1024)]
    o3 = k.send(part, part, mate)
    for cp in a1 + a3 + seg2 + [gn2, q3, o3]:
        cp.wait_recv()
    for cp in heres:
        cp.wait()
    gather_end(x_state)
    k.close()


def kv_kernel(kv, KV, ss, rs):
    q = coords()
    xx, xl, c = q["x"], q["xl"], q["c"]
    mate = device(q, c=1 - c)
    other = device(q, x=xx ^ 1)
    greet([mate, other])
    k = Copies(ss, rs)
    here = k.local(kv, KV.at[xl, :, c])
    near = k.send(kv, KV.at[xl, :, c], mate)
    far = pltpu.make_async_remote_copy(
        src_ref=kv,
        dst_ref=KV.at[0, :, c],
        send_sem=ss.at[2],
        recv_sem=rs.at[2],
        device_id=other,
        device_id_type=MESH,
    )
    on = pltpu.make_async_remote_copy(
        src_ref=KV.at[0, :, c],
        dst_ref=KV.at[0, :, c],
        send_sem=ss.at[3],
        recv_sem=rs.at[3],
        device_id=mate,
        device_id_type=MESH,
    )

    @pl.when(xl == 0)
    def _():
        far.start()
        far.wait_send()

    @pl.when(xl == 1)
    def _():
        far.wait_recv()
        on.start()
        on.wait_recv()
        on.wait_send()

    here.wait()
    near.wait_recv()
    k.close()


def middle_kernel(*refs):
    part, x, gain, t2 = refs[:4]
    a1, a3, gs = refs[4:7], refs[7:10], refs[10:14]
    N2, H, G, W13, W2 = refs[14:19]
    pass_top, pass_low, send_top, send_low, below, above, n2, b1, b3, gb, ss, rs = refs[19:]
    q = coords()
    y, xx, xh, xl, z, c = q["y"], q["x"], q["xh"], q["xl"], q["z"], q["c"]
    ys, xs = ring(q, "y"), ring(q, "x")
    up, down = device(q, z=(z + 1) % 4), device(q, z=(z + 3) % 4)
    mate = device(q, c=1 - c)
    k = Copies(ss, rs)
    loads = [
        [k.local(a1[j], b1.at[j]), k.local(a3[j], b3.at[j])] for j in range(3)
    ] + [[k.local(gs[j], gb.at[j]) for j in range(4)]]
    greet(ys + xs + [up, down, mate])
    state = sum_start(k, q, part, pass_top, pass_low, below, above)
    col = pl.ds(pl.multiple_of(128 * (c * 8 + y * 2 + xl), 128), 128)
    t_top, t_low = pl.ds(0, 352), pl.ds(352, 352)
    w2x = [k.send(t2.at[t_top], W2.at[xh, t_top, col], to) for to in xs]
    w2y = [k.send(t2.at[t_low], W2.at[xh, t_low, col], to) for to in ys]
    w2_here = k.local(t2, W2.at[xh, :, col])
    f1, f3 = pl.ds(0, FZ), pl.ds(FZ, FZ)
    for cp in loads[0]:
        cp.wait()
    far = [
        k.send(b1.at[0], W13.at[c, y, :, :, :, f1], ys[2]),
        k.send(b3.at[0], W13.at[c, :, xh, xl, :, f3], xs[2]),
    ]
    sent, heres = [], []
    for j, step in enumerate((0, 3, 1)):
        yy, x2 = (y + step) % 4, (xx + step) % 4
        if j:
            for cp in loads[j]:
                cp.wait()
        for src, dst in (
            (b1.at[j], W13.at[c, yy, :, :, :, f1]),
            (b3.at[j], W13.at[c, :, x2 // 2, x2 % 2, :, f3]),
        ):
            sent.append(k.send(src, dst, mate))
            heres.append(k.local(src, dst))
    sum_pass(k, q, part, pass_top, pass_low, send_top, send_low, below, above, state)
    for j, step in enumerate((0, 3, 1, 2)):
        loads[3][j].wait()
        heres.append(k.local(gb.at[j], G.at[(z + step) % 4]))
    w2_here.wait()
    for cp in w2x:
        cp.wait_recv()
    ref = W2.at[:, t_top, pl.ds(pl.multiple_of(128 * (c * 8 + y * 2), 256), 256)]
    legs = [k.send(ref, ref, to) for to in ys]
    for cp in w2y:
        cp.wait_recv()
    for b in range(4):
        ref = W2.at[xh, t_low, pl.ds(pl.multiple_of(128 * (c * 8 + b * 2 + xl), 128), 128)]
        legs += [k.send(ref, ref, to) for to in xs]
    sum_end(state)
    total = x[...].astype(F32) + (
        part[z].astype(F32) + (below[...].astype(F32) + above[...].astype(F32))
    )
    H[...] = total
    scale = lax.rsqrt(jnp.mean(total * total, axis=-1, keepdims=True) + EPS)
    n2[...] = to_pieces((total * scale * gain[...]).astype(BF))
    state = gather_start(k, q, n2, N2)
    for cp in far:
        cp.wait_recv()
    x2 = (xx + 2) % 4
    for ref in (
        W13.at[c, (y + 2) % 4, :, :, :, f1],
        W13.at[c, :, x2 // 2, x2 % 2, :, f3],
    ):
        sent.append(k.send(ref, ref, mate))
    gather_pass(k, q, N2, state)
    for cp in legs:
        cp.wait_recv()
    ref = W2.at[:, :, pl.ds(pl.multiple_of(1024 * c, 1024), 1024)]
    sent.append(k.send(ref, ref, mate))
    for cp in sent:
        cp.wait_recv()
    for cp in heres:
        cp.wait()
    gather_end(state)
    k.close()


def gather_kernel(v, sa, sb, s2, V, Ra, Rb, R2, ss, rs):
    q = coords()
    y, xx, z = q["y"], q["x"], q["z"]
    up, down = device(q, z=(z + 1) % 4), device(q, z=(z + 3) % 4)
    ys, xs = ring(q, "y")[:2], ring(q, "x")[:2]
    greet([up, down] + ys + xs)
    k = Copies(ss, rs)
    state = gather_start(k, q, v, V)
    legs = []
    for i, step in enumerate((1, 3)):
        yy, x2 = (y + step) % 4, (xx + step) % 4
        legs.append(k.send(sa.at[:, x2], Ra.at[i], xs[i]))
        legs.append(k.send(s2.at[:, pl.ds(pl.multiple_of(256 * yy, 256), 256)], R2.at[i], ys[i]))
        legs.append(k.send(sb.at[yy], Rb.at[i], ys[i]))
    gather_pass(k, q, V, state)
    gather_end(state)
    for cp in legs:
        cp.wait_recv()
    k.close()


def dkv_kernel(dkv, R, ss, rs):
    q = coords()
    xx, xl, c = q["x"], q["xl"], q["c"]
    mate = device(q, c=1 - c)
    other = device(q, x=xx ^ 1)
    other_mate = device(q, x=xx ^ 1, c=1 - c)
    greet([mate, other, other_mate])
    k = Copies(ss, rs)
    near = k.send(dkv.at[xl, :, 1 - c], R.at[0], mate)
    far = [
        pltpu.make_async_remote_copy(
            src_ref=dkv.at[0, :, cc],
            dst_ref=R.at[1 + i],
            send_sem=ss.at[1 + i],
            recv_sem=rs.at[1 + i],
            device_id=to,
            device_id_type=MESH,
        )
        for i, (to, cc) in enumerate(((other, c), (other_mate, 1 - c)))
    ]

    @pl.when(xl == 1)
    def _():
        for cp in far:
            cp.start()
        for cp in far:
            cp.wait_send()

    @pl.when(xl == 0)
    def _():
        for cp in far:
            cp.wait_recv()

    near.wait_recv()
    k.close()


def quarter(xt, rows):
    return (
        pl.ds(pl.multiple_of((xt // 2) * rows, rows), rows),
        pl.ds(pl.multiple_of((xt % 2) * 128, 128), 128),
    )


def wide_kernel(
    dn, fa, fb, f2, sq, so, D2, G1, G3, G2, Rq, Ro,
    pass_top, pass_low, send_top, send_low, la, lb, l2, pa, pb, p2, t2, ss, rs,
):
    q = coords()
    y, xx, xh, xl, z, c = q["y"], q["x"], q["xh"], q["xl"], q["z"], q["c"]
    zs, ys, xs = ring(q, "z"), ring(q, "y"), ring(q, "x")
    mate, other = device(q, c=1 - c), device(q, x=xx ^ 1)
    greet(zs + ys + xs + [mate], q)
    k = Copies(ss, rs)
    steps = (1, 3, 2)
    state = sum_start(k, q, dn, pass_top, pass_low, D2.at[0], D2.at[1])
    leg_a = [k.send(fa.at[(y + s) % 4], la.at[i], ys[i]) for i, s in enumerate(steps)]
    leg_b = [k.send(fb.at[(xx + s) % 4], lb.at[i], xs[i]) for i, s in enumerate(steps)]
    leg_2 = []
    for i, s in enumerate(steps):
        r, cc = quarter((xx + s) % 4, 704)
        leg_2.append(k.send(f2.at[r, cc], l2.at[i], xs[i]))
    heavy = []
    for i, s in enumerate(steps):
        heavy.append(k.send(sq.at[:, (xx + s) % 4], Rq.at[i], xs[i]))
        cols = pl.ds(pl.multiple_of(256 * ((y + s) % 4), 256), 256)
        heavy.append(k.send(so.at[:, cols], Ro.at[i], ys[i]))
    sum_pass(k, q, dn, pass_top, pass_low, send_top, send_low, D2.at[0], D2.at[1], state)
    for cp in leg_2:
        cp.wait_recv()
    r, cc = quarter(xx, 704)
    p2[...] = add4(f2[r, cc], l2[0], l2[1], l2[2])
    turned = turn(k, q, [(p2, t2)])
    for cp in leg_b:
        cp.wait_recv()
    pb[...] = add4(fb[xx], lb[0], lb[1], lb[2])
    for cp in leg_a:
        cp.wait_recv()
    pa[...] = add4(fa[y], la[0], la[1], la[2])
    rows = pl.ds(pl.multiple_of(128 * c + 64 * xl, 64), 64)
    rest = SPLIT - FZ

    def blocks(zz):
        at = lambda off, n: pl.ds(pl.multiple_of(FZ * zz + off, 128), n)
        return [G1.at[rows, at(0, FZ)], G3.at[rows, at(0, rest)], G3.at[rows, at(rest, FZ - rest)]]

    own = [pa.at[:, pl.ds(0, FZ)], pa.at[:, pl.ds(FZ, rest)], pb]
    leg_z = [[k.send(src, dst, to) for src, dst in zip(own, blocks(z))] for to in zs]
    heres = [k.local(src, dst) for src, dst in zip(own, blocks(z))]
    leg_zx = [k.send(src, dst, other) for src, dst in zip(own, blocks(z))]
    turned()
    col = pl.ds(pl.multiple_of(128 * (c * 8 + z * 2 + xl), 128), 128)
    leg_x = k.send(t2, G2.at[:, col], other)
    heres.append(k.local(t2, G2.at[:, col]))
    leg_x.wait_recv()
    heres[-1].wait()
    ref = G2.at[:, pl.ds(pl.multiple_of(128 * (c * 8 + z * 2), 256), 256)]
    leg_xz = [k.send(ref, ref, to) for to in zs]
    for i, s in enumerate(steps):
        for cp in leg_z[i]:
            cp.wait_recv()
        leg_zx += [k.send(ref, ref, other) for ref in blocks((z - s + 4) % 4)]
    for cp in leg_xz:
        cp.wait_recv()
    ref = G2.at[:, pl.ds(pl.multiple_of(1024 * c, 1024), 1024)]
    last = [k.send(ref, ref, mate)]
    for cp in heres[:-1]:
        cp.wait()
    for cp in leg_zx:
        cp.wait_recv()
    pair = pl.ds(pl.multiple_of(128 * c, 128), 128)
    last += [k.send(ref.at[pair], ref.at[pair], mate) for ref in (G1, G3)]
    for cp in heavy + last:
        cp.wait_recv()
    sum_end(state)
    k.close()


def last_kernel(
    part, fq, fo, gain, D2, GO, GQ, gain_out,
    pass_top, pass_low, send_top, send_low, lq, lo, pq, po, to_, s0, s1, s2, s3, s4, total, ss, rs,
):
    q = coords()
    y, xx, xh, xl, z, c = q["y"], q["x"], q["xh"], q["xl"], q["z"], q["c"]
    zs, ys, xs = ring(q, "z"), ring(q, "y"), ring(q, "x")
    mate, other, cross = device(q, c=1 - c), device(q, x=xx ^ 1), device(q, x=3 - xx)
    greet(zs + ys + xs + [mate], q)
    k = Copies(ss, rs)
    steps = (1, 3, 2)
    gain_y = [k.send(gain.at[(y + s) % 4], s0.at[y], ys[i]) for i, s in enumerate(steps)]
    gain_here = k.local(gain.at[y], s0.at[y])
    leg_o = []
    for i, s in enumerate(steps):
        r, cc = quarter((xx + s) % 4, 256)
        leg_o.append(k.send(fo.at[r, cc], lo.at[i], xs[i]))
    leg_q = [k.send(fq.at[(y + s) % 4], lq.at[i], ys[i]) for i, s in enumerate(steps)]
    for cp in gain_y:
        cp.wait_recv()
    gain_here.wait()
    s1[0] = (s0[0] + s0[1]) + (s0[2] + s0[3])
    gain_x = k.send(s1.at[0, 1 - xh], s1.at[1, 0], cross)
    for cp in leg_o:
        cp.wait_recv()
    r, cc = quarter(xx, 256)
    po[...] = add4(fo[r, cc], lo[0], lo[1], lo[2])
    turned = turn(k, q, [(po, to_)])
    gain_x.wait_recv()
    s2[z] = s1[0, xh] + s1[1, 0]
    gain_z = [k.send(s2.at[z], s2.at[z], to) for to in zs]
    for cp in leg_q:
        cp.wait_recv()
    pq[...] = add4(fq[y], lq[0], lq[1], lq[2])
    rows = pl.ds(pl.multiple_of(128 * c + 64 * xl, 64), 64)
    pair = pl.ds(pl.multiple_of(128 * c, 128), 128)
    mq = pl.ds(pl.multiple_of(MZ * z, 128), MZ)
    leg_x = [k.send(pq, GQ.at[rows, mq], other)]
    heres = [k.local(pq, GQ.at[rows, mq])]
    turned()
    col = pl.ds(pl.multiple_of(128 * (c * 8 + z * 2 + xl), 128), 128)
    leg_x.append(k.send(to_, GO.at[:, col], other))
    heres.append(k.local(to_, GO.at[:, col]))
    for cp in gain_z:
        cp.wait_recv()
    s3[0] = (s2[0] + s2[1]) + (s2[2] + s2[3])
    gain_x = k.send(s3.at[0], s3.at[1], other)
    for cp in leg_x:
        cp.wait_recv()
    for cp in heres:
        cp.wait()
    refs = [GQ.at[pair, mq], GO.at[:, pl.ds(pl.multiple_of(128 * (c * 8 + z * 2), 256), 256)]]
    leg_xz = [k.send(ref, ref, to) for ref in refs for to in zs]
    state = sum_start(k, q, part, pass_top, pass_low, D2.at[0], D2.at[1])
    gain_x.wait_recv()
    s4[0] = s3[0] + s3[1]
    gain_c = k.send(s4.at[0], s4.at[1], mate)
    sum_pass(k, q, part, pass_top, pass_low, send_top, send_low, D2.at[0], D2.at[1], state)
    gain_c.wait_recv()
    total[...] = s4[0] + s4[1]
    gain_done = k.local(total, gain_out)
    for cp in leg_xz:
        cp.wait_recv()
    refs = [GQ.at[pair], GO.at[:, pl.ds(pl.multiple_of(1024 * c, 1024), 1024)]]
    last = [k.send(ref, ref, mate) for ref in refs]
    for cp in last:
        cp.wait_recv()
    sum_end(state)
    gain_done.wait()
    k.close()


PARAMS = pltpu.CompilerParams(vmem_limit_bytes=VMEM_LIMIT)


def add4(a, b, c, d):
    a, b, c, d = (v.astype(F32) for v in (a, b, c, d))
    return ((a + b) + (c + d)).astype(BF)


def to_pieces(v):
    return jnp.concatenate(
        [v[:, 256 * d + 128 * c : 256 * d + 128 * c + 128] for c in range(2) for d in range(8)],
        axis=1,
    )


def from_pieces(v):
    return jnp.concatenate(
        [v[:, 1024 * c + 128 * d : 1024 * c + 128 * d + 128] for d in range(8) for c in range(2)],
        axis=1,
    )


def swapped(u):
    lane = lax.broadcasted_iota(jnp.int32, u.shape, 1)
    return jnp.where(lane % 64 < 32, pltpu.roll(u, 96, 1), pltpu.roll(u, 32, 1))


def project_kernel(x, gain, w, cosine, sine, n1, query, kv):
    xv = x[0].astype(F32)
    scale = lax.rsqrt(jnp.mean(xv * xv, axis=-1, keepdims=True) + EPS)
    normed = to_pieces((xv * scale * gain[...]).astype(BF))
    n1[0] = normed
    cos, sin = cosine[0], sine[0]
    for j in range(5):
        u = jnp.dot(normed, w[:, 128 * j : 128 * j + 128], preferred_element_type=F32)
        turned = u * cos + swapped(u) * sin
        if j < 4:
            query[0, :, 128 * j : 128 * j + 128] = turned.astype(BF)
        else:
            lane = lax.broadcasted_iota(jnp.int32, u.shape, 1)
            kv[0] = jnp.where(lane < HEAD_DIM, turned, u).astype(BF)


def project(x, gain, w, cosine, sine):
    chunk = lambda cols: pl.BlockSpec((1, TOK, cols), lambda i: (i, 0, 0))
    whole = lambda shape: pl.BlockSpec(shape, lambda i: (0,) * len(shape))
    return pl.pallas_call(
        project_kernel,
        name="project",
        cost_estimate=cost(7),
        grid=(RING,),
        in_specs=[chunk(D), whole((1, D)), whole((D, MZ)), chunk(128), chunk(128)],
        out_specs=[chunk(D), chunk(QZ), chunk(128)],
        out_shape=[
            jax.ShapeDtypeStruct((RING, TOK, D), BF),
            jax.ShapeDtypeStruct((RING, TOK, QZ), BF),
            jax.ShapeDtypeStruct((RING, TOK, 128), BF),
        ],
        compiler_params=PARAMS,
    )(x, gain, w, cosine, sine)


def stacked_low(tiles):
    out = []
    for pair in range(4):
        tile = tiles[:, 128 * pair : 128 * pair + 128].astype(F32)
        lane = lax.broadcasted_iota(jnp.int32, tile.shape, 1)
        out.append(jnp.where(lane < HEAD_DIM, tile, 0.0))
        out.append(jnp.where(lane < HEAD_DIM, pltpu.roll(tile, 64, 1), 0.0))
    return jnp.concatenate(out, axis=0)


def stacked_high(tiles):
    out = []
    for pair in range(4):
        tile = tiles[:, 128 * pair : 128 * pair + 128].astype(F32)
        lane = lax.broadcasted_iota(jnp.int32, tile.shape, 1)
        out.append(jnp.where(lane >= HEAD_DIM, pltpu.roll(tile, 64, 1), 0.0))
        out.append(jnp.where(lane >= HEAD_DIM, tile, 0.0))
    return jnp.concatenate(out, axis=0)


def unstacked(v):
    tiles = []
    for pair in range(4):
        both = jnp.concatenate(
            [v[:, 256 * pair : 256 * pair + 128], v[:, 256 * pair + 128 : 256 * pair + 256]],
            axis=0,
        )
        tiles.append(both.T)
    return tiles


def nt(a, b):
    return lax.dot_general(a, b, (((1,), (1,)), ((), ())), preferred_element_type=F32)


def tn(a, b):
    return lax.dot_general(a, b, (((0,), (0,)), ((), ())), preferred_element_type=F32)


def chunk_scores(keys, stacked, kc, chunk, start):
    raw = nt(keys, stacked)
    key = kc * TOK + lax.broadcasted_iota(jnp.int32, raw.shape, 0)
    query = chunk * TOK + lax.broadcasted_iota(jnp.int32, raw.shape, 1) % TOK
    return jnp.where((key <= query) & (key >= start), raw, -1e30)


def attend_kernel(info, query, kv, start, out, logsum):
    i = pl.program_id(0)
    low, chunk = info[0, i], info[1, i]
    stacked = (stacked_low(query[0]) * (1.0 / HEAD_DIM**0.5)).astype(BF)
    starts = jnp.concatenate([start[0]] * GROUP, axis=1)

    def step(kc, carry):
        top, summed, total = carry
        keys = kv[kc]
        scores = chunk_scores(keys, stacked, kc, chunk, starts)
        new_top = jnp.maximum(top, jnp.max(scores, axis=0, keepdims=True))
        weights = jnp.exp(scores - new_top)
        fade = jnp.exp(top - new_top)
        summed = summed * fade + jnp.sum(weights, axis=0, keepdims=True)
        part = tn(keys, weights.astype(BF))
        return new_top, summed, total * fade + part[HEAD_DIM:]

    rows = GROUP * TOK
    carry = (jnp.full((1, rows), -1e30, F32), jnp.zeros((1, rows), F32), jnp.zeros((64, rows), F32))
    top, summed, total = lax.fori_loop(low, chunk + 1, step, carry)
    for pair, tile in enumerate(unstacked(total / summed)):
        out[0, :, 128 * pair : 128 * pair + 128] = tile.astype(BF)
    logsum[0] = top + jnp.log(summed)


def attend(info, query, kv, start):
    chunk = lambda r, cols: pl.BlockSpec((1, r, cols), lambda i, s: (i, 0, 0))
    return pl.pallas_call(
        attend_kernel,
        name="attend",
        cost_estimate=cost(12),
        grid_spec=pltpu.PrefetchScalarGridSpec(
            num_scalar_prefetch=1,
            grid=(RING,),
            in_specs=[
                chunk(TOK, QZ),
                pl.BlockSpec((16, TOK, 128), lambda i, s: (0, 0, 0)),
                chunk(1, TOK),
            ],
            out_specs=[chunk(TOK, QZ), chunk(1, GROUP * TOK)],
        ),
        out_shape=[
            jax.ShapeDtypeStruct((RING, TOK, QZ), BF),
            jax.ShapeDtypeStruct((RING, 1, GROUP * TOK), F32),
        ],
        compiler_params=PARAMS,
    )(info, query, kv, start)


def attend_back_kernel(
    info, query, kv, start, out, grad_out, logsum, cosine, sine, dquery, dkv, total
):
    i = pl.program_id(0)
    low, chunk = info[0, i], info[1, i]
    stacked = (stacked_low(query[0]) * (1.0 / HEAD_DIM**0.5)).astype(BF)
    grads = stacked_high(grad_out[0]).astype(BF)
    starts = jnp.concatenate([start[0]] * GROUP, axis=1)
    lse = logsum[0]
    deltas = []
    for pair in range(4):
        cols = slice(128 * pair, 128 * pair + 128)
        prod = (out[0, :, cols].astype(F32) * grad_out[0, :, cols].astype(F32)).T
        deltas.append(jnp.sum(prod[:HEAD_DIM], axis=0, keepdims=True))
        deltas.append(jnp.sum(prod[HEAD_DIM:], axis=0, keepdims=True))
    delta = jnp.concatenate(deltas, axis=1)

    @pl.when(i == 0)
    def _():
        total[...] = jnp.zeros_like(total)

    def step(kc, dq):
        keys = kv[kc]
        scores = chunk_scores(keys, stacked, kc, chunk, starts)
        probs = jnp.exp(scores - lse)
        grad_probs = nt(keys, grads)
        grad_scores = (probs * (grad_probs - delta)).astype(BF)
        total[kc] += jnp.dot(grad_scores, stacked, preferred_element_type=F32) + jnp.dot(
            probs.astype(BF), grads, preferred_element_type=F32
        )
        return dq + tn(keys, grad_scores)[:HEAD_DIM]

    dq = lax.fori_loop(low, chunk + 1, step, jnp.zeros((64, GROUP * TOK), F32))
    cos, sin = cosine[0], sine[0]
    for pair, tile in enumerate(unstacked(dq)):
        tile = tile * (1.0 / HEAD_DIM**0.5)
        dquery[0, :, 128 * pair : 128 * pair + 128] = (tile * cos - swapped(tile) * sin).astype(BF)

    @pl.when(i == RING - 1)
    def _():
        dkv[...] = total[...].astype(BF)


def attend_back(info, query, kv, start, out, grad_out, logsum, cosine, sine):
    chunk = lambda r, cols: pl.BlockSpec((1, r, cols), lambda i, s: (i, 0, 0))
    whole = pl.BlockSpec((16, TOK, 128), lambda i, s: (0, 0, 0))
    return pl.pallas_call(
        attend_back_kernel,
        name="attend_back",
        cost_estimate=cost(15),
        grid_spec=pltpu.PrefetchScalarGridSpec(
            num_scalar_prefetch=1,
            grid=(RING,),
            in_specs=[
                chunk(TOK, QZ),
                whole,
                chunk(1, TOK),
                chunk(TOK, QZ),
                chunk(TOK, QZ),
                chunk(1, GROUP * TOK),
                chunk(TOK, 128),
                chunk(TOK, 128),
            ],
            out_specs=[chunk(TOK, QZ), whole],
            scratch_shapes=[pltpu.VMEM((16, TOK, 128), F32)],
        ),
        out_shape=[
            jax.ShapeDtypeStruct((RING, TOK, QZ), BF),
            jax.ShapeDtypeStruct((16, TOK, 128), BF),
        ],
        compiler_params=PARAMS,
    )(info, query, kv, start, out, grad_out, logsum, cosine, sine)


def dmixed_kernel(xl, dkv, received, cosine, sine, out):
    t = dkv[...].astype(F32) + received[0].astype(F32)
    far = received[1].astype(F32) + received[2].astype(F32)
    t = jnp.where(xl[0] == 0, t + far, t)
    for i in range(RING):
        w = t[i]
        lane = lax.broadcasted_iota(jnp.int32, w.shape, 1)
        out[i] = jnp.where(lane < HEAD_DIM, w * cosine[i] - swapped(w) * sine[i], w).astype(BF)


def dmixed_kv(xl, dkv, received, cosine, sine):
    vmem = pl.BlockSpec(memory_space=pltpu.VMEM)
    return pl.pallas_call(
        dmixed_kernel,
        name="dmixed_kv",
        cost_estimate=cost(2),
        in_specs=[pl.BlockSpec(memory_space=pltpu.SMEM)] + [vmem] * 4,
        out_specs=vmem,
        out_shape=jax.ShapeDtypeStruct((RING, TOK, 128), BF),
        compiler_params=PARAMS,
    )(xl, dkv, received, cosine, sine)


def rms_back(v, gain, grad):
    scale = lax.rsqrt(jnp.mean(v * v, axis=-1, keepdims=True) + EPS)
    unit = v * scale
    gain_grad = jnp.sum(grad * unit, axis=0, keepdims=True)
    inner = grad * gain
    return scale * (inner - unit * jnp.mean(inner * unit, axis=-1, keepdims=True)), gain_grad


def norm_back_kernel(n, v, base, *refs):
    parts, gain, grad, outs = refs[:n], refs[n], refs[n + 1], refs[n + 2 :]
    dn = from_pieces(functools.reduce(jnp.add, [p[...].astype(F32) for p in parts]))
    back, gain_grad = rms_back(v[...].astype(F32), gain[...], dn)
    total = base[...].astype(F32) + back
    grad[...] = total
    outs[-1][...] = gain_grad
    if len(outs) == 2:
        outs[0][...] = total.astype(BF)


def norm_back(v, base, parts, gain, rounded):
    shapes = [jax.ShapeDtypeStruct((TOK, D), F32)]
    if rounded:
        shapes.append(jax.ShapeDtypeStruct((TOK, D), BF))
    shapes.append(jax.ShapeDtypeStruct((1, D), F32))
    return pl.pallas_call(
        functools.partial(norm_back_kernel, len(parts)),
        name="norm_back",
        cost_estimate=cost(4),
        out_shape=shapes,
        compiler_params=PARAMS,
    )(v, base, *parts, gain)


def pick(v, index, axis=0):
    return lax.dynamic_index_in_dim(v, index, axis, keepdims=False)


def scatter(v, q, axis, dim):
    at = q[axis]
    got = [move(pick(v, (at + s) % 4, dim), axis, s) for s in (1, 3, 2)]
    return [pick(v, at, dim)] + got


def add(*parts):
    return functools.reduce(jnp.add, [p.astype(F32) for p in parts]).astype(BF)


def cut(v, j, width):
    return lax.dynamic_slice_in_dim(v, j * width, width, 1)


def dot(a, b):
    return jnp.dot(a, b, preferred_element_type=F32)


def body(tokens, segments, cotangent, norm_attn, norm_ffn, wqkv, wo, w1, w3, w2):
    q = coords()
    y, xx, xl, z, c = q["y"], q["x"], q["xl"], q["z"], q["c"]
    x = tokens[0]
    g = cotangent[0]
    seg = jnp.broadcast_to(segments, (8, TOK))
    gn = jnp.concatenate(
        [jnp.broadcast_to(v[None], (16, 256)) for v in (norm_attn, norm_ffn)], axis=0
    )
    heads = wqkv[:, :QDIM].reshape(256, 4, QZ)
    kz = wqkv[:, QDIM : QDIM + KVDIM].reshape(256, 4, HEAD_DIM)
    vz = wqkv[:, QDIM + KVDIM :].reshape(256, 4, HEAD_DIM)
    wq = jnp.concatenate([heads, kz, vz], axis=2).reshape(256, 4 * MZ)

    X, SEG, GN, WQ, WO, A1, A3 = talk(
        fetch_kernel,
        "fetch",
        1,
        30,
        80,
        (x, seg, gn, wq, wo, w1, w3),
        [
            ((RING, TOK, D), BF),
            ((2, 4, 2, 8, TOK), jnp.int32),
            ((4, 2, 32, 256), BF),
            ((2, 4, 2, 2, 64, MZ), BF),
            ((2, 256, D), BF),
            ((2, 2, 64, FZ), BF),
            ((4, 64, FZ), BF),
        ],
        scratch=[
            pltpu.VMEM((256, 128), BF),
            pltpu.VMEM((64, MZ), BF),
            pltpu.VMEM((64, FZ), BF),
            pltpu.VMEM((64, FZ), BF),
        ],
        near=(0, 1, 2),
    )
    a1 = [A1] + [move(A1, "y", s) for s in (1, 3)]
    a3 = [A3] + [move(A3, "x", s) for s in (1, 3)]
    t2 = lax.dynamic_slice_in_dim(w2, 128 * (c * 8 + z * 2 + xl), 128, 1)
    t2 = lax.ppermute(t2, ("dp", "ctx"), swap_pairs())

    docs = SEG[:, :, :, 0, :].reshape(16 * TOK)
    mine = pick(pick(SEG[:, :, :, 0, :], xl, 0), c, 1)
    chunks = xl * 8 + 2 * jnp.arange(4, dtype=jnp.int32) + c
    start = jnp.sum((docs[None, None, :] < mine[:, :, None]).astype(jnp.int32), axis=2)
    index = chunks[:, None] * TOK + jnp.arange(TOK, dtype=jnp.int32)[None]
    place = (index - start).astype(F32)
    lane = jnp.arange(128)
    freq = THETA ** (-(lane % 32).astype(F32) * 2.0 / HEAD_DIM)
    angle = place[:, :, None] * freq[None, None, :]
    cosine = jnp.cos(angle)
    sine = jnp.sin(angle) * jnp.where(lane % 64 < 32, -1.0, 1.0)
    info = jnp.stack([jnp.min(start, axis=1) // TOK, chunks])
    start = start[:, None, :]
    gain_attn = GN[:, :, 0, :].reshape(1, D).astype(F32)
    gain_ffn = GN[:, :, 16, :].reshape(1, D).astype(F32)

    WQ = WQ.reshape(D, MZ)
    WO = WO.reshape(QZ, D)
    n1, query, kv = project(X, gain_attn, WQ, cosine, sine)
    (KV,) = talk(
        kv_kernel, "kv", 2, 7, 4, (kv,), [((2, 4, 2, TOK, 128), BF)], near=(0,)
    )
    KV = KV.reshape(16, TOK, 128)
    KV, t2, a1, a3, g = lax.optimization_barrier((KV, t2, a1, a3, g))
    gs = [g] + [move(g, "z", s) for s in (1, 3, 2)]
    heads_out, logsum = attend(info, query, KV, start)
    o = heads_out.reshape(RING * TOK, QZ)
    part = dot(o, WO).astype(BF).reshape(RING, TOK, D)
    N2, h, G, W13, W2 = talk(
        middle_kernel,
        "middle",
        3,
        45,
        110,
        (part, x, gain_ffn, t2, *a1, *a3, *gs),
        [
            ((RING, TOK, D), BF),
            ((TOK, D), F32),
            ((RING, TOK, D), BF),
            ((2, 4, 2, 2, 64, 2 * FZ), BF),
            ((2, 704, D), BF),
        ],
        scratch=[
            *[pltpu.VMEM(HALF, BF)] * 4,
            *[pltpu.VMEM((TOK, D), BF)] * 3,
            pltpu.VMEM((3, 2, 2, 64, FZ), BF),
            pltpu.VMEM((3, 4, 64, FZ), BF),
            pltpu.VMEM((4, TOK, D), BF),
        ],
        near=(0, 1, 2, 3),
        near_out=(1,),
    )
    N2, G = N2.reshape(RING * TOK, D), G.reshape(RING * TOK, D)
    W13, W2 = W13.reshape(D, 2 * FZ), W2.reshape(FZ, D)
    gate, up = dot(N2, W13[:, :FZ]), dot(N2, W13[:, FZ:])
    hidden = (jax.nn.silu(gate) * up).astype(BF)
    out_part = dot(hidden, W2).astype(BF).reshape(RING, TOK, D)
    dhid = jnp.einsum("td,fd->tf", G, W2, preferred_element_type=F32)
    sigma = jax.nn.sigmoid(gate)
    dgate = (dhid * up * sigma * (1.0 + gate * (1.0 - sigma))).astype(BF)
    dup = (dhid * gate * sigma).astype(BF)
    both = jnp.concatenate([dgate, dup], axis=1)
    dn2 = jnp.einsum("tf,df->td", both, W13, preferred_element_type=F32)
    dn2 = dn2.astype(BF).reshape(RING, TOK, D)
    dn2_parts = scatter(dn2, q, "z", 0)

    half = lambda v, j: lax.dynamic_slice_in_dim(v, 1024 * j, 1024, 1)
    outer = lambda a, b: jnp.einsum("ta,tb->ab", a, b, preferred_element_type=F32)
    other13 = move(outer(half(N2, 1 - c), both).astype(BF), "c", 1)
    other2 = move(outer(hidden, half(G, 1 - c)).astype(BF), "c", 1)
    sum13 = (outer(half(N2, c), both) + other13.astype(F32)).astype(BF)
    sum2 = (outer(hidden, half(G, c)) + other2.astype(F32)).astype(BF)
    sum13 = sum13.reshape(4, 4, 64, 2 * FZ)
    sum_a, sum_b = sum13[..., :SPLIT], sum13[..., SPLIT:]

    dh, dhb, gain2 = norm_back(h, g, dn2_parts, gain_ffn, True)
    DH, Ra, Rb, R2 = talk(
        gather_kernel,
        "gather",
        4,
        30,
        20,
        (dhb, sum_a, sum_b, sum2),
        [
            ((RING, TOK, D), BF),
            ((2, 4, 64, SPLIT), BF),
            ((2, 4, 64, 2 * FZ - SPLIT), BF),
            ((2, 1408, 256), BF),
        ],
        near=(0,),
    )
    DH, sum_a, sum_b, sum2 = lax.optimization_barrier((DH, sum_a, sum_b, sum2))
    far_a = move(pick(sum_a, (xx + 2) % 4, 1), "x", 2)
    far_b = move(pick(sum_b, (y + 2) % 4), "y", 2)
    far_2 = move(cut(sum2, (y + 2) % 4, 256), "y", 2)
    DH = DH.reshape(RING * TOK, D)
    dheads = jnp.einsum("td,qd->tq", DH, WO, preferred_element_type=F32).astype(BF)
    dquery, dkv = attend_back(
        info, query, KV, start, heads_out, dheads.reshape(RING, TOK, QZ), logsum, cosine, sine
    )
    dkv = dkv.reshape(2, 4, 2, TOK, 128)
    (received,) = talk(
        dkv_kernel, "dkv", 5, 8, 4, (dkv,), [((3, 4, TOK, 128), BF)]
    )
    own_dkv = pick(pick(dkv, xl, 0), c, 1)
    dkv_rot = dmixed_kv(xl[None], own_dkv, received, cosine, sine)
    dmixed = jnp.concatenate([dquery, dkv_rot], axis=2).reshape(RING * TOK, MZ)
    dn1 = jnp.einsum("tc,dc->td", dmixed, WQ, preferred_element_type=F32)
    dn1 = dn1.astype(BF).reshape(RING, TOK, D)

    fa = add(pick(sum_a, xx, 1), Ra[0], Ra[1], far_a)
    fb = add(pick(sum_b, y), Rb[0], Rb[1], far_b)
    f2 = add(cut(sum2, y, 256), R2[0], R2[1], far_2)
    n1 = n1.reshape(RING * TOK, D)
    other_o = move(outer(o, half(DH, 1 - c)).astype(BF), "c", 1)
    sum_o = (outer(o, half(DH, c)) + other_o.astype(F32)).astype(BF)
    other_q = move(outer(half(n1, 1 - c), dmixed).astype(BF), "c", 1)
    sum_q = (outer(half(n1, c), dmixed) + other_q.astype(F32)).astype(BF)
    sum_q = sum_q.reshape(4, 4, 64, MZ)
    rest = 2 * FZ - SPLIT
    D1, G1, G3, G2, Rq, Ro = talk(
        wide_kernel,
        "wide",
        6,
        50,
        90,
        (dn1, fa, fb, f2, sum_q, sum_o),
        [
            ((2, TOK, D), BF),
            ((256, 4 * FZ), BF),
            ((256, 4 * FZ), BF),
            ((704, D), BF),
            ((3, 4, 64, MZ), BF),
            ((3, 512, 256), BF),
        ],
        scratch=[
            *[pltpu.VMEM(HALF, BF)] * 4,
            pltpu.VMEM((3, 64, SPLIT), BF),
            pltpu.VMEM((3, 64, rest), BF),
            pltpu.VMEM((3, 704, 128), BF),
            pltpu.VMEM((64, SPLIT), BF),
            pltpu.VMEM((64, rest), BF),
            pltpu.VMEM((704, 128), BF),
            pltpu.VMEM((704, 128), BF),
        ],
        near=(0, 1, 2, 3),
    )
    input_grad, gain1 = norm_back(x, dh, (pick(dn1, z), D1[0], D1[1]), gain_attn, False)
    fq = add(pick(sum_q, xx, 1), Rq[0], Rq[1], Rq[2])
    fo = add(cut(sum_o, y, 256), Ro[0], Ro[1], Ro[2])

    gains = jnp.concatenate([gain1, gain2], axis=0).reshape(2, 8, 256).transpose(1, 0, 2)
    gains = jnp.pad(gains, ((0, 0), (0, 6), (0, 0))).reshape(4, 2, 8, 256)
    small = (8, 256)
    D3, GO, GQ, gain_out = talk(
        last_kernel,
        "last",
        7,
        30,
        60,
        (out_part, fq, fo, gains),
        [
            ((2, TOK, D), BF),
            ((256, D), BF),
            ((256, 4 * MZ), BF),
            (small, F32),
        ],
        scratch=[
            *[pltpu.VMEM(HALF, BF)] * 4,
            pltpu.VMEM((3, 64, MZ), BF),
            pltpu.VMEM((3, 256, 128), BF),
            pltpu.VMEM((64, MZ), BF),
            pltpu.VMEM((256, 128), BF),
            pltpu.VMEM((256, 128), BF),
            pltpu.VMEM((4, 2) + small, F32),
            pltpu.VMEM((2, 2) + small, F32),
            pltpu.VMEM((4,) + small, F32),
            pltpu.VMEM((2,) + small, F32),
            pltpu.VMEM((2,) + small, F32),
            pltpu.VMEM(small, F32),
        ],
        near=(0, 1, 2, 3),
    )
    GQ = GQ.astype(F32).reshape(256, 4, MZ)
    flat = lambda v: v.reshape(256, -1)
    grad_qkv = jnp.concatenate(
        [flat(GQ[:, :, :QZ]), flat(GQ[:, :, QZ : QZ + 64]), flat(GQ[:, :, QZ + 64 :])], axis=1
    )
    own = pick(out_part, z).astype(F32)
    output = h + (own + (D3[0].astype(F32) + D3[1].astype(F32)))
    return (
        output[None],
        input_grad[None],
        gain_out[0],
        gain_out[1],
        grad_qkv,
        GO.astype(F32),
        G1.astype(F32),
        G3.astype(F32),
        G2.astype(F32),
    )


def solution(mesh):
    rows = P("dp", None)
    acts = P("dp", "ctx", None)
    return jax.shard_map(
        body,
        mesh=mesh,
        in_specs=(acts, P("dp", "ctx"), acts, P("dp"), P("dp"), rows, rows, rows, rows, rows),
        out_specs=(acts, acts, P("dp"), P("dp"), rows, rows, rows, rows, rows),
        check_vma=False,
    )
```

```python
import functools

import jax
import jax.numpy as jnp
from jax import lax
from jax.experimental import pallas as pl
from jax.experimental.pallas import tpu as pltpu
from jax.sharding import PartitionSpec as P

D = 2048
HEAD_DIM = 64
TOK = 128
RING = 4
QDIM = 2048
KVDIM = 256
GROUP = 8
QZ = 512
MZ = 640
FZ = 1408
SPLIT = 2048
EPS = 1e-05
THETA = 10000.0
MESH = pl.DeviceIdType.MESH
VMEM_LIMIT = 56 << 20
BF = jnp.bfloat16
F32 = jnp.float32
ANY = pl.BlockSpec(memory_space=pl.ANY)
VMEM = pl.BlockSpec(memory_space=pltpu.VMEM)


def coords():
    dp, ctx = lax.axis_index("dp"), lax.axis_index("ctx")
    y, xh = dp // 2, dp % 2
    xl, z, c = ctx // 8, (ctx // 2) % 4, ctx % 2
    return dict(y=y, x=xh * 2 + xl, xh=xh, xl=xl, z=z, c=c)


def device(q, **change):
    r = {k: change.get(k, q[k]) for k in ("y", "x", "z", "c")}
    return (r["y"] * 2 + r["x"] // 2, (r["x"] % 2) * 8 + r["z"] * 2 + r["c"])


def ring(q, axis):
    return [device(q, **{axis: (q[axis] + s) % 4}) for s in (1, 3, 2)]


def shift_pairs(axis, by):
    size = 2 if axis == "c" else 4
    pairs = []
    for y in range(4):
        for x in range(4):
            for z in range(4):
                for c in range(2):
                    q = dict(y=y, x=x, z=z, c=c)
                    pairs.append((device(q), device(q, **{axis: (q[axis] + by) % size})))
    return [(a[0] * 16 + a[1], b[0] * 16 + b[1]) for a, b in pairs]


def swap_pairs():
    pairs = []
    for y in range(4):
        for x in range(4):
            for z in range(4):
                for c in range(2):
                    q = dict(y=y, x=x, z=z, c=c)
                    pairs.append((device(q), device(q, y=z, z=y)))
    return [(a[0] * 16 + a[1], b[0] * 16 + b[1]) for a, b in pairs]


def move(v, axis, by):
    return lax.ppermute(v, ("dp", "ctx"), shift_pairs(axis, by))


class Copies:
    def __init__(self, send_sems, recv_sems):
        self.send_sems, self.recv_sems, self.n, self.open = send_sems, recv_sems, 0, []

    def send(self, src, dst, to):
        cp = pltpu.make_async_remote_copy(
            src_ref=src,
            dst_ref=dst,
            send_sem=self.send_sems.at[self.n],
            recv_sem=self.recv_sems.at[self.n],
            device_id=to,
            device_id_type=MESH,
        )
        cp.start()
        self.n += 1
        self.open.append(cp)
        return cp

    def local(self, src, dst):
        cp = pltpu.make_async_copy(src, dst, self.send_sems.at[self.n])
        cp.start()
        self.n += 1
        return cp

    def close(self):
        for cp in self.open:
            cp.wait_send()


def deal(k, q, src, col, dst):
    y, z = q["y"], q["z"]
    n = k.n
    k.n += 4
    copies = [
        pltpu.make_async_remote_copy(
            src_ref=src.at[:, col((y + s) % 4)],
            dst_ref=dst,
            send_sem=k.send_sems.at[n + i],
            recv_sem=k.recv_sems.at[n],
            device_id=to,
            device_id_type=MESH,
        )
        for i, (s, to) in enumerate(zip((1, 3, 2), ring(q, "y")))
    ]
    here = pltpu.make_async_copy(src.at[:, col(y)], dst, k.send_sems.at[n + 3])

    @pl.when(y == z)
    def _():
        for cp in copies:
            cp.start()
        here.start()

    def wait():
        @pl.when(y == z)
        def _():
            for cp in copies:
                cp.wait_send()
            here.wait()

        @pl.when(y != z)
        def _():
            copies[0].wait_recv()

    return wait


def greet(targets, q=None):
    barrier = pltpu.get_barrier_semaphore()
    for to in targets:
        pl.semaphore_signal(barrier, inc=1, device_id=to, device_id_type=MESH)
    if q is None:
        pl.semaphore_wait(barrier, len(targets))
    else:
        y, z = q["y"], q["z"]

        @pl.when(y != z)
        def _():
            to = device(q, y=z, z=y)
            pl.semaphore_signal(barrier, inc=1, device_id=to, device_id_type=MESH)

        pl.semaphore_wait(barrier, len(targets) + (y != z).astype(jnp.int32))


TOP, LOW = pl.ds(0, TOK // 2), pl.ds(TOK // 2, TOK // 2)
HALF = (TOK // 2, D)


class Gather:
    def __init__(self, k, q, axis, src, dst):
        at = q[axis]
        self.k, self.dst = k, dst
        self.above, self.below, self.far = (at + 1) % 4, (at + 3) % 4, (at + 2) % 4
        self.up, self.down = device(q, **{axis: self.above}), device(q, **{axis: self.below})
        self.low0 = k.send(src(0), dst(at, 0), self.up)
        self.top1 = k.send(src(1), dst(at, 1), self.down)
        self.low1 = k.send(src(1), dst(at, 1), self.up)
        self.top0 = k.send(src(0), dst(at, 0), self.down)

    def relay(self):
        self.low0.wait_recv()
        ref = self.dst(self.below, 0)
        self.far0 = self.k.send(ref, ref, self.up)
        self.top1.wait_recv()
        ref = self.dst(self.above, 1)
        self.far1 = self.k.send(ref, ref, self.down)

    def near(self):
        self.low1.wait_recv()
        self.top0.wait_recv()

    def end(self):
        self.far0.wait_recv()
        self.far1.wait_recv()


class Sum:
    def __init__(self, k, q, axis, block, below, above, passed):
        at = q[axis]
        self.k, self.below, self.above, self.passed = k, below, above, passed
        up, down, far = (at + 1) % 4, (at + 3) % 4, (at + 2) % 4
        self.up, self.down = device(q, **{axis: up}), device(q, **{axis: down})
        self.first = k.send(block(far, 0), passed[0], self.up)
        self.second = k.send(block(far, 1), passed[1], self.down)
        self.rest = [
            k.send(block(up, 1), below(1), self.up),
            k.send(block(down, 0), above(0), self.down),
        ]

    def relay(self, own0, own1, sent):
        self.first.wait_recv()
        sent[0][...] = (self.passed[0][...].astype(F32) + own0[...].astype(F32)).astype(BF)
        self.rest.append(self.k.send(sent[0], self.below(0), self.up))
        self.second.wait_recv()
        sent[1][...] = (self.passed[1][...].astype(F32) + own1[...].astype(F32)).astype(BF)
        self.rest.append(self.k.send(sent[1], self.above(1), self.down))

    def end(self):
        for cp in self.rest:
            cp.wait_recv()

    def sent(self):
        for cp in self.rest[2:]:
            cp.wait_send()
            self.k.open = [o for o in self.k.open if o is not cp]


def halves(ref):
    return lambda h: ref.at[(TOP, LOW)[h]]


def ring_halves(ref):
    return lambda j, h: ref.at[j, (TOP, LOW)[h]]


def turn(k, q, moves):
    y, z = q["y"], q["z"]
    swap = device(q, y=z, z=y)
    pairs = []
    for src, dst in moves:
        n = k.n
        k.n += 1
        remote = pltpu.make_async_remote_copy(
            src_ref=src,
            dst_ref=dst,
            send_sem=k.send_sems.at[n],
            recv_sem=k.recv_sems.at[n],
            device_id=swap,
            device_id_type=MESH,
        )
        pairs.append((remote, pltpu.make_async_copy(src, dst, k.send_sems.at[n])))

    @pl.when(y != z)
    def _():
        for remote, _ in pairs:
            remote.start()

    @pl.when(y == z)
    def _():
        for _, here in pairs:
            here.start()

    def wait():
        @pl.when(y != z)
        def _():
            for remote, _ in pairs:
                remote.wait_recv()
                remote.wait_send()

        @pl.when(y == z)
        def _():
            for _, here in pairs:
                here.wait()

    return wait


def cost(us):
    return pl.CostEstimate(flops=int(us * 1e9), bytes_accessed=0, transcendentals=0)


def talk(kernel, name, cid, us, copies, ins, outs, scratch=(), near=(), near_out=(), alias={}):
    return pl.pallas_call(
        kernel,
        name=name,
        out_shape=[jax.ShapeDtypeStruct(s, t) for s, t in outs],
        in_specs=[VMEM if i in near else ANY for i in range(len(ins))],
        out_specs=[VMEM if i in near_out else ANY for i in range(len(outs))],
        scratch_shapes=[
            *scratch,
            pltpu.SemaphoreType.DMA((copies,)),
            pltpu.SemaphoreType.DMA((copies,)),
        ],
        cost_estimate=cost(us),
        input_output_aliases=alias,
        compiler_params=pltpu.CompilerParams(
            collective_id=cid, has_side_effects=True, vmem_limit_bytes=VMEM_LIMIT
        ),
    )(*ins)


def fetch_kernel(
    x, g, seg, na, nf, wq, wo, w1, w3, w2, X, G, SEG, GN, WQ, WO, W13, T2,
    TO, TV, QP, KT, VT, P1, P3, SG, NG, ss, rs,
):
    q = coords()
    y, xx, xh, xl, z, c = q["y"], q["x"], q["xh"], q["xl"], q["z"], q["c"]
    zs, ys, xs = ring(q, "z"), ring(q, "y"), ring(q, "x")
    mate = device(q, c=1 - c)
    other = device(q, x=xx ^ 1)
    other_mate = device(q, x=xx ^ 1, c=1 - c)
    k = Copies(ss, rs)
    rows = pl.ds(pl.multiple_of(128 * c + 64 * xl, 64), 64)
    qcols = pl.ds(pl.multiple_of(QZ * z, 128), QZ)
    tile = 128 * (z // 2)
    kcols = pl.ds(pl.multiple_of(QDIM + tile, 128), 128)
    vcols = pl.ds(pl.multiple_of(QDIM + KVDIM + tile, 128), 128)
    fcols = pl.ds(pl.multiple_of(FZ * z, 128), FZ)
    loads = [
        k.local(wq.at[rows, qcols], QP.at[:, pl.ds(0, QZ)]),
        k.local(wq.at[rows, kcols], KT),
        k.local(wq.at[rows, vcols], VT),
        k.local(w1.at[rows, fcols], P1),
        k.local(w3.at[rows, fcols], P3),
    ]
    SG[...] = jnp.broadcast_to(seg[...], (8, TOK))
    NG[0:16] = jnp.broadcast_to(na[...].astype(F32), (16, 256)).astype(BF)
    NG[16:32] = jnp.broadcast_to(nf[...].astype(F32), (16, 256)).astype(BF)
    greet(zs + ys + xs + [mate, other_mate])
    lanes = lambda j, n=1: pl.ds(pl.multiple_of(128 * j, 128 * n), 128 * n)
    dealt = deal(k, q, wo, lambda j: lanes(c * 8 + j * 2 + xl), TO)
    x_ring = Gather(k, q, "z", halves(x), ring_halves(X))
    for cp in loads:
        cp.wait()
    odd = z % 2 == 1
    kt, vt = KT[...].astype(F32), VT[...].astype(F32)
    lane = lax.broadcasted_iota(jnp.int32, kt.shape, 1)
    kt = jnp.where(odd, pltpu.roll(kt, 64, 1), kt)
    vt = jnp.where(odd, vt, pltpu.roll(vt, 64, 1))
    QP[:, QZ:] = jnp.where(lane < HEAD_DIM, kt, vt).astype(BF)
    f1, f3 = pl.ds(0, FZ), pl.ds(FZ, FZ)
    top, low = pl.ds(0, 32), pl.ds(32, 32)
    q_top = [k.send(QP.at[top], WQ.at[c, y, xh, xl, top], to) for to in xs]
    q_low = [k.send(QP.at[low], WQ.at[c, y, xh, xl, low], to) for to in ys]
    seg_z = [k.send(SG, SEG.at[xl, z, c], to) for to in zs]
    gn_y = [k.send(NG, GN.at[y, xh], to) for to in ys]
    q_here = k.local(QP, WQ.at[c, y, xh, xl])
    seg_here = k.local(SG, SEG.at[xl, z, c])
    gn_here = k.local(NG, GN.at[y, xh])
    a3_here = k.local(P3, W13.at[c, y, xh, xl, :, f3])
    heres = [
        k.local(P1, W13.at[c, y, xh, xl, :, f1]),
        k.local(x, X.at[z]),
        k.local(g, G.at[z]),
    ]
    dealt()
    o1 = [k.send(TO, WO.at[xh, :, lanes(c * 8 + y * 2 + xl)], to) for to in xs]
    o1_here = k.local(TO, WO.at[xh, :, lanes(c * 8 + y * 2 + xl)])
    thirty = lambda h: pl.ds(32 * h, 32)
    up_y = Gather(
        k, q, "y", lambda h: P3.at[thirty(h)], lambda j, h: W13.at[c, j, xh, xl, thirty(h), f3]
    )
    gate_x = Gather(
        k, q, "x", lambda h: P1.at[thirty(h)],
        lambda j, h: W13.at[c, y, j // 2, j % 2, thirty(h), f1],
    )
    q_here.wait()
    for cp in q_top:
        cp.wait_recv()
    q_y = Gather(k, q, "y", lambda h: WQ.at[c, y, h, :, top], lambda j, h: WQ.at[c, j, h, :, top])
    for cp in q_low:
        cp.wait_recv()
    q_half = lambda j, h: WQ.at[c, pl.ds(2 * h, 2), j // 2, j % 2, low]
    q_x = Gather(k, q, "x", lambda h: q_half(xx, h), q_half)
    for cp in seg_z:
        cp.wait_recv()
    seg_here.wait()
    part = SEG.at[xl, :, c]
    seg2 = [k.send(part, part, to) for to in (mate, other, other_mate)]
    for cp in gn_y:
        cp.wait_recv()
    gn_here.wait()
    gn2 = k.send(GN.at[:, xh], GN.at[:, xh], device(q, x=3 - xx))
    x_ring.relay()
    g_ring = Gather(k, q, "z", halves(g), ring_halves(G))
    up_y.relay()
    gate_x.relay()
    for cp in o1:
        cp.wait_recv()
    o1_here.wait()
    o_half = lambda j, h: WO.at[h, :, lanes(c * 8 + j * 2, 2)]
    o_y = Gather(k, q, "y", lambda h: o_half(y, h), o_half)
    w2_dealt = deal(k, q, w2, lambda j: lanes(c * 8 + xl * 4 + j), TV)
    q_y.relay()
    q_x.relay()
    up_y.near()
    up_y.end()
    a3_here.wait()
    part = W13.at[c, :, xh, xl, :, f3]
    a3 = [k.send(part, part, to) for to in xs[:2]]
    o_y.relay()
    g_ring.relay()
    for r in (q_y, q_x):
        r.near()
        r.end()
    q3 = k.send(WQ.at[c], WQ.at[c], mate)
    o_y.near()
    o_y.end()
    part = WO.at[:, :, pl.ds(pl.multiple_of(1024 * c, 1024), 1024)]
    o3 = k.send(part, part, mate)
    w2_dealt()
    heres.append(k.local(TV, T2))
    for cp in a3 + seg2 + [gn2, q3, o3]:
        cp.wait_recv()
    for cp in heres:
        cp.wait()
    for r in (gate_x, x_ring, g_ring):
        r.near()
        r.end()
    k.close()


def kv_kernel(kv, KV, ss, rs):
    q = coords()
    xx, xl, c = q["x"], q["xl"], q["c"]
    mate = device(q, c=1 - c)
    other = device(q, x=xx ^ 1)
    greet([mate, other])
    k = Copies(ss, rs)
    here = k.local(kv, KV.at[xl, :, c])
    near = k.send(kv, KV.at[xl, :, c], mate)
    far = pltpu.make_async_remote_copy(
        src_ref=kv,
        dst_ref=KV.at[0, :, c],
        send_sem=ss.at[2],
        recv_sem=rs.at[2],
        device_id=other,
        device_id_type=MESH,
    )
    on = pltpu.make_async_remote_copy(
        src_ref=KV.at[0, :, c],
        dst_ref=KV.at[0, :, c],
        send_sem=ss.at[3],
        recv_sem=rs.at[3],
        device_id=mate,
        device_id_type=MESH,
    )

    @pl.when(xl == 0)
    def _():
        far.start()
        far.wait_send()

    @pl.when(xl == 1)
    def _():
        far.wait_recv()
        on.start()
        on.wait_recv()
        on.wait_send()

    here.wait()
    near.wait_recv()
    k.close()


def middle_kernel(
    part, x, gain, t2, _, N2, H, W13, W2, p0, p1, v0, v1, below, above, n2, ss, rs
):
    q = coords()
    y, xx, xh, xl, z, c = q["y"], q["x"], q["xh"], q["xl"], q["z"], q["c"]
    ys, xs = ring(q, "y"), ring(q, "x")
    up, down = device(q, z=(z + 1) % 4), device(q, z=(z + 3) % 4)
    mate = device(q, c=1 - c)
    k = Copies(ss, rs)
    greet(ys + xs + [up, down, mate])
    z_sum = Sum(k, q, "z", ring_halves(part), halves(below), halves(above), (p0, p1))
    f1, f3 = pl.ds(0, FZ), pl.ds(FZ, FZ)
    up1 = lambda j: W13.at[c, :, j // 2, j % 2, :, f3]
    up_half = lambda j, h: W13.at[c, pl.ds(2 * h, 2), j // 2, j % 2, :, f3]
    cols = lambda cc, j, n: pl.ds(pl.multiple_of(128 * (cc * 8 + j), 128 * n), 128 * n)
    w2_here = k.local(t2, W2.at[xh, :, cols(c, xl * 4 + y, 1)])
    w2y = Gather(
        k, q, "y", lambda h: t2.at[pl.ds(352 * h, 352)],
        lambda j, h: W2.at[xh, pl.ds(352 * h, 352), cols(c, xl * 4 + j, 1)],
    )
    lower, higher = (xx + 3) % 4, (xx + 1) % 4
    far = [
        k.send(up_half(lower, 0), up_half(lower, 0), xs[0]),
        k.send(up_half(higher, 1), up_half(higher, 1), xs[1]),
    ]
    sent = [k.send(up1(j), up1(j), mate) for j in (xx, lower, higher)]
    w2y.relay()
    block = lambda j: W13.at[c, j, :, :, :, f1]
    gate = Gather(
        k, q, "y", lambda h: W13.at[c, y, h, :, :, f1], lambda j, h: W13.at[c, j, h, :, :, f1]
    )
    sent.append(k.send(block(y), block(y), mate))
    z_sum.relay(part.at[(z + 1) % 4, TOP], part.at[(z + 3) % 4, LOW], (v0, v1))
    w2_here.wait()
    w2y.near()
    w2y.end()
    down2 = lambda j: W2.at[j // 2, :, cols(c, (j % 2) * 4, 4)]
    down_half = lambda j, h: W2.at[j // 2, pl.ds(352 * h, 352), cols(c, (j % 2) * 4, 4)]
    down_ring = Gather(k, q, "x", lambda h: down_half(xx, h), down_half)
    sent.append(k.send(down2(xx), down2(xx), mate))
    z_sum.end()
    total = x[...].astype(F32) + (
        part[z].astype(F32) + (below[...].astype(F32) + above[...].astype(F32))
    )
    H[...] = total
    scale = lax.rsqrt(jnp.mean(total * total, axis=-1, keepdims=True) + EPS)
    n2[...] = to_pieces((total * scale * gain[...]).astype(BF))
    n2_ring = Gather(k, q, "z", halves(n2), ring_halves(N2))
    n2_here = k.local(n2, N2.at[z])
    gate.relay()
    down_ring.relay()
    for cp in far:
        cp.wait_recv()
    ref = up1((xx + 2) % 4)
    sent.append(k.send(ref, ref, mate))
    gate.near()
    for j in (gate.below, gate.above):
        sent.append(k.send(block(j), block(j), mate))
    n2_ring.relay()
    gate.end()
    sent.append(k.send(block(gate.far), block(gate.far), mate))
    down_ring.near()
    for j in (down_ring.below, down_ring.above):
        sent.append(k.send(down2(j), down2(j), mate))
    down_ring.end()
    sent.append(k.send(down2(down_ring.far), down2(down_ring.far), mate))
    for cp in sent:
        cp.wait_recv()
    n2_here.wait()
    n2_ring.near()
    n2_ring.end()
    k.close()


def back_kernel(
    dn2, out_part, hidden, G, N2, both, h, gain, V, D3, FA, FB, F2, DH, GAIN, *scratch
):
    (
        p0, p1, p2, p3, v0, v1, below, above, near0, near1, mine, dhb, hv, gv, nv, bv, hT,
        mate2, mate13, sum2, sum13, *bufs, ss, rs,
    ) = scratch
    q = coords()
    y, xx, z, c = q["y"], q["x"], q["z"], q["c"]
    mate = device(q, c=1 - c)
    k = Copies(ss, rs)
    get_h, get_g = k.local(hidden, hv), k.local(G, gv)
    get_n, get_b = k.local(N2, nv), k.local(both, bv)
    get_part = [
        k.local(dn2.at[(z + 1) % 4, TOP], near0),
        k.local(dn2.at[(z + 3) % 4, LOW], near1),
        k.local(dn2.at[z], mine),
    ]
    targets = [mate]
    for axis in ("x", "y", "z"):
        targets += ring(q, axis)[:2]
    greet(targets)
    z_sum = Sum(k, q, "z", ring_halves(dn2), halves(below), halves(above), (p0, p1))
    get_h.wait()
    get_g.wait()
    hT[...] = hv[...].T
    lanes = lambda cc, j: pl.ds(pl.multiple_of(1024 * cc + 256 * j, 256), 256)
    sent2, sent13 = [], []
    for j in range(4):
        mate2[j] = dot(hT[...], gv[:, lanes(1 - c, j)]).astype(BF)
        sent2.append(k.send(mate2.at[j], sum2.at[j], mate))
    get_n.wait()
    get_b.wait()
    for j in range(4):
        mate13[j] = tn(nv[:, lanes(1 - c, j)], bv[...]).astype(BF).reshape(4, 64, 2 * FZ)
        sent13.append(k.send(mate13.at[j], sum13.at[j], mate))
        if j == 0:
            for cp in get_part:
                cp.wait()
            z_sum.relay(near0, near1, (v0, v1))
    z_sum.end()
    dn = from_pieces(
        mine[...].astype(F32) + (below[...].astype(F32) + above[...].astype(F32))
    )
    back, gain_grad = rms_back(h[...], gain[...], dn)
    total = gv[pl.ds(pl.multiple_of(TOK * z, TOK), TOK)].astype(F32) + back
    DH[...] = total
    GAIN[...] = gain_grad
    dhb[...] = total.astype(BF)
    v_ring = Gather(k, q, "z", halves(dhb), ring_halves(V))
    here = k.local(dhb, V.at[z])
    for j in range(4):
        sent2[j].wait_recv()
        sum2[j] = (dot(hT[...], gv[:, lanes(c, j)]) + sum2[j].astype(F32)).astype(BF)
    half = lambda ref: lambda i: ref.at[i]
    rest = 2 * FZ - SPLIT
    jobs = [
        ("y", lambda j, i: sum2.at[j, pl.ds(704 * i, 704)], F2),
        ("x", lambda j, i: sum13.at[pl.ds(2 * i, 2), j, :, pl.ds(0, SPLIT)], FA),
        ("y", lambda j, i: sum13.at[j, pl.ds(2 * i, 2), :, pl.ds(SPLIT, rest)], FB),
    ]
    sums = []

    def start(n):
        axis, block, _ = jobs[n]
        b = bufs[4 * n : 4 * n + 4]
        sums.append(Sum(k, q, axis, block, half(b[2]), half(b[3]), (b[0].at[0], b[0].at[1])))

    def relay(n):
        axis, block, _ = jobs[n]
        b = bufs[4 * n : 4 * n + 4]
        at = q[axis]
        sums[n].relay(block((at + 1) % 4, 0), block((at + 3) % 4, 1), (b[1].at[0], b[1].at[1]))

    start(0)
    for j in range(4):
        sent13[j].wait_recv()
        own = tn(nv[:, lanes(c, j)], bv[...]).reshape(4, 64, 2 * FZ)
        sum13[j] = (own + sum13[j].astype(F32)).astype(BF)
        if j == 1:
            v_ring.relay()
    start(1)
    start(2)
    out_sum = Sum(
        k, q, "z", ring_halves(out_part), halves(D3.at[0]), halves(D3.at[1]), (p2, p3)
    )
    get_part = [
        k.local(out_part.at[(z + 1) % 4, TOP], near0),
        k.local(out_part.at[(z + 3) % 4, LOW], near1),
    ]
    relay(0)
    relay(1)
    relay(2)
    for cp in get_part:
        cp.wait()
    z_sum.sent()
    out_sum.relay(near0, near1, (v0, v1))
    done = []
    for n in range(3):
        axis, block, out = jobs[n]
        b = bufs[4 * n : 4 * n + 4]
        sums[n].end()
        for i in range(2):
            total = block(q[axis], i)[...].astype(F32) + (
                b[2][i].astype(F32) + b[3][i].astype(F32)
            )
            b[2][i] = total.astype(BF)
        done.append(k.local(b[2], out))
    v_ring.near()
    v_ring.end()
    here.wait()
    out_sum.end()
    for cp in done:
        cp.wait()
    k.close()


def dkv_kernel(dkv, cosine, sine, out, R, ss, rs):
    q = coords()
    xx, xl, c = q["x"], q["xl"], q["c"]
    mate = device(q, c=1 - c)
    other = device(q, x=xx ^ 1)
    other_mate = device(q, x=xx ^ 1, c=1 - c)
    greet([mate, other, other_mate])
    k = Copies(ss, rs)
    near = k.send(dkv.at[xl, :, 1 - c], R.at[0], mate)
    far = [
        pltpu.make_async_remote_copy(
            src_ref=dkv.at[0, :, cc],
            dst_ref=R.at[1 + i],
            send_sem=ss.at[1 + i],
            recv_sem=rs.at[1 + i],
            device_id=to,
            device_id_type=MESH,
        )
        for i, (to, cc) in enumerate(((other, c), (other_mate, 1 - c)))
    ]

    @pl.when(xl == 1)
    def _():
        R[1] = jnp.zeros(R.shape[1:], BF)
        R[2] = jnp.zeros(R.shape[1:], BF)
        for cp in far:
            cp.start()
        for cp in far:
            cp.wait_send()

    @pl.when(xl == 0)
    def _():
        for cp in far:
            cp.wait_recv()

    near.wait_recv()
    for i in range(RING):
        w = dkv[xl, i, c].astype(F32) + R[0, i].astype(F32)
        w = w + (R[1, i].astype(F32) + R[2, i].astype(F32))
        lane = lax.broadcasted_iota(jnp.int32, w.shape, 1)
        out[i] = jnp.where(lane < HEAD_DIM, w * cosine[i] - swapped(w) * sine[i], w).astype(BF)
    k.close()


def quarter(xt, rows):
    return (
        pl.ds(pl.multiple_of((xt // 2) * rows, rows), rows),
        pl.ds(pl.multiple_of((xt % 2) * 128, 128), 128),
    )


def wide_kernel(
    dn, fa, fb, f2, sq, so, D2, G1, G3, G2, FQ, FO,
    p0, p1, v0, v1, la, lb, l2, pa, pb, p2, t2, rq, ro, ss, rs,
):
    q = coords()
    y, xx, xh, xl, z, c = q["y"], q["x"], q["xh"], q["xl"], q["z"], q["c"]
    zs, ys, xs = ring(q, "z"), ring(q, "y"), ring(q, "x")
    mate, other = device(q, c=1 - c), device(q, x=xx ^ 1)
    greet(zs + ys + xs + [mate], q)
    k = Copies(ss, rs)
    steps = (1, 3, 2)
    z_sum = Sum(k, q, "z", ring_halves(dn), halves(D2.at[0]), halves(D2.at[1]), (p0, p1))
    leg_2 = []
    for i, s in enumerate(steps):
        r, cc = quarter((xx + s) % 4, 704)
        leg_2.append(k.send(f2.at[r, cc], l2.at[i], xs[i]))
    leg_a = [k.send(fa.at[(y + s) % 4], la.at[i], ys[i]) for i, s in enumerate(steps)]
    leg_b = [k.send(fb.at[(xx + s) % 4], lb.at[i], xs[i]) for i, s in enumerate(steps)]
    z_sum.relay(dn.at[(z + 1) % 4, TOP], dn.at[(z + 3) % 4, LOW], (v0, v1))
    for cp in leg_2:
        cp.wait_recv()
    r, cc = quarter(xx, 704)
    p2[...] = add4(f2[r, cc], l2[0], l2[1], l2[2])
    turned = turn(k, q, [(p2, t2)])
    heavy = []
    for i, s in enumerate(steps):
        cols = pl.ds(pl.multiple_of(256 * ((y + s) % 4), 256), 256)
        heavy.append(k.send(so.at[:, cols], ro.at[i], ys[i]))
        heavy.append(k.send(sq.at[(y + s) % 4], rq.at[i], ys[i]))
    for cp in leg_a:
        cp.wait_recv()
    pa[...] = add4(fa[y], la[0], la[1], la[2])
    for cp in leg_b:
        cp.wait_recv()
    pb[...] = add4(fb[xx], lb[0], lb[1], lb[2])
    at = lambda zz, off, n: pl.ds(pl.multiple_of(FZ * zz + off, 128), n)
    rows = pl.ds(pl.multiple_of(128 * c + 64 * xl, 64), 64)
    pair = pl.ds(pl.multiple_of(128 * c, 128), 128)
    f1 = pl.ds(0, FZ)
    rest = SPLIT - FZ
    own = [
        (pa.at[:, f1], G1.at[rows, at(z, 0, FZ)]),
        (pa.at[:, pl.ds(FZ, rest)], G3.at[rows, at(z, 0, rest)]),
        (pb, G3.at[rows, at(z, rest, FZ - rest)]),
    ]
    half_rows = lambda h: pl.ds(pl.multiple_of(128 * c + 64 * xl + 32 * h, 32), 32)

    def over_z(src, ref, off, n):
        return Gather(
            k, q, "z", lambda h: src.at[pl.ds(32 * h, 32)],
            lambda j, h: ref.at[half_rows(h), at(j, off, n)],
        )

    rings = [
        over_z(pa.at[:, f1], G1, 0, FZ),
        over_z(pa.at[:, pl.ds(FZ, rest)], G3, 0, rest),
        over_z(pb, G3, rest, FZ - rest),
    ]
    to_x = [k.send(src, dst, other) for src, dst in own]
    heres = [k.local(src, dst) for src, dst in own]
    for r in rings:
        r.relay()
    turned()
    col = pl.ds(pl.multiple_of(128 * (c * 8 + z * 2 + xl), 128), 128)
    down_x = k.send(t2, G2.at[:, col], other)
    down_here = k.local(t2, G2.at[:, col])
    blocks = lambda j: [G1.at[rows, at(j, 0, FZ)], G3.at[rows, at(j, 0, FZ)]]
    for r in rings:
        r.near()
    for j in (rings[0].below, rings[0].above):
        to_x += [k.send(ref, ref, other) for ref in blocks(j)]
    down_x.wait_recv()
    down_here.wait()
    down_half = lambda j, h: G2.at[
        pl.ds(352 * h, 352), pl.ds(pl.multiple_of(128 * (c * 8 + j * 2), 256), 256)
    ]
    down_ring = Gather(k, q, "z", lambda h: down_half(z, h), down_half)
    for r in rings:
        r.end()
    to_x += [k.send(ref, ref, other) for ref in blocks(rings[0].far)]
    down_ring.relay()
    for cp in heavy:
        cp.wait_recv()
    cols = pl.ds(pl.multiple_of(256 * y, 256), 256)
    ro[0] = add4(so[:, cols], ro[0], ro[1], ro[2])
    rq[0] = add4(sq[y], rq[0], rq[1], rq[2])
    done = [k.local(ro.at[0], FO), k.local(rq.at[0], FQ)]
    down_ring.near()
    down_ring.end()
    ref = G2.at[:, pl.ds(pl.multiple_of(1024 * c, 1024), 1024)]
    last = [k.send(ref, ref, mate)]
    for cp in to_x:
        cp.wait_recv()
    for cp in heres:
        cp.wait()
    last += [k.send(ref.at[pair], ref.at[pair], mate) for ref in (G1, G3)]
    for cp in last:
        cp.wait_recv()
    for cp in done:
        cp.wait()
    z_sum.end()
    k.close()


def last_kernel(
    fq, fo, gain1, gain2, GO, GQ, GKV, gain_out,
    lq, lo, pq, po, to_, gain, s0, s1, s2, s3, s4, total, ss, rs,
):
    q = coords()
    y, xx, xh, xl, z, c = q["y"], q["x"], q["xh"], q["xl"], q["z"], q["c"]
    zs, ys, xs = ring(q, "z"), ring(q, "y"), ring(q, "x")
    mate, other, cross = device(q, c=1 - c), device(q, x=xx ^ 1), device(q, x=3 - xx)
    gain[...] = jnp.zeros_like(gain)
    for d in range(8):
        gain[d // 2, d % 2, 0:1] = gain1[:, 256 * d : 256 * d + 256]
        gain[d // 2, d % 2, 1:2] = gain2[:, 256 * d : 256 * d + 256]
    greet(zs + ys + xs + [mate], q)
    k = Copies(ss, rs)
    steps = (1, 3, 2)
    leg_o, leg_q = [], []
    for i, s in enumerate(steps):
        r, cc = quarter((xx + s) % 4, 256)
        leg_o.append(k.send(fo.at[r, cc], lo.at[i], xs[i]))
    gain_y = [k.send(gain.at[(y + s) % 4], s0.at[y], ys[i]) for i, s in enumerate(steps)]
    gain_here = k.local(gain.at[y], s0.at[y])
    for i, s in enumerate(steps):
        leg_q.append(k.send(fq.at[(xx + s) % 4], lq.at[i], xs[i]))
    for cp in leg_o:
        cp.wait_recv()
    r, cc = quarter(xx, 256)
    po[...] = add4(fo[r, cc], lo[0], lo[1], lo[2])
    turned = turn(k, q, [(po, to_)])
    for cp in gain_y:
        cp.wait_recv()
    gain_here.wait()
    s1[0] = (s0[0] + s0[1]) + (s0[2] + s0[3])
    gain_x = k.send(s1.at[0, 1 - xh], s1.at[1, 0], cross)
    for cp in leg_q:
        cp.wait_recv()
    pq[...] = add4(fq[xx], lq[0], lq[1], lq[2])
    rows = pl.ds(pl.multiple_of(128 * c + 64 * xl, 64), 64)
    qc = lambda j: pl.ds(pl.multiple_of(QZ * j, 128), QZ)
    kc = lambda j: pl.ds(pl.multiple_of(128 * j, 128), 128)
    own = [
        (pq.at[:, pl.ds(0, QZ)], GQ.at[rows, qc(z)]),
        (pq.at[:, pl.ds(QZ, 128)], GKV.at[rows, kc(z)]),
    ]
    q_x = [k.send(src, dst, other) for src, dst in own]
    q_here = [k.local(src, dst) for src, dst in own]
    gain_x.wait_recv()
    s2[z] = s1[0, xh] + s1[1, 0]
    gain_z = [k.send(s2.at[z], s2.at[z], to) for to in zs]
    turned()
    col = pl.ds(pl.multiple_of(128 * (c * 8 + z * 2 + xl), 128), 128)
    o_x = k.send(to_, GO.at[:, col], other)
    o_here = k.local(to_, GO.at[:, col])
    for cp in q_x:
        cp.wait_recv()
    for cp in q_here:
        cp.wait()
    half_rows = lambda h: pl.ds(pl.multiple_of(128 * c + 64 * h, 64), 64)
    q_half = lambda j, h: GQ.at[half_rows(h), qc(j)]
    kv_half = lambda j, h: GKV.at[half_rows(h), kc(j)]
    rings = [Gather(k, q, "z", lambda h: f(z, h), f) for f in (q_half, kv_half)]
    o_x.wait_recv()
    o_here.wait()
    o_half = lambda j, h: GO.at[
        pl.ds(128 * h, 128), pl.ds(pl.multiple_of(128 * (c * 8 + j * 2), 256), 256)
    ]
    rings.append(Gather(k, q, "z", lambda h: o_half(z, h), o_half))
    for cp in gain_z:
        cp.wait_recv()
    s3[0] = (s2[0] + s2[1]) + (s2[2] + s2[3])
    gain_x = k.send(s3.at[0], s3.at[1], other)
    for r in rings:
        r.relay()
    gain_x.wait_recv()
    s4[0] = s3[0] + s3[1]
    gain_c = k.send(s4.at[0], s4.at[1], mate)
    for r in rings:
        r.near()
        r.end()
    pair = pl.ds(pl.multiple_of(128 * c, 128), 128)
    refs = [GQ.at[pair], GKV.at[pair], GO.at[:, pl.ds(pl.multiple_of(1024 * c, 1024), 1024)]]
    last = [k.send(ref, ref, mate) for ref in refs]
    gain_c.wait_recv()
    total[...] = s4[0] + s4[1]
    gain_done = k.local(total, gain_out)
    for cp in last:
        cp.wait_recv()
    gain_done.wait()
    k.close()


PARAMS = pltpu.CompilerParams(vmem_limit_bytes=VMEM_LIMIT)


def add4(a, b, c, d):
    a, b, c, d = (v.astype(F32) for v in (a, b, c, d))
    return ((a + b) + (c + d)).astype(BF)


def to_pieces(v):
    return jnp.concatenate(
        [v[:, 256 * d + 128 * c : 256 * d + 128 * c + 128] for c in range(2) for d in range(8)],
        axis=1,
    )


def from_pieces(v):
    return jnp.concatenate(
        [v[:, 1024 * c + 128 * d : 1024 * c + 128 * d + 128] for d in range(8) for c in range(2)],
        axis=1,
    )


def swapped(u):
    lane = lax.broadcasted_iota(jnp.int32, u.shape, 1)
    return jnp.where(lane % 64 < 32, pltpu.roll(u, 96, 1), pltpu.roll(u, 32, 1))


def project_kernel(x, gain, w, cosine, sine, n1, query, kv):
    two = 2 * TOK
    xv = x[...].reshape(two, D).astype(F32)
    scale = lax.rsqrt(jnp.mean(xv * xv, axis=-1, keepdims=True) + EPS)
    normed = to_pieces((xv * scale * gain[...]).astype(BF))
    n1[...] = normed.reshape(2, TOK, D)
    cos, sin = cosine[...].reshape(two, 128), sine[...].reshape(two, 128)
    mixed = jnp.dot(normed, w[...], preferred_element_type=F32)
    for j in range(5):
        u = mixed[:, 128 * j : 128 * j + 128]
        turned = u * cos + swapped(u) * sin
        if j < 4:
            query[:, :, 128 * j : 128 * j + 128] = turned.astype(BF).reshape(2, TOK, 128)
        else:
            lane = lax.broadcasted_iota(jnp.int32, u.shape, 1)
            kv[...] = jnp.where(lane < HEAD_DIM, turned, u).astype(BF).reshape(2, TOK, 128)


def project(x, gain, w, cosine, sine):
    chunk = lambda cols: pl.BlockSpec((2, TOK, cols), lambda i: (i, 0, 0))
    whole = lambda shape: pl.BlockSpec(shape, lambda i: (0,) * len(shape))
    return pl.pallas_call(
        project_kernel,
        name="project",
        cost_estimate=cost(7),
        grid=(2,),
        in_specs=[chunk(D), whole((1, D)), whole((D, MZ)), chunk(128), chunk(128)],
        out_specs=[chunk(D), chunk(QZ), chunk(128)],
        out_shape=[
            jax.ShapeDtypeStruct((RING, TOK, D), BF),
            jax.ShapeDtypeStruct((RING, TOK, QZ), BF),
            jax.ShapeDtypeStruct((RING, TOK, 128), BF),
        ],
        compiler_params=PARAMS,
    )(x, gain, w, cosine, sine)


def stacked_low(tiles):
    out = []
    for pair in range(4):
        tile = tiles[:, 128 * pair : 128 * pair + 128].astype(F32)
        lane = lax.broadcasted_iota(jnp.int32, tile.shape, 1)
        out.append(jnp.where(lane < HEAD_DIM, tile, 0.0))
        out.append(jnp.where(lane < HEAD_DIM, pltpu.roll(tile, 64, 1), 0.0))
    return jnp.concatenate(out, axis=0)


def stacked_high(tiles):
    out = []
    for pair in range(4):
        tile = tiles[:, 128 * pair : 128 * pair + 128].astype(F32)
        lane = lax.broadcasted_iota(jnp.int32, tile.shape, 1)
        out.append(jnp.where(lane >= HEAD_DIM, pltpu.roll(tile, 64, 1), 0.0))
        out.append(jnp.where(lane >= HEAD_DIM, tile, 0.0))
    return jnp.concatenate(out, axis=0)


def unstacked(v):
    tiles = []
    for pair in range(4):
        both = jnp.concatenate(
            [v[:, 256 * pair : 256 * pair + 128], v[:, 256 * pair + 128 : 256 * pair + 256]],
            axis=0,
        )
        tiles.append(both.T)
    return tiles


def nt(a, b):
    return lax.dot_general(a, b, (((1,), (1,)), ((), ())), preferred_element_type=F32)


def tn(a, b):
    return lax.dot_general(a, b, (((0,), (0,)), ((), ())), preferred_element_type=F32)


def chunk_scores(keys, stacked, kc, chunk, start):
    raw = nt(keys, stacked)
    key = kc * TOK + lax.broadcasted_iota(jnp.int32, raw.shape, 0)
    query = chunk * TOK + lax.broadcasted_iota(jnp.int32, raw.shape, 1) % TOK
    return jnp.where((key <= query) & (key >= start), raw, -1e30)


def attend_kernel(info, query, kv, start, out, logsum):
    i = pl.program_id(0)
    low, chunk = info[0, i], info[1, i]
    stacked = (stacked_low(query[0]) * (1.0 / HEAD_DIM**0.5)).astype(BF)
    starts = jnp.concatenate([start[0]] * GROUP, axis=1)

    def step(kc, carry):
        top, summed, total = carry
        keys = kv[kc]
        scores = chunk_scores(keys, stacked, kc, chunk, starts)
        new_top = jnp.maximum(top, jnp.max(scores, axis=0, keepdims=True))
        weights = jnp.exp(scores - new_top)
        fade = jnp.exp(top - new_top)
        summed = summed * fade + jnp.sum(weights, axis=0, keepdims=True)
        part = tn(keys, weights.astype(BF))
        return new_top, summed, total * fade + part[HEAD_DIM:]

    rows = GROUP * TOK
    carry = (jnp.full((1, rows), -1e30, F32), jnp.zeros((1, rows), F32), jnp.zeros((64, rows), F32))
    top, summed, total = lax.fori_loop(low, chunk + 1, step, carry)
    for pair, tile in enumerate(unstacked(total / summed)):
        out[0, :, 128 * pair : 128 * pair + 128] = tile.astype(BF)
    logsum[0] = top + jnp.log(summed)


def attend(info, query, kv, start):
    chunk = lambda r, cols: pl.BlockSpec((1, r, cols), lambda i, s: (i, 0, 0))
    return pl.pallas_call(
        attend_kernel,
        name="attend",
        cost_estimate=cost(12),
        grid_spec=pltpu.PrefetchScalarGridSpec(
            num_scalar_prefetch=1,
            grid=(RING,),
            in_specs=[
                chunk(TOK, QZ),
                pl.BlockSpec((16, TOK, 128), lambda i, s: (0, 0, 0)),
                chunk(1, TOK),
            ],
            out_specs=[chunk(TOK, QZ), chunk(1, GROUP * TOK)],
        ),
        out_shape=[
            jax.ShapeDtypeStruct((RING, TOK, QZ), BF),
            jax.ShapeDtypeStruct((RING, 1, GROUP * TOK), F32),
        ],
        compiler_params=PARAMS,
    )(info, query, kv, start)


def attend_back_kernel(
    info, query, kv, start, out, grad_out, logsum, cosine, sine, dquery, dkv, total
):
    i = pl.program_id(0)
    low, chunk = info[0, i], info[1, i]
    stacked = (stacked_low(query[0]) * (1.0 / HEAD_DIM**0.5)).astype(BF)
    grads = stacked_high(grad_out[0]).astype(BF)
    starts = jnp.concatenate([start[0]] * GROUP, axis=1)
    lse = logsum[0]
    deltas = []
    for pair in range(4):
        cols = slice(128 * pair, 128 * pair + 128)
        prod = (out[0, :, cols].astype(F32) * grad_out[0, :, cols].astype(F32)).T
        deltas.append(jnp.sum(prod[:HEAD_DIM], axis=0, keepdims=True))
        deltas.append(jnp.sum(prod[HEAD_DIM:], axis=0, keepdims=True))
    delta = jnp.concatenate(deltas, axis=1)

    @pl.when(i == 0)
    def _():
        total[...] = jnp.zeros_like(total)

    def step(kc, dq):
        keys = kv[kc]
        scores = chunk_scores(keys, stacked, kc, chunk, starts)
        probs = jnp.exp(scores - lse)
        grad_probs = nt(keys, grads)
        grad_scores = (probs * (grad_probs - delta)).astype(BF)
        total[kc] += jnp.dot(grad_scores, stacked, preferred_element_type=F32) + jnp.dot(
            probs.astype(BF), grads, preferred_element_type=F32
        )
        return dq + tn(keys, grad_scores)[:HEAD_DIM]

    dq = lax.fori_loop(low, chunk + 1, step, jnp.zeros((64, GROUP * TOK), F32))
    cos, sin = cosine[0], sine[0]
    for pair, tile in enumerate(unstacked(dq)):
        tile = tile * (1.0 / HEAD_DIM**0.5)
        dquery[0, :, 128 * pair : 128 * pair + 128] = (tile * cos - swapped(tile) * sin).astype(BF)

    @pl.when(i == RING - 1)
    def _():
        dkv[...] = total[...].astype(BF)


def attend_back(info, query, kv, start, out, grad_out, logsum, cosine, sine):
    chunk = lambda r, cols: pl.BlockSpec((1, r, cols), lambda i, s: (i, 0, 0))
    whole = pl.BlockSpec((16, TOK, 128), lambda i, s: (0, 0, 0))
    return pl.pallas_call(
        attend_back_kernel,
        name="attend_back",
        cost_estimate=cost(15),
        grid_spec=pltpu.PrefetchScalarGridSpec(
            num_scalar_prefetch=1,
            grid=(RING,),
            in_specs=[
                chunk(TOK, QZ),
                whole,
                chunk(1, TOK),
                chunk(TOK, QZ),
                chunk(TOK, QZ),
                chunk(1, GROUP * TOK),
                chunk(TOK, 128),
                chunk(TOK, 128),
            ],
            out_specs=[chunk(TOK, QZ), whole],
            scratch_shapes=[pltpu.VMEM((16, TOK, 128), F32)],
        ),
        out_shape=[
            jax.ShapeDtypeStruct((RING, TOK, QZ), BF),
            jax.ShapeDtypeStruct((16, TOK, 128), BF),
        ],
        compiler_params=PARAMS,
    )(info, query, kv, start, out, grad_out, logsum, cosine, sine)


def rms_back(v, gain, grad):
    scale = lax.rsqrt(jnp.mean(v * v, axis=-1, keepdims=True) + EPS)
    unit = v * scale
    gain_grad = jnp.sum(grad * unit, axis=0, keepdims=True)
    inner = grad * gain
    return scale * (inner - unit * jnp.mean(inner * unit, axis=-1, keepdims=True)), gain_grad


def norm_back_kernel(v, base, a, b, c, gain, grad, gain_out):
    dn = from_pieces(a[...].astype(F32) + (b[...].astype(F32) + c[...].astype(F32)))
    back, gain_grad = rms_back(v[...].astype(F32), gain[...], dn)
    grad[...] = base[...] + back
    gain_out[...] = gain_grad


def norm_back(v, base, parts, gain):
    return pl.pallas_call(
        norm_back_kernel,
        name="norm_back",
        cost_estimate=cost(4),
        out_shape=[jax.ShapeDtypeStruct((TOK, D), F32), jax.ShapeDtypeStruct((1, D), F32)],
        compiler_params=PARAMS,
    )(v, base, *parts, gain)


def pick(v, index, axis=0):
    return lax.dynamic_index_in_dim(v, index, axis, keepdims=False)


def dot(a, b):
    return jnp.dot(a, b, preferred_element_type=F32)


def body(tokens, segments, cotangent, norm_attn, norm_ffn, wqkv, wo, w1, w3, w2):
    q = coords()
    y, xx, xl, z, c = q["y"], q["x"], q["xl"], q["z"], q["c"]
    x = tokens[0]
    g = cotangent[0]
    X, G, SEG, GN, WQ, WO, W13, t2 = talk(
        fetch_kernel,
        "fetch",
        1,
        40,
        100,
        (x, g, segments, norm_attn[None], norm_ffn[None], wqkv, wo, w1, w3, w2),
        [
            ((RING, TOK, D), BF),
            ((RING, TOK, D), BF),
            ((2, 4, 2, 8, TOK), jnp.int32),
            ((4, 2, 32, 256), BF),
            ((2, 4, 2, 2, 64, MZ), BF),
            ((2, 256, D), BF),
            ((2, 4, 2, 2, 64, 2 * FZ), BF),
            ((704, 128), BF),
        ],
        scratch=[
            pltpu.VMEM((256, 128), BF),
            pltpu.VMEM((704, 128), BF),
            pltpu.VMEM((64, MZ), BF),
            pltpu.VMEM((64, 128), BF),
            pltpu.VMEM((64, 128), BF),
            pltpu.VMEM((64, FZ), BF),
            pltpu.VMEM((64, FZ), BF),
            pltpu.VMEM((8, TOK), jnp.int32),
            pltpu.VMEM((32, 256), BF),
        ],
        near=(0, 1, 2, 3, 4),
    )

    docs = SEG[:, :, :, 0, :].reshape(16 * TOK)
    mine = pick(pick(SEG[:, :, :, 0, :], xl, 0), c, 1)
    chunks = xl * 8 + 2 * jnp.arange(4, dtype=jnp.int32) + c
    start = jnp.sum((docs[None, None, :] < mine[:, :, None]).astype(jnp.int32), axis=2)
    index = chunks[:, None] * TOK + jnp.arange(TOK, dtype=jnp.int32)[None]
    place = (index - start).astype(F32)
    lane = jnp.arange(128)
    freq = THETA ** (-(lane % 32).astype(F32) * 2.0 / HEAD_DIM)
    angle = place[:, :, None] * freq[None, None, :]
    cosine = jnp.cos(angle)
    sine = jnp.sin(angle) * jnp.where(lane % 64 < 32, -1.0, 1.0)
    info = jnp.stack([jnp.min(start, axis=1) // TOK, chunks])
    start = start[:, None, :]
    gain_attn = GN[:, :, 0, :].reshape(1, D).astype(F32)
    gain_ffn = GN[:, :, 16, :].reshape(1, D).astype(F32)

    WQ = WQ.reshape(D, MZ)
    WO = WO.reshape(QZ, D)
    n1, query, kv = project(X, gain_attn, WQ, cosine, sine)
    (KV,) = talk(
        kv_kernel, "kv", 2, 7, 4, (kv,), [((2, 4, 2, TOK, 128), BF)], near=(0,)
    )
    KV = KV.reshape(16, TOK, 128)
    heads_out, logsum = attend(info, query, KV, start)
    o = heads_out.reshape(RING * TOK, QZ)
    part = dot(o, WO).astype(BF).reshape(RING, TOK, D)
    N2, h, W13, W2 = talk(
        middle_kernel,
        "middle",
        3,
        42,
        60,
        (part, x, gain_ffn, t2, W13),
        [
            ((RING, TOK, D), BF),
            ((TOK, D), F32),
            ((2, 4, 2, 2, 64, 2 * FZ), BF),
            ((2, 704, D), BF),
        ],
        scratch=[
            *[pltpu.VMEM(HALF, BF)] * 4,
            *[pltpu.VMEM((TOK, D), BF)] * 3,
        ],
        near=(0, 1, 2, 3),
        near_out=(1,),
        alias={4: 2},
    )
    N2, G = N2.reshape(RING * TOK, D), G.reshape(RING * TOK, D)
    W13, W2 = W13.reshape(D, 2 * FZ), W2.reshape(FZ, D)
    gate, up = dot(N2, W13[:, :FZ]), dot(N2, W13[:, FZ:])
    hidden = (jax.nn.silu(gate) * up).astype(BF)
    dhid = jnp.einsum("td,fd->tf", G, W2, preferred_element_type=F32)
    sigma = jax.nn.sigmoid(gate)
    dgate = (dhid * up * sigma * (1.0 + gate * (1.0 - sigma))).astype(BF)
    dup = (dhid * gate * sigma).astype(BF)
    both = jnp.concatenate([dgate, dup], axis=1)
    dn2 = jnp.einsum("tf,df->td", both, W13, preferred_element_type=F32)
    dn2 = dn2.astype(BF).reshape(RING, TOK, D)
    out_part = dot(hidden, W2).astype(BF).reshape(RING, TOK, D)
    half = lambda v, j: lax.dynamic_slice_in_dim(v, 1024 * j, 1024, 1)
    outer = lambda a, b: jnp.einsum("ta,tb->ab", a, b, preferred_element_type=F32)
    rest = 2 * FZ - SPLIT
    buffers = []
    for shape in ((704, 256), (2, 64, SPLIT), (2, 64, rest)):
        buffers += [pltpu.VMEM((2,) + shape, BF)] * 4
    DH, D3, fa, fb, f2, dh, gain2 = talk(
        back_kernel,
        "back",
        4,
        60,
        100,
        (dn2, out_part, hidden, G, N2, both, h, gain_ffn),
        [
            ((RING, TOK, D), BF),
            ((2, TOK, D), BF),
            ((2, 2, 64, SPLIT), BF),
            ((2, 2, 64, rest), BF),
            ((2, 704, 256), BF),
            ((TOK, D), F32),
            ((1, D), F32),
        ],
        scratch=[
            *[pltpu.VMEM(HALF, BF)] * 6,
            *[pltpu.VMEM((TOK, D), BF)] * 2,
            *[pltpu.VMEM(HALF, BF)] * 2,
            *[pltpu.VMEM((TOK, D), BF)] * 2,
            pltpu.VMEM((RING * TOK, FZ), BF),
            pltpu.VMEM((RING * TOK, D), BF),
            pltpu.VMEM((RING * TOK, D), BF),
            pltpu.VMEM((RING * TOK, 2 * FZ), BF),
            pltpu.VMEM((FZ, RING * TOK), BF),
            pltpu.VMEM((4, FZ, 256), BF),
            pltpu.VMEM((4, 4, 64, 2 * FZ), BF),
            pltpu.VMEM((4, FZ, 256), BF),
            pltpu.VMEM((4, 4, 64, 2 * FZ), BF),
            *buffers,
        ],
        near=(6, 7),
        near_out=(5, 6),
    )
    fa, fb = fa.reshape(4, 64, SPLIT), fb.reshape(4, 64, rest)
    f2 = f2.reshape(1408, 256)
    DH = DH.reshape(RING * TOK, D)
    dheads = jnp.einsum("td,qd->tq", DH, WO, preferred_element_type=F32).astype(BF)
    dquery, dkv = attend_back(
        info, query, KV, start, heads_out, dheads.reshape(RING, TOK, QZ), logsum, cosine, sine
    )
    dkv = dkv.reshape(2, 4, 2, TOK, 128)
    (dkv_rot,) = talk(
        dkv_kernel,
        "dkv",
        5,
        8,
        4,
        (dkv, cosine, sine),
        [((RING, TOK, 128), BF)],
        scratch=[pltpu.VMEM((3, RING, TOK, 128), BF)],
        near=(0, 1, 2),
        near_out=(0,),
    )
    dmixed = jnp.concatenate([dquery, dkv_rot], axis=2).reshape(RING * TOK, MZ)
    dn1 = jnp.einsum("tc,dc->td", dmixed, WQ, preferred_element_type=F32)
    dn1 = dn1.astype(BF).reshape(RING, TOK, D)

    n1 = n1.reshape(RING * TOK, D)
    other_o = move(outer(o, half(DH, 1 - c)).astype(BF), "c", 1)
    sum_o = (outer(o, half(DH, c)) + other_o.astype(F32)).astype(BF)
    other_q = move(outer(half(n1, 1 - c), dmixed).astype(BF), "c", 1)
    sum_q = (outer(half(n1, c), dmixed) + other_q.astype(F32)).astype(BF)
    sum_q = sum_q.reshape(4, 4, 64, MZ)
    D1, G1, G3, G2, fq, fo = talk(
        wide_kernel,
        "wide",
        6,
        55,
        90,
        (dn1, fa, fb, f2, sum_q, sum_o),
        [
            ((2, TOK, D), BF),
            ((256, 4 * FZ), BF),
            ((256, 4 * FZ), BF),
            ((704, D), BF),
            ((4, 64, MZ), BF),
            ((512, 256), BF),
        ],
        scratch=[
            *[pltpu.VMEM(HALF, BF)] * 4,
            pltpu.VMEM((3, 64, SPLIT), BF),
            pltpu.VMEM((3, 64, rest), BF),
            pltpu.VMEM((3, 704, 128), BF),
            pltpu.VMEM((64, SPLIT), BF),
            pltpu.VMEM((64, rest), BF),
            pltpu.VMEM((704, 128), BF),
            pltpu.VMEM((704, 128), BF),
            pltpu.VMEM((3, 4, 64, MZ), BF),
            pltpu.VMEM((3, 512, 256), BF),
        ],
        near=(0, 1, 2, 3, 4, 5),
    )
    input_grad, gain1 = norm_back(x, dh, (pick(dn1, z), D1[0], D1[1]), gain_attn)

    small = (8, 256)
    GO, GQ, GKV, gain_out = talk(
        last_kernel,
        "last",
        7,
        30,
        60,
        (fq, fo, gain1, gain2),
        [
            ((256, D), BF),
            ((256, QDIM), BF),
            ((256, 2 * KVDIM), BF),
            (small, F32),
        ],
        scratch=[
            pltpu.VMEM((3, 64, MZ), BF),
            pltpu.VMEM((3, 256, 128), BF),
            pltpu.VMEM((64, MZ), BF),
            pltpu.VMEM((256, 128), BF),
            pltpu.VMEM((256, 128), BF),
            pltpu.VMEM((4, 2) + small, F32),
            pltpu.VMEM((4, 2) + small, F32),
            pltpu.VMEM((2, 2) + small, F32),
            pltpu.VMEM((4,) + small, F32),
            pltpu.VMEM((2,) + small, F32),
            pltpu.VMEM((2,) + small, F32),
            pltpu.VMEM(small, F32),
        ],
        near=(0, 1, 2, 3),
    )
    pairs = GKV.reshape(256, 4, 2, HEAD_DIM)
    flat = lambda v: v.reshape(256, -1)
    grad_qkv = jnp.concatenate([GQ, flat(pairs[:, :, 0]), flat(pairs[:, :, 1])], axis=1)
    own = pick(out_part, z).astype(F32)
    output = h + (own + (D3[0].astype(F32) + D3[1].astype(F32)))
    return (
        output[None],
        input_grad[None],
        gain_out[0],
        gain_out[1],
        grad_qkv.astype(F32),
        GO.astype(F32),
        G1.astype(F32),
        G3.astype(F32),
        G2.astype(F32),
    )


def solution(mesh):
    rows = P("dp", None)
    acts = P("dp", "ctx", None)
    return jax.shard_map(
        body,
        mesh=mesh,
        in_specs=(acts, P("dp", "ctx"), acts, P("dp"), P("dp"), rows, rows, rows, rows, rows),
        out_specs=(acts, acts, P("dp"), P("dp"), rows, rows, rows, rows, rows),
        check_vma=False,
    )
```

```python
import functools

import jax
import jax.numpy as jnp
from jax import lax
from jax.experimental import pallas as pl
from jax.experimental.pallas import tpu as pltpu
from jax.sharding import PartitionSpec as P

D = 2048
HEAD_DIM = 64
TOK = 128
RING = 4
QDIM = 2048
KVDIM = 256
GROUP = 8
QZ = 512
MZ = 640
FZ = 1408
SPLIT = 2048
EPS = 1e-05
THETA = 10000.0
MESH = pl.DeviceIdType.MESH
VMEM_LIMIT = 60 << 20
BF = jnp.bfloat16
F32 = jnp.float32
ANY = pl.BlockSpec(memory_space=pl.ANY)
VMEM = pl.BlockSpec(memory_space=pltpu.VMEM)


def coords():
    dp, ctx = lax.axis_index("dp"), lax.axis_index("ctx")
    y, xh = dp // 2, dp % 2
    xl, z, c = ctx // 8, (ctx // 2) % 4, ctx % 2
    return dict(y=y, x=xh * 2 + xl, xh=xh, xl=xl, z=z, c=c)


def device(q, **change):
    r = {k: change.get(k, q[k]) for k in ("y", "x", "z", "c")}
    return (r["y"] * 2 + r["x"] // 2, (r["x"] % 2) * 8 + r["z"] * 2 + r["c"])


def ring(q, axis):
    return [device(q, **{axis: (q[axis] + s) % 4}) for s in (1, 3, 2)]


def shift_pairs(axis, by):
    size = 2 if axis == "c" else 4
    pairs = []
    for y in range(4):
        for x in range(4):
            for z in range(4):
                for c in range(2):
                    q = dict(y=y, x=x, z=z, c=c)
                    pairs.append((device(q), device(q, **{axis: (q[axis] + by) % size})))
    return [(a[0] * 16 + a[1], b[0] * 16 + b[1]) for a, b in pairs]


def swap_pairs():
    pairs = []
    for y in range(4):
        for x in range(4):
            for z in range(4):
                for c in range(2):
                    q = dict(y=y, x=x, z=z, c=c)
                    pairs.append((device(q), device(q, y=z, z=y)))
    return [(a[0] * 16 + a[1], b[0] * 16 + b[1]) for a, b in pairs]


def move(v, axis, by):
    return lax.ppermute(v, ("dp", "ctx"), shift_pairs(axis, by))


class Copies:
    def __init__(self, send_sems, recv_sems):
        self.send_sems, self.recv_sems, self.n, self.open = send_sems, recv_sems, 0, []

    def send(self, src, dst, to):
        cp = pltpu.make_async_remote_copy(
            src_ref=src,
            dst_ref=dst,
            send_sem=self.send_sems.at[self.n],
            recv_sem=self.recv_sems.at[self.n],
            device_id=to,
            device_id_type=MESH,
        )
        cp.start()
        self.n += 1
        self.open.append(cp)
        return cp

    def local(self, src, dst):
        cp = pltpu.make_async_copy(src, dst, self.send_sems.at[self.n])
        cp.start()
        self.n += 1
        return cp

    def close(self):
        for cp in self.open:
            cp.wait_send()


def deal(k, q, src, col, dst):
    y, z = q["y"], q["z"]
    n = k.n
    k.n += 4
    copies = [
        pltpu.make_async_remote_copy(
            src_ref=src.at[:, col((y + s) % 4)],
            dst_ref=dst,
            send_sem=k.send_sems.at[n + i],
            recv_sem=k.recv_sems.at[n],
            device_id=to,
            device_id_type=MESH,
        )
        for i, (s, to) in enumerate(zip((1, 3, 2), ring(q, "y")))
    ]
    here = pltpu.make_async_copy(src.at[:, col(y)], dst, k.send_sems.at[n + 3])

    @pl.when(y == z)
    def _():
        for cp in copies:
            cp.start()
        here.start()

    def wait():
        @pl.when(y == z)
        def _():
            for cp in copies:
                cp.wait_send()
            here.wait()

        @pl.when(y != z)
        def _():
            copies[0].wait_recv()

    return wait


def greet(targets, q=None):
    barrier = pltpu.get_barrier_semaphore()
    for to in targets:
        pl.semaphore_signal(barrier, inc=1, device_id=to, device_id_type=MESH)
    if q is None:
        pl.semaphore_wait(barrier, len(targets))
    else:
        y, z = q["y"], q["z"]

        @pl.when(y != z)
        def _():
            to = device(q, y=z, z=y)
            pl.semaphore_signal(barrier, inc=1, device_id=to, device_id_type=MESH)

        pl.semaphore_wait(barrier, len(targets) + (y != z).astype(jnp.int32))


TOP, LOW = pl.ds(0, TOK // 2), pl.ds(TOK // 2, TOK // 2)
HALF = (TOK // 2, D)


class Gather:
    def __init__(self, k, q, axis, src, dst):
        at = q[axis]
        self.k, self.dst = k, dst
        self.above, self.below, self.far = (at + 1) % 4, (at + 3) % 4, (at + 2) % 4
        self.up, self.down = device(q, **{axis: self.above}), device(q, **{axis: self.below})
        self.low0 = k.send(src(0), dst(at, 0), self.up)
        self.top1 = k.send(src(1), dst(at, 1), self.down)
        self.low1 = k.send(src(1), dst(at, 1), self.up)
        self.top0 = k.send(src(0), dst(at, 0), self.down)

    def relay(self):
        self.low0.wait_recv()
        ref = self.dst(self.below, 0)
        self.far0 = self.k.send(ref, ref, self.up)
        self.top1.wait_recv()
        ref = self.dst(self.above, 1)
        self.far1 = self.k.send(ref, ref, self.down)

    def near(self):
        self.low1.wait_recv()
        self.top0.wait_recv()

    def end(self):
        self.far0.wait_recv()
        self.far1.wait_recv()


class Sum:
    def __init__(self, k, q, axis, block, below, above, passed):
        at = q[axis]
        self.k, self.below, self.above, self.passed = k, below, above, passed
        up, down, far = (at + 1) % 4, (at + 3) % 4, (at + 2) % 4
        self.up, self.down = device(q, **{axis: up}), device(q, **{axis: down})
        self.first = k.send(block(far, 0), passed[0], self.up)
        self.second = k.send(block(far, 1), passed[1], self.down)
        self.rest = [
            k.send(block(up, 1), below(1), self.up),
            k.send(block(down, 0), above(0), self.down),
        ]

    def relay(self, own0, own1, sent):
        self.first.wait_recv()
        sent[0][...] = (self.passed[0][...].astype(F32) + own0[...].astype(F32)).astype(BF)
        self.rest.append(self.k.send(sent[0], self.below(0), self.up))
        self.second.wait_recv()
        sent[1][...] = (self.passed[1][...].astype(F32) + own1[...].astype(F32)).astype(BF)
        self.rest.append(self.k.send(sent[1], self.above(1), self.down))

    def end(self):
        for cp in self.rest:
            cp.wait_recv()

    def sent(self):
        for cp in self.rest[2:]:
            cp.wait_send()
            self.k.open = [o for o in self.k.open if o is not cp]


def halves(ref):
    return lambda h: ref.at[(TOP, LOW)[h]]


def ring_halves(ref):
    return lambda j, h: ref.at[j, (TOP, LOW)[h]]


def turn(k, q, moves):
    y, z = q["y"], q["z"]
    swap = device(q, y=z, z=y)
    pairs = []
    for src, dst in moves:
        n = k.n
        k.n += 1
        remote = pltpu.make_async_remote_copy(
            src_ref=src,
            dst_ref=dst,
            send_sem=k.send_sems.at[n],
            recv_sem=k.recv_sems.at[n],
            device_id=swap,
            device_id_type=MESH,
        )
        pairs.append((remote, pltpu.make_async_copy(src, dst, k.send_sems.at[n])))

    @pl.when(y != z)
    def _():
        for remote, _ in pairs:
            remote.start()

    @pl.when(y == z)
    def _():
        for _, here in pairs:
            here.start()

    def wait():
        @pl.when(y != z)
        def _():
            for remote, _ in pairs:
                remote.wait_recv()
                remote.wait_send()

        @pl.when(y == z)
        def _():
            for _, here in pairs:
                here.wait()

    return wait


def cost(us):
    return pl.CostEstimate(flops=int(us * 1e9), bytes_accessed=0, transcendentals=0)


def talk(kernel, name, cid, us, copies, ins, outs, scratch=(), near=(), near_out=(), alias={}):
    return pl.pallas_call(
        kernel,
        name=name,
        out_shape=[jax.ShapeDtypeStruct(s, t) for s, t in outs],
        in_specs=[VMEM if i in near else ANY for i in range(len(ins))],
        out_specs=[VMEM if i in near_out else ANY for i in range(len(outs))],
        scratch_shapes=[
            *scratch,
            pltpu.SemaphoreType.DMA((copies,)),
            pltpu.SemaphoreType.DMA((copies,)),
        ],
        cost_estimate=cost(us),
        input_output_aliases=alias,
        compiler_params=pltpu.CompilerParams(
            collective_id=cid, has_side_effects=True, vmem_limit_bytes=VMEM_LIMIT
        ),
    )(*ins)


def fetch_kernel(
    x, g, seg, na, nf, wq, wo, w1, w3, w2, X, G, SEG, GN, WQ, WO, W13, T2,
    TO, TV, QP, KT, VT, P1, P3, SG, NG, ss, rs,
):
    q = coords()
    y, xx, xh, xl, z, c = q["y"], q["x"], q["xh"], q["xl"], q["z"], q["c"]
    zs, ys, xs = ring(q, "z"), ring(q, "y"), ring(q, "x")
    mate = device(q, c=1 - c)
    other = device(q, x=xx ^ 1)
    other_mate = device(q, x=xx ^ 1, c=1 - c)
    k = Copies(ss, rs)
    rows = pl.ds(pl.multiple_of(128 * c + 64 * xl, 64), 64)
    qcols = pl.ds(pl.multiple_of(QZ * z, 128), QZ)
    tile = 128 * (z // 2)
    kcols = pl.ds(pl.multiple_of(QDIM + tile, 128), 128)
    vcols = pl.ds(pl.multiple_of(QDIM + KVDIM + tile, 128), 128)
    fcols = pl.ds(pl.multiple_of(FZ * z, 128), FZ)
    loads = [
        k.local(wq.at[rows, qcols], QP.at[:, pl.ds(0, QZ)]),
        k.local(wq.at[rows, kcols], KT),
        k.local(wq.at[rows, vcols], VT),
        k.local(w1.at[rows, fcols], P1),
        k.local(w3.at[rows, fcols], P3),
    ]
    SG[...] = jnp.broadcast_to(seg[...], (8, TOK))
    NG[0:16] = jnp.broadcast_to(na[...].astype(F32), (16, 256)).astype(BF)
    NG[16:32] = jnp.broadcast_to(nf[...].astype(F32), (16, 256)).astype(BF)
    greet(zs + ys + xs + [mate, other_mate])
    lanes = lambda j, n=1: pl.ds(pl.multiple_of(128 * j, 128 * n), 128 * n)
    dealt = deal(k, q, wo, lambda j: lanes(c * 8 + j * 2 + xl), TO)
    x_ring = Gather(k, q, "z", halves(x), ring_halves(X))
    for cp in loads:
        cp.wait()
    odd = z % 2 == 1
    kt, vt = KT[...].astype(F32), VT[...].astype(F32)
    lane = lax.broadcasted_iota(jnp.int32, kt.shape, 1)
    kt = jnp.where(odd, pltpu.roll(kt, 64, 1), kt)
    vt = jnp.where(odd, vt, pltpu.roll(vt, 64, 1))
    QP[:, QZ:] = jnp.where(lane < HEAD_DIM, kt, vt).astype(BF)
    f1, f3 = pl.ds(0, FZ), pl.ds(FZ, FZ)
    top, low = pl.ds(0, 32), pl.ds(32, 32)
    q_top = [k.send(QP.at[top], WQ.at[c, y, xh, xl, top], to) for to in xs]
    q_low = [k.send(QP.at[low], WQ.at[c, y, xh, xl, low], to) for to in ys]
    seg_z = [k.send(SG, SEG.at[xl, z, c], to) for to in zs]
    gn_y = [k.send(NG, GN.at[y, xh], to) for to in ys]
    q_here = k.local(QP, WQ.at[c, y, xh, xl])
    seg_here = k.local(SG, SEG.at[xl, z, c])
    gn_here = k.local(NG, GN.at[y, xh])
    a3_here = k.local(P3, W13.at[c, y, xh, xl, :, f3])
    heres = [
        k.local(P1, W13.at[c, y, xh, xl, :, f1]),
        k.local(x, X.at[z]),
        k.local(g, G.at[z]),
    ]
    dealt()
    o1 = [k.send(TO, WO.at[xh, :, lanes(c * 8 + y * 2 + xl)], to) for to in xs]
    o1_here = k.local(TO, WO.at[xh, :, lanes(c * 8 + y * 2 + xl)])
    thirty = lambda h: pl.ds(32 * h, 32)
    up_y = Gather(
        k, q, "y", lambda h: P3.at[thirty(h)], lambda j, h: W13.at[c, j, xh, xl, thirty(h), f3]
    )
    gate_x = Gather(
        k, q, "x", lambda h: P1.at[thirty(h)],
        lambda j, h: W13.at[c, y, j // 2, j % 2, thirty(h), f1],
    )
    q_here.wait()
    for cp in q_top:
        cp.wait_recv()
    q_y = Gather(k, q, "y", lambda h: WQ.at[c, y, h, :, top], lambda j, h: WQ.at[c, j, h, :, top])
    for cp in q_low:
        cp.wait_recv()
    q_half = lambda j, h: WQ.at[c, pl.ds(2 * h, 2), j // 2, j % 2, low]
    q_x = Gather(k, q, "x", lambda h: q_half(xx, h), q_half)
    for cp in seg_z:
        cp.wait_recv()
    seg_here.wait()
    part = SEG.at[xl, :, c]
    seg2 = [k.send(part, part, to) for to in (mate, other, other_mate)]
    for cp in gn_y:
        cp.wait_recv()
    gn_here.wait()
    gn2 = k.send(GN.at[:, xh], GN.at[:, xh], device(q, x=3 - xx))
    x_ring.relay()
    g_ring = Gather(k, q, "z", halves(g), ring_halves(G))
    up_y.relay()
    gate_x.relay()
    for cp in o1:
        cp.wait_recv()
    o1_here.wait()
    o_half = lambda j, h: WO.at[h, :, lanes(c * 8 + j * 2, 2)]
    o_y = Gather(k, q, "y", lambda h: o_half(y, h), o_half)
    w2_dealt = deal(k, q, w2, lambda j: lanes(c * 8 + xl * 4 + j), TV)
    q_y.relay()
    q_x.relay()
    up_y.near()
    up_y.end()
    a3_here.wait()
    part = W13.at[c, :, xh, xl, :, f3]
    a3 = [k.send(part, part, to) for to in xs[:2]]
    o_y.relay()
    g_ring.relay()
    for r in (q_y, q_x):
        r.near()
        r.end()
    q3 = k.send(WQ.at[c], WQ.at[c], mate)
    o_y.near()
    o_y.end()
    part = WO.at[:, :, pl.ds(pl.multiple_of(1024 * c, 1024), 1024)]
    o3 = k.send(part, part, mate)
    w2_dealt()
    heres.append(k.local(TV, T2))
    for cp in a3 + seg2 + [gn2, q3, o3]:
        cp.wait_recv()
    for cp in heres:
        cp.wait()
    for r in (gate_x, x_ring, g_ring):
        r.near()
        r.end()
    k.close()


def kv_kernel(kv, KV, ss, rs):
    q = coords()
    xx, xl, c = q["x"], q["xl"], q["c"]
    mate = device(q, c=1 - c)
    other = device(q, x=xx ^ 1)
    greet([mate, other])
    k = Copies(ss, rs)
    here = k.local(kv, KV.at[xl, :, c])
    near = k.send(kv, KV.at[xl, :, c], mate)
    far = pltpu.make_async_remote_copy(
        src_ref=kv,
        dst_ref=KV.at[0, :, c],
        send_sem=ss.at[2],
        recv_sem=rs.at[2],
        device_id=other,
        device_id_type=MESH,
    )
    on = pltpu.make_async_remote_copy(
        src_ref=KV.at[0, :, c],
        dst_ref=KV.at[0, :, c],
        send_sem=ss.at[3],
        recv_sem=rs.at[3],
        device_id=mate,
        device_id_type=MESH,
    )

    @pl.when(xl == 0)
    def _():
        far.start()
        far.wait_send()

    @pl.when(xl == 1)
    def _():
        far.wait_recv()
        on.start()
        on.wait_recv()
        on.wait_send()

    here.wait()
    near.wait_recv()
    k.close()


def middle_kernel(
    part, x, gain, t2, _, N2, H, W13, W2, p0, p1, v0, v1, below, above, n2, ss, rs
):
    q = coords()
    y, xx, xh, xl, z, c = q["y"], q["x"], q["xh"], q["xl"], q["z"], q["c"]
    ys, xs = ring(q, "y"), ring(q, "x")
    up, down = device(q, z=(z + 1) % 4), device(q, z=(z + 3) % 4)
    mate = device(q, c=1 - c)
    k = Copies(ss, rs)
    greet(ys + xs + [up, down, mate])
    z_sum = Sum(k, q, "z", ring_halves(part), halves(below), halves(above), (p0, p1))
    f1, f3 = pl.ds(0, FZ), pl.ds(FZ, FZ)
    up1 = lambda j: W13.at[c, :, j // 2, j % 2, :, f3]
    up_half = lambda j, h: W13.at[c, pl.ds(2 * h, 2), j // 2, j % 2, :, f3]
    cols = lambda cc, j, n: pl.ds(pl.multiple_of(128 * (cc * 8 + j), 128 * n), 128 * n)
    w2_here = k.local(t2, W2.at[xh, :, cols(c, xl * 4 + y, 1)])
    w2y = Gather(
        k, q, "y", lambda h: t2.at[pl.ds(352 * h, 352)],
        lambda j, h: W2.at[xh, pl.ds(352 * h, 352), cols(c, xl * 4 + j, 1)],
    )
    lower, higher = (xx + 3) % 4, (xx + 1) % 4
    far = [
        k.send(up_half(lower, 0), up_half(lower, 0), xs[0]),
        k.send(up_half(higher, 1), up_half(higher, 1), xs[1]),
    ]
    sent = [k.send(up1(j), up1(j), mate) for j in (xx, lower, higher)]
    w2y.relay()
    block = lambda j: W13.at[c, j, :, :, :, f1]
    gate = Gather(
        k, q, "y", lambda h: W13.at[c, y, h, :, :, f1], lambda j, h: W13.at[c, j, h, :, :, f1]
    )
    sent.append(k.send(block(y), block(y), mate))
    z_sum.relay(part.at[(z + 1) % 4, TOP], part.at[(z + 3) % 4, LOW], (v0, v1))
    w2_here.wait()
    w2y.near()
    w2y.end()
    down2 = lambda j: W2.at[j // 2, :, cols(c, (j % 2) * 4, 4)]
    down_half = lambda j, h: W2.at[j // 2, pl.ds(352 * h, 352), cols(c, (j % 2) * 4, 4)]
    down_ring = Gather(k, q, "x", lambda h: down_half(xx, h), down_half)
    sent.append(k.send(down2(xx), down2(xx), mate))
    z_sum.end()
    total = x[...].astype(F32) + (
        part[z].astype(F32) + (below[...].astype(F32) + above[...].astype(F32))
    )
    H[...] = total
    scale = lax.rsqrt(jnp.mean(total * total, axis=-1, keepdims=True) + EPS)
    n2[...] = to_pieces((total * scale * gain[...]).astype(BF))
    n2_ring = Gather(k, q, "z", halves(n2), ring_halves(N2))
    n2_here = k.local(n2, N2.at[z])
    gate.relay()
    down_ring.relay()
    for cp in far:
        cp.wait_recv()
    ref = up1((xx + 2) % 4)
    sent.append(k.send(ref, ref, mate))
    gate.near()
    for j in (gate.below, gate.above):
        sent.append(k.send(block(j), block(j), mate))
    n2_ring.relay()
    gate.end()
    sent.append(k.send(block(gate.far), block(gate.far), mate))
    down_ring.near()
    for j in (down_ring.below, down_ring.above):
        sent.append(k.send(down2(j), down2(j), mate))
    down_ring.end()
    sent.append(k.send(down2(down_ring.far), down2(down_ring.far), mate))
    for cp in sent:
        cp.wait_recv()
    n2_here.wait()
    n2_ring.near()
    n2_ring.end()
    k.close()


def back_kernel(
    dn2, hidden, G, N2, both, W2, WO, h, gain, V, FA, FB, F2, DO, OUT, DH, GAIN, *scratch
):
    (
        p0, p1, p2, p3, v0, v1, below, above, out_below, out_above, near0, near1, mine, dhb,
        vv, hv, gv, nv, bv, ov, wv, hT, outs, mate2, mate13, sum2, sum13, *bufs, ss, rs,
    ) = scratch
    q = coords()
    y, xx, z, c = q["y"], q["x"], q["z"], q["c"]
    mate = device(q, c=1 - c)
    k = Copies(ss, rs)
    get_n, get_b = k.local(N2, nv), k.local(both, bv)
    get_h, get_g = k.local(hidden, hv), k.local(G, gv)
    get_part = [
        k.local(dn2.at[(z + 1) % 4, TOP], near0),
        k.local(dn2.at[(z + 3) % 4, LOW], near1),
        k.local(dn2.at[z], mine),
    ]
    tile = lambda j: pl.ds(512 * j, 512)
    get_w = [k.local(W2.at[:, tile(j)], wv.at[j]) for j in range(2)]
    get_o = k.local(WO, ov)
    targets = [mate]
    for axis in ("x", "y", "z"):
        targets += ring(q, axis)[:2]
    greet(targets)
    z_sum = Sum(k, q, "z", ring_halves(dn2), halves(below), halves(above), (p0, p1))
    lanes = lambda cc, j: pl.ds(pl.multiple_of(1024 * cc + 256 * j, 256), 256)
    sent2, sent13 = [], []
    get_n.wait()
    get_b.wait()
    for j in range(4):
        mate13[j] = tn(nv[:, lanes(1 - c, j)], bv[...]).astype(BF).reshape(4, 64, 2 * FZ)
        sent13.append(k.send(mate13.at[j], sum13.at[j], mate))
    get_h.wait()
    get_g.wait()
    hT[...] = hv[...].T
    for cp in get_part:
        cp.wait()
    for j in range(4):
        mate2[j] = dot(hT[...], gv[:, lanes(1 - c, j)]).astype(BF)
        sent2.append(k.send(mate2.at[j], sum2.at[j], mate))
        if j == 2:
            z_sum.relay(near0, near1, (v0, v1))
    half = lambda ref: lambda i: ref.at[i]
    rest = 2 * FZ - SPLIT
    jobs = [
        ("x", lambda j, i: sum13.at[pl.ds(2 * i, 2), j, :, pl.ds(0, SPLIT)], FA),
        ("y", lambda j, i: sum13.at[j, pl.ds(2 * i, 2), :, pl.ds(SPLIT, rest)], FB),
        ("y", lambda j, i: sum2.at[j, pl.ds(704 * i, 704)], F2),
    ]
    sums, done = [], []

    def start(n):
        axis, block, _ = jobs[n]
        b = bufs[4 * n : 4 * n + 4]
        sums.append(Sum(k, q, axis, block, half(b[2]), half(b[3]), (b[0].at[0], b[0].at[1])))

    def relay(n):
        axis, block, _ = jobs[n]
        b = bufs[4 * n : 4 * n + 4]
        at = q[axis]
        sums[n].relay(block((at + 1) % 4, 0), block((at + 3) % 4, 1), (b[1].at[0], b[1].at[1]))

    def end(n):
        axis, block, out = jobs[n]
        b = bufs[4 * n : 4 * n + 4]
        sums[n].end()
        for i in range(2):
            total = block(q[axis], i)[...].astype(F32) + (
                b[2][i].astype(F32) + b[3][i].astype(F32)
            )
            b[2][i] = total.astype(BF)
        done.append(k.local(b[2], out))

    for j in range(4):
        sent13[j].wait_recv()
        own = tn(nv[:, lanes(c, j)], bv[...]).reshape(4, 64, 2 * FZ)
        sum13[j] = (own + sum13[j].astype(F32)).astype(BF)
    start(0)
    start(1)
    for j in range(4):
        sent2[j].wait_recv()
        sum2[j] = (dot(hT[...], gv[:, lanes(c, j)]) + sum2[j].astype(F32)).astype(BF)
    start(2)
    z_sum.end()
    dn = from_pieces(
        mine[...].astype(F32) + (below[...].astype(F32) + above[...].astype(F32))
    )
    back, gain_grad = rms_back(h[...], gain[...], dn)
    total = gv[pl.ds(pl.multiple_of(TOK * z, TOK), TOK)].astype(F32) + back
    DH[...] = total
    GAIN[...] = gain_grad
    dhb[...] = total.astype(BF)
    v_ring = Gather(k, q, "z", halves(dhb), ring_halves(vv))
    here = k.local(dhb, vv.at[z])
    for j in range(4):
        get_w[j].wait()
        part = dot(hv[...], wv[j % 2]).astype(BF)
        outs[:, :, tile(j)] = part.reshape(RING, TOK, 512)
        if j < 2:
            get_w.append(k.local(W2.at[:, tile(j + 2)], wv.at[j]))
    out_sum = Sum(
        k, q, "z", ring_halves(outs), halves(out_below), halves(out_above), (p2, p3)
    )
    relay(1)
    relay(0)
    v_ring.relay()
    relay(2)
    z_sum.sent()
    out_sum.relay(outs.at[(z + 1) % 4, TOP], outs.at[(z + 3) % 4, LOW], (v0, v1))
    end(1)
    end(0)
    v_ring.near()
    v_ring.end()
    here.wait()
    get_o.wait()
    done.append(k.local(vv, V))
    DO[...] = nt(vv[...].reshape(RING * TOK, D), ov[...]).astype(BF)
    end(2)
    out_sum.end()
    OUT[...] = h[...] + (
        outs[z].astype(F32) + (out_below[...].astype(F32) + out_above[...].astype(F32))
    )
    for cp in done:
        cp.wait()
    k.close()


def quarter(xt, rows):
    return (
        pl.ds(pl.multiple_of((xt // 2) * rows, rows), rows),
        pl.ds(pl.multiple_of((xt % 2) * 128, 128), 128),
    )


def tail_kernel(
    dkv, dq, cosine, sine, x, dh, gain, gain2, fa, fb, f2, wq, n1, o, dho,
    IG, G1, G3, G2, GO, GQ, GKV, gain_out, *scratch,
):
    (
        wv, nv, ov, gv, R, dm, dn, p0, p1, v0, v1, below, above, mate_o, sum_o, mate_q, sum_q,
        ob0, ob1, ob2, ob3, qb0, qb1, qb2, qb3, la, lb, l2, pa, pb, p2, t2, lo, lq, fo, fq,
        po, pq, to_, gains, s0, s1, s2, s3, s4, total, ss, rs,
    ) = scratch
    q = coords()
    y, xx, xh, xl, z, c = q["y"], q["x"], q["xh"], q["xl"], q["z"], q["c"]
    zs, ys, xs = ring(q, "z"), ring(q, "y"), ring(q, "x")
    mate, other, cross = device(q, c=1 - c), device(q, x=xx ^ 1), device(q, x=3 - xx)
    other_mate = device(q, x=xx ^ 1, c=1 - c)
    steps = (1, 3, 2)
    k = Copies(ss, rs)
    get_o, get_g = k.local(o, ov), k.local(dho, gv)
    get_w, get_n = k.local(wq, wv), k.local(n1, nv)
    greet(zs + ys + xs + [mate, other_mate], q)
    near = k.send(dkv.at[xl, :, 1 - c], R.at[0], mate)
    n = k.n
    k.n += 2
    pre, far = [
        pltpu.make_async_remote_copy(
            src_ref=src,
            dst_ref=dst,
            send_sem=ss.at[n + i],
            recv_sem=rs.at[n + i],
            device_id=to,
            device_id_type=MESH,
        )
        for i, (src, dst, to) in enumerate(
            ((dkv.at[0, :, 1 - c], R.at[1], mate), (R.at[2], R.at[3], other))
        )
    ]

    @pl.when(xl == 1)
    def _():
        pre.start()

    leg_2 = []
    for i, s in enumerate(steps):
        r, cc = quarter((xx + s) % 4, 704)
        leg_2.append(k.send(f2.at[r, cc], l2.at[i], xs[i]))
    leg_a = [k.send(fa.at[(y + s) % 4], la.at[i], ys[i]) for i, s in enumerate(steps)]
    leg_b = [k.send(fb.at[(xx + s) % 4], lb.at[i], xs[i]) for i, s in enumerate(steps)]
    lanes = lambda cc, j: pl.ds(pl.multiple_of(1024 * cc + 256 * j, 256), 256)
    get_o.wait()
    get_g.wait()
    swaps = []
    for j in range(4):
        mate_o[j] = tn(ov[...], gv[:, lanes(1 - c, j)]).astype(BF)
        swaps.append(k.send(mate_o.at[j], sum_o.at[j], mate))

    @pl.when(xl == 1)
    def _():
        R[3] = jnp.zeros(R.shape[1:], BF)
        pre.wait()
        for i in range(RING):
            R[2, i] = (dkv[0, i, c].astype(F32) + R[1, i].astype(F32)).astype(BF)
        far.start()

    for j in range(4):
        swaps[j].wait_recv()
        sum_o[j] = (tn(ov[...], gv[:, lanes(c, j)]) + sum_o[j].astype(F32)).astype(BF)
    half = lambda ref: lambda h: ref.at[h]
    o_block = lambda j, h: sum_o.at[j, pl.ds(256 * h, 256)]
    q_block = lambda j, h: sum_q.at[j, pl.ds(2 * h, 2)]
    o_sum = Sum(k, q, "y", o_block, half(ob2), half(ob3), (ob0.at[0], ob0.at[1]))
    for cp in leg_2:
        cp.wait_recv()
    r, cc = quarter(xx, 704)
    p2[...] = add4(f2[r, cc], l2[0], l2[1], l2[2])
    turned = turn(k, q, [(p2, t2)])
    at = lambda zz, off, n: pl.ds(pl.multiple_of(FZ * zz + off, 128), n)
    rows = pl.ds(pl.multiple_of(128 * c + 64 * xl, 64), 64)
    pair = pl.ds(pl.multiple_of(128 * c, 128), 128)
    f1 = pl.ds(0, FZ)
    rest = SPLIT - FZ
    quarter_rows = lambda h: pl.ds(pl.multiple_of(128 * c + 64 * xl + 32 * h, 32), 32)

    def over_z(src, ref, off, n):
        return Gather(
            k, q, "z", lambda h: src.at[pl.ds(32 * h, 32)],
            lambda j, h: ref.at[quarter_rows(h), at(j, off, n)],
        )

    spans = [(G1, 0, FZ), (G3, 0, rest), (G3, rest, FZ - rest)]
    pieces = [pa.at[:, f1], pa.at[:, pl.ds(FZ, rest)], pb]
    block = lambda i, j: spans[i][0].at[rows, at(j, spans[i][1], spans[i][2])]
    for cp in leg_a:
        cp.wait_recv()
    pa[...] = add4(fa[y], la[0], la[1], la[2])
    rings = [over_z(pieces[i], *spans[i]) for i in range(2)]
    to_x = [k.send(pieces[i], block(i, z), other) for i in range(2)]
    for cp in leg_b:
        cp.wait_recv()
    pb[...] = add4(fb[xx], lb[0], lb[1], lb[2])
    rings.append(over_z(pieces[2], *spans[2]))
    to_x.append(k.send(pieces[2], block(2, z), other))
    heres = [k.local(pieces[i], block(i, z)) for i in range(3)]
    o_sum.relay(o_block((y + 1) % 4, 0), o_block((y + 3) % 4, 1), (ob1.at[0], ob1.at[1]))

    @pl.when(xl == 1)
    def _():
        far.wait_send()

    @pl.when(xl == 0)
    def _():
        far.wait_recv()

    near.wait_recv()
    for i in range(RING):
        part = slice(TOK * i, TOK * i + TOK)
        w = dkv[xl, i, c].astype(F32) + (R[0, i].astype(F32) + R[3, i].astype(F32))
        lane = lax.broadcasted_iota(jnp.int32, w.shape, 1)
        dm[part, :QZ] = dq[i]
        dm[part, QZ:] = jnp.where(
            lane < HEAD_DIM, w * cosine[i] - swapped(w) * sine[i], w
        ).astype(BF)
    get_w.wait()
    dn[...] = nt(dm[...], wv[...]).astype(BF).reshape(RING, TOK, D)
    z_sum = Sum(k, q, "z", ring_halves(dn), halves(below), halves(above), (p0, p1))
    get_n.wait()
    cols = lambda cc: pl.ds(pl.multiple_of(1024 * cc, 1024), 1024)
    shape = (4, 4, 64, MZ)
    mate_q[...] = tn(nv[:, cols(1 - c)], dm[...]).astype(BF).reshape(shape)
    swap = k.send(mate_q, sum_q, mate)

    def onward(i):
        rings[i].near()
        for j in (rings[i].below, rings[i].above):
            to_x.append(k.send(block(i, j), block(i, j), other))

    rings[0].relay()
    onward(0)
    rings[1].relay()
    onward(1)
    swap.wait_recv()
    own = tn(nv[:, cols(c)], dm[...]).reshape(shape)
    sum_q[...] = (own + sum_q[...].astype(F32)).astype(BF)
    q_sum = Sum(k, q, "y", q_block, half(qb2), half(qb3), (qb0.at[0], qb0.at[1]))
    rings[2].relay()
    turned()
    col = pl.ds(pl.multiple_of(128 * (c * 8 + z * 2 + xl), 128), 128)
    down_x = k.send(t2, G2.at[:, col], other)
    down_here = k.local(t2, G2.at[:, col])
    onward(2)
    o_sum.end()
    for h in range(2):
        part = o_block(y, h)[...].astype(F32) + (ob2[h].astype(F32) + ob3[h].astype(F32))
        fo[pl.ds(256 * h, 256)] = part.astype(BF)
    leg_o, leg_q = [], []
    for i, s in enumerate(steps):
        r, cc = quarter((xx + s) % 4, 256)
        leg_o.append(k.send(fo.at[r, cc], lo.at[i], xs[i]))
    q_sum.relay(q_block((y + 1) % 4, 0), q_block((y + 3) % 4, 1), (qb1.at[0], qb1.at[1]))
    z_sum.relay(dn.at[(z + 1) % 4, TOP], dn.at[(z + 3) % 4, LOW], (v0, v1))
    q_sum.end()
    for h in range(2):
        part = q_block(y, h)[...].astype(F32) + (qb2[h].astype(F32) + qb3[h].astype(F32))
        fq[pl.ds(2 * h, 2)] = part.astype(BF)
    for i, s in enumerate(steps):
        leg_q.append(k.send(fq.at[(xx + s) % 4], lq.at[i], xs[i]))
    rings[0].end()
    to_x.append(k.send(block(0, rings[0].far), block(0, rings[0].far), other))
    down_x.wait_recv()
    down_here.wait()
    down_half = lambda j, h: G2.at[
        pl.ds(352 * h, 352), pl.ds(pl.multiple_of(128 * (c * 8 + j * 2), 256), 256)
    ]
    down_ring = Gather(k, q, "z", lambda h: down_half(z, h), down_half)
    for i in (1, 2):
        rings[i].end()
        to_x.append(k.send(block(i, rings[i].far), block(i, rings[i].far), other))
    z_sum.end()
    back, gain1 = rms_back(
        x[...].astype(F32),
        gain[...],
        from_pieces(dn[z].astype(F32) + (below[...].astype(F32) + above[...].astype(F32))),
    )
    IG[...] = dh[...] + back
    gains[...] = jnp.zeros_like(gains)
    for d in range(8):
        gains[d // 2, d % 2, 0:1] = gain1[:, 256 * d : 256 * d + 256]
        gains[d // 2, d % 2, 1:2] = gain2[:, 256 * d : 256 * d + 256]
    gain_y = [k.send(gains.at[(y + s) % 4], s0.at[y], ys[i]) for i, s in enumerate(steps)]
    gain_here = k.local(gains.at[y], s0.at[y])
    for cp in leg_o:
        cp.wait_recv()
    r, cc = quarter(xx, 256)
    po[...] = add4(fo[r, cc], lo[0], lo[1], lo[2])
    o_turned = turn(k, q, [(po, to_)])
    down_ring.relay()
    for cp in leg_q:
        cp.wait_recv()
    pq[...] = add4(fq[xx], lq[0], lq[1], lq[2])
    qc = lambda j: pl.ds(pl.multiple_of(QZ * j, 128), QZ)
    kc = lambda j: pl.ds(pl.multiple_of(128 * j, 128), 128)
    q_pieces = [
        (pq.at[:, pl.ds(0, QZ)], GQ.at[rows, qc(z)]),
        (pq.at[:, pl.ds(QZ, 128)], GKV.at[rows, kc(z)]),
    ]
    q_x = [k.send(src, dst, other) for src, dst in q_pieces]
    q_here = [k.local(src, dst) for src, dst in q_pieces]
    for cp in gain_y:
        cp.wait_recv()
    gain_here.wait()
    s1[0] = (s0[0] + s0[1]) + (s0[2] + s0[3])
    gain_x = k.send(s1.at[0, 1 - xh], s1.at[1, 0], cross)
    gain_x.wait_recv()
    s2[z] = s1[0, xh] + s1[1, 0]
    gain_z = [k.send(s2.at[z], s2.at[z], to) for to in zs]
    o_turned()
    o_x = k.send(to_, GO.at[:, col], other)
    o_here = k.local(to_, GO.at[:, col])
    for cp in to_x:
        cp.wait_recv()
    for cp in heres:
        cp.wait()
    last = [k.send(ref.at[pair], ref.at[pair], mate) for ref in (G1, G3)]
    for cp in q_x:
        cp.wait_recv()
    for cp in q_here:
        cp.wait()
    half_rows = lambda h: pl.ds(pl.multiple_of(128 * c + 64 * h, 64), 64)
    q_half = lambda j, h: GQ.at[half_rows(h), qc(j)]
    kv_half = lambda j, h: GKV.at[half_rows(h), kc(j)]
    last_rings = [
        Gather(k, q, "z", lambda h: q_half(z, h), q_half),
        Gather(k, q, "z", lambda h: kv_half(z, h), kv_half),
    ]
    down_ring.near()
    down_ring.end()
    last.append(k.send(G2.at[:, cols(c)], G2.at[:, cols(c)], mate))
    o_x.wait_recv()
    o_here.wait()
    o_half = lambda j, h: GO.at[
        pl.ds(128 * h, 128), pl.ds(pl.multiple_of(128 * (c * 8 + j * 2), 256), 256)
    ]
    last_rings.append(Gather(k, q, "z", lambda h: o_half(z, h), o_half))
    for cp in gain_z:
        cp.wait_recv()
    s3[0] = (s2[0] + s2[1]) + (s2[2] + s2[3])
    gain_x = k.send(s3.at[0], s3.at[1], other)
    last_rings[0].relay()
    last_rings[1].relay()
    gain_x.wait_recv()
    s4[0] = s3[0] + s3[1]
    gain_c = k.send(s4.at[0], s4.at[1], mate)
    last_rings[2].relay()
    for r in last_rings:
        r.near()
        r.end()
    refs = [GQ.at[pair], GKV.at[pair], GO.at[:, cols(c)]]
    last += [k.send(ref, ref, mate) for ref in refs]
    gain_c.wait_recv()
    total[...] = s4[0] + s4[1]
    gain_done = k.local(total, gain_out)
    for cp in last:
        cp.wait_recv()
    gain_done.wait()
    k.close()


PARAMS = pltpu.CompilerParams(vmem_limit_bytes=VMEM_LIMIT)


def add4(a, b, c, d):
    a, b, c, d = (v.astype(F32) for v in (a, b, c, d))
    return ((a + b) + (c + d)).astype(BF)


def to_pieces(v):
    return jnp.concatenate(
        [v[:, 256 * d + 128 * c : 256 * d + 128 * c + 128] for c in range(2) for d in range(8)],
        axis=1,
    )


def from_pieces(v):
    return jnp.concatenate(
        [v[:, 1024 * c + 128 * d : 1024 * c + 128 * d + 128] for d in range(8) for c in range(2)],
        axis=1,
    )


def swapped(u):
    lane = lax.broadcasted_iota(jnp.int32, u.shape, 1)
    return jnp.where(lane % 64 < 32, pltpu.roll(u, 96, 1), pltpu.roll(u, 32, 1))


def project_kernel(x, gain, w, cosine, sine, n1, query, kv):
    two = 2 * TOK
    xv = x[...].reshape(two, D).astype(F32)
    scale = lax.rsqrt(jnp.mean(xv * xv, axis=-1, keepdims=True) + EPS)
    normed = to_pieces((xv * scale * gain[...]).astype(BF))
    n1[...] = normed.reshape(2, TOK, D)
    cos, sin = cosine[...].reshape(two, 128), sine[...].reshape(two, 128)
    mixed = jnp.dot(normed, w[...], preferred_element_type=F32)
    for j in range(5):
        u = mixed[:, 128 * j : 128 * j + 128]
        turned = u * cos + swapped(u) * sin
        if j < 4:
            query[:, :, 128 * j : 128 * j + 128] = turned.astype(BF).reshape(2, TOK, 128)
        else:
            lane = lax.broadcasted_iota(jnp.int32, u.shape, 1)
            kv[...] = jnp.where(lane < HEAD_DIM, turned, u).astype(BF).reshape(2, TOK, 128)


def project(x, gain, w, cosine, sine):
    chunk = lambda cols: pl.BlockSpec((2, TOK, cols), lambda i: (i, 0, 0))
    whole = lambda shape: pl.BlockSpec(shape, lambda i: (0,) * len(shape))
    return pl.pallas_call(
        project_kernel,
        name="project",
        cost_estimate=cost(7),
        grid=(2,),
        in_specs=[chunk(D), whole((1, D)), whole((D, MZ)), chunk(128), chunk(128)],
        out_specs=[chunk(D), chunk(QZ), chunk(128)],
        out_shape=[
            jax.ShapeDtypeStruct((RING, TOK, D), BF),
            jax.ShapeDtypeStruct((RING, TOK, QZ), BF),
            jax.ShapeDtypeStruct((RING, TOK, 128), BF),
        ],
        compiler_params=PARAMS,
    )(x, gain, w, cosine, sine)


def stacked_low(tiles):
    out = []
    for pair in range(4):
        tile = tiles[:, 128 * pair : 128 * pair + 128].astype(F32)
        lane = lax.broadcasted_iota(jnp.int32, tile.shape, 1)
        out.append(jnp.where(lane < HEAD_DIM, tile, 0.0))
        out.append(jnp.where(lane < HEAD_DIM, pltpu.roll(tile, 64, 1), 0.0))
    return jnp.concatenate(out, axis=0)


def stacked_high(tiles):
    out = []
    for pair in range(4):
        tile = tiles[:, 128 * pair : 128 * pair + 128].astype(F32)
        lane = lax.broadcasted_iota(jnp.int32, tile.shape, 1)
        out.append(jnp.where(lane >= HEAD_DIM, pltpu.roll(tile, 64, 1), 0.0))
        out.append(jnp.where(lane >= HEAD_DIM, tile, 0.0))
    return jnp.concatenate(out, axis=0)


def unstacked(v):
    tiles = []
    for pair in range(4):
        both = jnp.concatenate(
            [v[:, 256 * pair : 256 * pair + 128], v[:, 256 * pair + 128 : 256 * pair + 256]],
            axis=0,
        )
        tiles.append(both.T)
    return tiles


def nt(a, b):
    return lax.dot_general(a, b, (((1,), (1,)), ((), ())), preferred_element_type=F32)


def tn(a, b):
    return lax.dot_general(a, b, (((0,), (0,)), ((), ())), preferred_element_type=F32)


def chunk_scores(keys, stacked, kc, chunk, start):
    raw = nt(keys, stacked)
    key = kc * TOK + lax.broadcasted_iota(jnp.int32, raw.shape, 0)
    query = chunk * TOK + lax.broadcasted_iota(jnp.int32, raw.shape, 1) % TOK
    return jnp.where((key <= query) & (key >= start), raw, -1e30)


def attend_kernel(info, query, kv, start, out, logsum):
    i = pl.program_id(0)
    low, chunk = info[0, i], info[1, i]
    stacked = (stacked_low(query[0]) * (1.0 / HEAD_DIM**0.5)).astype(BF)
    starts = jnp.concatenate([start[0]] * GROUP, axis=1)

    def step(kc, carry):
        top, summed, total = carry
        keys = kv[kc]
        scores = chunk_scores(keys, stacked, kc, chunk, starts)
        new_top = jnp.maximum(top, jnp.max(scores, axis=0, keepdims=True))
        weights = jnp.exp(scores - new_top)
        fade = jnp.exp(top - new_top)
        summed = summed * fade + jnp.sum(weights, axis=0, keepdims=True)
        part = tn(keys, weights.astype(BF))
        return new_top, summed, total * fade + part[HEAD_DIM:]

    rows = GROUP * TOK
    carry = (jnp.full((1, rows), -1e30, F32), jnp.zeros((1, rows), F32), jnp.zeros((64, rows), F32))
    top, summed, total = lax.fori_loop(low, chunk + 1, step, carry)
    for pair, tile in enumerate(unstacked(total / summed)):
        out[0, :, 128 * pair : 128 * pair + 128] = tile.astype(BF)
    logsum[0] = top + jnp.log(summed)


def attend(info, query, kv, start):
    chunk = lambda r, cols: pl.BlockSpec((1, r, cols), lambda i, s: (i, 0, 0))
    return pl.pallas_call(
        attend_kernel,
        name="attend",
        cost_estimate=cost(12),
        grid_spec=pltpu.PrefetchScalarGridSpec(
            num_scalar_prefetch=1,
            grid=(RING,),
            in_specs=[
                chunk(TOK, QZ),
                pl.BlockSpec((16, TOK, 128), lambda i, s: (0, 0, 0)),
                chunk(1, TOK),
            ],
            out_specs=[chunk(TOK, QZ), chunk(1, GROUP * TOK)],
        ),
        out_shape=[
            jax.ShapeDtypeStruct((RING, TOK, QZ), BF),
            jax.ShapeDtypeStruct((RING, 1, GROUP * TOK), F32),
        ],
        compiler_params=PARAMS,
    )(info, query, kv, start)


def attend_back_kernel(
    info, query, kv, start, out, grad_out, logsum, cosine, sine, dquery, dkv, total
):
    i = pl.program_id(0)
    low, chunk = info[0, i], info[1, i]
    stacked = (stacked_low(query[0]) * (1.0 / HEAD_DIM**0.5)).astype(BF)
    grads = stacked_high(grad_out[0]).astype(BF)
    starts = jnp.concatenate([start[0]] * GROUP, axis=1)
    lse = logsum[0]
    deltas = []
    for pair in range(4):
        cols = slice(128 * pair, 128 * pair + 128)
        prod = (out[0, :, cols].astype(F32) * grad_out[0, :, cols].astype(F32)).T
        deltas.append(jnp.sum(prod[:HEAD_DIM], axis=0, keepdims=True))
        deltas.append(jnp.sum(prod[HEAD_DIM:], axis=0, keepdims=True))
    delta = jnp.concatenate(deltas, axis=1)

    @pl.when(i == 0)
    def _():
        total[...] = jnp.zeros_like(total)

    def step(kc, dq):
        keys = kv[kc]
        scores = chunk_scores(keys, stacked, kc, chunk, starts)
        probs = jnp.exp(scores - lse)
        grad_probs = nt(keys, grads)
        grad_scores = (probs * (grad_probs - delta)).astype(BF)
        total[kc] += jnp.dot(grad_scores, stacked, preferred_element_type=F32) + jnp.dot(
            probs.astype(BF), grads, preferred_element_type=F32
        )
        return dq + tn(keys, grad_scores)[:HEAD_DIM]

    dq = lax.fori_loop(low, chunk + 1, step, jnp.zeros((64, GROUP * TOK), F32))
    cos, sin = cosine[0], sine[0]
    for pair, tile in enumerate(unstacked(dq)):
        tile = tile * (1.0 / HEAD_DIM**0.5)
        dquery[0, :, 128 * pair : 128 * pair + 128] = (tile * cos - swapped(tile) * sin).astype(BF)

    @pl.when(i == RING - 1)
    def _():
        dkv[...] = total[...].astype(BF)


def attend_back(info, query, kv, start, out, grad_out, logsum, cosine, sine):
    chunk = lambda r, cols: pl.BlockSpec((1, r, cols), lambda i, s: (i, 0, 0))
    whole = pl.BlockSpec((16, TOK, 128), lambda i, s: (0, 0, 0))
    return pl.pallas_call(
        attend_back_kernel,
        name="attend_back",
        cost_estimate=cost(15),
        grid_spec=pltpu.PrefetchScalarGridSpec(
            num_scalar_prefetch=1,
            grid=(RING,),
            in_specs=[
                chunk(TOK, QZ),
                whole,
                chunk(1, TOK),
                chunk(TOK, QZ),
                chunk(TOK, QZ),
                chunk(1, GROUP * TOK),
                chunk(TOK, 128),
                chunk(TOK, 128),
            ],
            out_specs=[chunk(TOK, QZ), whole],
            scratch_shapes=[pltpu.VMEM((16, TOK, 128), F32)],
        ),
        out_shape=[
            jax.ShapeDtypeStruct((RING, TOK, QZ), BF),
            jax.ShapeDtypeStruct((16, TOK, 128), BF),
        ],
        compiler_params=PARAMS,
    )(info, query, kv, start, out, grad_out, logsum, cosine, sine)


def rms_back(v, gain, grad):
    scale = lax.rsqrt(jnp.mean(v * v, axis=-1, keepdims=True) + EPS)
    unit = v * scale
    gain_grad = jnp.sum(grad * unit, axis=0, keepdims=True)
    inner = grad * gain
    return scale * (inner - unit * jnp.mean(inner * unit, axis=-1, keepdims=True)), gain_grad


def pick(v, index, axis=0):
    return lax.dynamic_index_in_dim(v, index, axis, keepdims=False)


def dot(a, b):
    return jnp.dot(a, b, preferred_element_type=F32)


def body(tokens, segments, cotangent, norm_attn, norm_ffn, wqkv, wo, w1, w3, w2):
    q = coords()
    y, xx, xl, z, c = q["y"], q["x"], q["xl"], q["z"], q["c"]
    x = tokens[0]
    g = cotangent[0]
    X, G, SEG, GN, WQ, WO, W13, t2 = talk(
        fetch_kernel,
        "fetch",
        1,
        40,
        100,
        (x, g, segments, norm_attn[None], norm_ffn[None], wqkv, wo, w1, w3, w2),
        [
            ((RING, TOK, D), BF),
            ((RING, TOK, D), BF),
            ((2, 4, 2, 8, TOK), jnp.int32),
            ((4, 2, 32, 256), BF),
            ((2, 4, 2, 2, 64, MZ), BF),
            ((2, 256, D), BF),
            ((2, 4, 2, 2, 64, 2 * FZ), BF),
            ((704, 128), BF),
        ],
        scratch=[
            pltpu.VMEM((256, 128), BF),
            pltpu.VMEM((704, 128), BF),
            pltpu.VMEM((64, MZ), BF),
            pltpu.VMEM((64, 128), BF),
            pltpu.VMEM((64, 128), BF),
            pltpu.VMEM((64, FZ), BF),
            pltpu.VMEM((64, FZ), BF),
            pltpu.VMEM((8, TOK), jnp.int32),
            pltpu.VMEM((32, 256), BF),
        ],
        near=(0, 1, 2, 3, 4),
    )

    docs = SEG[:, :, :, 0, :].reshape(16 * TOK)
    mine = pick(pick(SEG[:, :, :, 0, :], xl, 0), c, 1)
    chunks = xl * 8 + 2 * jnp.arange(4, dtype=jnp.int32) + c
    start = jnp.sum((docs[None, None, :] < mine[:, :, None]).astype(jnp.int32), axis=2)
    index = chunks[:, None] * TOK + jnp.arange(TOK, dtype=jnp.int32)[None]
    place = (index - start).astype(F32)
    lane = jnp.arange(128)
    freq = THETA ** (-(lane % 32).astype(F32) * 2.0 / HEAD_DIM)
    angle = place[:, :, None] * freq[None, None, :]
    cosine = jnp.cos(angle)
    sine = jnp.sin(angle) * jnp.where(lane % 64 < 32, -1.0, 1.0)
    info = jnp.stack([jnp.min(start, axis=1) // TOK, chunks])
    start = start[:, None, :]
    gain_attn = GN[:, :, 0, :].reshape(1, D).astype(F32)
    gain_ffn = GN[:, :, 16, :].reshape(1, D).astype(F32)

    WQ = WQ.reshape(D, MZ)
    WO = WO.reshape(QZ, D)
    n1, query, kv = project(X, gain_attn, WQ, cosine, sine)
    (KV,) = talk(
        kv_kernel, "kv", 2, 7, 4, (kv,), [((2, 4, 2, TOK, 128), BF)], near=(0,)
    )
    KV = KV.reshape(16, TOK, 128)
    heads_out, logsum = attend(info, query, KV, start)
    o = heads_out.reshape(RING * TOK, QZ)
    part = dot(o, WO).astype(BF).reshape(RING, TOK, D)
    N2, h, W13, W2 = talk(
        middle_kernel,
        "middle",
        3,
        42,
        60,
        (part, x, gain_ffn, t2, W13),
        [
            ((RING, TOK, D), BF),
            ((TOK, D), F32),
            ((2, 4, 2, 2, 64, 2 * FZ), BF),
            ((2, 704, D), BF),
        ],
        scratch=[
            *[pltpu.VMEM(HALF, BF)] * 4,
            *[pltpu.VMEM((TOK, D), BF)] * 3,
        ],
        near=(0, 1, 2, 3),
        near_out=(1,),
        alias={4: 2},
    )
    N2, G = N2.reshape(RING * TOK, D), G.reshape(RING * TOK, D)
    W13, W2 = W13.reshape(D, 2 * FZ), W2.reshape(FZ, D)
    gate, up = dot(N2, W13[:, :FZ]), dot(N2, W13[:, FZ:])
    hidden = (jax.nn.silu(gate) * up).astype(BF)
    dhid = jnp.einsum("td,fd->tf", G, W2, preferred_element_type=F32)
    sigma = jax.nn.sigmoid(gate)
    dgate = (dhid * up * sigma * (1.0 + gate * (1.0 - sigma))).astype(BF)
    dup = (dhid * gate * sigma).astype(BF)
    both = jnp.concatenate([dgate, dup], axis=1)
    dn2 = jnp.einsum("tf,df->td", both, W13, preferred_element_type=F32)
    dn2 = dn2.astype(BF).reshape(RING, TOK, D)
    rest = 2 * FZ - SPLIT
    buffers = []
    for shape in ((2, 64, SPLIT), (2, 64, rest), (704, 256)):
        buffers += [pltpu.VMEM((2,) + shape, BF)] * 4
    DH, fa, fb, f2, dheads, output, dh, gain2 = talk(
        back_kernel,
        "back",
        4,
        60,
        100,
        (dn2, hidden, G, N2, both, W2, WO, h, gain_ffn),
        [
            ((RING, TOK, D), BF),
            ((2, 2, 64, SPLIT), BF),
            ((2, 2, 64, rest), BF),
            ((2, 704, 256), BF),
            ((RING * TOK, QZ), BF),
            ((TOK, D), F32),
            ((TOK, D), F32),
            ((1, D), F32),
        ],
        scratch=[
            *[pltpu.VMEM(HALF, BF)] * 6,
            *[pltpu.VMEM((TOK, D), BF)] * 4,
            *[pltpu.VMEM(HALF, BF)] * 2,
            *[pltpu.VMEM((TOK, D), BF)] * 2,
            pltpu.VMEM((RING, TOK, D), BF),
            pltpu.VMEM((RING * TOK, FZ), BF),
            pltpu.VMEM((RING * TOK, D), BF),
            pltpu.VMEM((RING * TOK, D), BF),
            pltpu.VMEM((RING * TOK, 2 * FZ), BF),
            pltpu.VMEM((QZ, D), BF),
            pltpu.VMEM((2, FZ, 512), BF),
            pltpu.VMEM((FZ, RING * TOK), BF),
            pltpu.VMEM((RING, TOK, D), BF),
            pltpu.VMEM((4, FZ, 256), BF),
            pltpu.VMEM((4, 4, 64, 2 * FZ), BF),
            pltpu.VMEM((4, FZ, 256), BF),
            pltpu.VMEM((4, 4, 64, 2 * FZ), BF),
            *buffers,
        ],
        near=(7, 8),
        near_out=(4, 5, 6, 7),
    )
    fa, fb = fa.reshape(4, 64, SPLIT), fb.reshape(4, 64, rest)
    f2 = f2.reshape(1408, 256)
    DH = DH.reshape(RING * TOK, D)
    dquery, dkv = attend_back(
        info, query, KV, start, heads_out, dheads.reshape(RING, TOK, QZ), logsum, cosine, sine
    )
    small = (8, 256)
    input_grad, G1, G3, G2, GO, GQ, GKV, gain_out = talk(
        tail_kernel,
        "tail",
        6,
        75,
        170,
        (
            dkv.reshape(2, 4, 2, TOK, 128), dquery, cosine, sine, x, dh, gain_attn, gain2,
            fa, fb, f2, WQ, n1.reshape(RING * TOK, D), o, DH,
        ),
        [
            ((TOK, D), F32),
            ((256, 4 * FZ), BF),
            ((256, 4 * FZ), BF),
            ((704, D), BF),
            ((256, D), BF),
            ((256, QDIM), BF),
            ((256, 2 * KVDIM), BF),
            (small, F32),
        ],
        scratch=[
            pltpu.VMEM((D, MZ), BF),
            pltpu.VMEM((RING * TOK, D), BF),
            pltpu.VMEM((RING * TOK, QZ), BF),
            pltpu.VMEM((RING * TOK, D), BF),
            pltpu.VMEM((4, RING, TOK, 128), BF),
            pltpu.VMEM((RING * TOK, MZ), BF),
            pltpu.VMEM((RING, TOK, D), BF),
            *[pltpu.VMEM(HALF, BF)] * 4,
            *[pltpu.VMEM((TOK, D), BF)] * 2,
            *[pltpu.VMEM((4, QZ, 256), BF)] * 2,
            *[pltpu.VMEM((4, 4, 64, MZ), BF)] * 2,
            *[pltpu.VMEM((2, 256, 256), BF)] * 4,
            *[pltpu.VMEM((2, 2, 64, MZ), BF)] * 4,
            pltpu.VMEM((3, 64, SPLIT), BF),
            pltpu.VMEM((3, 64, rest), BF),
            pltpu.VMEM((3, 704, 128), BF),
            pltpu.VMEM((64, SPLIT), BF),
            pltpu.VMEM((64, rest), BF),
            pltpu.VMEM((704, 128), BF),
            pltpu.VMEM((704, 128), BF),
            pltpu.VMEM((3, 256, 128), BF),
            pltpu.VMEM((3, 64, MZ), BF),
            pltpu.VMEM((512, 256), BF),
            pltpu.VMEM((4, 64, MZ), BF),
            pltpu.VMEM((256, 128), BF),
            pltpu.VMEM((64, MZ), BF),
            pltpu.VMEM((256, 128), BF),
            pltpu.VMEM((4, 2) + small, F32),
            pltpu.VMEM((4, 2) + small, F32),
            pltpu.VMEM((2, 2) + small, F32),
            pltpu.VMEM((4,) + small, F32),
            pltpu.VMEM((2,) + small, F32),
            pltpu.VMEM((2,) + small, F32),
            pltpu.VMEM(small, F32),
        ],
        near=tuple(range(11)),
        near_out=(0,),
    )
    pairs = GKV.reshape(256, 4, 2, HEAD_DIM)
    flat = lambda v: v.reshape(256, -1)
    grad_qkv = jnp.concatenate([GQ, flat(pairs[:, :, 0]), flat(pairs[:, :, 1])], axis=1)
    return (
        output[None],
        input_grad[None],
        gain_out[0],
        gain_out[1],
        grad_qkv.astype(F32),
        GO.astype(F32),
        G1.astype(F32),
        G3.astype(F32),
        G2.astype(F32),
    )


def solution(mesh):
    rows = P("dp", None)
    acts = P("dp", "ctx", None)
    return jax.shard_map(
        body,
        mesh=mesh,
        in_specs=(acts, P("dp", "ctx"), acts, P("dp"), P("dp"), rows, rows, rows, rows, rows),
        out_specs=(acts, acts, P("dp"), P("dp"), rows, rows, rows, rows, rows),
        check_vma=False,
    )
```

```python
import functools

import jax
import jax.numpy as jnp
from jax import lax
from jax.experimental import pallas as pl
from jax.experimental.pallas import tpu as pltpu
from jax.sharding import PartitionSpec as P

D = 2048
HEAD_DIM = 64
TOK = 128
RING = 4
QDIM = 2048
KVDIM = 256
GROUP = 8
QZ = 512
MZ = 640
FZ = 1408
SPLIT = 2048
EPS = 1e-05
THETA = 10000.0
MESH = pl.DeviceIdType.MESH
VMEM_LIMIT = 60 << 20
BF = jnp.bfloat16
F32 = jnp.float32
ANY = pl.BlockSpec(memory_space=pl.ANY)
VMEM = pl.BlockSpec(memory_space=pltpu.VMEM)


def coords():
    dp, ctx = lax.axis_index("dp"), lax.axis_index("ctx")
    y, xh = dp // 2, dp % 2
    xl, z, c = ctx // 8, (ctx // 2) % 4, ctx % 2
    return dict(y=y, x=xh * 2 + xl, xh=xh, xl=xl, z=z, c=c)


def device(q, **change):
    r = {k: change.get(k, q[k]) for k in ("y", "x", "z", "c")}
    return (r["y"] * 2 + r["x"] // 2, (r["x"] % 2) * 8 + r["z"] * 2 + r["c"])


def ring(q, axis):
    return [device(q, **{axis: (q[axis] + s) % 4}) for s in (1, 3, 2)]


def shift_pairs(axis, by):
    size = 2 if axis == "c" else 4
    pairs = []
    for y in range(4):
        for x in range(4):
            for z in range(4):
                for c in range(2):
                    q = dict(y=y, x=x, z=z, c=c)
                    pairs.append((device(q), device(q, **{axis: (q[axis] + by) % size})))
    return [(a[0] * 16 + a[1], b[0] * 16 + b[1]) for a, b in pairs]


def swap_pairs():
    pairs = []
    for y in range(4):
        for x in range(4):
            for z in range(4):
                for c in range(2):
                    q = dict(y=y, x=x, z=z, c=c)
                    pairs.append((device(q), device(q, y=z, z=y)))
    return [(a[0] * 16 + a[1], b[0] * 16 + b[1]) for a, b in pairs]


def move(v, axis, by):
    return lax.ppermute(v, ("dp", "ctx"), shift_pairs(axis, by))


class Copies:
    def __init__(self, send_sems, recv_sems):
        self.send_sems, self.recv_sems, self.n, self.open = send_sems, recv_sems, 0, []

    def send(self, src, dst, to):
        cp = pltpu.make_async_remote_copy(
            src_ref=src,
            dst_ref=dst,
            send_sem=self.send_sems.at[self.n],
            recv_sem=self.recv_sems.at[self.n],
            device_id=to,
            device_id_type=MESH,
        )
        cp.start()
        self.n += 1
        self.open.append(cp)
        return cp

    def local(self, src, dst):
        cp = pltpu.make_async_copy(src, dst, self.send_sems.at[self.n])
        cp.start()
        self.n += 1
        return cp

    def close(self):
        for cp in self.open:
            cp.wait_send()


def deal(k, q, src, col, dst):
    y, z = q["y"], q["z"]
    n = k.n
    k.n += 4
    copies = [
        pltpu.make_async_remote_copy(
            src_ref=src.at[:, col((y + s) % 4)],
            dst_ref=dst,
            send_sem=k.send_sems.at[n + i],
            recv_sem=k.recv_sems.at[n],
            device_id=to,
            device_id_type=MESH,
        )
        for i, (s, to) in enumerate(zip((1, 3, 2), ring(q, "y")))
    ]
    here = pltpu.make_async_copy(src.at[:, col(y)], dst, k.send_sems.at[n + 3])

    @pl.when(y == z)
    def _():
        for cp in copies:
            cp.start()
        here.start()

    def wait():
        @pl.when(y == z)
        def _():
            for cp in copies:
                cp.wait_send()
            here.wait()

        @pl.when(y != z)
        def _():
            copies[0].wait_recv()

    return wait


def greet(targets, q=None):
    barrier = pltpu.get_barrier_semaphore()
    for to in targets:
        pl.semaphore_signal(barrier, inc=1, device_id=to, device_id_type=MESH)
    if q is None:
        pl.semaphore_wait(barrier, len(targets))
    else:
        y, z = q["y"], q["z"]

        @pl.when(y != z)
        def _():
            to = device(q, y=z, z=y)
            pl.semaphore_signal(barrier, inc=1, device_id=to, device_id_type=MESH)

        pl.semaphore_wait(barrier, len(targets) + (y != z).astype(jnp.int32))


TOP, LOW = pl.ds(0, TOK // 2), pl.ds(TOK // 2, TOK // 2)
HALF = (TOK // 2, D)


class Gather:
    def __init__(self, k, q, axis, src, dst):
        at = q[axis]
        self.k, self.dst = k, dst
        self.above, self.below, self.far = (at + 1) % 4, (at + 3) % 4, (at + 2) % 4
        self.up, self.down = device(q, **{axis: self.above}), device(q, **{axis: self.below})
        self.low0 = k.send(src(0), dst(at, 0), self.up)
        self.top1 = k.send(src(1), dst(at, 1), self.down)
        self.low1 = k.send(src(1), dst(at, 1), self.up)
        self.top0 = k.send(src(0), dst(at, 0), self.down)

    def relay(self):
        self.low0.wait_recv()
        ref = self.dst(self.below, 0)
        self.far0 = self.k.send(ref, ref, self.up)
        self.top1.wait_recv()
        ref = self.dst(self.above, 1)
        self.far1 = self.k.send(ref, ref, self.down)

    def near(self):
        self.low1.wait_recv()
        self.top0.wait_recv()

    def end(self):
        self.far0.wait_recv()
        self.far1.wait_recv()


class Sum:
    def __init__(self, k, q, axis, block, below, above, passed):
        at = q[axis]
        self.k, self.below, self.above, self.passed = k, below, above, passed
        up, down, far = (at + 1) % 4, (at + 3) % 4, (at + 2) % 4
        self.up, self.down = device(q, **{axis: up}), device(q, **{axis: down})
        self.first = k.send(block(far, 0), passed[0], self.up)
        self.second = k.send(block(far, 1), passed[1], self.down)
        self.rest = [
            k.send(block(up, 1), below(1), self.up),
            k.send(block(down, 0), above(0), self.down),
        ]

    def relay(self, own0, own1, sent):
        self.first.wait_recv()
        sent[0][...] = (self.passed[0][...].astype(F32) + own0[...].astype(F32)).astype(BF)
        self.rest.append(self.k.send(sent[0], self.below(0), self.up))
        self.second.wait_recv()
        sent[1][...] = (self.passed[1][...].astype(F32) + own1[...].astype(F32)).astype(BF)
        self.rest.append(self.k.send(sent[1], self.above(1), self.down))

    def end(self):
        for cp in self.rest:
            cp.wait_recv()

    def sent(self):
        for cp in self.rest[2:]:
            cp.wait_send()
            self.k.open = [o for o in self.k.open if o is not cp]


def halves(ref):
    return lambda h: ref.at[(TOP, LOW)[h]]


def ring_halves(ref):
    return lambda j, h: ref.at[j, (TOP, LOW)[h]]


def turn(k, q, moves):
    y, z = q["y"], q["z"]
    swap = device(q, y=z, z=y)
    pairs = []
    for src, dst in moves:
        n = k.n
        k.n += 1
        remote = pltpu.make_async_remote_copy(
            src_ref=src,
            dst_ref=dst,
            send_sem=k.send_sems.at[n],
            recv_sem=k.recv_sems.at[n],
            device_id=swap,
            device_id_type=MESH,
        )
        pairs.append((remote, pltpu.make_async_copy(src, dst, k.send_sems.at[n])))

    @pl.when(y != z)
    def _():
        for remote, _ in pairs:
            remote.start()

    @pl.when(y == z)
    def _():
        for _, here in pairs:
            here.start()

    def wait():
        @pl.when(y != z)
        def _():
            for remote, _ in pairs:
                remote.wait_recv()
                remote.wait_send()

        @pl.when(y == z)
        def _():
            for _, here in pairs:
                here.wait()

    return wait


def cost(us):
    return pl.CostEstimate(flops=int(us * 1e9), bytes_accessed=0, transcendentals=0)


def talk(kernel, name, cid, us, copies, ins, outs, scratch=(), near=(), near_out=(), alias={}):
    return pl.pallas_call(
        kernel,
        name=name,
        out_shape=[jax.ShapeDtypeStruct(s, t) for s, t in outs],
        in_specs=[VMEM if i in near else ANY for i in range(len(ins))],
        out_specs=[VMEM if i in near_out else ANY for i in range(len(outs))],
        scratch_shapes=[
            *scratch,
            pltpu.SemaphoreType.DMA((copies,)),
            pltpu.SemaphoreType.DMA((copies,)),
        ],
        cost_estimate=cost(us),
        input_output_aliases=alias,
        compiler_params=pltpu.CompilerParams(
            collective_id=cid, has_side_effects=True, vmem_limit_bytes=VMEM_LIMIT
        ),
    )(*ins)


def front_kernel(
    x, g, seg, na, nf, freq, wq, wo, w1, w3, w2,
    G, WQ, WO, W13, T2, N1, Q, KV, COS, SIN, START, GA, GF,
    TO, TV, QP, KT, VT, P1, P3, SG, NG, SEGS, GN, XV, WV, NV, QV, KVV, ss, rs,
):
    q = coords()
    y, xx, xh, xl, z, c = q["y"], q["x"], q["xh"], q["xl"], q["z"], q["c"]
    zs, ys, xs = ring(q, "z"), ring(q, "y"), ring(q, "x")
    mate = device(q, c=1 - c)
    other = device(q, x=xx ^ 1)
    other_mate = device(q, x=xx ^ 1, c=1 - c)
    k = Copies(ss, rs)
    rows = pl.ds(pl.multiple_of(128 * c + 64 * xl, 64), 64)
    qcols = pl.ds(pl.multiple_of(QZ * z, 128), QZ)
    tile = 128 * (z // 2)
    kcols = pl.ds(pl.multiple_of(QDIM + tile, 128), 128)
    vcols = pl.ds(pl.multiple_of(QDIM + KVDIM + tile, 128), 128)
    fcols = pl.ds(pl.multiple_of(FZ * z, 128), FZ)
    loads = [
        k.local(wq.at[rows, qcols], QP.at[:, pl.ds(0, QZ)]),
        k.local(wq.at[rows, kcols], KT),
        k.local(wq.at[rows, vcols], VT),
        k.local(w1.at[rows, fcols], P1),
        k.local(w3.at[rows, fcols], P3),
    ]
    SG[...] = jnp.broadcast_to(seg[...], (8, TOK))
    NG[0:16] = jnp.broadcast_to(na[...].astype(F32), (16, 256)).astype(BF)
    NG[16:32] = jnp.broadcast_to(nf[...].astype(F32), (16, 256)).astype(BF)
    greet(zs + ys + xs + [mate, other_mate])
    seg_z = [k.send(SG, SEGS.at[xl, z, c], to) for to in zs]
    x_ring = Gather(k, q, "z", halves(x), ring_halves(XV))
    lanes = lambda j, n=1: pl.ds(pl.multiple_of(128 * j, 128 * n), 128 * n)
    dealt = deal(k, q, wo, lambda j: lanes(c * 8 + j * 2 + xl), TO)
    for cp in loads:
        cp.wait()
    odd = z % 2 == 1
    kt, vt = KT[...].astype(F32), VT[...].astype(F32)
    lane = lax.broadcasted_iota(jnp.int32, kt.shape, 1)
    kt = jnp.where(odd, pltpu.roll(kt, 64, 1), kt)
    vt = jnp.where(odd, vt, pltpu.roll(vt, 64, 1))
    QP[:, QZ:] = jnp.where(lane < HEAD_DIM, kt, vt).astype(BF)
    f1, f3 = pl.ds(0, FZ), pl.ds(FZ, FZ)
    top, low = pl.ds(0, 32), pl.ds(32, 32)
    thirty = lambda h: pl.ds(32 * h, 32)
    q_top = [k.send(QP.at[top], WV.at[c, y, xh, xl, top], to) for to in xs]
    q_low = [k.send(QP.at[low], WV.at[c, y, xh, xl, low], to) for to in ys]
    gn_y = [k.send(NG, GN.at[y, xh], to) for to in ys]
    up_y = Gather(
        k, q, "y", lambda h: P3.at[thirty(h)], lambda j, h: W13.at[c, j, xh, xl, thirty(h), f3]
    )
    gate_x = Gather(
        k, q, "x", lambda h: P1.at[thirty(h)],
        lambda j, h: W13.at[c, y, j // 2, j % 2, thirty(h), f1],
    )
    q_here = k.local(QP, WV.at[c, y, xh, xl])
    seg_here = k.local(SG, SEGS.at[xl, z, c])
    gn_here = k.local(NG, GN.at[y, xh])
    x_here = k.local(x, XV.at[z])
    up_here = k.local(P3, W13.at[c, y, xh, xl, :, f3])
    heres = [k.local(P1, W13.at[c, y, xh, xl, :, f1]), k.local(g, G.at[z])]
    dealt()
    o1 = [k.send(TO, WO.at[xh, :, lanes(c * 8 + y * 2 + xl)], to) for to in xs]
    o1_here = k.local(TO, WO.at[xh, :, lanes(c * 8 + y * 2 + xl)])
    for cp in seg_z:
        cp.wait_recv()
    seg_here.wait()
    part = SEGS.at[xl, :, c]
    seg2 = [k.send(part, part, to) for to in (mate, other, other_mate)]
    q_here.wait()
    for cp in q_top:
        cp.wait_recv()
    q_y = Gather(k, q, "y", lambda h: WV.at[c, y, h, :, top], lambda j, h: WV.at[c, j, h, :, top])
    for cp in gn_y:
        cp.wait_recv()
    gn_here.wait()
    gn2 = k.send(GN.at[:, xh], GN.at[:, xh], device(q, x=3 - xx))
    gate_x.relay()
    for cp in q_low:
        cp.wait_recv()
    q_half = lambda j, h: WV.at[c, pl.ds(2 * h, 2), j // 2, j % 2, low]
    q_x = Gather(k, q, "x", lambda h: q_half(xx, h), q_half)
    x_ring.relay()
    g_ring = Gather(k, q, "z", halves(g), ring_halves(G))
    up_y.relay()
    for cp in o1:
        cp.wait_recv()
    o1_here.wait()
    o_half = lambda j, h: WO.at[h, :, lanes(c * 8 + j * 2, 2)]
    o_y = Gather(k, q, "y", lambda h: o_half(y, h), o_half)
    for cp in seg2:
        cp.wait_recv()
    docs = [SEGS[i // 8, (i // 2) % 4, i % 2, 0:1].astype(F32) for i in range(16)]
    columns = jnp.concatenate(docs + [jnp.zeros((TOK - 16, TOK), F32)], axis=0).T
    for i in range(RING):
        mine = SEGS[xl, i, c, 0:1].astype(F32)
        count = jnp.zeros((TOK, TOK), F32)
        for j in range(16):
            count = count + jnp.where(columns[:, j : j + 1] < mine, 1.0, 0.0)
        first = jnp.sum(count, axis=0, keepdims=True)
        START[i] = first.astype(jnp.int32)
        index = TOK * (8 * xl + 2 * i + c) + lax.broadcasted_iota(jnp.int32, (1, TOK), 1)
        place = index.astype(F32) - first
        angle = jnp.broadcast_to(place, (TOK, TOK)).T * freq[...]
        COS[i] = jnp.cos(angle)
        sine = jnp.sin(angle)
        lane = lax.broadcasted_iota(jnp.int32, sine.shape, 1)
        SIN[i] = jnp.where(lane % 64 < 32, -sine, sine)
    q_y.relay()
    w2_dealt = deal(k, q, w2, lambda j: lanes(c * 8 + xl * 4 + j), TV)
    q_x.relay()
    up_y.near()
    up_y.end()
    up_here.wait()
    part = W13.at[c, :, xh, xl, :, f3]
    a3 = [k.send(part, part, to) for to in xs[:2]]
    o_y.relay()
    gn2.wait_recv()
    whole = lambda r: jnp.concatenate(
        [GN[d // 2, d % 2, r : r + 1].astype(F32) for d in range(8)], axis=1
    )
    gain = whole(0)
    GA[...] = gain
    GF[...] = whole(16)
    x_ring.near()
    x_ring.end()
    x_here.wait()
    for i in range(RING):
        xv = XV[i].astype(F32)
        scale = lax.rsqrt(jnp.mean(xv * xv, axis=-1, keepdims=True) + EPS)
        NV[i] = to_pieces((xv * scale * gain).astype(BF))
    done = [k.local(NV, N1)]
    for r in (q_y, q_x):
        r.near()
        r.end()
    q3 = k.send(WV.at[c], WV.at[c], mate)
    g_ring.relay()
    q3.wait_recv()
    done.append(k.local(WV, WQ))
    mixed = dot(NV[...].reshape(RING * TOK, D), WV[...].reshape(D, MZ))
    for i in range(RING):
        cos, sin = COS[i], SIN[i]
        for j in range(5):
            u = mixed[TOK * i : TOK * i + TOK, 128 * j : 128 * j + 128]
            turned = u * cos + swapped(u) * sin
            if j < 4:
                QV[i, :, 128 * j : 128 * j + 128] = turned.astype(BF)
            else:
                lane = lax.broadcasted_iota(jnp.int32, u.shape, 1)
                KVV[i] = jnp.where(lane < HEAD_DIM, turned, u).astype(BF)
    near = k.send(KVV, KV.at[xl, :, c], mate)
    n = k.n
    k.n += 2
    far, on = [
        pltpu.make_async_remote_copy(
            src_ref=src,
            dst_ref=KV.at[0, :, c],
            send_sem=ss.at[n + i],
            recv_sem=rs.at[n + i],
            device_id=to,
            device_id_type=MESH,
        )
        for i, (src, to) in enumerate(((KVV, other), (KV.at[0, :, c], mate)))
    ]

    @pl.when(xl == 0)
    def _():
        far.start()

    done += [k.local(KVV, KV.at[xl, :, c]), k.local(QV, Q)]
    o_y.near()
    o_y.end()
    part = WO.at[:, :, pl.ds(pl.multiple_of(1024 * c, 1024), 1024)]
    o3 = k.send(part, part, mate)
    w2_dealt()
    done.append(k.local(TV, T2))

    @pl.when(xl == 0)
    def _():
        far.wait_send()

    @pl.when(xl == 1)
    def _():
        far.wait_recv()
        on.start()
        on.wait_recv()
        on.wait_send()

    near.wait_recv()
    for cp in a3 + [o3]:
        cp.wait_recv()
    for cp in heres + done:
        cp.wait()
    for r in (gate_x, g_ring):
        r.near()
        r.end()
    k.close()


def middle_kernel(
    part, x, gain, t2, _, N2, H, W13, W2, p0, p1, v0, v1, below, above, n2, ss, rs
):
    q = coords()
    y, xx, xh, xl, z, c = q["y"], q["x"], q["xh"], q["xl"], q["z"], q["c"]
    ys, xs = ring(q, "y"), ring(q, "x")
    up, down = device(q, z=(z + 1) % 4), device(q, z=(z + 3) % 4)
    mate = device(q, c=1 - c)
    k = Copies(ss, rs)
    greet(ys + xs + [up, down, mate])
    z_sum = Sum(k, q, "z", ring_halves(part), halves(below), halves(above), (p0, p1))
    f1, f3 = pl.ds(0, FZ), pl.ds(FZ, FZ)
    up1 = lambda j: W13.at[c, :, j // 2, j % 2, :, f3]
    up_half = lambda j, h: W13.at[c, pl.ds(2 * h, 2), j // 2, j % 2, :, f3]
    cols = lambda cc, j, n: pl.ds(pl.multiple_of(128 * (cc * 8 + j), 128 * n), 128 * n)
    w2_here = k.local(t2, W2.at[xh, :, cols(c, xl * 4 + y, 1)])
    w2y = Gather(
        k, q, "y", lambda h: t2.at[pl.ds(352 * h, 352)],
        lambda j, h: W2.at[xh, pl.ds(352 * h, 352), cols(c, xl * 4 + j, 1)],
    )
    lower, higher = (xx + 3) % 4, (xx + 1) % 4
    far = [
        k.send(up_half(lower, 0), up_half(lower, 0), xs[0]),
        k.send(up_half(higher, 1), up_half(higher, 1), xs[1]),
    ]
    sent = [k.send(up1(j), up1(j), mate) for j in (xx, lower, higher)]
    w2y.relay()
    block = lambda j: W13.at[c, j, :, :, :, f1]
    gate = Gather(
        k, q, "y", lambda h: W13.at[c, y, h, :, :, f1], lambda j, h: W13.at[c, j, h, :, :, f1]
    )
    sent.append(k.send(block(y), block(y), mate))
    z_sum.relay(part.at[(z + 1) % 4, TOP], part.at[(z + 3) % 4, LOW], (v0, v1))
    w2_here.wait()
    w2y.near()
    w2y.end()
    down2 = lambda j: W2.at[j // 2, :, cols(c, (j % 2) * 4, 4)]
    down_half = lambda j, h: W2.at[j // 2, pl.ds(352 * h, 352), cols(c, (j % 2) * 4, 4)]
    down_ring = Gather(k, q, "x", lambda h: down_half(xx, h), down_half)
    sent.append(k.send(down2(xx), down2(xx), mate))
    z_sum.end()
    total = x[...].astype(F32) + (
        part[z].astype(F32) + (below[...].astype(F32) + above[...].astype(F32))
    )
    H[...] = total
    scale = lax.rsqrt(jnp.mean(total * total, axis=-1, keepdims=True) + EPS)
    n2[...] = to_pieces((total * scale * gain[...]).astype(BF))
    n2_ring = Gather(k, q, "z", halves(n2), ring_halves(N2))
    n2_here = k.local(n2, N2.at[z])
    gate.relay()
    down_ring.relay()
    for cp in far:
        cp.wait_recv()
    ref = up1((xx + 2) % 4)
    sent.append(k.send(ref, ref, mate))
    gate.near()
    for j in (gate.below, gate.above):
        sent.append(k.send(block(j), block(j), mate))
    n2_ring.relay()
    gate.end()
    sent.append(k.send(block(gate.far), block(gate.far), mate))
    down_ring.near()
    for j in (down_ring.below, down_ring.above):
        sent.append(k.send(down2(j), down2(j), mate))
    down_ring.end()
    sent.append(k.send(down2(down_ring.far), down2(down_ring.far), mate))
    for cp in sent:
        cp.wait_recv()
    n2_here.wait()
    n2_ring.near()
    n2_ring.end()
    k.close()


def back_kernel(
    dn2, hidden, G, N2, both, W2, WO, h, gain, V, FA, FB, F2, DO, OUT, DH, GAIN, *scratch
):
    (
        p0, p1, p2, p3, v0, v1, below, above, out_below, out_above, near0, near1, mine, dhb,
        vv, hv, gv, nv, bv, ov, wv, hT, outs, mate2, mate13, sum2, sum13, *bufs, ss, rs,
    ) = scratch
    q = coords()
    y, xx, z, c = q["y"], q["x"], q["z"], q["c"]
    mate = device(q, c=1 - c)
    k = Copies(ss, rs)
    get_n, get_b = k.local(N2, nv), k.local(both, bv)
    get_h, get_g = k.local(hidden, hv), k.local(G, gv)
    get_part = [
        k.local(dn2.at[(z + 1) % 4, TOP], near0),
        k.local(dn2.at[(z + 3) % 4, LOW], near1),
        k.local(dn2.at[z], mine),
    ]
    tile = lambda j: pl.ds(512 * j, 512)
    get_w = [k.local(W2.at[:, tile(j)], wv.at[j]) for j in range(2)]
    get_o = k.local(WO, ov)
    targets = [mate]
    for axis in ("x", "y", "z"):
        targets += ring(q, axis)[:2]
    greet(targets)
    z_sum = Sum(k, q, "z", ring_halves(dn2), halves(below), halves(above), (p0, p1))
    lanes = lambda cc, j: pl.ds(pl.multiple_of(1024 * cc + 256 * j, 256), 256)
    sent2, sent13 = [], []
    get_n.wait()
    get_b.wait()
    for j in range(4):
        mate13[j] = tn(nv[:, lanes(1 - c, j)], bv[...]).astype(BF).reshape(4, 64, 2 * FZ)
        sent13.append(k.send(mate13.at[j], sum13.at[j], mate))
    get_h.wait()
    get_g.wait()
    hT[...] = hv[...].T
    for cp in get_part:
        cp.wait()
    for j in range(4):
        mate2[j] = dot(hT[...], gv[:, lanes(1 - c, j)]).astype(BF)
        sent2.append(k.send(mate2.at[j], sum2.at[j], mate))
        if j == 2:
            z_sum.relay(near0, near1, (v0, v1))
    half = lambda ref: lambda i: ref.at[i]
    rest = 2 * FZ - SPLIT
    jobs = [
        ("x", lambda j, i: sum13.at[pl.ds(2 * i, 2), j, :, pl.ds(0, SPLIT)], FA),
        ("y", lambda j, i: sum13.at[j, pl.ds(2 * i, 2), :, pl.ds(SPLIT, rest)], FB),
        ("y", lambda j, i: sum2.at[j, pl.ds(704 * i, 704)], F2),
    ]
    sums, done = [], []

    def start(n):
        axis, block, _ = jobs[n]
        b = bufs[4 * n : 4 * n + 4]
        sums.append(Sum(k, q, axis, block, half(b[2]), half(b[3]), (b[0].at[0], b[0].at[1])))

    def relay(n):
        axis, block, _ = jobs[n]
        b = bufs[4 * n : 4 * n + 4]
        at = q[axis]
        sums[n].relay(block((at + 1) % 4, 0), block((at + 3) % 4, 1), (b[1].at[0], b[1].at[1]))

    def end(n):
        axis, block, out = jobs[n]
        b = bufs[4 * n : 4 * n + 4]
        sums[n].end()
        for i in range(2):
            total = block(q[axis], i)[...].astype(F32) + (
                b[2][i].astype(F32) + b[3][i].astype(F32)
            )
            b[2][i] = total.astype(BF)
        done.append(k.local(b[2], out))

    for j in range(4):
        sent13[j].wait_recv()
        own = tn(nv[:, lanes(c, j)], bv[...]).reshape(4, 64, 2 * FZ)
        sum13[j] = (own + sum13[j].astype(F32)).astype(BF)
    start(0)
    start(1)
    for j in range(4):
        sent2[j].wait_recv()
        sum2[j] = (dot(hT[...], gv[:, lanes(c, j)]) + sum2[j].astype(F32)).astype(BF)
    start(2)
    z_sum.end()
    dn = from_pieces(
        mine[...].astype(F32) + (below[...].astype(F32) + above[...].astype(F32))
    )
    back, gain_grad = rms_back(h[...], gain[...], dn)
    total = gv[pl.ds(pl.multiple_of(TOK * z, TOK), TOK)].astype(F32) + back
    DH[...] = total
    GAIN[...] = gain_grad
    dhb[...] = total.astype(BF)
    v_ring = Gather(k, q, "z", halves(dhb), ring_halves(vv))
    here = k.local(dhb, vv.at[z])
    for j in range(4):
        get_w[j].wait()
        part = dot(hv[...], wv[j % 2]).astype(BF)
        outs[:, :, tile(j)] = part.reshape(RING, TOK, 512)
        if j < 2:
            get_w.append(k.local(W2.at[:, tile(j + 2)], wv.at[j]))
    out_sum = Sum(
        k, q, "z", ring_halves(outs), halves(out_below), halves(out_above), (p2, p3)
    )
    relay(1)
    relay(0)
    v_ring.relay()
    relay(2)
    z_sum.sent()
    out_sum.relay(outs.at[(z + 1) % 4, TOP], outs.at[(z + 3) % 4, LOW], (v0, v1))
    end(1)
    end(0)
    v_ring.near()
    v_ring.end()
    here.wait()
    get_o.wait()
    done.append(k.local(vv, V))
    DO[...] = nt(vv[...].reshape(RING * TOK, D), ov[...]).astype(BF)
    end(2)
    out_sum.end()
    OUT[...] = h[...] + (
        outs[z].astype(F32) + (out_below[...].astype(F32) + out_above[...].astype(F32))
    )
    for cp in done:
        cp.wait()
    k.close()


def quarter(xt, rows):
    return (
        pl.ds(pl.multiple_of((xt // 2) * rows, rows), rows),
        pl.ds(pl.multiple_of((xt % 2) * 128, 128), 128),
    )


def tail_kernel(
    dkv, dq, cosine, sine, x, dh, gain, gain2, fa, fb, f2, wq, n1, o, dho,
    IG, G1, G3, G2, GO, GQ, GKV, gain_out, *scratch,
):
    (
        wv, nv, ov, gv, R, dm, dn, p0, p1, v0, v1, below, above, mate_o, sum_o, mate_q, sum_q,
        ob0, ob1, ob2, ob3, qb0, qb1, qb2, qb3, la, lb, l2, pa, pb, p2, t2, lo, lq, fo, fq,
        po, pq, to_, gains, s0, s1, s2, s3, s4, total, ss, rs,
    ) = scratch
    q = coords()
    y, xx, xh, xl, z, c = q["y"], q["x"], q["xh"], q["xl"], q["z"], q["c"]
    zs, ys, xs = ring(q, "z"), ring(q, "y"), ring(q, "x")
    mate, other, cross = device(q, c=1 - c), device(q, x=xx ^ 1), device(q, x=3 - xx)
    other_mate = device(q, x=xx ^ 1, c=1 - c)
    steps = (1, 3, 2)
    k = Copies(ss, rs)
    get_o, get_g = k.local(o, ov), k.local(dho, gv)
    get_w, get_n = k.local(wq, wv), k.local(n1, nv)
    greet(zs + ys + xs + [mate, other_mate], q)
    near = k.send(dkv.at[xl, :, 1 - c], R.at[0], mate)
    n = k.n
    k.n += 2
    pre, far = [
        pltpu.make_async_remote_copy(
            src_ref=src,
            dst_ref=dst,
            send_sem=ss.at[n + i],
            recv_sem=rs.at[n + i],
            device_id=to,
            device_id_type=MESH,
        )
        for i, (src, dst, to) in enumerate(
            ((dkv.at[0, :, 1 - c], R.at[1], mate), (R.at[2], R.at[3], other))
        )
    ]

    @pl.when(xl == 1)
    def _():
        pre.start()

    leg_2 = []
    for i, s in enumerate(steps):
        r, cc = quarter((xx + s) % 4, 704)
        leg_2.append(k.send(f2.at[r, cc], l2.at[i], xs[i]))
    leg_a = [k.send(fa.at[(y + s) % 4], la.at[i], ys[i]) for i, s in enumerate(steps)]
    leg_b = [k.send(fb.at[(xx + s) % 4], lb.at[i], xs[i]) for i, s in enumerate(steps)]
    lanes = lambda cc, j: pl.ds(pl.multiple_of(1024 * cc + 256 * j, 256), 256)
    get_o.wait()
    get_g.wait()
    swaps = []
    for j in range(4):
        mate_o[j] = tn(ov[...], gv[:, lanes(1 - c, j)]).astype(BF)
        swaps.append(k.send(mate_o.at[j], sum_o.at[j], mate))

    @pl.when(xl == 1)
    def _():
        R[3] = jnp.zeros(R.shape[1:], BF)
        pre.wait()
        for i in range(RING):
            R[2, i] = (dkv[0, i, c].astype(F32) + R[1, i].astype(F32)).astype(BF)
        far.start()

    for j in range(4):
        swaps[j].wait_recv()
        sum_o[j] = (tn(ov[...], gv[:, lanes(c, j)]) + sum_o[j].astype(F32)).astype(BF)
    half = lambda ref: lambda h: ref.at[h]
    o_block = lambda j, h: sum_o.at[j, pl.ds(256 * h, 256)]
    q_block = lambda j, h: sum_q.at[j, pl.ds(2 * h, 2)]
    o_sum = Sum(k, q, "y", o_block, half(ob2), half(ob3), (ob0.at[0], ob0.at[1]))
    for cp in leg_2:
        cp.wait_recv()
    r, cc = quarter(xx, 704)
    p2[...] = add4(f2[r, cc], l2[0], l2[1], l2[2])
    turned = turn(k, q, [(p2, t2)])
    at = lambda zz, off, n: pl.ds(pl.multiple_of(FZ * zz + off, 128), n)
    rows = pl.ds(pl.multiple_of(128 * c + 64 * xl, 64), 64)
    pair = pl.ds(pl.multiple_of(128 * c, 128), 128)
    f1 = pl.ds(0, FZ)
    rest = SPLIT - FZ
    quarter_rows = lambda h: pl.ds(pl.multiple_of(128 * c + 64 * xl + 32 * h, 32), 32)

    def over_z(src, ref, off, n):
        return Gather(
            k, q, "z", lambda h: src.at[pl.ds(32 * h, 32)],
            lambda j, h: ref.at[quarter_rows(h), at(j, off, n)],
        )

    spans = [(G1, 0, FZ), (G3, 0, rest), (G3, rest, FZ - rest)]
    pieces = [pa.at[:, f1], pa.at[:, pl.ds(FZ, rest)], pb]
    block = lambda i, j: spans[i][0].at[rows, at(j, spans[i][1], spans[i][2])]
    for cp in leg_a:
        cp.wait_recv()
    pa[...] = add4(fa[y], la[0], la[1], la[2])
    rings = [over_z(pieces[i], *spans[i]) for i in range(2)]
    to_x = [k.send(pieces[i], block(i, z), other) for i in range(2)]
    for cp in leg_b:
        cp.wait_recv()
    pb[...] = add4(fb[xx], lb[0], lb[1], lb[2])
    rings.append(over_z(pieces[2], *spans[2]))
    to_x.append(k.send(pieces[2], block(2, z), other))
    heres = [k.local(pieces[i], block(i, z)) for i in range(3)]
    o_sum.relay(o_block((y + 1) % 4, 0), o_block((y + 3) % 4, 1), (ob1.at[0], ob1.at[1]))

    @pl.when(xl == 1)
    def _():
        far.wait_send()

    @pl.when(xl == 0)
    def _():
        far.wait_recv()

    near.wait_recv()
    for i in range(RING):
        part = slice(TOK * i, TOK * i + TOK)
        w = dkv[xl, i, c].astype(F32) + (R[0, i].astype(F32) + R[3, i].astype(F32))
        lane = lax.broadcasted_iota(jnp.int32, w.shape, 1)
        dm[part, :QZ] = dq[i]
        dm[part, QZ:] = jnp.where(
            lane < HEAD_DIM, w * cosine[i] - swapped(w) * sine[i], w
        ).astype(BF)
    get_w.wait()
    dn[...] = nt(dm[...], wv[...]).astype(BF).reshape(RING, TOK, D)
    z_sum = Sum(k, q, "z", ring_halves(dn), halves(below), halves(above), (p0, p1))
    get_n.wait()
    cols = lambda cc: pl.ds(pl.multiple_of(1024 * cc, 1024), 1024)
    shape = (4, 4, 64, MZ)
    mate_q[...] = tn(nv[:, cols(1 - c)], dm[...]).astype(BF).reshape(shape)
    swap = k.send(mate_q, sum_q, mate)

    def onward(i):
        rings[i].near()
        for j in (rings[i].below, rings[i].above):
            to_x.append(k.send(block(i, j), block(i, j), other))

    rings[0].relay()
    onward(0)
    rings[1].relay()
    onward(1)
    swap.wait_recv()
    own = tn(nv[:, cols(c)], dm[...]).reshape(shape)
    sum_q[...] = (own + sum_q[...].astype(F32)).astype(BF)
    q_sum = Sum(k, q, "y", q_block, half(qb2), half(qb3), (qb0.at[0], qb0.at[1]))
    rings[2].relay()
    turned()
    col = pl.ds(pl.multiple_of(128 * (c * 8 + z * 2 + xl), 128), 128)
    down_x = k.send(t2, G2.at[:, col], other)
    down_here = k.local(t2, G2.at[:, col])
    onward(2)
    o_sum.end()
    for h in range(2):
        part = o_block(y, h)[...].astype(F32) + (ob2[h].astype(F32) + ob3[h].astype(F32))
        fo[pl.ds(256 * h, 256)] = part.astype(BF)
    leg_o, leg_q = [], []
    for i, s in enumerate(steps):
        r, cc = quarter((xx + s) % 4, 256)
        leg_o.append(k.send(fo.at[r, cc], lo.at[i], xs[i]))
    q_sum.relay(q_block((y + 1) % 4, 0), q_block((y + 3) % 4, 1), (qb1.at[0], qb1.at[1]))
    z_sum.relay(dn.at[(z + 1) % 4, TOP], dn.at[(z + 3) % 4, LOW], (v0, v1))
    q_sum.end()
    for h in range(2):
        part = q_block(y, h)[...].astype(F32) + (qb2[h].astype(F32) + qb3[h].astype(F32))
        fq[pl.ds(2 * h, 2)] = part.astype(BF)
    for i, s in enumerate(steps):
        leg_q.append(k.send(fq.at[(xx + s) % 4], lq.at[i], xs[i]))
    rings[0].end()
    to_x.append(k.send(block(0, rings[0].far), block(0, rings[0].far), other))
    down_x.wait_recv()
    down_here.wait()
    down_half = lambda j, h: G2.at[
        pl.ds(352 * h, 352), pl.ds(pl.multiple_of(128 * (c * 8 + j * 2), 256), 256)
    ]
    down_ring = Gather(k, q, "z", lambda h: down_half(z, h), down_half)
    for i in (1, 2):
        rings[i].end()
        to_x.append(k.send(block(i, rings[i].far), block(i, rings[i].far), other))
    z_sum.end()
    back, gain1 = rms_back(
        x[...].astype(F32),
        gain[...],
        from_pieces(dn[z].astype(F32) + (below[...].astype(F32) + above[...].astype(F32))),
    )
    IG[...] = dh[...] + back
    gains[...] = jnp.zeros_like(gains)
    for d in range(8):
        gains[d // 2, d % 2, 0:1] = gain1[:, 256 * d : 256 * d + 256]
        gains[d // 2, d % 2, 1:2] = gain2[:, 256 * d : 256 * d + 256]
    gain_y = [k.send(gains.at[(y + s) % 4], s0.at[y], ys[i]) for i, s in enumerate(steps)]
    gain_here = k.local(gains.at[y], s0.at[y])
    for cp in leg_o:
        cp.wait_recv()
    r, cc = quarter(xx, 256)
    po[...] = add4(fo[r, cc], lo[0], lo[1], lo[2])
    o_turned = turn(k, q, [(po, to_)])
    down_ring.relay()
    for cp in leg_q:
        cp.wait_recv()
    pq[...] = add4(fq[xx], lq[0], lq[1], lq[2])
    qc = lambda j: pl.ds(pl.multiple_of(QZ * j, 128), QZ)
    kc = lambda j: pl.ds(pl.multiple_of(128 * j, 128), 128)
    q_pieces = [
        (pq.at[:, pl.ds(0, QZ)], GQ.at[rows, qc(z)]),
        (pq.at[:, pl.ds(QZ, 128)], GKV.at[rows, kc(z)]),
    ]
    q_x = [k.send(src, dst, other) for src, dst in q_pieces]
    q_here = [k.local(src, dst) for src, dst in q_pieces]
    for cp in gain_y:
        cp.wait_recv()
    gain_here.wait()
    s1[0] = (s0[0] + s0[1]) + (s0[2] + s0[3])
    gain_x = k.send(s1.at[0, 1 - xh], s1.at[1, 0], cross)
    gain_x.wait_recv()
    s2[z] = s1[0, xh] + s1[1, 0]
    gain_z = [k.send(s2.at[z], s2.at[z], to) for to in zs]
    o_turned()
    o_x = k.send(to_, GO.at[:, col], other)
    o_here = k.local(to_, GO.at[:, col])
    for cp in to_x:
        cp.wait_recv()
    for cp in heres:
        cp.wait()
    last = [k.send(ref.at[pair], ref.at[pair], mate) for ref in (G1, G3)]
    for cp in q_x:
        cp.wait_recv()
    for cp in q_here:
        cp.wait()
    half_rows = lambda h: pl.ds(pl.multiple_of(128 * c + 64 * h, 64), 64)
    q_half = lambda j, h: GQ.at[half_rows(h), qc(j)]
    kv_half = lambda j, h: GKV.at[half_rows(h), kc(j)]
    last_rings = [
        Gather(k, q, "z", lambda h: q_half(z, h), q_half),
        Gather(k, q, "z", lambda h: kv_half(z, h), kv_half),
    ]
    down_ring.near()
    down_ring.end()
    last.append(k.send(G2.at[:, cols(c)], G2.at[:, cols(c)], mate))
    o_x.wait_recv()
    o_here.wait()
    o_half = lambda j, h: GO.at[
        pl.ds(128 * h, 128), pl.ds(pl.multiple_of(128 * (c * 8 + j * 2), 256), 256)
    ]
    last_rings.append(Gather(k, q, "z", lambda h: o_half(z, h), o_half))
    for cp in gain_z:
        cp.wait_recv()
    s3[0] = (s2[0] + s2[1]) + (s2[2] + s2[3])
    gain_x = k.send(s3.at[0], s3.at[1], other)
    last_rings[0].relay()
    last_rings[1].relay()
    gain_x.wait_recv()
    s4[0] = s3[0] + s3[1]
    gain_c = k.send(s4.at[0], s4.at[1], mate)
    last_rings[2].relay()
    for r in last_rings:
        r.near()
        r.end()
    refs = [GQ.at[pair], GKV.at[pair], GO.at[:, cols(c)]]
    last += [k.send(ref, ref, mate) for ref in refs]
    gain_c.wait_recv()
    total[...] = s4[0] + s4[1]
    gain_done = k.local(total, gain_out)
    for cp in last:
        cp.wait_recv()
    gain_done.wait()
    k.close()


PARAMS = pltpu.CompilerParams(vmem_limit_bytes=VMEM_LIMIT)


def add4(a, b, c, d):
    a, b, c, d = (v.astype(F32) for v in (a, b, c, d))
    return ((a + b) + (c + d)).astype(BF)


def to_pieces(v):
    return jnp.concatenate(
        [v[:, 256 * d + 128 * c : 256 * d + 128 * c + 128] for c in range(2) for d in range(8)],
        axis=1,
    )


def from_pieces(v):
    return jnp.concatenate(
        [v[:, 1024 * c + 128 * d : 1024 * c + 128 * d + 128] for d in range(8) for c in range(2)],
        axis=1,
    )


def swapped(u):
    lane = lax.broadcasted_iota(jnp.int32, u.shape, 1)
    return jnp.where(lane % 64 < 32, pltpu.roll(u, 96, 1), pltpu.roll(u, 32, 1))


def stacked_low(tiles):
    out = []
    for pair in range(4):
        tile = tiles[:, 128 * pair : 128 * pair + 128].astype(F32)
        lane = lax.broadcasted_iota(jnp.int32, tile.shape, 1)
        out.append(jnp.where(lane < HEAD_DIM, tile, 0.0))
        out.append(jnp.where(lane < HEAD_DIM, pltpu.roll(tile, 64, 1), 0.0))
    return jnp.concatenate(out, axis=0)


def stacked_high(tiles):
    out = []
    for pair in range(4):
        tile = tiles[:, 128 * pair : 128 * pair + 128].astype(F32)
        lane = lax.broadcasted_iota(jnp.int32, tile.shape, 1)
        out.append(jnp.where(lane >= HEAD_DIM, pltpu.roll(tile, 64, 1), 0.0))
        out.append(jnp.where(lane >= HEAD_DIM, tile, 0.0))
    return jnp.concatenate(out, axis=0)


def unstacked(v):
    tiles = []
    for pair in range(4):
        both = jnp.concatenate(
            [v[:, 256 * pair : 256 * pair + 128], v[:, 256 * pair + 128 : 256 * pair + 256]],
            axis=0,
        )
        tiles.append(both.T)
    return tiles


def nt(a, b):
    return lax.dot_general(a, b, (((1,), (1,)), ((), ())), preferred_element_type=F32)


def tn(a, b):
    return lax.dot_general(a, b, (((0,), (0,)), ((), ())), preferred_element_type=F32)


def own_chunk(i):
    ctx = lax.axis_index("ctx")
    return (ctx // 8) * 8 + 2 * i + ctx % 2


def over_chunks(start, chunk, step, carry):
    first = start.astype(F32)
    low = jnp.min(first).astype(jnp.int32) // TOK
    high = jnp.minimum((jnp.max(first).astype(jnp.int32) + TOK - 1) // TOK, chunk)
    carry = lax.fori_loop(low, high, lambda kc, cr: step(kc, 1, True, cr), carry)
    pairs = (chunk - high) // 2
    carry = lax.fori_loop(0, pairs, lambda n, cr: step(high + 2 * n, 2, False, cr), carry)
    carry = lax.fori_loop(
        high + 2 * pairs, chunk, lambda kc, cr: step(kc, 1, False, cr), carry
    )
    return step(chunk, 1, True, carry)


def chunk_scores(keys, stacked, kc, chunk, starts, masked):
    raw = nt(keys, stacked)
    if not masked:
        return raw
    key = kc * TOK + lax.broadcasted_iota(jnp.int32, raw.shape, 0)
    query = chunk * TOK + lax.broadcasted_iota(jnp.int32, raw.shape, 1) % TOK
    return jnp.where((key <= query) & (key >= starts), raw, -1e30)


def attend_kernel(query, kv, start, out, logsum):
    chunk = own_chunk(pl.program_id(0))
    stacked = (stacked_low(query[0]) * (1.0 / HEAD_DIM**0.5)).astype(BF)
    starts = jnp.concatenate([start[0]] * GROUP, axis=1)

    def step(kc, size, masked, carry):
        top, summed, total = carry
        keys = kv[pl.ds(kc, size)].reshape(size * TOK, 128)
        scores = chunk_scores(keys, stacked, kc, chunk, starts, masked)
        new_top = jnp.maximum(top, jnp.max(scores, axis=0, keepdims=True))
        weights = jnp.exp(scores - new_top)
        fade = jnp.exp(top - new_top)
        summed = summed * fade + jnp.sum(weights, axis=0, keepdims=True)
        part = tn(keys, weights.astype(BF))
        return new_top, summed, total * fade + part[HEAD_DIM:]

    rows = GROUP * TOK
    carry = (jnp.full((1, rows), -1e30, F32), jnp.zeros((1, rows), F32), jnp.zeros((64, rows), F32))
    top, summed, total = over_chunks(start[0], chunk, step, carry)
    for pair, tile in enumerate(unstacked(total / summed)):
        out[0, :, 128 * pair : 128 * pair + 128] = tile.astype(BF)
    logsum[0] = top + jnp.log(summed)


def attend(query, kv, start):
    chunk = lambda r, cols: pl.BlockSpec((1, r, cols), lambda i: (i, 0, 0))
    return pl.pallas_call(
        attend_kernel,
        name="attend",
        cost_estimate=cost(12),
        grid=(RING,),
        in_specs=[
            chunk(TOK, QZ),
            pl.BlockSpec((16, TOK, 128), lambda i: (0, 0, 0)),
            chunk(1, TOK),
        ],
        out_specs=[chunk(TOK, QZ), chunk(1, GROUP * TOK)],
        out_shape=[
            jax.ShapeDtypeStruct((RING, TOK, QZ), BF),
            jax.ShapeDtypeStruct((RING, 1, GROUP * TOK), F32),
        ],
        compiler_params=PARAMS,
    )(query, kv, start)


def attend_back_kernel(
    query, kv, start, out, grad_out, logsum, cosine, sine, dquery, dkv, total
):
    i = pl.program_id(0)
    chunk = own_chunk(i)
    stacked = (stacked_low(query[0]) * (1.0 / HEAD_DIM**0.5)).astype(BF)
    grads = stacked_high(grad_out[0]).astype(BF)
    starts = jnp.concatenate([start[0]] * GROUP, axis=1)
    lse = logsum[0]
    deltas = []
    for pair in range(4):
        cols = slice(128 * pair, 128 * pair + 128)
        prod = (out[0, :, cols].astype(F32) * grad_out[0, :, cols].astype(F32)).T
        deltas.append(jnp.sum(prod[:HEAD_DIM], axis=0, keepdims=True))
        deltas.append(jnp.sum(prod[HEAD_DIM:], axis=0, keepdims=True))
    delta = jnp.concatenate(deltas, axis=1)

    @pl.when(i == 0)
    def _():
        total[...] = jnp.zeros_like(total)

    def step(kc, size, masked, dq):
        keys = kv[pl.ds(kc, size)].reshape(size * TOK, 128)
        scores = chunk_scores(keys, stacked, kc, chunk, starts, masked)
        probs = jnp.exp(scores - lse)
        grad_probs = nt(keys, grads)
        grad_scores = (probs * (grad_probs - delta)).astype(BF)
        part = dot(grad_scores, stacked) + dot(probs.astype(BF), grads)
        total[pl.ds(kc, size)] += part.reshape(size, TOK, 128)
        return dq + tn(keys, grad_scores)[:HEAD_DIM]

    dq = over_chunks(start[0], chunk, step, jnp.zeros((64, GROUP * TOK), F32))
    cos, sin = cosine[0], sine[0]
    for pair, tile in enumerate(unstacked(dq)):
        tile = tile * (1.0 / HEAD_DIM**0.5)
        dquery[0, :, 128 * pair : 128 * pair + 128] = (tile * cos - swapped(tile) * sin).astype(BF)

    @pl.when(i == RING - 1)
    def _():
        dkv[...] = total[...].astype(BF)


def attend_back(query, kv, start, out, grad_out, logsum, cosine, sine):
    chunk = lambda r, cols: pl.BlockSpec((1, r, cols), lambda i: (i, 0, 0))
    whole = pl.BlockSpec((16, TOK, 128), lambda i: (0, 0, 0))
    return pl.pallas_call(
        attend_back_kernel,
        name="attend_back",
        cost_estimate=cost(15),
        grid=(RING,),
        in_specs=[
            chunk(TOK, QZ),
            whole,
            chunk(1, TOK),
            chunk(TOK, QZ),
            chunk(TOK, QZ),
            chunk(1, GROUP * TOK),
            chunk(TOK, 128),
            chunk(TOK, 128),
        ],
        out_specs=[chunk(TOK, QZ), whole],
        scratch_shapes=[pltpu.VMEM((16, TOK, 128), F32)],
        out_shape=[
            jax.ShapeDtypeStruct((RING, TOK, QZ), BF),
            jax.ShapeDtypeStruct((16, TOK, 128), BF),
        ],
        compiler_params=PARAMS,
    )(query, kv, start, out, grad_out, logsum, cosine, sine)


def rms_back(v, gain, grad):
    scale = lax.rsqrt(jnp.mean(v * v, axis=-1, keepdims=True) + EPS)
    unit = v * scale
    gain_grad = jnp.sum(grad * unit, axis=0, keepdims=True)
    inner = grad * gain
    return scale * (inner - unit * jnp.mean(inner * unit, axis=-1, keepdims=True)), gain_grad


def finish_kernel(a, b, g1, g3, g2, go, gq, gkv, out, grad, gate, up, down, proj, qkv):
    out[...] = a[...]
    grad[...] = b[...]
    for src, dst in ((g1, gate), (g3, up), (g2, down), (go, proj)):
        dst[...] = src[...].astype(F32)
    qkv[:, :QDIM] = gq[...].astype(F32)
    kv = gkv[...].astype(F32)
    tiles = [kv[:, 128 * j : 128 * j + 128] for j in range(4)]
    lane = lax.broadcasted_iota(jnp.int32, tiles[0].shape, 1)
    for j in range(2):
        one, two = tiles[2 * j], tiles[2 * j + 1]
        keys = jnp.where(lane < HEAD_DIM, one, pltpu.roll(two, 64, 1))
        values = jnp.where(lane < HEAD_DIM, pltpu.roll(one, 64, 1), two)
        qkv[:, QDIM + 128 * j : QDIM + 128 * j + 128] = keys
        qkv[:, QDIM + KVDIM + 128 * j : QDIM + KVDIM + 128 * j + 128] = values


def finish(*arrays):
    steps = 4
    spec = lambda v: pl.BlockSpec((v.shape[0] // steps, v.shape[1]), lambda i: (i, 0))
    outs = [jax.ShapeDtypeStruct(v.shape, F32) for v in arrays[:-2]]
    outs.append(jax.ShapeDtypeStruct((256, QDIM + 2 * KVDIM), F32))
    return pl.pallas_call(
        finish_kernel,
        name="finish",
        cost_estimate=cost(12),
        grid=(steps,),
        in_specs=[spec(v) for v in arrays],
        out_specs=[spec(v) for v in outs],
        out_shape=outs,
        compiler_params=PARAMS,
    )(*arrays)


def pick(v, index, axis=0):
    return lax.dynamic_index_in_dim(v, index, axis, keepdims=False)


def dot(a, b):
    return jnp.dot(a, b, preferred_element_type=F32)


def body(tokens, segments, cotangent, norm_attn, norm_ffn, wqkv, wo, w1, w3, w2):
    q = coords()
    y, xx, xl, z, c = q["y"], q["x"], q["xl"], q["z"], q["c"]
    x = tokens[0]
    g = cotangent[0]
    lane = jnp.arange(128)
    freq = THETA ** (-(lane % 32).astype(F32) * 2.0 / HEAD_DIM)
    table = ((RING, TOK, 128), F32)
    G, WQ, WO, W13, t2, n1, query, KV, cosine, sine, start, gain_attn, gain_ffn = talk(
        front_kernel,
        "front",
        1,
        46,
        120,
        (
            x, g, segments, norm_attn[None], norm_ffn[None], freq[None],
            wqkv, wo, w1, w3, w2,
        ),
        [
            ((RING, TOK, D), BF),
            ((2, 4, 2, 2, 64, MZ), BF),
            ((2, 256, D), BF),
            ((2, 4, 2, 2, 64, 2 * FZ), BF),
            ((704, 128), BF),
            ((RING, TOK, D), BF),
            ((RING, TOK, QZ), BF),
            ((2, 4, 2, TOK, 128), BF),
            table,
            table,
            ((RING, 1, TOK), jnp.int32),
            ((1, D), F32),
            ((1, D), F32),
        ],
        scratch=[
            pltpu.VMEM((256, 128), BF),
            pltpu.VMEM((704, 128), BF),
            pltpu.VMEM((64, MZ), BF),
            pltpu.VMEM((64, 128), BF),
            pltpu.VMEM((64, 128), BF),
            pltpu.VMEM((64, FZ), BF),
            pltpu.VMEM((64, FZ), BF),
            pltpu.VMEM((8, TOK), jnp.int32),
            pltpu.VMEM((32, 256), BF),
            pltpu.VMEM((2, 4, 2, 8, TOK), jnp.int32),
            pltpu.VMEM((4, 2, 32, 256), BF),
            pltpu.VMEM((RING, TOK, D), BF),
            pltpu.VMEM((2, 4, 2, 2, 64, MZ), BF),
            pltpu.VMEM((RING, TOK, D), BF),
            pltpu.VMEM((RING, TOK, QZ), BF),
            pltpu.VMEM((RING, TOK, 128), BF),
        ],
        near=tuple(range(6)),
        near_out=(8, 9, 10, 11, 12),
    )
    WQ = WQ.reshape(D, MZ)
    WO = WO.reshape(QZ, D)
    KV = KV.reshape(16, TOK, 128)
    heads_out, logsum = attend(query, KV, start)
    o = heads_out.reshape(RING * TOK, QZ)
    part = dot(o, WO).astype(BF).reshape(RING, TOK, D)
    N2, h, W13, W2 = talk(
        middle_kernel,
        "middle",
        3,
        42,
        60,
        (part, x, gain_ffn, t2, W13),
        [
            ((RING, TOK, D), BF),
            ((TOK, D), F32),
            ((2, 4, 2, 2, 64, 2 * FZ), BF),
            ((2, 704, D), BF),
        ],
        scratch=[
            *[pltpu.VMEM(HALF, BF)] * 4,
            *[pltpu.VMEM((TOK, D), BF)] * 3,
        ],
        near=(0, 1, 2, 3),
        near_out=(1,),
        alias={4: 2},
    )
    N2, G = N2.reshape(RING * TOK, D), G.reshape(RING * TOK, D)
    W13, W2 = W13.reshape(D, 2 * FZ), W2.reshape(FZ, D)
    gate, up = dot(N2, W13[:, :FZ]), dot(N2, W13[:, FZ:])
    hidden = (jax.nn.silu(gate) * up).astype(BF)
    dhid = jnp.einsum("td,fd->tf", G, W2, preferred_element_type=F32)
    sigma = jax.nn.sigmoid(gate)
    dgate = (dhid * up * sigma * (1.0 + gate * (1.0 - sigma))).astype(BF)
    dup = (dhid * gate * sigma).astype(BF)
    both = jnp.concatenate([dgate, dup], axis=1)
    dn2 = jnp.einsum("tf,df->td", both, W13, preferred_element_type=F32)
    dn2 = dn2.astype(BF).reshape(RING, TOK, D)
    rest = 2 * FZ - SPLIT
    buffers = []
    for shape in ((2, 64, SPLIT), (2, 64, rest), (704, 256)):
        buffers += [pltpu.VMEM((2,) + shape, BF)] * 4
    DH, fa, fb, f2, dheads, output, dh, gain2 = talk(
        back_kernel,
        "back",
        4,
        60,
        100,
        (dn2, hidden, G, N2, both, W2, WO, h, gain_ffn),
        [
            ((RING, TOK, D), BF),
            ((2, 2, 64, SPLIT), BF),
            ((2, 2, 64, rest), BF),
            ((2, 704, 256), BF),
            ((RING * TOK, QZ), BF),
            ((TOK, D), F32),
            ((TOK, D), F32),
            ((1, D), F32),
        ],
        scratch=[
            *[pltpu.VMEM(HALF, BF)] * 6,
            *[pltpu.VMEM((TOK, D), BF)] * 4,
            *[pltpu.VMEM(HALF, BF)] * 2,
            *[pltpu.VMEM((TOK, D), BF)] * 2,
            pltpu.VMEM((RING, TOK, D), BF),
            pltpu.VMEM((RING * TOK, FZ), BF),
            pltpu.VMEM((RING * TOK, D), BF),
            pltpu.VMEM((RING * TOK, D), BF),
            pltpu.VMEM((RING * TOK, 2 * FZ), BF),
            pltpu.VMEM((QZ, D), BF),
            pltpu.VMEM((2, FZ, 512), BF),
            pltpu.VMEM((FZ, RING * TOK), BF),
            pltpu.VMEM((RING, TOK, D), BF),
            pltpu.VMEM((4, FZ, 256), BF),
            pltpu.VMEM((4, 4, 64, 2 * FZ), BF),
            pltpu.VMEM((4, FZ, 256), BF),
            pltpu.VMEM((4, 4, 64, 2 * FZ), BF),
            *buffers,
        ],
        near=(7, 8),
        near_out=(4, 5, 6, 7),
    )
    fa, fb = fa.reshape(4, 64, SPLIT), fb.reshape(4, 64, rest)
    f2 = f2.reshape(1408, 256)
    DH = DH.reshape(RING * TOK, D)
    dquery, dkv = attend_back(
        query, KV, start, heads_out, dheads.reshape(RING, TOK, QZ), logsum, cosine, sine
    )
    small = (8, 256)
    input_grad, G1, G3, G2, GO, GQ, GKV, gain_out = talk(
        tail_kernel,
        "tail",
        6,
        75,
        170,
        (
            dkv.reshape(2, 4, 2, TOK, 128), dquery, cosine, sine, x, dh, gain_attn, gain2,
            fa, fb, f2, WQ, n1.reshape(RING * TOK, D), o, DH,
        ),
        [
            ((TOK, D), F32),
            ((256, 4 * FZ), BF),
            ((256, 4 * FZ), BF),
            ((704, D), BF),
            ((256, D), BF),
            ((256, QDIM), BF),
            ((256, 2 * KVDIM), BF),
            (small, F32),
        ],
        scratch=[
            pltpu.VMEM((D, MZ), BF),
            pltpu.VMEM((RING * TOK, D), BF),
            pltpu.VMEM((RING * TOK, QZ), BF),
            pltpu.VMEM((RING * TOK, D), BF),
            pltpu.VMEM((4, RING, TOK, 128), BF),
            pltpu.VMEM((RING * TOK, MZ), BF),
            pltpu.VMEM((RING, TOK, D), BF),
            *[pltpu.VMEM(HALF, BF)] * 4,
            *[pltpu.VMEM((TOK, D), BF)] * 2,
            *[pltpu.VMEM((4, QZ, 256), BF)] * 2,
            *[pltpu.VMEM((4, 4, 64, MZ), BF)] * 2,
            *[pltpu.VMEM((2, 256, 256), BF)] * 4,
            *[pltpu.VMEM((2, 2, 64, MZ), BF)] * 4,
            pltpu.VMEM((3, 64, SPLIT), BF),
            pltpu.VMEM((3, 64, rest), BF),
            pltpu.VMEM((3, 704, 128), BF),
            pltpu.VMEM((64, SPLIT), BF),
            pltpu.VMEM((64, rest), BF),
            pltpu.VMEM((704, 128), BF),
            pltpu.VMEM((704, 128), BF),
            pltpu.VMEM((3, 256, 128), BF),
            pltpu.VMEM((3, 64, MZ), BF),
            pltpu.VMEM((512, 256), BF),
            pltpu.VMEM((4, 64, MZ), BF),
            pltpu.VMEM((256, 128), BF),
            pltpu.VMEM((64, MZ), BF),
            pltpu.VMEM((256, 128), BF),
            pltpu.VMEM((4, 2) + small, F32),
            pltpu.VMEM((4, 2) + small, F32),
            pltpu.VMEM((2, 2) + small, F32),
            pltpu.VMEM((4,) + small, F32),
            pltpu.VMEM((2,) + small, F32),
            pltpu.VMEM((2,) + small, F32),
            pltpu.VMEM(small, F32),
        ],
        near=tuple(range(11)),
        near_out=(0,),
    )
    output, input_grad, gate_grad, up_grad, down_grad, out_grad, qkv_grad = finish(
        output, input_grad, G1, G3, G2, GO, GQ, GKV
    )
    return (
        output[None],
        input_grad[None],
        gain_out[0],
        gain_out[1],
        qkv_grad,
        out_grad,
        gate_grad,
        up_grad,
        down_grad,
    )


def solution(mesh):
    rows = P("dp", None)
    acts = P("dp", "ctx", None)
    return jax.shard_map(
        body,
        mesh=mesh,
        in_specs=(acts, P("dp", "ctx"), acts, P("dp"), P("dp"), rows, rows, rows, rows, rows),
        out_specs=(acts, acts, P("dp"), P("dp"), rows, rows, rows, rows, rows),
        check_vma=False,
    )
```

```python
import functools

import jax
import jax.numpy as jnp
from jax import lax
from jax.experimental import pallas as pl
from jax.experimental.pallas import tpu as pltpu
from jax.sharding import PartitionSpec as P

D = 2048
HEAD_DIM = 64
TOK = 128
RING = 4
QDIM = 2048
KVDIM = 256
GROUP = 8
QZ = 512
MZ = 640
FZ = 1408
SPLIT = 1536
EPS = 1e-05
THETA = 10000.0
MESH = pl.DeviceIdType.MESH
VMEM_LIMIT = 60 << 20
BF = jnp.bfloat16
F32 = jnp.float32
ANY = pl.BlockSpec(memory_space=pl.ANY)
VMEM = pl.BlockSpec(memory_space=pltpu.VMEM)


def coords():
    dp, ctx = lax.axis_index("dp"), lax.axis_index("ctx")
    y, xh = dp // 2, dp % 2
    xl, z, c = ctx // 8, (ctx // 2) % 4, ctx % 2
    return dict(y=y, x=xh * 2 + xl, xh=xh, xl=xl, z=z, c=c)


def device(q, **change):
    r = {k: change.get(k, q[k]) for k in ("y", "x", "z", "c")}
    return (r["y"] * 2 + r["x"] // 2, (r["x"] % 2) * 8 + r["z"] * 2 + r["c"])


def ring(q, axis):
    return [device(q, **{axis: (q[axis] + s) % 4}) for s in (1, 3, 2)]


def shift_pairs(axis, by):
    size = 2 if axis == "c" else 4
    pairs = []
    for y in range(4):
        for x in range(4):
            for z in range(4):
                for c in range(2):
                    q = dict(y=y, x=x, z=z, c=c)
                    pairs.append((device(q), device(q, **{axis: (q[axis] + by) % size})))
    return [(a[0] * 16 + a[1], b[0] * 16 + b[1]) for a, b in pairs]


def swap_pairs():
    pairs = []
    for y in range(4):
        for x in range(4):
            for z in range(4):
                for c in range(2):
                    q = dict(y=y, x=x, z=z, c=c)
                    pairs.append((device(q), device(q, y=z, z=y)))
    return [(a[0] * 16 + a[1], b[0] * 16 + b[1]) for a, b in pairs]


def move(v, axis, by):
    return lax.ppermute(v, ("dp", "ctx"), shift_pairs(axis, by))


class Copies:
    def __init__(self, send_sems, recv_sems):
        self.send_sems, self.recv_sems, self.n, self.open = send_sems, recv_sems, 0, []

    def send(self, src, dst, to):
        cp = pltpu.make_async_remote_copy(
            src_ref=src,
            dst_ref=dst,
            send_sem=self.send_sems.at[self.n],
            recv_sem=self.recv_sems.at[self.n],
            device_id=to,
            device_id_type=MESH,
        )
        cp.start()
        self.n += 1
        self.open.append(cp)
        return cp

    def local(self, src, dst):
        cp = pltpu.make_async_copy(src, dst, self.send_sems.at[self.n])
        cp.start()
        self.n += 1
        return cp

    def close(self):
        for cp in self.open:
            cp.wait_send()
        self.open = []


def deal(k, q, src, col, dst):
    y, z = q["y"], q["z"]
    n = k.n
    k.n += 4
    copies = [
        pltpu.make_async_remote_copy(
            src_ref=src.at[:, col((y + s) % 4)],
            dst_ref=dst,
            send_sem=k.send_sems.at[n + i],
            recv_sem=k.recv_sems.at[n],
            device_id=to,
            device_id_type=MESH,
        )
        for i, (s, to) in enumerate(zip((1, 3, 2), ring(q, "y")))
    ]
    here = pltpu.make_async_copy(src.at[:, col(y)], dst, k.send_sems.at[n + 3])

    @pl.when(y == z)
    def _():
        for cp in copies:
            cp.start()
        here.start()

    def wait():
        @pl.when(y == z)
        def _():
            for cp in copies:
                cp.wait_send()
            here.wait()

        @pl.when(y != z)
        def _():
            copies[0].wait_recv()

    return wait


def greet(targets, q=None):
    barrier = pltpu.get_barrier_semaphore()
    for to in targets:
        pl.semaphore_signal(barrier, inc=1, device_id=to, device_id_type=MESH)
    if q is None:
        pl.semaphore_wait(barrier, len(targets))
    else:
        y, z = q["y"], q["z"]

        @pl.when(y != z)
        def _():
            to = device(q, y=z, z=y)
            pl.semaphore_signal(barrier, inc=1, device_id=to, device_id_type=MESH)

        pl.semaphore_wait(barrier, len(targets) + (y != z).astype(jnp.int32))


TOP, LOW = pl.ds(0, TOK // 2), pl.ds(TOK // 2, TOK // 2)
HALF = (TOK // 2, D)


class Gather:
    def __init__(self, k, q, axis, src, dst):
        at = q[axis]
        self.k, self.dst = k, dst
        self.above, self.below, self.far = (at + 1) % 4, (at + 3) % 4, (at + 2) % 4
        self.up, self.down = device(q, **{axis: self.above}), device(q, **{axis: self.below})
        self.low0 = k.send(src(0), dst(at, 0), self.up)
        self.top1 = k.send(src(1), dst(at, 1), self.down)
        self.low1 = k.send(src(1), dst(at, 1), self.up)
        self.top0 = k.send(src(0), dst(at, 0), self.down)

    def relay(self):
        self.low0.wait_recv()
        ref = self.dst(self.below, 0)
        self.far0 = self.k.send(ref, ref, self.up)
        self.top1.wait_recv()
        ref = self.dst(self.above, 1)
        self.far1 = self.k.send(ref, ref, self.down)

    def near(self):
        self.low1.wait_recv()
        self.top0.wait_recv()

    def end(self):
        self.far0.wait_recv()
        self.far1.wait_recv()


class Sum:
    def __init__(self, k, q, axis, block, below, above, passed):
        at = q[axis]
        self.k, self.below, self.above, self.passed = k, below, above, passed
        up, down, far = (at + 1) % 4, (at + 3) % 4, (at + 2) % 4
        self.up, self.down = device(q, **{axis: up}), device(q, **{axis: down})
        self.first = k.send(block(far, 0), passed[0], self.up)
        self.second = k.send(block(far, 1), passed[1], self.down)
        self.rest = [
            k.send(block(up, 1), below(1), self.up),
            k.send(block(down, 0), above(0), self.down),
        ]

    def relay(self, own0, own1, sent):
        self.first.wait_recv()
        sent[0][...] = (self.passed[0][...].astype(F32) + own0[...].astype(F32)).astype(BF)
        self.rest.append(self.k.send(sent[0], self.below(0), self.up))
        self.second.wait_recv()
        sent[1][...] = (self.passed[1][...].astype(F32) + own1[...].astype(F32)).astype(BF)
        self.rest.append(self.k.send(sent[1], self.above(1), self.down))

    def end(self):
        for cp in self.rest:
            cp.wait_recv()


def halves(ref):
    return lambda h: ref.at[(TOP, LOW)[h]]


def ring_halves(ref):
    return lambda j, h: ref.at[j, (TOP, LOW)[h]]


def turn(k, q, moves):
    y, z = q["y"], q["z"]
    swap = device(q, y=z, z=y)
    pairs = []
    for src, dst in moves:
        n = k.n
        k.n += 1
        remote = pltpu.make_async_remote_copy(
            src_ref=src,
            dst_ref=dst,
            send_sem=k.send_sems.at[n],
            recv_sem=k.recv_sems.at[n],
            device_id=swap,
            device_id_type=MESH,
        )
        pairs.append((remote, pltpu.make_async_copy(src, dst, k.send_sems.at[n])))

    @pl.when(y != z)
    def _():
        for remote, _ in pairs:
            remote.start()

    @pl.when(y == z)
    def _():
        for _, here in pairs:
            here.start()

    def wait():
        @pl.when(y != z)
        def _():
            for remote, _ in pairs:
                remote.wait_recv()
                remote.wait_send()

        @pl.when(y == z)
        def _():
            for _, here in pairs:
                here.wait()

    return wait


def cost(us):
    return pl.CostEstimate(flops=int(us * 1e9), bytes_accessed=0, transcendentals=0)


def talk(kernel, name, cid, us, copies, ins, outs, scratch=(), near=(), near_out=(), alias={}):
    return pl.pallas_call(
        kernel,
        name=name,
        out_shape=[jax.ShapeDtypeStruct(s, t) for s, t in outs],
        in_specs=[VMEM if i in near else ANY for i in range(len(ins))],
        out_specs=[VMEM if i in near_out else ANY for i in range(len(outs))],
        scratch_shapes=[
            *scratch,
            pltpu.SemaphoreType.DMA((copies,)),
            pltpu.SemaphoreType.DMA((copies,)),
        ],
        cost_estimate=cost(us),
        input_output_aliases=alias,
        compiler_params=pltpu.CompilerParams(
            collective_id=cid, has_side_effects=True, vmem_limit_bytes=VMEM_LIMIT
        ),
    )(*ins)


def front_kernel(
    x, g, seg, na, nf, freq, wq, wo, w1, w3, w2,
    G, WQ, WO, W13, T2, N1, Q, KV, COS, SIN, START, GA, GF,
    TO, TV, QP, KT, VT, P1, P3, SG, NG, SEGS, GN, XV, WV, NV, QV, KVV, ss, rs,
):
    q = coords()
    y, xx, xh, xl, z, c = q["y"], q["x"], q["xh"], q["xl"], q["z"], q["c"]
    zs, ys, xs = ring(q, "z"), ring(q, "y"), ring(q, "x")
    mate = device(q, c=1 - c)
    other = device(q, x=xx ^ 1)
    other_mate = device(q, x=xx ^ 1, c=1 - c)
    k = Copies(ss, rs)
    rows = pl.ds(pl.multiple_of(128 * c + 64 * xl, 64), 64)
    qcols = pl.ds(pl.multiple_of(QZ * z, 128), QZ)
    tile = 128 * (z // 2)
    kcols = pl.ds(pl.multiple_of(QDIM + tile, 128), 128)
    vcols = pl.ds(pl.multiple_of(QDIM + KVDIM + tile, 128), 128)
    fcols = pl.ds(pl.multiple_of(FZ * z, 128), FZ)
    loads = [
        k.local(wq.at[rows, qcols], QP.at[:, pl.ds(0, QZ)]),
        k.local(wq.at[rows, kcols], KT),
        k.local(wq.at[rows, vcols], VT),
        k.local(w1.at[rows, fcols], P1),
        k.local(w3.at[rows, fcols], P3),
    ]
    SG[...] = jnp.broadcast_to(seg[...], (8, TOK))
    NG[0:16] = jnp.broadcast_to(na[...].astype(F32), (16, 256)).astype(BF)
    NG[16:32] = jnp.broadcast_to(nf[...].astype(F32), (16, 256)).astype(BF)
    greet(zs + ys + xs + [mate, other_mate])
    seg_z = [k.send(SG, SEGS.at[xl, z, c], to) for to in zs]
    x_ring = Gather(k, q, "z", halves(x), ring_halves(XV))
    lanes = lambda j, n=1: pl.ds(pl.multiple_of(128 * j, 128 * n), 128 * n)
    dealt = deal(k, q, wo, lambda j: lanes(c * 8 + j * 2 + xl), TO)
    for cp in loads:
        cp.wait()
    odd = z % 2 == 1
    kt, vt = KT[...].astype(F32), VT[...].astype(F32)
    lane = lax.broadcasted_iota(jnp.int32, kt.shape, 1)
    kt = jnp.where(odd, pltpu.roll(kt, 64, 1), kt)
    vt = jnp.where(odd, vt, pltpu.roll(vt, 64, 1))
    QP[:, QZ:] = jnp.where(lane < HEAD_DIM, kt, vt).astype(BF)
    f1, f3 = pl.ds(0, FZ), pl.ds(FZ, FZ)
    top, low = pl.ds(0, 32), pl.ds(32, 32)
    thirty = lambda h: pl.ds(32 * h, 32)
    q_top = [k.send(QP.at[top], WV.at[c, y, xh, xl, top], to) for to in xs]
    q_low = [k.send(QP.at[low], WV.at[c, y, xh, xl, low], to) for to in ys]
    gn_y = [k.send(NG, GN.at[y, xh], to) for to in ys]
    up_y = Gather(
        k, q, "y", lambda h: P3.at[thirty(h)], lambda j, h: W13.at[c, j, xh, xl, thirty(h), f3]
    )
    gate_x = Gather(
        k, q, "x", lambda h: P1.at[thirty(h)],
        lambda j, h: W13.at[c, y, j // 2, j % 2, thirty(h), f1],
    )
    q_here = k.local(QP, WV.at[c, y, xh, xl])
    seg_here = k.local(SG, SEGS.at[xl, z, c])
    gn_here = k.local(NG, GN.at[y, xh])
    x_here = k.local(x, XV.at[z])
    up_here = k.local(P3, W13.at[c, y, xh, xl, :, f3])
    heres = [k.local(P1, W13.at[c, y, xh, xl, :, f1]), k.local(g, G.at[z])]
    dealt()
    o1 = [k.send(TO, WO.at[xh, :, lanes(c * 8 + y * 2 + xl)], to) for to in xs]
    o1_here = k.local(TO, WO.at[xh, :, lanes(c * 8 + y * 2 + xl)])
    for cp in seg_z:
        cp.wait_recv()
    seg_here.wait()
    part = SEGS.at[xl, :, c]
    seg2 = [k.send(part, part, to) for to in (mate, other, other_mate)]
    q_here.wait()
    for cp in q_top:
        cp.wait_recv()
    q_y = Gather(k, q, "y", lambda h: WV.at[c, y, h, :, top], lambda j, h: WV.at[c, j, h, :, top])
    for cp in gn_y:
        cp.wait_recv()
    gn_here.wait()
    gn2 = k.send(GN.at[:, xh], GN.at[:, xh], device(q, x=3 - xx))
    gate_x.relay()
    for cp in q_low:
        cp.wait_recv()
    q_half = lambda j, h: WV.at[c, pl.ds(2 * h, 2), j // 2, j % 2, low]
    q_x = Gather(k, q, "x", lambda h: q_half(xx, h), q_half)
    x_ring.relay()
    g_ring = Gather(k, q, "z", halves(g), ring_halves(G))
    up_y.relay()
    for cp in o1:
        cp.wait_recv()
    o1_here.wait()
    o_half = lambda j, h: WO.at[h, :, lanes(c * 8 + j * 2, 2)]
    o_y = Gather(k, q, "y", lambda h: o_half(y, h), o_half)
    for cp in seg2:
        cp.wait_recv()
    docs = [SEGS[i // 8, (i // 2) % 4, i % 2, 0:1].astype(F32) for i in range(16)]
    columns = jnp.concatenate(docs + [jnp.zeros((TOK - 16, TOK), F32)], axis=0).T
    for i in range(RING):
        mine = SEGS[xl, i, c, 0:1].astype(F32)
        count = jnp.zeros((TOK, TOK), F32)
        for j in range(16):
            count = count + jnp.where(columns[:, j : j + 1] < mine, 1.0, 0.0)
        first = jnp.sum(count, axis=0, keepdims=True)
        START[i] = first.astype(jnp.int32)
        index = TOK * (8 * xl + 2 * i + c) + lax.broadcasted_iota(jnp.int32, (1, TOK), 1)
        place = index.astype(F32) - first
        angle = jnp.broadcast_to(place, (TOK, TOK)).T * freq[...]
        COS[i] = jnp.cos(angle)
        sine = jnp.sin(angle)
        lane = lax.broadcasted_iota(jnp.int32, sine.shape, 1)
        SIN[i] = jnp.where(lane % 64 < 32, -sine, sine)
    q_y.relay()
    w2_dealt = deal(k, q, w2, lambda j: lanes(c * 8 + xl * 4 + j), TV)
    q_x.relay()
    up_y.near()
    up_y.end()
    up_here.wait()
    part = W13.at[c, :, xh, xl, :, f3]
    a3 = [k.send(part, part, to) for to in xs[:2]]
    o_y.relay()
    gn2.wait_recv()
    whole = lambda r: jnp.concatenate(
        [GN[d // 2, d % 2, r : r + 1].astype(F32) for d in range(8)], axis=1
    )
    gain = whole(0)
    GA[...] = gain
    GF[...] = whole(16)
    x_ring.near()
    x_ring.end()
    x_here.wait()
    for i in range(RING):
        xv = XV[i].astype(F32)
        scale = lax.rsqrt(jnp.mean(xv * xv, axis=-1, keepdims=True) + EPS)
        NV[i] = to_pieces((xv * scale * gain).astype(BF))
    done = [k.local(NV, N1)]
    for r in (q_y, q_x):
        r.near()
        r.end()
    q3 = k.send(WV.at[c], WV.at[c], mate)
    g_ring.relay()
    q3.wait_recv()
    done.append(k.local(WV, WQ))
    mixed = dot(NV[...].reshape(RING * TOK, D), WV[...].reshape(D, MZ))
    for i in range(RING):
        cos, sin = COS[i], SIN[i]
        for j in range(5):
            u = mixed[TOK * i : TOK * i + TOK, 128 * j : 128 * j + 128]
            turned = u * cos + swapped(u) * sin
            if j < 4:
                QV[i, :, 128 * j : 128 * j + 128] = turned.astype(BF)
            else:
                lane = lax.broadcasted_iota(jnp.int32, u.shape, 1)
                KVV[i] = jnp.where(lane < HEAD_DIM, turned, u).astype(BF)
    near = k.send(KVV, KV.at[xl, :, c], mate)
    n = k.n
    k.n += 2
    far, on = [
        pltpu.make_async_remote_copy(
            src_ref=src,
            dst_ref=KV.at[0, :, c],
            send_sem=ss.at[n + i],
            recv_sem=rs.at[n + i],
            device_id=to,
            device_id_type=MESH,
        )
        for i, (src, to) in enumerate(((KVV, other), (KV.at[0, :, c], mate)))
    ]

    @pl.when(xl == 0)
    def _():
        far.start()

    done += [k.local(KVV, KV.at[xl, :, c]), k.local(QV, Q)]
    o_y.near()
    o_y.end()
    part = WO.at[:, :, pl.ds(pl.multiple_of(1024 * c, 1024), 1024)]
    o3 = k.send(part, part, mate)
    w2_dealt()
    done.append(k.local(TV, T2))

    @pl.when(xl == 0)
    def _():
        far.wait_send()

    @pl.when(xl == 1)
    def _():
        far.wait_recv()
        on.start()
        on.wait_recv()
        on.wait_send()

    near.wait_recv()
    for cp in a3 + [o3]:
        cp.wait_recv()
    for cp in heres + done:
        cp.wait()
    for r in (gate_x, g_ring):
        r.near()
        r.end()
    k.close()


def core_kernel(
    o, x, gain, t2, w13, wo_in, G, V, FA, FB, F2, DO, OUT, DH, GAIN, *scratch
):
    (
        W, W2, N2, gv, hv, hT, bv, part, outs, wo, ov, vv, hf, xb,
        p0, p1, p2, p3, v0, v1, v2, v3, below, above, out_below, out_above, *rest_of,
    ) = scratch
    bufs, (used, ss, rs) = rest_of[:-3], rest_of[-3:]
    q = coords()
    y, xx, xh, xl, z, c = q["y"], q["x"], q["xh"], q["xl"], q["z"], q["c"]
    ys, xs = ring(q, "y"), ring(q, "x")
    up, down = device(q, z=(z + 1) % 4), device(q, z=(z + 3) % 4)
    mate = device(q, c=1 - c)
    k = Copies(ss, rs)
    f1, f3 = pl.ds(0, FZ), pl.ds(FZ, FZ)
    lower, higher = (xx + 3) % 4, (xx + 1) % 4
    gate_at = lambda ref, j: ref.at[c, j, :, :, :, f1]
    gate_half = lambda ref, j, h: ref.at[c, j, h, :, :, f1]
    up_at = lambda ref, j: ref.at[c, :, j // 2, j % 2, :, f3]
    up_half = lambda ref, j, h: ref.at[c, pl.ds(2 * h, 2), j // 2, j % 2, :, f3]
    get_wo, get_o = k.local(wo_in, wo), k.local(o, ov)
    loads = [k.local(x, xb), k.local(gate_at(w13, y), gate_at(W, y))]
    loads += [k.local(up_at(w13, j), up_at(W, j)) for j in (xx, lower, higher)]
    get_g = k.local(G, gv)
    greet(ys + xs + [up, down, mate])
    cols = lambda j, n: pl.ds(pl.multiple_of(128 * (8 * c + j), 128 * n), 128 * n)
    frows = lambda j, h: pl.ds(pl.multiple_of(704 * (j // 2) + 352 * h, 32), 352)
    w2_here = k.local(t2, W2.at[pl.ds(pl.multiple_of(704 * xh, 64), 704), cols(xl * 4 + y, 1)])
    w2y = Gather(
        k, q, "y", lambda h: t2.at[pl.ds(352 * h, 352)],
        lambda j, h: W2.at[frows(xx, h), cols(xl * 4 + j, 1)],
    )
    far = [
        k.send(up_half(w13, lower, 0), up_half(W, lower, 0), xs[0]),
        k.send(up_half(w13, higher, 1), up_half(W, higher, 1), xs[1]),
    ]
    sent = [k.send(up_at(w13, j), up_at(W, j), mate) for j in (xx, lower, higher)]
    get_wo.wait()
    get_o.wait()
    rows = RING * TOK
    part[...] = dot(ov[...].reshape(rows, QZ), wo[...]).astype(BF).reshape(RING, TOK, D)
    z_sum = Sum(k, q, "z", ring_halves(part), halves(below), halves(above), (p0, p1))
    w2y.relay()
    gate = Gather(
        k, q, "y", lambda h: gate_half(w13, y, h), lambda j, h: gate_half(W, j, h)
    )
    sent.append(k.send(gate_at(w13, y), gate_at(W, y), mate))
    w2_here.wait()
    w2y.near()
    w2y.end()
    down2 = lambda j: W2.at[
        pl.ds(pl.multiple_of(704 * (j // 2), 64), 704), cols((j % 2) * 4, 4)
    ]
    down_half = lambda j, h: W2.at[frows(j, h), cols((j % 2) * 4, 4)]
    down_ring = Gather(k, q, "x", lambda h: down_half(xx, h), down_half)
    sent.append(k.send(down2(xx), down2(xx), mate))
    z_sum.relay(part.at[(z + 1) % 4, TOP], part.at[(z + 3) % 4, LOW], (v0, v1))
    z_sum.end()
    for cp in loads:
        cp.wait()
    total = xb[...].astype(F32) + (
        part[z].astype(F32) + (below[...].astype(F32) + above[...].astype(F32))
    )
    hf[...] = total
    scale = lax.rsqrt(jnp.mean(total * total, axis=-1, keepdims=True) + EPS)
    N2[z] = to_pieces((total * scale * gain[...]).astype(BF))
    n2_ring = Gather(k, q, "z", halves(N2.at[z]), ring_halves(N2))
    gate.relay()
    down_ring.relay()
    for cp in far:
        cp.wait_recv()
    ref = up_at(W, (xx + 2) % 4)
    sent.append(k.send(ref, ref, mate))
    gate.near()
    for j in (gate.below, gate.above):
        sent.append(k.send(gate_at(W, j), gate_at(W, j), mate))
    down_ring.near()
    for j in (down_ring.below, down_ring.above):
        sent.append(k.send(down2(j), down2(j), mate))
    n2_ring.relay()
    gate.end()
    sent.append(k.send(gate_at(W, gate.far), gate_at(W, gate.far), mate))
    down_ring.end()
    sent.append(k.send(down2(down_ring.far), down2(down_ring.far), mate))
    get_g.wait()
    for cp in sent:
        cp.wait_recv()
    tiles = [(256 * i, min(256 * i + 256, FZ)) for i in range(6)]
    gs = gv[...].reshape(rows, D)
    for a, b in tiles:
        bv[:, a:b] = nt(gs, W2[a:b]).astype(BF)
    n2_ring.near()
    n2_ring.end()
    k.close()
    n2 = N2[...].reshape(rows, D)
    for a, b in tiles:
        gates = dot(n2, W[:, :, :, :, :, a:b].reshape(D, b - a))
        ups = dot(n2, W[:, :, :, :, :, FZ + a : FZ + b].reshape(D, b - a))
        sigma = jax.nn.sigmoid(gates)
        silu = gates * sigma
        hv[:, a:b] = (silu * ups).astype(BF)
        dhid = bv[:, a:b].astype(F32)
        bv[:, a:b] = (dhid * ups * sigma * (1.0 + gates * (1.0 - sigma))).astype(BF)
        bv[:, FZ + a : FZ + b] = (dhid * silu).astype(BF)
    for j in range(4):
        at = slice(512 * j, 512 * j + 512)
        outs[:, :, at] = dot(hv[...], W2[:, at]).astype(BF).reshape(RING, TOK, 512)
    out_sum = Sum(
        k, q, "z", ring_halves(outs), halves(out_below), halves(out_above), (p2, p3)
    )
    pl.semaphore_signal(used.at[0], inc=1, device_id=mate, device_id_type=MESH)
    half = lambda ref: lambda i: ref.at[i]
    rest = 2 * FZ - SPLIT
    jobs = [
        ("y", lambda j, i: W2.at[pl.ds(704 * i, 704), lanes(0, j)], F2),
        ("x", lambda j, i: W.at[0, pl.ds(2 * i, 2), j // 2, j % 2, :, pl.ds(0, SPLIT)], FA),
        ("y", lambda j, i: W.at[0, j, i, :, :, pl.ds(SPLIT, rest)], FB),
    ]
    sums, done = [], []
    lanes = lambda cc, j: pl.ds(pl.multiple_of(1024 * cc + 256 * j, 256), 256)

    def start(n):
        axis, block, _ = jobs[n]
        b = bufs[4 * n : 4 * n + 4]
        sums.append(Sum(k, q, axis, block, half(b[2]), half(b[3]), (b[0].at[0], b[0].at[1])))

    def relay(n):
        axis, block, _ = jobs[n]
        b = bufs[4 * n : 4 * n + 4]
        at = q[axis]
        sums[n].relay(block((at + 1) % 4, 0), block((at + 3) % 4, 1), (b[1].at[0], b[1].at[1]))

    def end(n):
        axis, block, out = jobs[n]
        b = bufs[4 * n : 4 * n + 4]
        sums[n].end()
        for i in range(2):
            total = block(q[axis], i)[...].astype(F32) + (
                b[2][i].astype(F32) + b[3][i].astype(F32)
            )
            b[2][i] = total.astype(BF)
        done.append(k.local(b[2], out))

    hT[...] = hv[...].T
    pl.semaphore_wait(used.at[0], 1)
    sent2, sent13 = [], []
    for j in range(4):
        W2[:, 1024 + 256 * j : 1280 + 256 * j] = dot(
            hT[...], gv[:, :, lanes(1 - c, j)].reshape(rows, 256)
        ).astype(BF)
        sent2.append(k.send(W2.at[:, lanes(1, j)], W2.at[:, lanes(0, j)], mate))
    for j in range(4):
        sent2[j].wait_recv()
        at = slice(256 * j, 256 * j + 256)
        own = dot(hT[...], gv[:, :, lanes(c, j)].reshape(rows, 256))
        W2[:, at] = (own + W2[:, at].astype(F32)).astype(BF)
    start(0)
    out_sum.relay(outs.at[(z + 1) % 4, TOP], outs.at[(z + 3) % 4, LOW], (v2, v3))
    for j in range(2):
        at = slice(1024 * j, 1024 * j + 1024)
        dn = nt(bv[...], W[j].reshape(1024, 2 * FZ))
        part[:, :, at] = dn.astype(BF).reshape(RING, TOK, 1024)
    z_sum = Sum(k, q, "z", ring_halves(part), halves(below), halves(above), (p0, p1))
    pl.semaphore_signal(used.at[1], inc=1, device_id=mate, device_id_type=MESH)
    pl.semaphore_wait(used.at[1], 1)
    shape = (2, 2, 64, 2 * FZ)
    for j in range(4):
        W[1, j] = tn(N2[:, :, lanes(1 - c, j)].reshape(rows, 256), bv[...]).astype(BF).reshape(shape)
        sent13.append(k.send(W.at[1, j], W.at[0, j], mate))
        if j == 0:
            relay(0)
    for j in range(4):
        sent13[j].wait_recv()
        own = tn(N2[:, :, lanes(c, j)].reshape(rows, 256), bv[...]).reshape(shape)
        W[0, j] = (own + W[0, j].astype(F32)).astype(BF)
        if j == 1:
            z_sum.relay(part.at[(z + 1) % 4, TOP], part.at[(z + 3) % 4, LOW], (v0, v1))
    start(1)
    start(2)
    end(0)
    z_sum.end()
    dn = from_pieces(
        part[z].astype(F32) + (below[...].astype(F32) + above[...].astype(F32))
    )
    back, gain_grad = rms_back(hf[...], gain[...], dn)
    total = gv[z].astype(F32) + back
    DH[...] = total
    GAIN[...] = gain_grad
    vv[z] = total.astype(BF)
    v_ring = Gather(k, q, "z", halves(vv.at[z]), ring_halves(vv))
    out_sum.end()
    OUT[...] = hf[...] + (
        outs[z].astype(F32) + (out_below[...].astype(F32) + out_above[...].astype(F32))
    )
    relay(1)
    relay(2)
    v_ring.relay()
    end(2)
    v_ring.near()
    v_ring.end()
    done.append(k.local(vv, V))
    DO[...] = nt(vv[...].reshape(rows, D), wo[...]).astype(BF)
    end(1)
    for cp in done:
        cp.wait()
    k.close()


def quarter(xt, rows):
    return (
        pl.ds(pl.multiple_of((xt // 2) * rows, rows), rows),
        pl.ds(pl.multiple_of((xt % 2) * 128, 128), 128),
    )


def tail_kernel(
    dkv, dq, cosine, sine, x, dh, gain, gain2, fa, fb, f2, wq, n1, o, dho,
    IG, G1, G3, G2, GO, GQ, GKV, gain_out, *scratch,
):
    (
        wv, nv, ov, gv, R, dm, dn, p0, p1, v0, v1, below, above, mate_o, sum_o, mate_q, sum_q,
        ob0, ob1, ob2, ob3, qb0, qb1, qb2, qb3, la, lb, l2, pa, pb, p2, t2, lo, lq, fo, fq,
        po, pq, to_, gains, s0, s1, s2, s3, s4, total, ss, rs,
    ) = scratch
    q = coords()
    y, xx, xh, xl, z, c = q["y"], q["x"], q["xh"], q["xl"], q["z"], q["c"]
    zs, ys, xs = ring(q, "z"), ring(q, "y"), ring(q, "x")
    mate, other, cross = device(q, c=1 - c), device(q, x=xx ^ 1), device(q, x=3 - xx)
    other_mate = device(q, x=xx ^ 1, c=1 - c)
    steps = (1, 3, 2)
    k = Copies(ss, rs)
    get_o, get_g = k.local(o, ov), k.local(dho, gv)
    get_w, get_n = k.local(wq, wv), k.local(n1, nv)
    greet(zs + ys + xs + [mate, other_mate], q)
    near = k.send(dkv.at[xl, :, 1 - c], R.at[0], mate)
    n = k.n
    k.n += 2
    pre, far = [
        pltpu.make_async_remote_copy(
            src_ref=src,
            dst_ref=dst,
            send_sem=ss.at[n + i],
            recv_sem=rs.at[n + i],
            device_id=to,
            device_id_type=MESH,
        )
        for i, (src, dst, to) in enumerate(
            ((dkv.at[0, :, 1 - c], R.at[1], mate), (R.at[2], R.at[3], other))
        )
    ]

    @pl.when(xl == 1)
    def _():
        pre.start()

    leg_2 = []
    for i, s in enumerate(steps):
        r, cc = quarter((xx + s) % 4, 704)
        leg_2.append(k.send(f2.at[r, cc], l2.at[i], xs[i]))
    leg_a = [k.send(fa.at[(y + s) % 4], la.at[i], ys[i]) for i, s in enumerate(steps)]
    leg_b = [k.send(fb.at[(xx + s) % 4], lb.at[i], xs[i]) for i, s in enumerate(steps)]
    lanes = lambda cc, j: pl.ds(pl.multiple_of(1024 * cc + 256 * j, 256), 256)
    get_o.wait()
    get_g.wait()
    swaps = []
    for j in range(4):
        mate_o[j] = tn(ov[...], gv[:, lanes(1 - c, j)]).astype(BF)
        swaps.append(k.send(mate_o.at[j], sum_o.at[j], mate))

    @pl.when(xl == 1)
    def _():
        R[3] = jnp.zeros(R.shape[1:], BF)
        pre.wait()
        for i in range(RING):
            R[2, i] = (dkv[0, i, c].astype(F32) + R[1, i].astype(F32)).astype(BF)
        far.start()

    for j in range(4):
        swaps[j].wait_recv()
        sum_o[j] = (tn(ov[...], gv[:, lanes(c, j)]) + sum_o[j].astype(F32)).astype(BF)
    half = lambda ref: lambda h: ref.at[h]
    o_block = lambda j, h: sum_o.at[j, pl.ds(256 * h, 256)]
    q_block = lambda j, h: sum_q.at[j, pl.ds(2 * h, 2)]
    o_sum = Sum(k, q, "y", o_block, half(ob2), half(ob3), (ob0.at[0], ob0.at[1]))
    for cp in leg_2:
        cp.wait_recv()
    r, cc = quarter(xx, 704)
    p2[...] = add4(f2[r, cc], l2[0], l2[1], l2[2])
    turned = turn(k, q, [(p2, t2)])
    at = lambda zz, off, n: pl.ds(pl.multiple_of(FZ * zz + off, 128), n)
    rows = pl.ds(pl.multiple_of(128 * c + 64 * xl, 64), 64)
    pair = pl.ds(pl.multiple_of(128 * c, 128), 128)
    f1 = pl.ds(0, FZ)
    rest = SPLIT - FZ
    quarter_rows = lambda h: pl.ds(pl.multiple_of(128 * c + 64 * xl + 32 * h, 32), 32)

    def over_z(src, ref, off, n):
        return Gather(
            k, q, "z", lambda h: src.at[pl.ds(32 * h, 32)],
            lambda j, h: ref.at[quarter_rows(h), at(j, off, n)],
        )

    spans = [(G1, 0, FZ), (G3, 0, rest), (G3, rest, FZ - rest)]
    pieces = [pa.at[:, f1], pa.at[:, pl.ds(FZ, rest)], pb]
    block = lambda i, j: spans[i][0].at[rows, at(j, spans[i][1], spans[i][2])]
    for cp in leg_a:
        cp.wait_recv()
    pa[...] = add4(fa[y], la[0], la[1], la[2])
    rings = [over_z(pieces[i], *spans[i]) for i in range(2)]
    to_x = [k.send(pieces[i], block(i, z), other) for i in range(2)]
    for cp in leg_b:
        cp.wait_recv()
    pb[...] = add4(fb[xx], lb[0], lb[1], lb[2])
    rings.append(over_z(pieces[2], *spans[2]))
    to_x.append(k.send(pieces[2], block(2, z), other))
    heres = [k.local(pieces[i], block(i, z)) for i in range(3)]
    o_sum.relay(o_block((y + 1) % 4, 0), o_block((y + 3) % 4, 1), (ob1.at[0], ob1.at[1]))

    @pl.when(xl == 1)
    def _():
        far.wait_send()

    @pl.when(xl == 0)
    def _():
        far.wait_recv()

    near.wait_recv()
    for i in range(RING):
        part = slice(TOK * i, TOK * i + TOK)
        w = dkv[xl, i, c].astype(F32) + (R[0, i].astype(F32) + R[3, i].astype(F32))
        lane = lax.broadcasted_iota(jnp.int32, w.shape, 1)
        dm[part, :QZ] = dq[i]
        dm[part, QZ:] = jnp.where(
            lane < HEAD_DIM, w * cosine[i] - swapped(w) * sine[i], w
        ).astype(BF)
    get_w.wait()
    dn[...] = nt(dm[...], wv[...]).astype(BF).reshape(RING, TOK, D)
    z_sum = Sum(k, q, "z", ring_halves(dn), halves(below), halves(above), (p0, p1))
    get_n.wait()
    cols = lambda cc: pl.ds(pl.multiple_of(1024 * cc, 1024), 1024)
    shape = (4, 4, 64, MZ)
    mate_q[...] = tn(nv[:, cols(1 - c)], dm[...]).astype(BF).reshape(shape)
    swap = k.send(mate_q, sum_q, mate)

    def onward(i):
        rings[i].near()
        for j in (rings[i].below, rings[i].above):
            to_x.append(k.send(block(i, j), block(i, j), other))

    rings[0].relay()
    onward(0)
    rings[1].relay()
    onward(1)
    swap.wait_recv()
    own = tn(nv[:, cols(c)], dm[...]).reshape(shape)
    sum_q[...] = (own + sum_q[...].astype(F32)).astype(BF)
    q_sum = Sum(k, q, "y", q_block, half(qb2), half(qb3), (qb0.at[0], qb0.at[1]))
    rings[2].relay()
    turned()
    col = pl.ds(pl.multiple_of(128 * (c * 8 + z * 2 + xl), 128), 128)
    down_x = k.send(t2, G2.at[:, col], other)
    down_here = k.local(t2, G2.at[:, col])
    onward(2)
    o_sum.end()
    for h in range(2):
        part = o_block(y, h)[...].astype(F32) + (ob2[h].astype(F32) + ob3[h].astype(F32))
        fo[pl.ds(256 * h, 256)] = part.astype(BF)
    leg_o, leg_q = [], []
    for i, s in enumerate(steps):
        r, cc = quarter((xx + s) % 4, 256)
        leg_o.append(k.send(fo.at[r, cc], lo.at[i], xs[i]))
    q_sum.relay(q_block((y + 1) % 4, 0), q_block((y + 3) % 4, 1), (qb1.at[0], qb1.at[1]))
    z_sum.relay(dn.at[(z + 1) % 4, TOP], dn.at[(z + 3) % 4, LOW], (v0, v1))
    q_sum.end()
    for h in range(2):
        part = q_block(y, h)[...].astype(F32) + (qb2[h].astype(F32) + qb3[h].astype(F32))
        fq[pl.ds(2 * h, 2)] = part.astype(BF)
    for i, s in enumerate(steps):
        leg_q.append(k.send(fq.at[(xx + s) % 4], lq.at[i], xs[i]))
    rings[0].end()
    to_x.append(k.send(block(0, rings[0].far), block(0, rings[0].far), other))
    down_x.wait_recv()
    down_here.wait()
    down_half = lambda j, h: G2.at[
        pl.ds(352 * h, 352), pl.ds(pl.multiple_of(128 * (c * 8 + j * 2), 256), 256)
    ]
    down_ring = Gather(k, q, "z", lambda h: down_half(z, h), down_half)
    for i in (1, 2):
        rings[i].end()
        to_x.append(k.send(block(i, rings[i].far), block(i, rings[i].far), other))
    z_sum.end()
    back, gain1 = rms_back(
        x[...].astype(F32),
        gain[...],
        from_pieces(dn[z].astype(F32) + (below[...].astype(F32) + above[...].astype(F32))),
    )
    IG[...] = dh[...] + back
    gains[...] = jnp.zeros_like(gains)
    for d in range(8):
        gains[d // 2, d % 2, 0:1] = gain1[:, 256 * d : 256 * d + 256]
        gains[d // 2, d % 2, 1:2] = gain2[:, 256 * d : 256 * d + 256]
    gain_y = [k.send(gains.at[(y + s) % 4], s0.at[y], ys[i]) for i, s in enumerate(steps)]
    gain_here = k.local(gains.at[y], s0.at[y])
    for cp in leg_o:
        cp.wait_recv()
    r, cc = quarter(xx, 256)
    po[...] = add4(fo[r, cc], lo[0], lo[1], lo[2])
    o_turned = turn(k, q, [(po, to_)])
    down_ring.relay()
    for cp in leg_q:
        cp.wait_recv()
    pq[...] = add4(fq[xx], lq[0], lq[1], lq[2])
    qc = lambda j: pl.ds(pl.multiple_of(QZ * j, 128), QZ)
    kc = lambda j: pl.ds(pl.multiple_of(128 * j, 128), 128)
    q_pieces = [
        (pq.at[:, pl.ds(0, QZ)], GQ.at[rows, qc(z)]),
        (pq.at[:, pl.ds(QZ, 128)], GKV.at[rows, kc(z)]),
    ]
    q_x = [k.send(src, dst, other) for src, dst in q_pieces]
    q_here = [k.local(src, dst) for src, dst in q_pieces]
    for cp in gain_y:
        cp.wait_recv()
    gain_here.wait()
    s1[0] = (s0[0] + s0[1]) + (s0[2] + s0[3])
    gain_x = k.send(s1.at[0, 1 - xh], s1.at[1, 0], cross)
    gain_x.wait_recv()
    s2[z] = s1[0, xh] + s1[1, 0]
    gain_z = [k.send(s2.at[z], s2.at[z], to) for to in zs]
    o_turned()
    o_x = k.send(to_, GO.at[:, col], other)
    o_here = k.local(to_, GO.at[:, col])
    for cp in to_x:
        cp.wait_recv()
    for cp in heres:
        cp.wait()
    last = [k.send(ref.at[pair], ref.at[pair], mate) for ref in (G1, G3)]
    for cp in q_x:
        cp.wait_recv()
    for cp in q_here:
        cp.wait()
    half_rows = lambda h: pl.ds(pl.multiple_of(128 * c + 64 * h, 64), 64)
    q_half = lambda j, h: GQ.at[half_rows(h), qc(j)]
    kv_half = lambda j, h: GKV.at[half_rows(h), kc(j)]
    last_rings = [
        Gather(k, q, "z", lambda h: q_half(z, h), q_half),
        Gather(k, q, "z", lambda h: kv_half(z, h), kv_half),
    ]
    down_ring.near()
    down_ring.end()
    last.append(k.send(G2.at[:, cols(c)], G2.at[:, cols(c)], mate))
    o_x.wait_recv()
    o_here.wait()
    o_half = lambda j, h: GO.at[
        pl.ds(128 * h, 128), pl.ds(pl.multiple_of(128 * (c * 8 + j * 2), 256), 256)
    ]
    last_rings.append(Gather(k, q, "z", lambda h: o_half(z, h), o_half))
    for cp in gain_z:
        cp.wait_recv()
    s3[0] = (s2[0] + s2[1]) + (s2[2] + s2[3])
    gain_x = k.send(s3.at[0], s3.at[1], other)
    last_rings[0].relay()
    last_rings[1].relay()
    gain_x.wait_recv()
    s4[0] = s3[0] + s3[1]
    gain_c = k.send(s4.at[0], s4.at[1], mate)
    last_rings[2].relay()
    for r in last_rings:
        r.near()
        r.end()
    refs = [GQ.at[pair], GKV.at[pair], GO.at[:, cols(c)]]
    last += [k.send(ref, ref, mate) for ref in refs]
    gain_c.wait_recv()
    total[...] = s4[0] + s4[1]
    gain_done = k.local(total, gain_out)
    for cp in last:
        cp.wait_recv()
    gain_done.wait()
    k.close()


PARAMS = pltpu.CompilerParams(vmem_limit_bytes=VMEM_LIMIT)


def add4(a, b, c, d):
    a, b, c, d = (v.astype(F32) for v in (a, b, c, d))
    return ((a + b) + (c + d)).astype(BF)


def to_pieces(v):
    return jnp.concatenate(
        [v[:, 256 * d + 128 * c : 256 * d + 128 * c + 128] for c in range(2) for d in range(8)],
        axis=1,
    )


def from_pieces(v):
    return jnp.concatenate(
        [v[:, 1024 * c + 128 * d : 1024 * c + 128 * d + 128] for d in range(8) for c in range(2)],
        axis=1,
    )


def swapped(u):
    lane = lax.broadcasted_iota(jnp.int32, u.shape, 1)
    return jnp.where(lane % 64 < 32, pltpu.roll(u, 96, 1), pltpu.roll(u, 32, 1))


def stacked_low(tiles):
    out = []
    for pair in range(4):
        tile = tiles[:, 128 * pair : 128 * pair + 128].astype(F32)
        lane = lax.broadcasted_iota(jnp.int32, tile.shape, 1)
        out.append(jnp.where(lane < HEAD_DIM, tile, 0.0))
        out.append(jnp.where(lane < HEAD_DIM, pltpu.roll(tile, 64, 1), 0.0))
    return jnp.concatenate(out, axis=0)


def stacked_high(tiles):
    out = []
    for pair in range(4):
        tile = tiles[:, 128 * pair : 128 * pair + 128].astype(F32)
        lane = lax.broadcasted_iota(jnp.int32, tile.shape, 1)
        out.append(jnp.where(lane >= HEAD_DIM, pltpu.roll(tile, 64, 1), 0.0))
        out.append(jnp.where(lane >= HEAD_DIM, tile, 0.0))
    return jnp.concatenate(out, axis=0)


def unstacked(v):
    tiles = []
    for pair in range(4):
        both = jnp.concatenate(
            [v[:, 256 * pair : 256 * pair + 128], v[:, 256 * pair + 128 : 256 * pair + 256]],
            axis=0,
        )
        tiles.append(both.T)
    return tiles


def nt(a, b):
    return lax.dot_general(a, b, (((1,), (1,)), ((), ())), preferred_element_type=F32)


def tn(a, b):
    return lax.dot_general(a, b, (((0,), (0,)), ((), ())), preferred_element_type=F32)


def own_chunk(i):
    ctx = lax.axis_index("ctx")
    return (ctx // 8) * 8 + 2 * i + ctx % 2


def over_chunks(start, chunk, step, carry):
    first = start.astype(F32)
    low = jnp.min(first).astype(jnp.int32) // TOK
    high = jnp.minimum((jnp.max(first).astype(jnp.int32) + TOK - 1) // TOK, chunk)
    carry = lax.fori_loop(low, high, lambda kc, cr: step(kc, 1, True, cr), carry)
    pairs = (chunk - high) // 2
    carry = lax.fori_loop(0, pairs, lambda n, cr: step(high + 2 * n, 2, False, cr), carry)
    carry = lax.fori_loop(
        high + 2 * pairs, chunk, lambda kc, cr: step(kc, 1, False, cr), carry
    )
    return step(chunk, 1, True, carry)


def chunk_scores(keys, stacked, kc, chunk, starts, masked):
    raw = nt(keys, stacked)
    if not masked:
        return raw
    key = kc * TOK + lax.broadcasted_iota(jnp.int32, raw.shape, 0)
    query = chunk * TOK + lax.broadcasted_iota(jnp.int32, raw.shape, 1) % TOK
    return jnp.where((key <= query) & (key >= starts), raw, -1e30)


def attend_kernel(query, kv, start, out, logsum):
    chunk = own_chunk(pl.program_id(0))
    stacked = (stacked_low(query[0]) * (1.0 / HEAD_DIM**0.5)).astype(BF)
    starts = jnp.concatenate([start[0]] * GROUP, axis=1)

    def step(kc, size, masked, carry):
        top, summed, total = carry
        keys = kv[pl.ds(kc, size)].reshape(size * TOK, 128)
        scores = chunk_scores(keys, stacked, kc, chunk, starts, masked)
        new_top = jnp.maximum(top, jnp.max(scores, axis=0, keepdims=True))
        weights = jnp.exp(scores - new_top)
        fade = jnp.exp(top - new_top)
        summed = summed * fade + jnp.sum(weights, axis=0, keepdims=True)
        part = tn(keys, weights.astype(BF))
        return new_top, summed, total * fade + part[HEAD_DIM:]

    rows = GROUP * TOK
    carry = (jnp.full((1, rows), -1e30, F32), jnp.zeros((1, rows), F32), jnp.zeros((64, rows), F32))
    top, summed, total = over_chunks(start[0], chunk, step, carry)
    for pair, tile in enumerate(unstacked(total / summed)):
        out[0, :, 128 * pair : 128 * pair + 128] = tile.astype(BF)
    logsum[0] = top + jnp.log(summed)


def attend(query, kv, start):
    chunk = lambda r, cols: pl.BlockSpec((1, r, cols), lambda i: (i, 0, 0))
    return pl.pallas_call(
        attend_kernel,
        name="attend",
        cost_estimate=cost(12),
        grid=(RING,),
        in_specs=[
            chunk(TOK, QZ),
            pl.BlockSpec((16, TOK, 128), lambda i: (0, 0, 0)),
            chunk(1, TOK),
        ],
        out_specs=[chunk(TOK, QZ), chunk(1, GROUP * TOK)],
        out_shape=[
            jax.ShapeDtypeStruct((RING, TOK, QZ), BF),
            jax.ShapeDtypeStruct((RING, 1, GROUP * TOK), F32),
        ],
        compiler_params=PARAMS,
    )(query, kv, start)


def attend_back_kernel(
    query, kv, start, out, grad_out, logsum, cosine, sine, dquery, dkv, total
):
    i = pl.program_id(0)
    chunk = own_chunk(i)
    stacked = (stacked_low(query[0]) * (1.0 / HEAD_DIM**0.5)).astype(BF)
    grads = stacked_high(grad_out[0]).astype(BF)
    starts = jnp.concatenate([start[0]] * GROUP, axis=1)
    lse = logsum[0]
    deltas = []
    for pair in range(4):
        cols = slice(128 * pair, 128 * pair + 128)
        prod = (out[0, :, cols].astype(F32) * grad_out[0, :, cols].astype(F32)).T
        deltas.append(jnp.sum(prod[:HEAD_DIM], axis=0, keepdims=True))
        deltas.append(jnp.sum(prod[HEAD_DIM:], axis=0, keepdims=True))
    delta = jnp.concatenate(deltas, axis=1)

    @pl.when(i == 0)
    def _():
        total[...] = jnp.zeros_like(total)

    def step(kc, size, masked, dq):
        keys = kv[pl.ds(kc, size)].reshape(size * TOK, 128)
        scores = chunk_scores(keys, stacked, kc, chunk, starts, masked)
        probs = jnp.exp(scores - lse)
        grad_probs = nt(keys, grads)
        grad_scores = (probs * (grad_probs - delta)).astype(BF)
        part = dot(grad_scores, stacked) + dot(probs.astype(BF), grads)
        total[pl.ds(kc, size)] += part.reshape(size, TOK, 128)
        return dq + tn(keys, grad_scores)[:HEAD_DIM]

    dq = over_chunks(start[0], chunk, step, jnp.zeros((64, GROUP * TOK), F32))
    cos, sin = cosine[0], sine[0]
    for pair, tile in enumerate(unstacked(dq)):
        tile = tile * (1.0 / HEAD_DIM**0.5)
        dquery[0, :, 128 * pair : 128 * pair + 128] = (tile * cos - swapped(tile) * sin).astype(BF)

    @pl.when(i == RING - 1)
    def _():
        dkv[...] = total[...].astype(BF)


def attend_back(query, kv, start, out, grad_out, logsum, cosine, sine):
    chunk = lambda r, cols: pl.BlockSpec((1, r, cols), lambda i: (i, 0, 0))
    whole = pl.BlockSpec((16, TOK, 128), lambda i: (0, 0, 0))
    return pl.pallas_call(
        attend_back_kernel,
        name="attend_back",
        cost_estimate=cost(15),
        grid=(RING,),
        in_specs=[
            chunk(TOK, QZ),
            whole,
            chunk(1, TOK),
            chunk(TOK, QZ),
            chunk(TOK, QZ),
            chunk(1, GROUP * TOK),
            chunk(TOK, 128),
            chunk(TOK, 128),
        ],
        out_specs=[chunk(TOK, QZ), whole],
        scratch_shapes=[pltpu.VMEM((16, TOK, 128), F32)],
        out_shape=[
            jax.ShapeDtypeStruct((RING, TOK, QZ), BF),
            jax.ShapeDtypeStruct((16, TOK, 128), BF),
        ],
        compiler_params=PARAMS,
    )(query, kv, start, out, grad_out, logsum, cosine, sine)


def rms_back(v, gain, grad):
    scale = lax.rsqrt(jnp.mean(v * v, axis=-1, keepdims=True) + EPS)
    unit = v * scale
    gain_grad = jnp.sum(grad * unit, axis=0, keepdims=True)
    inner = grad * gain
    return scale * (inner - unit * jnp.mean(inner * unit, axis=-1, keepdims=True)), gain_grad


def finish_kernel(a, b, g1, g3, g2, go, gq, gkv, out, grad, gate, up, down, proj, qkv):
    out[...] = a[...]
    grad[...] = b[...]
    for src, dst in ((g1, gate), (g3, up), (g2, down), (go, proj)):
        dst[...] = src[...].astype(F32)
    qkv[:, :QDIM] = gq[...].astype(F32)
    kv = gkv[...].astype(F32)
    tiles = [kv[:, 128 * j : 128 * j + 128] for j in range(4)]
    lane = lax.broadcasted_iota(jnp.int32, tiles[0].shape, 1)
    for j in range(2):
        one, two = tiles[2 * j], tiles[2 * j + 1]
        keys = jnp.where(lane < HEAD_DIM, one, pltpu.roll(two, 64, 1))
        values = jnp.where(lane < HEAD_DIM, pltpu.roll(one, 64, 1), two)
        qkv[:, QDIM + 128 * j : QDIM + 128 * j + 128] = keys
        qkv[:, QDIM + KVDIM + 128 * j : QDIM + KVDIM + 128 * j + 128] = values


def finish(*arrays):
    steps = 4
    spec = lambda v: pl.BlockSpec((v.shape[0] // steps, v.shape[1]), lambda i: (i, 0))
    outs = [jax.ShapeDtypeStruct(v.shape, F32) for v in arrays[:-2]]
    outs.append(jax.ShapeDtypeStruct((256, QDIM + 2 * KVDIM), F32))
    return pl.pallas_call(
        finish_kernel,
        name="finish",
        cost_estimate=cost(12),
        grid=(steps,),
        in_specs=[spec(v) for v in arrays],
        out_specs=[spec(v) for v in outs],
        out_shape=outs,
        compiler_params=PARAMS,
    )(*arrays)


def pick(v, index, axis=0):
    return lax.dynamic_index_in_dim(v, index, axis, keepdims=False)


def dot(a, b):
    return jnp.dot(a, b, preferred_element_type=F32)


def body(tokens, segments, cotangent, norm_attn, norm_ffn, wqkv, wo, w1, w3, w2):
    q = coords()
    y, xx, xl, z, c = q["y"], q["x"], q["xl"], q["z"], q["c"]
    x = tokens[0]
    g = cotangent[0]
    lane = jnp.arange(128)
    freq = THETA ** (-(lane % 32).astype(F32) * 2.0 / HEAD_DIM)
    table = ((RING, TOK, 128), F32)
    G, WQ, WO, W13, t2, n1, query, KV, cosine, sine, start, gain_attn, gain_ffn = talk(
        front_kernel,
        "front",
        1,
        46,
        120,
        (
            x, g, segments, norm_attn[None], norm_ffn[None], freq[None],
            wqkv, wo, w1, w3, w2,
        ),
        [
            ((RING, TOK, D), BF),
            ((2, 4, 2, 2, 64, MZ), BF),
            ((2, 256, D), BF),
            ((2, 4, 2, 2, 64, 2 * FZ), BF),
            ((704, 128), BF),
            ((RING, TOK, D), BF),
            ((RING, TOK, QZ), BF),
            ((2, 4, 2, TOK, 128), BF),
            table,
            table,
            ((RING, 1, TOK), jnp.int32),
            ((1, D), F32),
            ((1, D), F32),
        ],
        scratch=[
            pltpu.VMEM((256, 128), BF),
            pltpu.VMEM((704, 128), BF),
            pltpu.VMEM((64, MZ), BF),
            pltpu.VMEM((64, 128), BF),
            pltpu.VMEM((64, 128), BF),
            pltpu.VMEM((64, FZ), BF),
            pltpu.VMEM((64, FZ), BF),
            pltpu.VMEM((8, TOK), jnp.int32),
            pltpu.VMEM((32, 256), BF),
            pltpu.VMEM((2, 4, 2, 8, TOK), jnp.int32),
            pltpu.VMEM((4, 2, 32, 256), BF),
            pltpu.VMEM((RING, TOK, D), BF),
            pltpu.VMEM((2, 4, 2, 2, 64, MZ), BF),
            pltpu.VMEM((RING, TOK, D), BF),
            pltpu.VMEM((RING, TOK, QZ), BF),
            pltpu.VMEM((RING, TOK, 128), BF),
        ],
        near=tuple(range(6)),
        near_out=(8, 9, 10, 11, 12),
    )
    WQ = WQ.reshape(D, MZ)
    WO = WO.reshape(QZ, D)
    KV = KV.reshape(16, TOK, 128)
    heads_out, logsum = attend(query, KV, start)
    o = heads_out.reshape(RING * TOK, QZ)
    rest = 2 * FZ - SPLIT
    buffers = []
    for shape in ((704, 256), (2, 64, SPLIT), (2, 64, rest)):
        buffers += [pltpu.VMEM((2,) + shape, BF)] * 4
    chunks = pltpu.VMEM((RING, TOK, D), BF)
    DH, fa, fb, f2, dheads, output, dh, gain2 = talk(
        core_kernel,
        "core",
        3,
        120,
        150,
        (heads_out, x, gain_ffn, t2, W13, WO, G),
        [
            ((RING, TOK, D), BF),
            ((2, 2, 64, SPLIT), BF),
            ((2, 2, 64, rest), BF),
            ((2, 704, 256), BF),
            ((RING * TOK, QZ), BF),
            ((TOK, D), F32),
            ((TOK, D), F32),
            ((1, D), F32),
        ],
        scratch=[
            pltpu.VMEM((2, 4, 2, 2, 64, 2 * FZ), BF),
            pltpu.VMEM((FZ, D), BF),
            chunks,
            chunks,
            pltpu.VMEM((RING * TOK, FZ), BF),
            pltpu.VMEM((FZ, RING * TOK), BF),
            pltpu.VMEM((RING * TOK, 2 * FZ), BF),
            chunks,
            chunks,
            pltpu.VMEM((QZ, D), BF),
            pltpu.VMEM((RING, TOK, QZ), BF),
            chunks,
            pltpu.VMEM((TOK, D), F32),
            pltpu.VMEM((TOK, D), BF),
            *[pltpu.VMEM(HALF, BF)] * 8,
            *[pltpu.VMEM((TOK, D), BF)] * 4,
            *buffers,
            pltpu.SemaphoreType.REGULAR((2,)),
        ],
        near=(2,),
        near_out=(4, 5, 6, 7),
    )
    fa, fb = fa.reshape(4, 64, SPLIT), fb.reshape(4, 64, rest)
    f2 = f2.reshape(1408, 256)
    DH = DH.reshape(RING * TOK, D)
    dquery, dkv = attend_back(
        query, KV, start, heads_out, dheads.reshape(RING, TOK, QZ), logsum, cosine, sine
    )
    small = (8, 256)
    input_grad, G1, G3, G2, GO, GQ, GKV, gain_out = talk(
        tail_kernel,
        "tail",
        6,
        75,
        170,
        (
            dkv.reshape(2, 4, 2, TOK, 128), dquery, cosine, sine, x, dh, gain_attn, gain2,
            fa, fb, f2, WQ, n1.reshape(RING * TOK, D), o, DH,
        ),
        [
            ((TOK, D), F32),
            ((256, 4 * FZ), BF),
            ((256, 4 * FZ), BF),
            ((704, D), BF),
            ((256, D), BF),
            ((256, QDIM), BF),
            ((256, 2 * KVDIM), BF),
            (small, F32),
        ],
        scratch=[
            pltpu.VMEM((D, MZ), BF),
            pltpu.VMEM((RING * TOK, D), BF),
            pltpu.VMEM((RING * TOK, QZ), BF),
            pltpu.VMEM((RING * TOK, D), BF),
            pltpu.VMEM((4, RING, TOK, 128), BF),
            pltpu.VMEM((RING * TOK, MZ), BF),
            pltpu.VMEM((RING, TOK, D), BF),
            *[pltpu.VMEM(HALF, BF)] * 4,
            *[pltpu.VMEM((TOK, D), BF)] * 2,
            *[pltpu.VMEM((4, QZ, 256), BF)] * 2,
            *[pltpu.VMEM((4, 4, 64, MZ), BF)] * 2,
            *[pltpu.VMEM((2, 256, 256), BF)] * 4,
            *[pltpu.VMEM((2, 2, 64, MZ), BF)] * 4,
            pltpu.VMEM((3, 64, SPLIT), BF),
            pltpu.VMEM((3, 64, rest), BF),
            pltpu.VMEM((3, 704, 128), BF),
            pltpu.VMEM((64, SPLIT), BF),
            pltpu.VMEM((64, rest), BF),
            pltpu.VMEM((704, 128), BF),
            pltpu.VMEM((704, 128), BF),
            pltpu.VMEM((3, 256, 128), BF),
            pltpu.VMEM((3, 64, MZ), BF),
            pltpu.VMEM((512, 256), BF),
            pltpu.VMEM((4, 64, MZ), BF),
            pltpu.VMEM((256, 128), BF),
            pltpu.VMEM((64, MZ), BF),
            pltpu.VMEM((256, 128), BF),
            pltpu.VMEM((4, 2) + small, F32),
            pltpu.VMEM((4, 2) + small, F32),
            pltpu.VMEM((2, 2) + small, F32),
            pltpu.VMEM((4,) + small, F32),
            pltpu.VMEM((2,) + small, F32),
            pltpu.VMEM((2,) + small, F32),
            pltpu.VMEM(small, F32),
        ],
        near=tuple(range(11)),
        near_out=(0,),
    )
    output, input_grad, gate_grad, up_grad, down_grad, out_grad, qkv_grad = finish(
        output, input_grad, G1, G3, G2, GO, GQ, GKV
    )
    return (
        output[None],
        input_grad[None],
        gain_out[0],
        gain_out[1],
        qkv_grad,
        out_grad,
        gate_grad,
        up_grad,
        down_grad,
    )


def solution(mesh):
    rows = P("dp", None)
    acts = P("dp", "ctx", None)
    return jax.shard_map(
        body,
        mesh=mesh,
        in_specs=(acts, P("dp", "ctx"), acts, P("dp"), P("dp"), rows, rows, rows, rows, rows),
        out_specs=(acts, acts, P("dp"), P("dp"), rows, rows, rows, rows, rows),
        check_vma=False,
    )
```

```python
import functools

import jax
import jax.numpy as jnp
import numpy as np
from jax import lax
from jax.experimental import pallas as pl
from jax.experimental.pallas import tpu as pltpu
from jax.sharding import PartitionSpec as P

D = 2048
HEAD_DIM = 64
TOK = 128
RING = 4
QDIM = 2048
KVDIM = 256
GROUP = 8
QZ = 512
MZ = 640
FZ = 1408
SPLIT = 1536
EPS = 1e-05
THETA = 10000.0
MESH = pl.DeviceIdType.MESH
VMEM_LIMIT = 60 << 20
BF = jnp.bfloat16
F32 = jnp.float32
ANY = pl.BlockSpec(memory_space=pl.ANY)
VMEM = pl.BlockSpec(memory_space=pltpu.VMEM)


def coords():
    dp, ctx = lax.axis_index("dp"), lax.axis_index("ctx")
    y, xh = dp // 2, dp % 2
    xl, z, c = ctx // 8, (ctx // 2) % 4, ctx % 2
    return dict(y=y, x=xh * 2 + xl, xh=xh, xl=xl, z=z, c=c)


def device(q, **change):
    r = {k: change.get(k, q[k]) for k in ("y", "x", "z", "c")}
    return (r["y"] * 2 + r["x"] // 2, (r["x"] % 2) * 8 + r["z"] * 2 + r["c"])


def ring(q, axis):
    return [device(q, **{axis: (q[axis] + s) % 4}) for s in (1, 3, 2)]


def shift_pairs(axis, by):
    size = 2 if axis == "c" else 4
    pairs = []
    for y in range(4):
        for x in range(4):
            for z in range(4):
                for c in range(2):
                    q = dict(y=y, x=x, z=z, c=c)
                    pairs.append((device(q), device(q, **{axis: (q[axis] + by) % size})))
    return [(a[0] * 16 + a[1], b[0] * 16 + b[1]) for a, b in pairs]


def swap_pairs():
    pairs = []
    for y in range(4):
        for x in range(4):
            for z in range(4):
                for c in range(2):
                    q = dict(y=y, x=x, z=z, c=c)
                    pairs.append((device(q), device(q, y=z, z=y)))
    return [(a[0] * 16 + a[1], b[0] * 16 + b[1]) for a, b in pairs]


def move(v, axis, by):
    return lax.ppermute(v, ("dp", "ctx"), shift_pairs(axis, by))


class Copies:
    def __init__(self, send_sems, recv_sems):
        self.send_sems, self.recv_sems, self.n, self.open = send_sems, recv_sems, 0, []

    def send(self, src, dst, to):
        cp = pltpu.make_async_remote_copy(
            src_ref=src,
            dst_ref=dst,
            send_sem=self.send_sems.at[self.n],
            recv_sem=self.recv_sems.at[self.n],
            device_id=to,
            device_id_type=MESH,
        )
        cp.start()
        self.n += 1
        self.open.append(cp)
        return cp

    def local(self, src, dst):
        cp = pltpu.make_async_copy(src, dst, self.send_sems.at[self.n])
        cp.start()
        self.n += 1
        return cp

    def close(self):
        for cp in self.open:
            cp.wait_send()
        self.open = []


def deal(k, q, src, col, dst):
    y, z = q["y"], q["z"]
    n = k.n
    k.n += 4
    copies = [
        pltpu.make_async_remote_copy(
            src_ref=src.at[:, col((y + s) % 4)],
            dst_ref=dst,
            send_sem=k.send_sems.at[n + i],
            recv_sem=k.recv_sems.at[n],
            device_id=to,
            device_id_type=MESH,
        )
        for i, (s, to) in enumerate(zip((1, 3, 2), ring(q, "y")))
    ]
    here = pltpu.make_async_copy(src.at[:, col(y)], dst, k.send_sems.at[n + 3])

    @pl.when(y == z)
    def _():
        for cp in copies:
            cp.start()
        here.start()

    def wait():
        @pl.when(y == z)
        def _():
            for cp in copies:
                cp.wait_send()
            here.wait()

        @pl.when(y != z)
        def _():
            copies[0].wait_recv()

    return wait


def greet(targets, q=None):
    barrier = pltpu.get_barrier_semaphore()
    for to in targets:
        pl.semaphore_signal(barrier, inc=1, device_id=to, device_id_type=MESH)
    if q is None:
        pl.semaphore_wait(barrier, len(targets))
    else:
        y, z = q["y"], q["z"]

        @pl.when(y != z)
        def _():
            to = device(q, y=z, z=y)
            pl.semaphore_signal(barrier, inc=1, device_id=to, device_id_type=MESH)

        pl.semaphore_wait(barrier, len(targets) + (y != z).astype(jnp.int32))


TOP, LOW = pl.ds(0, TOK // 2), pl.ds(TOK // 2, TOK // 2)
HALF = (TOK // 2, D)


class Gather:
    def __init__(self, k, q, axis, src, dst):
        at = q[axis]
        self.k, self.dst = k, dst
        self.above, self.below, self.far = (at + 1) % 4, (at + 3) % 4, (at + 2) % 4
        self.up, self.down = device(q, **{axis: self.above}), device(q, **{axis: self.below})
        self.low0 = k.send(src(0), dst(at, 0), self.up)
        self.top1 = k.send(src(1), dst(at, 1), self.down)
        self.low1 = k.send(src(1), dst(at, 1), self.up)
        self.top0 = k.send(src(0), dst(at, 0), self.down)

        self.waiting = {0: self.low0, 1: self.top1}

    def arrived(self, half):
        cp = self.waiting.pop(half, None)
        if cp is not None:
            cp.wait_recv()

    def relay(self):
        self.arrived(0)
        ref = self.dst(self.below, 0)
        self.far0 = self.k.send(ref, ref, self.up)
        self.arrived(1)
        ref = self.dst(self.above, 1)
        self.far1 = self.k.send(ref, ref, self.down)

    def near(self):
        self.arrived(0)
        self.arrived(1)
        self.low1.wait_recv()
        self.top0.wait_recv()

    def end(self):
        self.far0.wait_recv()
        self.far1.wait_recv()


class Sum:
    def __init__(self, k, q, axis, block, below, above, passed):
        at = q[axis]
        self.k, self.below, self.above, self.passed = k, below, above, passed
        up, down, far = (at + 1) % 4, (at + 3) % 4, (at + 2) % 4
        self.up, self.down = device(q, **{axis: up}), device(q, **{axis: down})
        self.first = k.send(block(far, 0), passed[0], self.up)
        self.second = k.send(block(far, 1), passed[1], self.down)
        self.rest = [
            k.send(block(up, 1), below(1), self.up),
            k.send(block(down, 0), above(0), self.down),
        ]

    def relay(self, own0, own1, sent):
        self.first.wait_recv()
        sent[0][...] = (self.passed[0][...].astype(F32) + own0[...].astype(F32)).astype(BF)
        self.rest.append(self.k.send(sent[0], self.below(0), self.up))
        self.second.wait_recv()
        sent[1][...] = (self.passed[1][...].astype(F32) + own1[...].astype(F32)).astype(BF)
        self.rest.append(self.k.send(sent[1], self.above(1), self.down))

    def end(self):
        for cp in self.rest:
            cp.wait_recv()


def halves(ref):
    return lambda h: ref.at[(TOP, LOW)[h]]


def ring_halves(ref):
    return lambda j, h: ref.at[j, (TOP, LOW)[h]]


def turn(k, q, moves):
    y, z = q["y"], q["z"]
    swap = device(q, y=z, z=y)
    pairs = []
    for src, dst in moves:
        n = k.n
        k.n += 1
        remote = pltpu.make_async_remote_copy(
            src_ref=src,
            dst_ref=dst,
            send_sem=k.send_sems.at[n],
            recv_sem=k.recv_sems.at[n],
            device_id=swap,
            device_id_type=MESH,
        )
        pairs.append((remote, pltpu.make_async_copy(src, dst, k.send_sems.at[n])))

    @pl.when(y != z)
    def _():
        for remote, _ in pairs:
            remote.start()

    @pl.when(y == z)
    def _():
        for _, here in pairs:
            here.start()

    def wait():
        @pl.when(y != z)
        def _():
            for remote, _ in pairs:
                remote.wait_recv()
                remote.wait_send()

        @pl.when(y == z)
        def _():
            for _, here in pairs:
                here.wait()

    return wait


def cost(us):
    return pl.CostEstimate(flops=int(us * 1e9), bytes_accessed=0, transcendentals=0)


def talk(kernel, name, cid, us, copies, ins, outs, scratch=(), near=(), near_out=(), alias={}):
    return pl.pallas_call(
        kernel,
        name=name,
        out_shape=[jax.ShapeDtypeStruct(s, t) for s, t in outs],
        in_specs=[VMEM if i in near else ANY for i in range(len(ins))],
        out_specs=[VMEM if i in near_out else ANY for i in range(len(outs))],
        scratch_shapes=[
            *scratch,
            pltpu.SemaphoreType.DMA((copies,)),
            pltpu.SemaphoreType.DMA((copies,)),
        ],
        cost_estimate=cost(us),
        input_output_aliases=alias,
        compiler_params=pltpu.CompilerParams(
            collective_id=cid, has_side_effects=True, vmem_limit_bytes=VMEM_LIMIT
        ),
    )(*ins)


def front_kernel(
    x, g, seg, na, nf, freq, wq, wo, w1, w3, w2,
    G, WQ, WO, W13, T2, N1, Q, KV, COS, SIN, START, GA, GF,
    TO, TV, QP, KT, VT, P1, P3, SG, NG, SEGS, GN, XV, WV, NV, QV, KVV, ss, rs,
):
    q = coords()
    y, xx, xh, xl, z, c = q["y"], q["x"], q["xh"], q["xl"], q["z"], q["c"]
    zs, ys, xs = ring(q, "z"), ring(q, "y"), ring(q, "x")
    mate = device(q, c=1 - c)
    other = device(q, x=xx ^ 1)
    other_mate = device(q, x=xx ^ 1, c=1 - c)
    k = Copies(ss, rs)
    rows = pl.ds(pl.multiple_of(128 * c + 64 * xl, 64), 64)
    qcols = pl.ds(pl.multiple_of(QZ * z, 128), QZ)
    tile = 128 * (z // 2)
    kcols = pl.ds(pl.multiple_of(QDIM + tile, 128), 128)
    vcols = pl.ds(pl.multiple_of(QDIM + KVDIM + tile, 128), 128)
    fcols = pl.ds(pl.multiple_of(FZ * z, 128), FZ)
    loads = [
        k.local(wq.at[rows, qcols], QP.at[:, pl.ds(0, QZ)]),
        k.local(wq.at[rows, kcols], KT),
        k.local(wq.at[rows, vcols], VT),
        k.local(w1.at[rows, fcols], P1),
        k.local(w3.at[rows, fcols], P3),
    ]
    SG[...] = jnp.broadcast_to(seg[...], (8, TOK))
    NG[0:16] = jnp.broadcast_to(na[...].astype(F32)[None], (16, 256)).astype(BF)
    NG[16:32] = jnp.broadcast_to(nf[...].astype(F32)[None], (16, 256)).astype(BF)
    greet(zs + ys + xs + [mate, other_mate])
    seg_z = [k.send(SG, SEGS.at[xl, z, c], to) for to in zs]
    x_ring = Gather(k, q, "z", halves(x), ring_halves(XV))
    lanes = lambda j, n=1: pl.ds(pl.multiple_of(128 * j, 128 * n), 128 * n)
    dealt = deal(k, q, wo, lambda j: lanes(c * 8 + j * 2 + xl), TO)
    for cp in loads:
        cp.wait()
    odd = z % 2 == 1
    kt, vt = KT[...].astype(F32), VT[...].astype(F32)
    lane = lax.broadcasted_iota(jnp.int32, kt.shape, 1)
    kt = jnp.where(odd, pltpu.roll(kt, 64, 1), kt)
    vt = jnp.where(odd, vt, pltpu.roll(vt, 64, 1))
    QP[:, QZ:] = jnp.where(lane < HEAD_DIM, kt, vt).astype(BF)
    f1, f3 = pl.ds(0, FZ), pl.ds(FZ, FZ)
    top, low = pl.ds(0, 32), pl.ds(32, 32)
    thirty = lambda h: pl.ds(32 * h, 32)
    q_top = [k.send(QP.at[top], WV.at[c, y, xh, xl, top], to) for to in xs]
    q_low = [k.send(QP.at[low], WV.at[c, y, xh, xl, low], to) for to in ys]
    gn_y = [k.send(NG, GN.at[y, xh], to) for to in ys]
    up_y = Gather(
        k, q, "y", lambda h: P3.at[thirty(h)], lambda j, h: W13.at[c, j, xh, xl, thirty(h), f3]
    )
    gate_x = Gather(
        k, q, "x", lambda h: P1.at[thirty(h)],
        lambda j, h: W13.at[c, y, j // 2, j % 2, thirty(h), f1],
    )
    q_here = k.local(QP, WV.at[c, y, xh, xl])
    seg_here = k.local(SG, SEGS.at[xl, z, c])
    gn_here = k.local(NG, GN.at[y, xh])
    x_here = k.local(x, XV.at[z])
    up_here = k.local(P3, W13.at[c, y, xh, xl, :, f3])
    heres = [k.local(P1, W13.at[c, y, xh, xl, :, f1]), k.local(g, G.at[z])]
    dealt()
    o1 = [k.send(TO, WO.at[xh, :, lanes(c * 8 + y * 2 + xl)], to) for to in xs]
    o1_here = k.local(TO, WO.at[xh, :, lanes(c * 8 + y * 2 + xl)])
    for cp in seg_z:
        cp.wait_recv()
    seg_here.wait()
    part = SEGS.at[xl, :, c]
    seg2 = [k.send(part, part, to) for to in (mate, other, other_mate)]
    q_here.wait()
    for cp in q_top:
        cp.wait_recv()
    q_y = Gather(k, q, "y", lambda h: WV.at[c, y, h, :, top], lambda j, h: WV.at[c, j, h, :, top])
    for cp in gn_y:
        cp.wait_recv()
    gn_here.wait()
    gn2 = k.send(GN.at[:, xh], GN.at[:, xh], device(q, x=3 - xx))
    gate_x.relay()
    for cp in q_low:
        cp.wait_recv()
    q_half = lambda j, h: WV.at[c, pl.ds(2 * h, 2), j // 2, j % 2, low]
    q_x = Gather(k, q, "x", lambda h: q_half(xx, h), q_half)
    x_ring.relay()
    g_ring = Gather(k, q, "z", halves(g), ring_halves(G))
    up_y.relay()
    for cp in o1:
        cp.wait_recv()
    o1_here.wait()
    o_half = lambda j, h: WO.at[h, :, lanes(c * 8 + j * 2, 2)]
    o_y = Gather(k, q, "y", lambda h: o_half(y, h), o_half)
    for cp in seg2:
        cp.wait_recv()
    docs = [SEGS[i // 8, (i // 2) % 4, i % 2, 0:1].astype(F32) for i in range(16)]
    columns = jnp.concatenate(docs + [jnp.zeros((TOK - 16, TOK), F32)], axis=0).T
    for i in range(RING):
        mine = SEGS[xl, i, c, 0:1].astype(F32)
        count = jnp.zeros((TOK, TOK), F32)
        for j in range(16):
            count = count + jnp.where(columns[:, j : j + 1] < mine, 1.0, 0.0)
        first = jnp.sum(count, axis=0, keepdims=True)
        START[i] = first.astype(jnp.int32)
        index = TOK * (8 * xl + 2 * i + c) + lax.broadcasted_iota(jnp.int32, (1, TOK), 1)
        place = index.astype(F32) - first
        angle = jnp.broadcast_to(place, (TOK, TOK)).T * freq[...]
        COS[i] = jnp.cos(angle)
        sine = jnp.sin(angle)
        lane = lax.broadcasted_iota(jnp.int32, sine.shape, 1)
        SIN[i] = jnp.where(lane % 64 < 32, -sine, sine)
    q_y.relay()
    w2_dealt = deal(k, q, w2, lambda j: lanes(c * 8 + xl * 4 + j), TV)
    q_x.relay()
    up_y.near()
    up_y.end()
    up_here.wait()
    part = W13.at[c, :, xh, xl, :, f3]
    a3 = [k.send(part, part, to) for to in xs[:2]]
    o_y.relay()
    gn2.wait_recv()
    whole = lambda r: jnp.concatenate(
        [GN[d // 2, d % 2, r : r + 1].astype(F32) for d in range(8)], axis=1
    )
    gain = whole(0)
    GA[...] = gain
    GF[...] = whole(16)
    x_ring.near()
    x_ring.end()
    x_here.wait()
    for i in range(RING):
        xv = XV[i].astype(F32)
        scale = lax.rsqrt(jnp.mean(xv * xv, axis=-1, keepdims=True) + EPS)
        NV[i] = to_pieces((xv * scale * gain).astype(BF))
    done = [k.local(NV, N1)]
    for r in (q_y, q_x):
        r.near()
        r.end()
    q3 = k.send(WV.at[c], WV.at[c], mate)
    g_ring.relay()
    q3.wait_recv()
    done.append(k.local(WV, WQ))
    mixed = dot(NV[...].reshape(RING * TOK, D), WV[...].reshape(D, MZ))
    for i in range(RING):
        cos, sin = COS[i], SIN[i]
        for j in range(5):
            u = mixed[TOK * i : TOK * i + TOK, 128 * j : 128 * j + 128]
            turned = u * cos + swapped(u) * sin
            if j < 4:
                QV[i, :, 128 * j : 128 * j + 128] = turned.astype(BF)
            else:
                lane = lax.broadcasted_iota(jnp.int32, u.shape, 1)
                KVV[i] = jnp.where(lane < HEAD_DIM, turned, u).astype(BF)
    near = k.send(KVV, KV.at[xl, :, c], mate)
    n = k.n
    k.n += 2
    far, on = [
        pltpu.make_async_remote_copy(
            src_ref=src,
            dst_ref=KV.at[0, :, c],
            send_sem=ss.at[n + i],
            recv_sem=rs.at[n + i],
            device_id=to,
            device_id_type=MESH,
        )
        for i, (src, to) in enumerate(((KVV, other), (KV.at[0, :, c], mate)))
    ]

    @pl.when(xl == 0)
    def _():
        far.start()

    done += [k.local(KVV, KV.at[xl, :, c]), k.local(QV, Q)]
    o_y.near()
    o_y.end()
    part = WO.at[:, :, pl.ds(pl.multiple_of(1024 * c, 1024), 1024)]
    o3 = k.send(part, part, mate)
    w2_dealt()
    done.append(k.local(TV, T2))

    @pl.when(xl == 0)
    def _():
        far.wait_send()

    @pl.when(xl == 1)
    def _():
        far.wait_recv()
        on.start()
        on.wait_recv()
        on.wait_send()

    near.wait_recv()
    for cp in a3 + [o3]:
        cp.wait_recv()
    for cp in heres + done:
        cp.wait()
    for r in (gate_x, g_ring):
        r.near()
        r.end()
    k.close()


def core_kernel(
    o, x, gain, t2, w13, wo_in, G, V, FA, FB, F2, DO, OUT, DH, GAIN, *scratch
):
    (
        W, W2, N2, gv, hv, hT, bv, part, outs, wo, ov, vv, hf, xb,
        p0, p1, p2, p3, v0, v1, v2, v3, below, above, out_below, out_above, *rest_of,
    ) = scratch
    bufs, (used, ss, rs) = rest_of[:-3], rest_of[-3:]
    q = coords()
    y, xx, xh, xl, z, c = q["y"], q["x"], q["xh"], q["xl"], q["z"], q["c"]
    ys, xs = ring(q, "y"), ring(q, "x")
    up, down = device(q, z=(z + 1) % 4), device(q, z=(z + 3) % 4)
    mate = device(q, c=1 - c)
    k = Copies(ss, rs)
    f1, f3 = pl.ds(0, FZ), pl.ds(FZ, FZ)
    lower, higher = (xx + 3) % 4, (xx + 1) % 4
    gate_at = lambda ref, j: ref.at[c, j, :, :, :, f1]
    gate_half = lambda ref, j, h: ref.at[c, j, h, :, :, f1]
    up_at = lambda ref, j: ref.at[c, :, j // 2, j % 2, :, f3]
    up_half = lambda ref, j, h: ref.at[c, pl.ds(2 * h, 2), j // 2, j % 2, :, f3]
    get_wo, get_o = k.local(wo_in, wo), k.local(o, ov)
    loads = [k.local(x, xb), k.local(gate_at(w13, y), gate_at(W, y))]
    loads += [k.local(up_at(w13, j), up_at(W, j)) for j in (xx, lower, higher)]
    get_g = k.local(G, gv)
    greet(ys + xs + [up, down, mate])
    cols = lambda j, n: pl.ds(pl.multiple_of(128 * (8 * c + j), 128 * n), 128 * n)
    frows = lambda j, h: pl.ds(pl.multiple_of(704 * (j // 2) + 352 * h, 32), 352)
    w2_here = k.local(t2, W2.at[pl.ds(pl.multiple_of(704 * xh, 64), 704), cols(xl * 4 + y, 1)])
    w2y = Gather(
        k, q, "y", lambda h: t2.at[pl.ds(352 * h, 352)],
        lambda j, h: W2.at[frows(xx, h), cols(xl * 4 + j, 1)],
    )
    far = [
        k.send(up_half(w13, lower, 0), up_half(W, lower, 0), xs[0]),
        k.send(up_half(w13, higher, 1), up_half(W, higher, 1), xs[1]),
    ]
    sent = [k.send(up_at(w13, j), up_at(W, j), mate) for j in (xx, lower, higher)]
    get_wo.wait()
    get_o.wait()
    rows = RING * TOK
    part[...] = dot(ov[...].reshape(rows, QZ), wo[...]).astype(BF).reshape(RING, TOK, D)
    z_sum = Sum(k, q, "z", ring_halves(part), halves(below), halves(above), (p0, p1))
    w2y.relay()
    gate = Gather(
        k, q, "y", lambda h: gate_half(w13, y, h), lambda j, h: gate_half(W, j, h)
    )
    sent.append(k.send(gate_at(w13, y), gate_at(W, y), mate))
    w2_here.wait()
    w2y.near()
    w2y.end()
    down2 = lambda j: W2.at[
        pl.ds(pl.multiple_of(704 * (j // 2), 64), 704), cols((j % 2) * 4, 4)
    ]
    down_half = lambda j, h: W2.at[frows(j, h), cols((j % 2) * 4, 4)]
    down_ring = Gather(k, q, "x", lambda h: down_half(xx, h), down_half)
    sent.append(k.send(down2(xx), down2(xx), mate))
    z_sum.relay(part.at[(z + 1) % 4, TOP], part.at[(z + 3) % 4, LOW], (v0, v1))
    z_sum.end()
    for cp in loads:
        cp.wait()
    total = xb[...].astype(F32) + (
        part[z].astype(F32) + (below[...].astype(F32) + above[...].astype(F32))
    )
    hf[...] = total
    scale = lax.rsqrt(jnp.mean(total * total, axis=-1, keepdims=True) + EPS)
    N2[z] = to_pieces((total * scale * gain[...]).astype(BF))
    n2_ring = Gather(k, q, "z", halves(N2.at[z]), ring_halves(N2))
    gate.relay()
    down_ring.relay()
    for cp in far:
        cp.wait_recv()
    ref = up_at(W, (xx + 2) % 4)
    sent.append(k.send(ref, ref, mate))
    gate.near()
    for j in (gate.below, gate.above):
        sent.append(k.send(gate_at(W, j), gate_at(W, j), mate))
    down_ring.near()
    for j in (down_ring.below, down_ring.above):
        sent.append(k.send(down2(j), down2(j), mate))
    n2_ring.relay()
    gate.end()
    sent.append(k.send(gate_at(W, gate.far), gate_at(W, gate.far), mate))
    down_ring.end()
    sent.append(k.send(down2(down_ring.far), down2(down_ring.far), mate))
    get_g.wait()
    for cp in sent:
        cp.wait_recv()
    tiles = [(256 * i, min(256 * i + 256, FZ)) for i in range(6)]
    gs = gv[...].reshape(rows, D)
    for a, b in tiles:
        bv[:, a:b] = nt(gs, W2[a:b]).astype(BF)
    n2_ring.near()
    n2_ring.end()
    k.close()
    n2 = N2[...].reshape(rows, D)
    for a, b in tiles:
        gates = dot(n2, W[:, :, :, :, :, a:b].reshape(D, b - a))
        ups = dot(n2, W[:, :, :, :, :, FZ + a : FZ + b].reshape(D, b - a))
        sigma = jax.nn.sigmoid(gates)
        silu = gates * sigma
        hv[:, a:b] = (silu * ups).astype(BF)
        dhid = bv[:, a:b].astype(F32)
        bv[:, a:b] = (dhid * ups * sigma * (1.0 + gates * (1.0 - sigma))).astype(BF)
        bv[:, FZ + a : FZ + b] = (dhid * silu).astype(BF)
    for j in range(4):
        at = slice(512 * j, 512 * j + 512)
        outs[:, :, at] = dot(hv[...], W2[:, at]).astype(BF).reshape(RING, TOK, 512)
    out_sum = Sum(
        k, q, "z", ring_halves(outs), halves(out_below), halves(out_above), (p2, p3)
    )
    pl.semaphore_signal(used.at[0], inc=1, device_id=mate, device_id_type=MESH)
    half = lambda ref: lambda i: ref.at[i]
    rest = 2 * FZ - SPLIT
    jobs = [
        ("y", lambda j, i: W2.at[pl.ds(704 * i, 704), lanes(0, j)], F2),
        ("x", lambda j, i: W.at[0, pl.ds(2 * i, 2), j // 2, j % 2, :, pl.ds(0, SPLIT)], FA),
        ("y", lambda j, i: W.at[0, j, i, :, :, pl.ds(SPLIT, rest)], FB),
    ]
    sums, done = [], []
    lanes = lambda cc, j: pl.ds(pl.multiple_of(1024 * cc + 256 * j, 256), 256)

    def start(n):
        axis, block, _ = jobs[n]
        b = bufs[4 * n : 4 * n + 4]
        sums.append(Sum(k, q, axis, block, half(b[2]), half(b[3]), (b[0].at[0], b[0].at[1])))

    def relay(n):
        axis, block, _ = jobs[n]
        b = bufs[4 * n : 4 * n + 4]
        at = q[axis]
        sums[n].relay(block((at + 1) % 4, 0), block((at + 3) % 4, 1), (b[1].at[0], b[1].at[1]))

    def end(n):
        axis, block, out = jobs[n]
        b = bufs[4 * n : 4 * n + 4]
        sums[n].end()
        for i in range(2):
            total = block(q[axis], i)[...].astype(F32) + (
                b[2][i].astype(F32) + b[3][i].astype(F32)
            )
            b[2][i] = total.astype(BF)
        done.append(k.local(b[2], out))

    hT[...] = hv[...].T
    pl.semaphore_wait(used.at[0], 1)
    sent2, sent13 = [], []
    for j in range(4):
        W2[:, 1024 + 256 * j : 1280 + 256 * j] = dot(
            hT[...], gv[:, :, lanes(1 - c, j)].reshape(rows, 256)
        ).astype(BF)
        sent2.append(k.send(W2.at[:, lanes(1, j)], W2.at[:, lanes(0, j)], mate))

    def back_half(j):
        at = slice(1024 * j, 1024 * j + 1024)
        dn = nt(bv[...], W[j].reshape(1024, 2 * FZ))
        part[:, :, at] = dn.astype(BF).reshape(RING, TOK, 1024)

    back_half(0)
    for j in range(4):
        sent2[j].wait_recv()
        at = slice(256 * j, 256 * j + 256)
        own = dot(hT[...], gv[:, :, lanes(c, j)].reshape(rows, 256))
        W2[:, at] = (own + W2[:, at].astype(F32)).astype(BF)
    start(0)
    back_half(1)
    z_sum = Sum(k, q, "z", ring_halves(part), halves(below), halves(above), (p0, p1))
    pl.semaphore_signal(used.at[1], inc=1, device_id=mate, device_id_type=MESH)
    pl.semaphore_wait(used.at[1], 1)
    shape = (2, 2, 64, 2 * FZ)
    for j in range(4):
        W[1, j] = tn(N2[:, :, lanes(1 - c, j)].reshape(rows, 256), bv[...]).astype(BF).reshape(shape)
        sent13.append(k.send(W.at[1, j], W.at[0, j], mate))
        if j == 1:
            relay(0)
    z_sum.relay(part.at[(z + 1) % 4, TOP], part.at[(z + 3) % 4, LOW], (v0, v1))
    for j in range(4):
        sent13[j].wait_recv()
        own = tn(N2[:, :, lanes(c, j)].reshape(rows, 256), bv[...]).reshape(shape)
        W[0, j] = (own + W[0, j].astype(F32)).astype(BF)
        if j == 1:
            out_sum.relay(outs.at[(z + 1) % 4, TOP], outs.at[(z + 3) % 4, LOW], (v2, v3))
    start(1)
    start(2)
    z_sum.end()
    dn = from_pieces(
        part[z].astype(F32) + (below[...].astype(F32) + above[...].astype(F32))
    )
    back, gain_grad = rms_back(hf[...], gain[...], dn)
    total = gv[z].astype(F32) + back
    DH[...] = total
    GAIN[...] = gain_grad
    vv[z] = total.astype(BF)
    v_ring = Gather(k, q, "z", halves(vv.at[z]), ring_halves(vv))
    end(0)
    out_sum.end()
    OUT[...] = hf[...] + (
        outs[z].astype(F32) + (out_below[...].astype(F32) + out_above[...].astype(F32))
    )
    relay(1)
    relay(2)
    v_ring.relay()
    end(2)
    v_ring.near()
    v_ring.end()
    done.append(k.local(vv, V))
    DO[...] = nt(vv[...].reshape(rows, D), wo[...]).astype(BF)
    end(1)
    for cp in done:
        cp.wait()
    k.close()


def quarter(xt, rows):
    return (
        pl.ds(pl.multiple_of((xt // 2) * rows, rows), rows),
        pl.ds(pl.multiple_of((xt % 2) * 128, 128), 128),
    )


def tail_kernel(
    dkv, dq, cosine, sine, x, dh, gain, gain2, fa, fb, f2, wq, n1, o, dho,
    IG, G1, G3, G2, GO, GQ, GKV, gain_out, *scratch,
):
    (
        wv, nv, ov, gv, R, dm, dn, p0, p1, v0, v1, below, above, mate_o, sum_o, mate_q, sum_q,
        ob0, ob1, ob2, ob3, qb0, qb1, qb2, qb3, la, lb, l2, pa, pb, p2, t2, lo, lq, fo, fq,
        po, pq, to_, gains, s0, s1, s2, s3, s4, total,
        kv_own, kv_low, cv, sv, xv, dv, fav, fbv, f2v, ss, rs,
    ) = scratch
    q = coords()
    y, xx, xh, xl, z, c = q["y"], q["x"], q["xh"], q["xl"], q["z"], q["c"]
    zs, ys, xs = ring(q, "z"), ring(q, "y"), ring(q, "x")
    mate, other, cross = device(q, c=1 - c), device(q, x=xx ^ 1), device(q, x=3 - xx)
    other_mate = device(q, x=xx ^ 1, c=1 - c)
    steps = (1, 3, 2)
    rows_all = RING * TOK
    k = Copies(ss, rs)
    get_o, get_g = k.local(o, ov), k.local(dho, gv)
    r, cc = quarter(xx, 704)
    get_f = [k.local(fb.at[xx], fbv), k.local(fa.at[y], fav), k.local(f2.at[r, cc], f2v)]
    get_kv = [k.local(dkv.at[xl, :, c], kv_own), k.local(dkv.at[0, :, c], kv_low)]
    get_d = [
        k.local(dq, dm.at[:, :, pl.ds(0, QZ)]),
        k.local(cosine, cv),
        k.local(sine, sv),
        k.local(wq, wv),
    ]
    get_n = k.local(n1, nv)
    get_x = [k.local(x, xv), k.local(dh, dv)]
    greet(zs + ys + xs + [mate, other_mate], q)
    leg_b = [k.send(fb.at[(xx + s) % 4], lb.at[i], xs[i]) for i, s in enumerate(steps)]
    leg_a = [k.send(fa.at[(y + s) % 4], la.at[i], ys[i]) for i, s in enumerate(steps)]
    lanes = lambda cc, j: pl.ds(pl.multiple_of(1024 * cc + 256 * j, 256), 256)
    get_o.wait()
    get_g.wait()
    swaps = []
    for j in range(4):
        mate_o[j] = tn(ov[...], gv[:, lanes(1 - c, j)]).astype(BF)
        swaps.append(k.send(mate_o.at[j], sum_o.at[j], mate))
    leg_2 = []
    for i, s in enumerate(steps):
        r, cc = quarter((xx + s) % 4, 704)
        leg_2.append(k.send(f2.at[r, cc], l2.at[i], xs[i]))
    for j in range(4):
        swaps[j].wait_recv()
        sum_o[j] = (tn(ov[...], gv[:, lanes(c, j)]) + sum_o[j].astype(F32)).astype(BF)
    half = lambda ref: lambda h: ref.at[h]
    o_block = lambda j, h: sum_o.at[j, pl.ds(256 * h, 256)]
    q_block = lambda j, h: sum_q.at[j, pl.ds(2 * h, 2)]
    o_sum = Sum(k, q, "y", o_block, half(ob2), half(ob3), (ob0.at[0], ob0.at[1]))
    at = lambda zz, off, n: pl.ds(pl.multiple_of(FZ * zz + off, 128), n)
    rows = pl.ds(pl.multiple_of(128 * c + 64 * xl, 64), 64)
    pair = pl.ds(pl.multiple_of(128 * c, 128), 128)
    f1 = pl.ds(0, FZ)
    rest = SPLIT - FZ
    quarter_rows = lambda h: pl.ds(pl.multiple_of(128 * c + 64 * xl + 32 * h, 32), 32)

    def over_z(src, ref, off, n):
        return Gather(
            k, q, "z", lambda h: src.at[pl.ds(32 * h, 32)],
            lambda j, h: ref.at[quarter_rows(h), at(j, off, n)],
        )

    spans = [(G1, 0, FZ), (G3, 0, rest), (G3, rest, FZ - rest)]
    pieces = [pa.at[:, f1], pa.at[:, pl.ds(FZ, rest)], pb]
    block = lambda i, j: spans[i][0].at[rows, at(j, spans[i][1], spans[i][2])]
    rings, to_x, heres = [None] * 3, [], []

    def across(i, j):
        to_x.append(k.send(block(i, j), block(i, j), other))

    def own_across(i):
        to_x.append(k.send(pieces[i], block(i, z), other))
        heres.append(k.local(pieces[i], block(i, z)))

    def onward(i):
        rings[i].near()
        across(i, rings[i].below)
        across(i, rings[i].above)

    for cp in get_f:
        cp.wait()
    for cp in leg_b:
        cp.wait_recv()
    pb[...] = add4(fbv[...], lb[0], lb[1], lb[2])
    rings[2] = over_z(pieces[2], *spans[2])
    near = k.send(dkv.at[xl, :, 1 - c], R.at[0], mate)
    n = k.n
    k.n += 2
    pre, far = [
        pltpu.make_async_remote_copy(
            src_ref=src,
            dst_ref=dst,
            send_sem=ss.at[n + i],
            recv_sem=rs.at[n + i],
            device_id=to,
            device_id_type=MESH,
        )
        for i, (src, dst, to) in enumerate(
            ((dkv.at[0, :, 1 - c], R.at[1], mate), (R.at[2], R.at[3], other))
        )
    ]

    @pl.when(xl == 1)
    def _():
        pre.start()

    for cp in get_kv:
        cp.wait()
    rings[2].relay()
    o_sum.relay(o_block((y + 1) % 4, 0), o_block((y + 3) % 4, 1), (ob1.at[0], ob1.at[1]))

    @pl.when(xl == 1)
    def _():
        R[3] = jnp.zeros(R.shape[1:], BF)
        pre.wait()
        for i in range(RING):
            R[2, i] = (kv_low[i].astype(F32) + R[1, i].astype(F32)).astype(BF)
        far.start()

    for cp in leg_a:
        cp.wait_recv()
    pa[...] = add4(fav[...], la[0], la[1], la[2])
    rings[0] = over_z(pieces[0], *spans[0])
    rings[1] = over_z(pieces[1], *spans[1])
    for cp in leg_2:
        cp.wait_recv()
    p2[...] = add4(f2v[...], l2[0], l2[1], l2[2])
    turned = turn(k, q, [(p2, t2)])
    onward(2)
    own_across(2)

    @pl.when(xl == 1)
    def _():
        far.wait_send()

    @pl.when(xl == 0)
    def _():
        far.wait_recv()

    near.wait_recv()
    for cp in get_d:
        cp.wait()
    for i in range(RING):
        w = kv_own[i].astype(F32) + (R[0, i].astype(F32) + R[3, i].astype(F32))
        lane = lax.broadcasted_iota(jnp.int32, w.shape, 1)
        dm[i, :, QZ:] = jnp.where(
            lane < HEAD_DIM, w * cv[i] - swapped(w) * sv[i], w
        ).astype(BF)
    dmixed = dm[...].reshape(rows_all, MZ)
    dn[...] = nt(dmixed, wv[...]).astype(BF).reshape(RING, TOK, D)
    z_sum = Sum(k, q, "z", ring_halves(dn), halves(below), halves(above), (p0, p1))
    onward(0)
    rings[1].relay()
    get_n.wait()
    cols = lambda cc: pl.ds(pl.multiple_of(1024 * cc, 1024), 1024)
    shape = (4, 4, 64, MZ)
    mate_q[...] = tn(nv[:, cols(1 - c)], dmixed).astype(BF).reshape(shape)
    swap = k.send(mate_q, sum_q, mate)
    own = tn(nv[:, cols(c)], dmixed).reshape(shape)
    swap.wait_recv()
    sum_q[...] = (own + sum_q[...].astype(F32)).astype(BF)
    q_sum = Sum(k, q, "y", q_block, half(qb2), half(qb3), (qb0.at[0], qb0.at[1]))
    o_sum.end()
    for h in range(2):
        part = o_block(y, h)[...].astype(F32) + (ob2[h].astype(F32) + ob3[h].astype(F32))
        fo[pl.ds(256 * h, 256)] = part.astype(BF)
    leg_o, leg_q = [], []
    for i, s in enumerate(steps):
        r, cc = quarter((xx + s) % 4, 256)
        leg_o.append(k.send(fo.at[r, cc], lo.at[i], xs[i]))
    turned()
    col = pl.ds(pl.multiple_of(128 * (c * 8 + z * 2 + xl), 128), 128)
    down_x = k.send(t2, G2.at[:, col], other)
    down_here = k.local(t2, G2.at[:, col])
    z_sum.relay(dn.at[(z + 1) % 4, TOP], dn.at[(z + 3) % 4, LOW], (v0, v1))
    q_sum.relay(q_block((y + 1) % 4, 0), q_block((y + 3) % 4, 1), (qb1.at[0], qb1.at[1]))
    onward(1)
    for cp in leg_o:
        cp.wait_recv()
    r, cc = quarter(xx, 256)
    po[...] = add4(fo[r, cc], lo[0], lo[1], lo[2])
    o_turned = turn(k, q, [(po, to_)])
    q_sum.end()
    for h in range(2):
        part = q_block(y, h)[...].astype(F32) + (qb2[h].astype(F32) + qb3[h].astype(F32))
        fq[pl.ds(2 * h, 2)] = part.astype(BF)
    for i, s in enumerate(steps):
        leg_q.append(k.send(fq.at[(xx + s) % 4], lq.at[i], xs[i]))
    rings[1].end()
    across(1, rings[1].far)
    rings[0].relay()
    z_sum.end()
    for cp in get_x:
        cp.wait()
    back, gain1 = rms_back(
        xv[...].astype(F32),
        gain[...],
        from_pieces(dn[z].astype(F32) + (below[...].astype(F32) + above[...].astype(F32))),
    )
    IG[...] = dv[...] + back
    gains[...] = jnp.zeros_like(gains)
    for d in range(8):
        gains[d // 2, d % 2, 0:1] = gain1[:, 256 * d : 256 * d + 256]
        gains[d // 2, d % 2, 1:2] = gain2[:, 256 * d : 256 * d + 256]
    gain_y = [k.send(gains.at[(y + s) % 4], s0.at[y], ys[i]) for i, s in enumerate(steps)]
    gain_here = k.local(gains.at[y], s0.at[y])
    down_x.wait_recv()
    down_here.wait()
    down_half = lambda j, h: G2.at[
        pl.ds(352 * h, 352), pl.ds(pl.multiple_of(128 * (c * 8 + j * 2), 256), 256)
    ]
    down_ring = Gather(k, q, "z", lambda h: down_half(z, h), down_half)
    own_across(0)
    own_across(1)
    for cp in leg_q:
        cp.wait_recv()
    pq[...] = add4(fq[xx], lq[0], lq[1], lq[2])
    qc = lambda j: pl.ds(pl.multiple_of(QZ * j, 128), QZ)
    kc = lambda j: pl.ds(pl.multiple_of(128 * j, 128), 128)
    q_pieces = [
        (pq.at[:, pl.ds(0, QZ)], GQ.at[rows, qc(z)]),
        (pq.at[:, pl.ds(QZ, 128)], GKV.at[rows, kc(z)]),
    ]
    q_x = [k.send(src, dst, other) for src, dst in q_pieces]
    q_here = [k.local(src, dst) for src, dst in q_pieces]
    o_turned()
    o_x = k.send(to_, GO.at[:, col], other)
    o_here = k.local(to_, GO.at[:, col])
    for cp in gain_y:
        cp.wait_recv()
    gain_here.wait()
    s1[0] = (s0[0] + s0[1]) + (s0[2] + s0[3])
    gain_x = k.send(s1.at[0, 1 - xh], s1.at[1, 0], cross)
    gain_x.wait_recv()
    s2[z] = s1[0, xh] + s1[1, 0]
    gain_z = [k.send(s2.at[z], s2.at[z], to) for to in zs]
    down_ring.relay()
    rings[0].end()
    across(0, rings[0].far)
    o_x.wait_recv()
    o_here.wait()
    o_half = lambda j, h: GO.at[
        pl.ds(128 * h, 128), pl.ds(pl.multiple_of(128 * (c * 8 + j * 2), 256), 256)
    ]
    o_ring = Gather(k, q, "z", lambda h: o_half(z, h), o_half)
    for cp in q_x:
        cp.wait_recv()
    for cp in q_here:
        cp.wait()
    half_rows = lambda h: pl.ds(pl.multiple_of(128 * c + 64 * h, 64), 64)
    q_half = lambda j, h: GQ.at[half_rows(h), qc(j)]
    kv_half = lambda j, h: GKV.at[half_rows(h), kc(j)]
    q_rings = [
        Gather(k, q, "z", lambda h: q_half(z, h), q_half),
        Gather(k, q, "z", lambda h: kv_half(z, h), kv_half),
    ]
    rings[2].end()
    across(2, rings[2].far)
    down_ring.near()
    down_ring.end()
    last = [k.send(G2.at[:, cols(c)], G2.at[:, cols(c)], mate)]
    for cp in to_x:
        cp.wait_recv()
    for cp in heres:
        cp.wait()
    last += [k.send(ref.at[pair], ref.at[pair], mate) for ref in (G1, G3)]
    o_ring.relay()
    for cp in gain_z:
        cp.wait_recv()
    s3[0] = (s2[0] + s2[1]) + (s2[2] + s2[3])
    gain_x = k.send(s3.at[0], s3.at[1], other)
    for one in q_rings:
        one.relay()
    o_ring.near()
    o_ring.end()
    last.append(k.send(GO.at[:, cols(c)], GO.at[:, cols(c)], mate))
    gain_x.wait_recv()
    s4[0] = s3[0] + s3[1]
    gain_c = k.send(s4.at[0], s4.at[1], mate)
    for one in q_rings:
        one.near()
        one.end()
    last += [k.send(ref.at[pair], ref.at[pair], mate) for ref in (GQ, GKV)]
    gain_c.wait_recv()
    total[...] = s4[0] + s4[1]
    gain_done = k.local(total, gain_out)
    for cp in last:
        cp.wait_recv()
    gain_done.wait()
    k.close()


PARAMS = pltpu.CompilerParams(vmem_limit_bytes=VMEM_LIMIT)


def add4(a, b, c, d):
    a, b, c, d = (v.astype(F32) for v in (a, b, c, d))
    return ((a + b) + (c + d)).astype(BF)


def to_pieces(v):
    return jnp.concatenate(
        [v[:, 256 * d + 128 * c : 256 * d + 128 * c + 128] for c in range(2) for d in range(8)],
        axis=1,
    )


def from_pieces(v):
    return jnp.concatenate(
        [v[:, 1024 * c + 128 * d : 1024 * c + 128 * d + 128] for d in range(8) for c in range(2)],
        axis=1,
    )


def swapped(u):
    lane = lax.broadcasted_iota(jnp.int32, u.shape, 1)
    return jnp.where(lane % 64 < 32, pltpu.roll(u, 96, 1), pltpu.roll(u, 32, 1))


def stacked_low(tiles):
    out = []
    for pair in range(4):
        tile = tiles[:, 128 * pair : 128 * pair + 128].astype(F32)
        lane = lax.broadcasted_iota(jnp.int32, tile.shape, 1)
        out.append(jnp.where(lane < HEAD_DIM, tile, 0.0))
        out.append(jnp.where(lane < HEAD_DIM, pltpu.roll(tile, 64, 1), 0.0))
    return jnp.concatenate(out, axis=0)


def stacked_high(tiles):
    out = []
    for pair in range(4):
        tile = tiles[:, 128 * pair : 128 * pair + 128].astype(F32)
        lane = lax.broadcasted_iota(jnp.int32, tile.shape, 1)
        out.append(jnp.where(lane >= HEAD_DIM, pltpu.roll(tile, 64, 1), 0.0))
        out.append(jnp.where(lane >= HEAD_DIM, tile, 0.0))
    return jnp.concatenate(out, axis=0)


def unstacked(v):
    tiles = []
    for pair in range(4):
        both = jnp.concatenate(
            [v[:, 256 * pair : 256 * pair + 128], v[:, 256 * pair + 128 : 256 * pair + 256]],
            axis=0,
        )
        tiles.append(both.T)
    return tiles


def nt(a, b):
    return lax.dot_general(a, b, (((1,), (1,)), ((), ())), preferred_element_type=F32)


def tn(a, b):
    return lax.dot_general(a, b, (((0,), (0,)), ((), ())), preferred_element_type=F32)


def own_chunk(i):
    ctx = lax.axis_index("ctx")
    return (ctx // 8) * 8 + 2 * i + ctx % 2


def over_chunks(start, chunk, step, carry):
    first = start.astype(F32)
    low = jnp.min(first).astype(jnp.int32) // TOK
    high = jnp.minimum((jnp.max(first).astype(jnp.int32) + TOK - 1) // TOK, chunk)
    carry = lax.fori_loop(low, high, lambda kc, cr: step(kc, 1, True, cr), carry)
    pairs = (chunk - high) // 2
    carry = lax.fori_loop(0, pairs, lambda n, cr: step(high + 2 * n, 2, False, cr), carry)
    carry = lax.fori_loop(
        high + 2 * pairs, chunk, lambda kc, cr: step(kc, 1, False, cr), carry
    )
    return step(chunk, 1, True, carry)


def chunk_scores(keys, stacked, kc, chunk, starts, masked):
    raw = nt(keys, stacked)
    if not masked:
        return raw
    key = kc * TOK + lax.broadcasted_iota(jnp.int32, raw.shape, 0)
    query = chunk * TOK + lax.broadcasted_iota(jnp.int32, raw.shape, 1) % TOK
    return jnp.where((key <= query) & (key >= starts), raw, -1e30)


def attend_kernel(query, kv, start, out, logsum):
    chunk = own_chunk(pl.program_id(0))
    stacked = (stacked_low(query[0]) * (1.0 / HEAD_DIM**0.5)).astype(BF)
    starts = jnp.concatenate([start[0]] * GROUP, axis=1)

    def step(kc, size, masked, carry):
        top, summed, total = carry
        keys = kv[pl.ds(kc, size)].reshape(size * TOK, 128)
        scores = chunk_scores(keys, stacked, kc, chunk, starts, masked)
        new_top = jnp.maximum(top, jnp.max(scores, axis=0, keepdims=True))
        weights = jnp.exp(scores - new_top)
        fade = jnp.exp(top - new_top)
        summed = summed * fade + jnp.sum(weights, axis=0, keepdims=True)
        part = tn(keys, weights.astype(BF))
        return new_top, summed, total * fade + part[HEAD_DIM:]

    rows = GROUP * TOK
    carry = (jnp.full((1, rows), -1e30, F32), jnp.zeros((1, rows), F32), jnp.zeros((64, rows), F32))
    top, summed, total = over_chunks(start[0], chunk, step, carry)
    for pair, tile in enumerate(unstacked(total / summed)):
        out[0, :, 128 * pair : 128 * pair + 128] = tile.astype(BF)
    logsum[0] = top + jnp.log(summed)


def attend(query, kv, start):
    chunk = lambda r, cols: pl.BlockSpec((1, r, cols), lambda i: (i, 0, 0))
    return pl.pallas_call(
        attend_kernel,
        name="attend",
        cost_estimate=cost(12),
        grid=(RING,),
        in_specs=[
            chunk(TOK, QZ),
            pl.BlockSpec((16, TOK, 128), lambda i: (0, 0, 0)),
            chunk(1, TOK),
        ],
        out_specs=[chunk(TOK, QZ), chunk(1, GROUP * TOK)],
        out_shape=[
            jax.ShapeDtypeStruct((RING, TOK, QZ), BF),
            jax.ShapeDtypeStruct((RING, 1, GROUP * TOK), F32),
        ],
        compiler_params=PARAMS,
    )(query, kv, start)


def attend_back_kernel(
    query, kv, start, out, grad_out, logsum, cosine, sine, dquery, dkv, total
):
    i = pl.program_id(0)
    chunk = own_chunk(i)
    stacked = (stacked_low(query[0]) * (1.0 / HEAD_DIM**0.5)).astype(BF)
    grads = stacked_high(grad_out[0]).astype(BF)
    starts = jnp.concatenate([start[0]] * GROUP, axis=1)
    lse = logsum[0]
    deltas = []
    for pair in range(4):
        cols = slice(128 * pair, 128 * pair + 128)
        prod = (out[0, :, cols].astype(F32) * grad_out[0, :, cols].astype(F32)).T
        deltas.append(jnp.sum(prod[:HEAD_DIM], axis=0, keepdims=True))
        deltas.append(jnp.sum(prod[HEAD_DIM:], axis=0, keepdims=True))
    delta = jnp.concatenate(deltas, axis=1)

    @pl.when(i == 0)
    def _():
        total[...] = jnp.zeros_like(total)

    def step(kc, size, masked, dq):
        keys = kv[pl.ds(kc, size)].reshape(size * TOK, 128)
        scores = chunk_scores(keys, stacked, kc, chunk, starts, masked)
        probs = jnp.exp(scores - lse)
        grad_probs = nt(keys, grads)
        grad_scores = (probs * (grad_probs - delta)).astype(BF)
        part = dot(grad_scores, stacked) + dot(probs.astype(BF), grads)
        total[pl.ds(kc, size)] += part.reshape(size, TOK, 128)
        return dq + tn(keys, grad_scores)[:HEAD_DIM]

    dq = over_chunks(start[0], chunk, step, jnp.zeros((64, GROUP * TOK), F32))
    cos, sin = cosine[0], sine[0]
    for pair, tile in enumerate(unstacked(dq)):
        tile = tile * (1.0 / HEAD_DIM**0.5)
        dquery[0, :, 128 * pair : 128 * pair + 128] = (tile * cos - swapped(tile) * sin).astype(BF)

    @pl.when(i == RING - 1)
    def _():
        dkv[...] = total[...].astype(BF)


def attend_back(query, kv, start, out, grad_out, logsum, cosine, sine):
    chunk = lambda r, cols: pl.BlockSpec((1, r, cols), lambda i: (i, 0, 0))
    whole = pl.BlockSpec((16, TOK, 128), lambda i: (0, 0, 0))
    return pl.pallas_call(
        attend_back_kernel,
        name="attend_back",
        cost_estimate=cost(15),
        grid=(RING,),
        in_specs=[
            chunk(TOK, QZ),
            whole,
            chunk(1, TOK),
            chunk(TOK, QZ),
            chunk(TOK, QZ),
            chunk(1, GROUP * TOK),
            chunk(TOK, 128),
            chunk(TOK, 128),
        ],
        out_specs=[chunk(TOK, QZ), whole],
        scratch_shapes=[pltpu.VMEM((16, TOK, 128), F32)],
        out_shape=[
            jax.ShapeDtypeStruct((RING, TOK, QZ), BF),
            jax.ShapeDtypeStruct((16, TOK, 128), BF),
        ],
        compiler_params=PARAMS,
    )(query, kv, start, out, grad_out, logsum, cosine, sine)


def rms_back(v, gain, grad):
    scale = lax.rsqrt(jnp.mean(v * v, axis=-1, keepdims=True) + EPS)
    unit = v * scale
    gain_grad = jnp.sum(grad * unit, axis=0, keepdims=True)
    inner = grad * gain
    return scale * (inner - unit * jnp.mean(inner * unit, axis=-1, keepdims=True)), gain_grad


def finish_kernel(
    a, b, g1, g3, g2, go, gq, gkv, gains, out, grad, gate, up, down, proj, qkv, gain1, gain2
):
    gain1[...] = gains[0]
    gain2[...] = gains[1]
    out[...] = a[...]
    grad[...] = b[...]
    for src, dst in ((g1, gate), (g3, up), (g2, down), (go, proj)):
        dst[...] = src[...].astype(F32)
    qkv[:, :QDIM] = gq[...].astype(F32)
    kv = gkv[...].astype(F32)
    tiles = [kv[:, 128 * j : 128 * j + 128] for j in range(4)]
    lane = lax.broadcasted_iota(jnp.int32, tiles[0].shape, 1)
    for j in range(2):
        one, two = tiles[2 * j], tiles[2 * j + 1]
        keys = jnp.where(lane < HEAD_DIM, one, pltpu.roll(two, 64, 1))
        values = jnp.where(lane < HEAD_DIM, pltpu.roll(one, 64, 1), two)
        qkv[:, QDIM + 128 * j : QDIM + 128 * j + 128] = keys
        qkv[:, QDIM + KVDIM + 128 * j : QDIM + KVDIM + 128 * j + 128] = values


def finish(*arrays):
    steps = 4
    spec = lambda v: pl.BlockSpec((v.shape[0] // steps, v.shape[1]), lambda i: (i, 0))
    outs = [jax.ShapeDtypeStruct(v.shape, F32) for v in arrays[:-3]]
    outs.append(jax.ShapeDtypeStruct((256, QDIM + 2 * KVDIM), F32))
    gain = jax.ShapeDtypeStruct((256,), F32)
    return pl.pallas_call(
        finish_kernel,
        name="finish",
        cost_estimate=cost(12),
        grid=(steps,),
        in_specs=[spec(v) for v in arrays[:-1]] + [pl.BlockSpec((8, 256), lambda i: (0, 0))],
        out_specs=[spec(v) for v in outs] + [pl.BlockSpec((256,), lambda i: (0,))] * 2,
        out_shape=outs + [gain] * 2,
        compiler_params=PARAMS,
    )(*arrays)


def pick(v, index, axis=0):
    return lax.dynamic_index_in_dim(v, index, axis, keepdims=False)


def dot(a, b):
    return jnp.dot(a, b, preferred_element_type=F32)


def body(tokens, segments, cotangent, norm_attn, norm_ffn, wqkv, wo, w1, w3, w2):
    q = coords()
    y, xx, xl, z, c = q["y"], q["x"], q["xl"], q["z"], q["c"]
    x = tokens[0]
    g = cotangent[0]
    freq = THETA ** (-(np.arange(128) % 32) * 2.0 / HEAD_DIM)
    freq = jnp.asarray(freq[None], F32)
    table = ((RING, TOK, 128), F32)
    G, WQ, WO, W13, t2, n1, query, KV, cosine, sine, start, gain_attn, gain_ffn = talk(
        front_kernel,
        "front",
        1,
        46,
        120,
        (
            x, g, segments, norm_attn, norm_ffn, freq,
            wqkv, wo, w1, w3, w2,
        ),
        [
            ((RING, TOK, D), BF),
            ((2, 4, 2, 2, 64, MZ), BF),
            ((2, 256, D), BF),
            ((2, 4, 2, 2, 64, 2 * FZ), BF),
            ((704, 128), BF),
            ((RING, TOK, D), BF),
            ((RING, TOK, QZ), BF),
            ((2, 4, 2, TOK, 128), BF),
            table,
            table,
            ((RING, 1, TOK), jnp.int32),
            ((1, D), F32),
            ((1, D), F32),
        ],
        scratch=[
            pltpu.VMEM((256, 128), BF),
            pltpu.VMEM((704, 128), BF),
            pltpu.VMEM((64, MZ), BF),
            pltpu.VMEM((64, 128), BF),
            pltpu.VMEM((64, 128), BF),
            pltpu.VMEM((64, FZ), BF),
            pltpu.VMEM((64, FZ), BF),
            pltpu.VMEM((8, TOK), jnp.int32),
            pltpu.VMEM((32, 256), BF),
            pltpu.VMEM((2, 4, 2, 8, TOK), jnp.int32),
            pltpu.VMEM((4, 2, 32, 256), BF),
            pltpu.VMEM((RING, TOK, D), BF),
            pltpu.VMEM((2, 4, 2, 2, 64, MZ), BF),
            pltpu.VMEM((RING, TOK, D), BF),
            pltpu.VMEM((RING, TOK, QZ), BF),
            pltpu.VMEM((RING, TOK, 128), BF),
        ],
        near=tuple(range(6)),
        near_out=(8, 9, 10, 11, 12),
    )
    WQ = WQ.reshape(D, MZ)
    WO = WO.reshape(QZ, D)
    KV = KV.reshape(16, TOK, 128)
    heads_out, logsum = attend(query, KV, start)
    o = heads_out.reshape(RING * TOK, QZ)
    rest = 2 * FZ - SPLIT
    buffers = []
    for shape in ((704, 256), (2, 64, SPLIT), (2, 64, rest)):
        buffers += [pltpu.VMEM((2,) + shape, BF)] * 4
    chunks = pltpu.VMEM((RING, TOK, D), BF)
    DH, fa, fb, f2, dheads, output, dh, gain2 = talk(
        core_kernel,
        "core",
        3,
        120,
        150,
        (heads_out, x, gain_ffn, t2, W13, WO, G),
        [
            ((RING, TOK, D), BF),
            ((2, 2, 64, SPLIT), BF),
            ((2, 2, 64, rest), BF),
            ((2, 704, 256), BF),
            ((RING * TOK, QZ), BF),
            ((TOK, D), F32),
            ((TOK, D), F32),
            ((1, D), F32),
        ],
        scratch=[
            pltpu.VMEM((2, 4, 2, 2, 64, 2 * FZ), BF),
            pltpu.VMEM((FZ, D), BF),
            chunks,
            chunks,
            pltpu.VMEM((RING * TOK, FZ), BF),
            pltpu.VMEM((FZ, RING * TOK), BF),
            pltpu.VMEM((RING * TOK, 2 * FZ), BF),
            chunks,
            chunks,
            pltpu.VMEM((QZ, D), BF),
            pltpu.VMEM((RING, TOK, QZ), BF),
            chunks,
            pltpu.VMEM((TOK, D), F32),
            pltpu.VMEM((TOK, D), BF),
            *[pltpu.VMEM(HALF, BF)] * 8,
            *[pltpu.VMEM((TOK, D), BF)] * 4,
            *buffers,
            pltpu.SemaphoreType.REGULAR((2,)),
        ],
        near=(2,),
        near_out=(4, 5, 6, 7),
    )
    fa, fb = fa.reshape(4, 64, SPLIT), fb.reshape(4, 64, rest)
    f2 = f2.reshape(1408, 256)
    DH = DH.reshape(RING * TOK, D)
    dquery, dkv = attend_back(
        query, KV, start, heads_out, dheads.reshape(RING, TOK, QZ), logsum, cosine, sine
    )
    small = (8, 256)
    input_grad, G1, G3, G2, GO, GQ, GKV, gain_out = talk(
        tail_kernel,
        "tail",
        6,
        75,
        170,
        (
            dkv.reshape(2, 4, 2, TOK, 128), dquery, cosine, sine, x, dh, gain_attn, gain2,
            fa, fb, f2, WQ, n1.reshape(RING * TOK, D), o, DH,
        ),
        [
            ((TOK, D), F32),
            ((256, 4 * FZ), BF),
            ((256, 4 * FZ), BF),
            ((704, D), BF),
            ((256, D), BF),
            ((256, QDIM), BF),
            ((256, 2 * KVDIM), BF),
            (small, F32),
        ],
        scratch=[
            pltpu.VMEM((D, MZ), BF),
            pltpu.VMEM((RING * TOK, D), BF),
            pltpu.VMEM((RING * TOK, QZ), BF),
            pltpu.VMEM((RING * TOK, D), BF),
            pltpu.VMEM((4, RING, TOK, 128), BF),
            pltpu.VMEM((RING, TOK, MZ), BF),
            pltpu.VMEM((RING, TOK, D), BF),
            *[pltpu.VMEM(HALF, BF)] * 4,
            *[pltpu.VMEM((TOK, D), BF)] * 2,
            *[pltpu.VMEM((4, QZ, 256), BF)] * 2,
            *[pltpu.VMEM((4, 4, 64, MZ), BF)] * 2,
            *[pltpu.VMEM((2, 256, 256), BF)] * 4,
            *[pltpu.VMEM((2, 2, 64, MZ), BF)] * 4,
            pltpu.VMEM((3, 64, SPLIT), BF),
            pltpu.VMEM((3, 64, rest), BF),
            pltpu.VMEM((3, 704, 128), BF),
            pltpu.VMEM((64, SPLIT), BF),
            pltpu.VMEM((64, rest), BF),
            pltpu.VMEM((704, 128), BF),
            pltpu.VMEM((704, 128), BF),
            pltpu.VMEM((3, 256, 128), BF),
            pltpu.VMEM((3, 64, MZ), BF),
            pltpu.VMEM((512, 256), BF),
            pltpu.VMEM((4, 64, MZ), BF),
            pltpu.VMEM((256, 128), BF),
            pltpu.VMEM((64, MZ), BF),
            pltpu.VMEM((256, 128), BF),
            pltpu.VMEM((4, 2) + small, F32),
            pltpu.VMEM((4, 2) + small, F32),
            pltpu.VMEM((2, 2) + small, F32),
            pltpu.VMEM((4,) + small, F32),
            pltpu.VMEM((2,) + small, F32),
            pltpu.VMEM((2,) + small, F32),
            pltpu.VMEM(small, F32),
            *[pltpu.VMEM((RING, TOK, 128), BF)] * 2,
            *[pltpu.VMEM((RING, TOK, 128), F32)] * 2,
            pltpu.VMEM((TOK, D), BF),
            pltpu.VMEM((TOK, D), F32),
            pltpu.VMEM((64, SPLIT), BF),
            pltpu.VMEM((64, rest), BF),
            pltpu.VMEM((704, 128), BF),
        ],
        near=(6, 7),
        near_out=(0,),
    )
    output, input_grad, gate_grad, up_grad, down_grad, out_grad, qkv_grad, gain1, gain2 = finish(
        output, input_grad, G1, G3, G2, GO, GQ, GKV, gain_out
    )
    return (
        output[None],
        input_grad[None],
        gain1,
        gain2,
        qkv_grad,
        out_grad,
        gate_grad,
        up_grad,
        down_grad,
    )


def solution(mesh):
    rows = P("dp", None)
    acts = P("dp", "ctx", None)
    return jax.shard_map(
        body,
        mesh=mesh,
        in_specs=(acts, P("dp", "ctx"), acts, P("dp"), P("dp"), rows, rows, rows, rows, rows),
        out_specs=(acts, acts, P("dp"), P("dp"), rows, rows, rows, rows, rows),
        check_vma=False,
    )
```

```python
import functools

import jax
import jax.numpy as jnp
import numpy as np
from jax import lax
from jax.experimental import pallas as pl
from jax.experimental.pallas import tpu as pltpu
from jax.sharding import PartitionSpec as P

D = 2048
HEAD_DIM = 64
TOK = 128
RING = 4
QDIM = 2048
KVDIM = 256
GROUP = 8
QZ = 512
MZ = 640
FZ = 1408
SPLIT = 1536
EPS = 1e-05
THETA = 10000.0
MESH = pl.DeviceIdType.MESH
VMEM_LIMIT = 60 << 20
BF = jnp.bfloat16
F32 = jnp.float32
ANY = pl.BlockSpec(memory_space=pl.ANY)
VMEM = pl.BlockSpec(memory_space=pltpu.VMEM)


def coords():
    dp, ctx = lax.axis_index("dp"), lax.axis_index("ctx")
    y, xh = dp // 2, dp % 2
    xl, z, c = ctx // 8, (ctx // 2) % 4, ctx % 2
    return dict(y=y, x=xh * 2 + xl, xh=xh, xl=xl, z=z, c=c)


def device(q, **change):
    r = {k: change.get(k, q[k]) for k in ("y", "x", "z", "c")}
    return (r["y"] * 2 + r["x"] // 2, (r["x"] % 2) * 8 + r["z"] * 2 + r["c"])


def ring(q, axis):
    return [device(q, **{axis: (q[axis] + s) % 4}) for s in (1, 3, 2)]


def shift_pairs(axis, by):
    size = 2 if axis == "c" else 4
    pairs = []
    for y in range(4):
        for x in range(4):
            for z in range(4):
                for c in range(2):
                    q = dict(y=y, x=x, z=z, c=c)
                    pairs.append((device(q), device(q, **{axis: (q[axis] + by) % size})))
    return [(a[0] * 16 + a[1], b[0] * 16 + b[1]) for a, b in pairs]


def swap_pairs():
    pairs = []
    for y in range(4):
        for x in range(4):
            for z in range(4):
                for c in range(2):
                    q = dict(y=y, x=x, z=z, c=c)
                    pairs.append((device(q), device(q, y=z, z=y)))
    return [(a[0] * 16 + a[1], b[0] * 16 + b[1]) for a, b in pairs]


def move(v, axis, by):
    return lax.ppermute(v, ("dp", "ctx"), shift_pairs(axis, by))


class Copies:
    def __init__(self, send_sems, recv_sems):
        self.send_sems, self.recv_sems, self.n, self.open = send_sems, recv_sems, 0, []

    def send(self, src, dst, to):
        cp = pltpu.make_async_remote_copy(
            src_ref=src,
            dst_ref=dst,
            send_sem=self.send_sems.at[self.n],
            recv_sem=self.recv_sems.at[self.n],
            device_id=to,
            device_id_type=MESH,
        )
        cp.start()
        self.n += 1
        self.open.append(cp)
        return cp

    def local(self, src, dst):
        cp = pltpu.make_async_copy(src, dst, self.send_sems.at[self.n])
        cp.start()
        self.n += 1
        return cp

    def close(self):
        for cp in self.open:
            cp.wait_send()
        self.open = []


def deal(k, q, src, col, dst):
    y, z = q["y"], q["z"]
    n = k.n
    k.n += 4
    copies = [
        pltpu.make_async_remote_copy(
            src_ref=src.at[:, col((y + s) % 4)],
            dst_ref=dst,
            send_sem=k.send_sems.at[n + i],
            recv_sem=k.recv_sems.at[n],
            device_id=to,
            device_id_type=MESH,
        )
        for i, (s, to) in enumerate(zip((1, 3, 2), ring(q, "y")))
    ]
    here = pltpu.make_async_copy(src.at[:, col(y)], dst, k.send_sems.at[n + 3])

    @pl.when(y == z)
    def _():
        for cp in copies:
            cp.start()
        here.start()

    def wait():
        @pl.when(y == z)
        def _():
            for cp in copies:
                cp.wait_send()
            here.wait()

        @pl.when(y != z)
        def _():
            copies[0].wait_recv()

    return wait


def greet(targets, q=None):
    barrier = pltpu.get_barrier_semaphore()
    for to in targets:
        pl.semaphore_signal(barrier, inc=1, device_id=to, device_id_type=MESH)
    if q is None:
        pl.semaphore_wait(barrier, len(targets))
    else:
        y, z = q["y"], q["z"]

        @pl.when(y != z)
        def _():
            to = device(q, y=z, z=y)
            pl.semaphore_signal(barrier, inc=1, device_id=to, device_id_type=MESH)

        pl.semaphore_wait(barrier, len(targets) + (y != z).astype(jnp.int32))


TOP, LOW = pl.ds(0, TOK // 2), pl.ds(TOK // 2, TOK // 2)
HALF = (TOK // 2, D)


class Gather:
    def __init__(self, k, q, axis, src, dst):
        at = q[axis]
        self.k, self.dst = k, dst
        self.above, self.below, self.far = (at + 1) % 4, (at + 3) % 4, (at + 2) % 4
        self.up, self.down = device(q, **{axis: self.above}), device(q, **{axis: self.below})
        self.low0 = k.send(src(0), dst(at, 0), self.up)
        self.top1 = k.send(src(1), dst(at, 1), self.down)
        self.low1 = k.send(src(1), dst(at, 1), self.up)
        self.top0 = k.send(src(0), dst(at, 0), self.down)

        self.waiting = {0: self.low0, 1: self.top1}

    def arrived(self, half):
        cp = self.waiting.pop(half, None)
        if cp is not None:
            cp.wait_recv()

    def relay(self):
        self.arrived(0)
        ref = self.dst(self.below, 0)
        self.far0 = self.k.send(ref, ref, self.up)
        self.arrived(1)
        ref = self.dst(self.above, 1)
        self.far1 = self.k.send(ref, ref, self.down)

    def near(self):
        self.arrived(0)
        self.arrived(1)
        self.low1.wait_recv()
        self.top0.wait_recv()

    def end(self):
        self.far0.wait_recv()
        self.far1.wait_recv()


class Sum:
    def __init__(self, k, q, axis, block, below, above, passed):
        at = q[axis]
        self.k, self.below, self.above, self.passed = k, below, above, passed
        up, down, far = (at + 1) % 4, (at + 3) % 4, (at + 2) % 4
        self.up, self.down = device(q, **{axis: up}), device(q, **{axis: down})
        self.first = k.send(block(far, 0), passed[0], self.up)
        self.second = k.send(block(far, 1), passed[1], self.down)
        self.rest = [
            k.send(block(up, 1), below(1), self.up),
            k.send(block(down, 0), above(0), self.down),
        ]

    def relay(self, own0, own1, sent):
        self.first.wait_recv()
        sent[0][...] = (self.passed[0][...].astype(F32) + own0[...].astype(F32)).astype(BF)
        self.rest.append(self.k.send(sent[0], self.below(0), self.up))
        self.second.wait_recv()
        sent[1][...] = (self.passed[1][...].astype(F32) + own1[...].astype(F32)).astype(BF)
        self.rest.append(self.k.send(sent[1], self.above(1), self.down))

    def end(self):
        for cp in self.rest:
            cp.wait_recv()


def halves(ref):
    return lambda h: ref.at[(TOP, LOW)[h]]


def ring_halves(ref):
    return lambda j, h: ref.at[j, (TOP, LOW)[h]]


def turn(k, q, moves):
    y, z = q["y"], q["z"]
    swap = device(q, y=z, z=y)
    pairs = []
    for src, dst in moves:
        n = k.n
        k.n += 1
        remote = pltpu.make_async_remote_copy(
            src_ref=src,
            dst_ref=dst,
            send_sem=k.send_sems.at[n],
            recv_sem=k.recv_sems.at[n],
            device_id=swap,
            device_id_type=MESH,
        )
        pairs.append((remote, pltpu.make_async_copy(src, dst, k.send_sems.at[n])))

    @pl.when(y != z)
    def _():
        for remote, _ in pairs:
            remote.start()

    @pl.when(y == z)
    def _():
        for _, here in pairs:
            here.start()

    def wait():
        @pl.when(y != z)
        def _():
            for remote, _ in pairs:
                remote.wait_recv()
                remote.wait_send()

        @pl.when(y == z)
        def _():
            for _, here in pairs:
                here.wait()

    return wait


def cost(us):
    return pl.CostEstimate(flops=int(us * 1e9), bytes_accessed=0, transcendentals=0)


def talk(kernel, name, cid, us, copies, ins, outs, scratch=(), near=(), near_out=(), alias={}):
    return pl.pallas_call(
        kernel,
        name=name,
        out_shape=[jax.ShapeDtypeStruct(s, t) for s, t in outs],
        in_specs=[VMEM if i in near else ANY for i in range(len(ins))],
        out_specs=[VMEM if i in near_out else ANY for i in range(len(outs))],
        scratch_shapes=[
            *scratch,
            pltpu.SemaphoreType.DMA((copies,)),
            pltpu.SemaphoreType.DMA((copies,)),
        ],
        cost_estimate=cost(us),
        input_output_aliases=alias,
        compiler_params=pltpu.CompilerParams(
            collective_id=cid, has_side_effects=True, vmem_limit_bytes=VMEM_LIMIT
        ),
    )(*ins)


def front_kernel(
    x, g, seg, na, nf, freq, wq, wo, w1, w3, w2,
    G, WQ, WO, W13, T2, N1, Q, KV, COS, SIN, START, GA, GF,
    TO, TV, QP, KT, VT, P1, P3, SG, NG, SEGS, GN, XV, WV, NV, QV, KVV, ss, rs,
):
    q = coords()
    y, xx, xh, xl, z, c = q["y"], q["x"], q["xh"], q["xl"], q["z"], q["c"]
    zs, ys, xs = ring(q, "z"), ring(q, "y"), ring(q, "x")
    mate = device(q, c=1 - c)
    other = device(q, x=xx ^ 1)
    other_mate = device(q, x=xx ^ 1, c=1 - c)
    k = Copies(ss, rs)
    rows = pl.ds(pl.multiple_of(128 * c + 64 * xl, 64), 64)
    qcols = pl.ds(pl.multiple_of(QZ * z, 128), QZ)
    tile = 128 * (z // 2)
    kcols = pl.ds(pl.multiple_of(QDIM + tile, 128), 128)
    vcols = pl.ds(pl.multiple_of(QDIM + KVDIM + tile, 128), 128)
    fcols = pl.ds(pl.multiple_of(FZ * z, 128), FZ)
    loads = [
        k.local(wq.at[rows, qcols], QP.at[:, pl.ds(0, QZ)]),
        k.local(wq.at[rows, kcols], KT),
        k.local(wq.at[rows, vcols], VT),
        k.local(w1.at[rows, fcols], P1),
        k.local(w3.at[rows, fcols], P3),
    ]
    SG[...] = jnp.broadcast_to(seg[...], (8, TOK))
    NG[0:16] = jnp.broadcast_to(na[...].astype(F32)[None], (16, 256)).astype(BF)
    NG[16:32] = jnp.broadcast_to(nf[...].astype(F32)[None], (16, 256)).astype(BF)
    greet(zs + ys + xs + [mate, other_mate])
    seg_z = [k.send(SG, SEGS.at[xl, z, c], to) for to in zs]
    x_ring = Gather(k, q, "z", halves(x), ring_halves(XV))
    lanes = lambda j, n=1: pl.ds(pl.multiple_of(128 * j, 128 * n), 128 * n)
    dealt = deal(k, q, wo, lambda j: lanes(c * 8 + j * 2 + xl), TO)
    for cp in loads:
        cp.wait()
    odd = z % 2 == 1
    kt, vt = KT[...].astype(F32), VT[...].astype(F32)
    lane = lax.broadcasted_iota(jnp.int32, kt.shape, 1)
    kt = jnp.where(odd, pltpu.roll(kt, 64, 1), kt)
    vt = jnp.where(odd, vt, pltpu.roll(vt, 64, 1))
    QP[:, QZ:] = jnp.where(lane < HEAD_DIM, kt, vt).astype(BF)
    f1, f3 = pl.ds(0, FZ), pl.ds(FZ, FZ)
    top, low = pl.ds(0, 32), pl.ds(32, 32)
    thirty = lambda h: pl.ds(32 * h, 32)
    q_top = [k.send(QP.at[top], WV.at[c, y, xh, xl, top], to) for to in xs]
    q_low = [k.send(QP.at[low], WV.at[c, y, xh, xl, low], to) for to in ys]
    gn_y = [k.send(NG, GN.at[y, xh], to) for to in ys]
    up_y = Gather(
        k, q, "y", lambda h: P3.at[thirty(h)], lambda j, h: W13.at[c, j, xh, xl, thirty(h), f3]
    )
    gate_x = Gather(
        k, q, "x", lambda h: P1.at[thirty(h)],
        lambda j, h: W13.at[c, y, j // 2, j % 2, thirty(h), f1],
    )
    q_here = k.local(QP, WV.at[c, y, xh, xl])
    seg_here = k.local(SG, SEGS.at[xl, z, c])
    gn_here = k.local(NG, GN.at[y, xh])
    x_here = k.local(x, XV.at[z])
    up_here = k.local(P3, W13.at[c, y, xh, xl, :, f3])
    heres = [k.local(P1, W13.at[c, y, xh, xl, :, f1]), k.local(g, G.at[z])]
    dealt()
    o1 = [k.send(TO, WO.at[xh, :, lanes(c * 8 + y * 2 + xl)], to) for to in xs]
    o1_here = k.local(TO, WO.at[xh, :, lanes(c * 8 + y * 2 + xl)])
    for cp in seg_z:
        cp.wait_recv()
    seg_here.wait()
    part = SEGS.at[xl, :, c]
    seg2 = [k.send(part, part, to) for to in (mate, other, other_mate)]
    q_here.wait()
    for cp in q_top:
        cp.wait_recv()
    q_y = Gather(k, q, "y", lambda h: WV.at[c, y, h, :, top], lambda j, h: WV.at[c, j, h, :, top])
    for cp in gn_y:
        cp.wait_recv()
    gn_here.wait()
    gn2 = k.send(GN.at[:, xh], GN.at[:, xh], device(q, x=3 - xx))
    gate_x.relay()
    for cp in q_low:
        cp.wait_recv()
    q_half = lambda j, h: WV.at[c, pl.ds(2 * h, 2), j // 2, j % 2, low]
    q_x = Gather(k, q, "x", lambda h: q_half(xx, h), q_half)
    x_ring.relay()
    g_ring = Gather(k, q, "z", halves(g), ring_halves(G))
    up_y.relay()
    for cp in o1:
        cp.wait_recv()
    o1_here.wait()
    o_half = lambda j, h: WO.at[h, :, lanes(c * 8 + j * 2, 2)]
    o_y = Gather(k, q, "y", lambda h: o_half(y, h), o_half)
    for cp in seg2:
        cp.wait_recv()
    docs = [SEGS[i // 8, (i // 2) % 4, i % 2, 0:1].astype(F32) for i in range(16)]
    columns = jnp.concatenate(docs + [jnp.zeros((TOK - 16, TOK), F32)], axis=0).T
    for i in range(RING):
        mine = SEGS[xl, i, c, 0:1].astype(F32)
        count = jnp.zeros((TOK, TOK), F32)
        for j in range(16):
            count = count + jnp.where(columns[:, j : j + 1] < mine, 1.0, 0.0)
        first = jnp.sum(count, axis=0, keepdims=True)
        START[i] = first.astype(jnp.int32)
        index = TOK * (8 * xl + 2 * i + c) + lax.broadcasted_iota(jnp.int32, (1, TOK), 1)
        place = index.astype(F32) - first
        angle = jnp.broadcast_to(place, (TOK, TOK)).T * freq[...]
        COS[i] = jnp.cos(angle)
        sine = jnp.sin(angle)
        lane = lax.broadcasted_iota(jnp.int32, sine.shape, 1)
        SIN[i] = jnp.where(lane % 64 < 32, -sine, sine)
    q_y.relay()
    w2_dealt = deal(k, q, w2, lambda j: lanes(c * 8 + xl * 4 + j), TV)
    q_x.relay()
    up_y.near()
    up_y.end()
    up_here.wait()
    part = W13.at[c, :, xh, xl, :, f3]
    a3 = [k.send(part, part, to) for to in xs[:2]]
    o_y.relay()
    gn2.wait_recv()
    whole = lambda r: jnp.concatenate(
        [GN[d // 2, d % 2, r : r + 1].astype(F32) for d in range(8)], axis=1
    )
    gain = whole(0)
    GA[...] = gain
    GF[...] = whole(16)
    x_ring.near()
    x_ring.end()
    x_here.wait()
    for i in range(RING):
        xv = XV[i].astype(F32)
        scale = lax.rsqrt(jnp.mean(xv * xv, axis=-1, keepdims=True) + EPS)
        NV[i] = to_pieces((xv * scale * gain).astype(BF))
    done = [k.local(NV, N1)]
    for r in (q_y, q_x):
        r.near()
        r.end()
    q3 = k.send(WV.at[c], WV.at[c], mate)
    w2_dealt()
    t_half = lambda h: pl.ds(352 * h, 352)
    t_y = Gather(k, q, "y", lambda h: TV.at[t_half(h)], lambda j, h: T2.at[j, t_half(h)])
    done.append(k.local(TV, T2.at[y]))
    g_ring.relay()
    q3.wait_recv()
    done.append(k.local(WV, WQ))
    mixed = dot(NV[...].reshape(RING * TOK, D), WV[...].reshape(D, MZ))
    for i in range(RING):
        cos, sin = COS[i], SIN[i]
        for j in range(5):
            u = mixed[TOK * i : TOK * i + TOK, 128 * j : 128 * j + 128]
            turned = u * cos + swapped(u) * sin
            if j < 4:
                QV[i, :, 128 * j : 128 * j + 128] = turned.astype(BF)
            else:
                lane = lax.broadcasted_iota(jnp.int32, u.shape, 1)
                KVV[i] = jnp.where(lane < HEAD_DIM, turned, u).astype(BF)
    near = k.send(KVV, KV.at[xl, :, c], mate)
    n = k.n
    k.n += 2
    far, on = [
        pltpu.make_async_remote_copy(
            src_ref=src,
            dst_ref=KV.at[0, :, c],
            send_sem=ss.at[n + i],
            recv_sem=rs.at[n + i],
            device_id=to,
            device_id_type=MESH,
        )
        for i, (src, to) in enumerate(((KVV, other), (KV.at[0, :, c], mate)))
    ]

    @pl.when(xl == 0)
    def _():
        far.start()

    done += [k.local(KVV, KV.at[xl, :, c]), k.local(QV, Q)]
    t_y.relay()
    o_y.near()
    o_y.end()
    part = WO.at[:, :, pl.ds(pl.multiple_of(1024 * c, 1024), 1024)]
    o3 = k.send(part, part, mate)

    @pl.when(xl == 0)
    def _():
        far.wait_send()

    @pl.when(xl == 1)
    def _():
        far.wait_recv()
        on.start()
        on.wait_recv()
        on.wait_send()

    near.wait_recv()
    for cp in a3 + [o3]:
        cp.wait_recv()
    for cp in heres + done:
        cp.wait()
    for r in (gate_x, g_ring, t_y):
        r.near()
        r.end()
    k.close()


def core_kernel(
    o, x, gain, t2, w13, wo_in, G, V, FA, FB, F2, DO, OUT, DH, GAIN, *scratch
):
    (
        W, W2, N2, gv, hv, hT, bv, part, outs, wo, ov, vv, hf, xb,
        p0, p1, p2, p3, v0, v1, v2, v3, below, above, out_below, out_above, *rest_of,
    ) = scratch
    bufs, (used, ss, rs) = rest_of[:-3], rest_of[-3:]
    q = coords()
    y, xx, xh, xl, z, c = q["y"], q["x"], q["xh"], q["xl"], q["z"], q["c"]
    ys, xs = ring(q, "y"), ring(q, "x")
    up, down = device(q, z=(z + 1) % 4), device(q, z=(z + 3) % 4)
    mate = device(q, c=1 - c)
    k = Copies(ss, rs)
    f1, f3 = pl.ds(0, FZ), pl.ds(FZ, FZ)
    lower, higher = (xx + 3) % 4, (xx + 1) % 4
    gate_at = lambda ref, j: ref.at[c, j, :, :, :, f1]
    gate_half = lambda ref, j, h: ref.at[c, j, h, :, :, f1]
    up_at = lambda ref, j: ref.at[c, :, j // 2, j % 2, :, f3]
    up_half = lambda ref, j, h: ref.at[c, pl.ds(2 * h, 2), j // 2, j % 2, :, f3]
    get_wo, get_o = k.local(wo_in, wo), k.local(o, ov)
    loads = [k.local(x, xb), k.local(gate_at(w13, y), gate_at(W, y))]
    loads += [k.local(up_at(w13, j), up_at(W, j)) for j in (xx, lower, higher)]
    cols = lambda j, n: pl.ds(pl.multiple_of(128 * (8 * c + j), 128 * n), 128 * n)
    frows = lambda j, h: pl.ds(pl.multiple_of(704 * (j // 2) + 352 * h, 32), 352)
    own_rows = pl.ds(pl.multiple_of(704 * xh, 64), 704)
    get_t = [k.local(t2.at[j], W2.at[own_rows, cols(xl * 4 + j, 1)]) for j in range(4)]
    get_g = k.local(G, gv)
    greet(ys + xs + [up, down, mate])
    gate = Gather(
        k, q, "y", lambda h: gate_half(w13, y, h), lambda j, h: gate_half(W, j, h)
    )
    for cp in get_t:
        cp.wait()
    down2 = lambda j: W2.at[
        pl.ds(pl.multiple_of(704 * (j // 2), 64), 704), cols((j % 2) * 4, 4)
    ]
    down_half = lambda j, h: W2.at[frows(j, h), cols((j % 2) * 4, 4)]
    down_ring = Gather(k, q, "x", lambda h: down_half(xx, h), down_half)
    sent_down = []
    sent = [k.send(up_at(w13, j), up_at(W, j), mate) for j in (xx, lower, higher)]
    sent.append(k.send(gate_at(w13, y), gate_at(W, y), mate))
    sent_down.append(k.send(down2(xx), down2(xx), mate))
    get_wo.wait()
    get_o.wait()
    rows = RING * TOK
    part[...] = dot(ov[...].reshape(rows, QZ), wo[...]).astype(BF).reshape(RING, TOK, D)

    def part_rows(i, h):
        return pl.ds(64 * i + 32 * h, 32)

    def sum_of(i):
        at = pl.ds(32 * i, 32)
        return Sum(
            k, q, "z", lambda j, h: part.at[j, part_rows(i, h)],
            lambda h: below.at[part_rows(i, h)], lambda h: above.at[part_rows(i, h)],
            (p0.at[at], p1.at[at]),
        )

    def relay_of(one, i):
        at = pl.ds(32 * i, 32)
        one.relay(
            part.at[(z + 1) % 4, part_rows(i, 0)], part.at[(z + 3) % 4, part_rows(i, 1)],
            (v0.at[at], v1.at[at]),
        )

    def gather_of(ref, i):
        return Gather(
            k, q, "z", lambda h: ref.at[z, part_rows(i, h)], lambda j, h: ref.at[j, part_rows(i, h)]
        )

    def summed(at):
        return part[z, at].astype(F32) + (below[at].astype(F32) + above[at].astype(F32))

    z_low = sum_of(0)
    relay_of(z_low, 0)
    z_high = sum_of(1)
    gate.relay()
    down_ring.relay()
    far = [
        k.send(up_half(w13, lower, 0), up_half(W, lower, 0), xs[0]),
        k.send(up_half(w13, higher, 1), up_half(W, higher, 1), xs[1]),
    ]
    relay_of(z_high, 1)
    for cp in loads:
        cp.wait()
    n2_rings = []
    for i, one in enumerate((z_low, z_high)):
        one.end()
        at = slice(64 * i, 64 * i + 64)
        total = xb[at].astype(F32) + summed(at)
        hf[at] = total
        scale = lax.rsqrt(jnp.mean(total * total, axis=-1, keepdims=True) + EPS)
        N2[z, at] = to_pieces((total * scale * gain[...]).astype(BF))
        n2_rings.append(gather_of(N2, i))
    n2_rings[0].relay()
    gate.near()
    for j in (gate.below, gate.above):
        sent.append(k.send(gate_at(W, j), gate_at(W, j), mate))
    down_ring.near()
    for j in (down_ring.below, down_ring.above):
        sent_down.append(k.send(down2(j), down2(j), mate))
    down_ring.end()
    sent_down.append(k.send(down2(down_ring.far), down2(down_ring.far), mate))
    n2_rings[1].relay()
    gate.end()
    sent.append(k.send(gate_at(W, gate.far), gate_at(W, gate.far), mate))
    for cp in far:
        cp.wait_recv()
    ref = up_at(W, (xx + 2) % 4)
    sent.append(k.send(ref, ref, mate))
    get_g.wait()
    for cp in sent_down:
        cp.wait_recv()
    tiles = [(256 * i, min(256 * i + 256, FZ)) for i in range(6)]
    gs = gv[...].reshape(rows, D)
    for a, b in tiles:
        bv[:, a:b] = nt(gs, W2[a:b]).astype(BF)
    for cp in sent:
        cp.wait_recv()
    for one in n2_rings:
        one.near()
        one.end()
    k.close()
    n2 = N2[...].reshape(rows, D)
    for a, b in tiles:
        gates = dot(n2, W[:, :, :, :, :, a:b].reshape(D, b - a))
        ups = dot(n2, W[:, :, :, :, :, FZ + a : FZ + b].reshape(D, b - a))
        sigma = jax.nn.sigmoid(gates)
        silu = gates * sigma
        hv[:, a:b] = (silu * ups).astype(BF)
        dhid = bv[:, a:b].astype(F32)
        bv[:, a:b] = (dhid * ups * sigma * (1.0 + gates * (1.0 - sigma))).astype(BF)
        bv[:, FZ + a : FZ + b] = (dhid * silu).astype(BF)
    for j in range(4):
        at = slice(512 * j, 512 * j + 512)
        outs[:, :, at] = dot(hv[...], W2[:, at]).astype(BF).reshape(RING, TOK, 512)
    out_sum = Sum(
        k, q, "z", ring_halves(outs), halves(out_below), halves(out_above), (p2, p3)
    )
    pl.semaphore_signal(used.at[0], inc=1, device_id=mate, device_id_type=MESH)
    half = lambda ref: lambda i: ref.at[i]
    rest = 2 * FZ - SPLIT
    jobs = [
        ("y", lambda j, i: W2.at[pl.ds(704 * i, 704), lanes(0, j)], F2),
        ("x", lambda j, i: W.at[0, pl.ds(2 * i, 2), j // 2, j % 2, :, pl.ds(0, SPLIT)], FA),
        ("y", lambda j, i: W.at[0, j, i, :, :, pl.ds(SPLIT, rest)], FB),
    ]
    sums, done = [], []
    lanes = lambda cc, j: pl.ds(pl.multiple_of(1024 * cc + 256 * j, 256), 256)

    def start(n):
        axis, block, _ = jobs[n]
        b = bufs[4 * n : 4 * n + 4]
        sums.append(Sum(k, q, axis, block, half(b[2]), half(b[3]), (b[0].at[0], b[0].at[1])))

    def relay(n):
        axis, block, _ = jobs[n]
        b = bufs[4 * n : 4 * n + 4]
        at = q[axis]
        sums[n].relay(block((at + 1) % 4, 0), block((at + 3) % 4, 1), (b[1].at[0], b[1].at[1]))

    def end(n):
        axis, block, out = jobs[n]
        b = bufs[4 * n : 4 * n + 4]
        sums[n].end()
        for i in range(2):
            total = block(q[axis], i)[...].astype(F32) + (
                b[2][i].astype(F32) + b[3][i].astype(F32)
            )
            b[2][i] = total.astype(BF)
        done.append(k.local(b[2], out))

    hT[...] = hv[...].T
    pl.semaphore_wait(used.at[0], 1)
    sent2, sent13 = [], []
    for j in range(4):
        W2[:, 1024 + 256 * j : 1280 + 256 * j] = dot(
            hT[...], gv[:, :, lanes(1 - c, j)].reshape(rows, 256)
        ).astype(BF)
        sent2.append(k.send(W2.at[:, lanes(1, j)], W2.at[:, lanes(0, j)], mate))
    for j in range(4):
        sent2[j].wait_recv()
        at = slice(256 * j, 256 * j + 256)
        own = dot(hT[...], gv[:, :, lanes(c, j)].reshape(rows, 256))
        W2[:, at] = (own + W2[:, at].astype(F32)).astype(BF)
    start(0)
    out_sum.relay(outs.at[(z + 1) % 4, TOP], outs.at[(z + 3) % 4, LOW], (v2, v3))
    for j in range(2):
        at = slice(1024 * j, 1024 * j + 1024)
        dn = nt(bv[...], W[j].reshape(1024, 2 * FZ))
        part[:, :, at] = dn.astype(BF).reshape(RING, TOK, 1024)
    z_sum = Sum(k, q, "z", ring_halves(part), halves(below), halves(above), (p0, p1))
    pl.semaphore_signal(used.at[1], inc=1, device_id=mate, device_id_type=MESH)
    pl.semaphore_wait(used.at[1], 1)
    shape = (2, 2, 64, 2 * FZ)
    for j in range(4):
        W[1, j] = tn(N2[:, :, lanes(1 - c, j)].reshape(rows, 256), bv[...]).astype(BF).reshape(shape)
        sent13.append(k.send(W.at[1, j], W.at[0, j], mate))
        if j == 0:
            relay(0)
    for j in range(4):
        sent13[j].wait_recv()
        own = tn(N2[:, :, lanes(c, j)].reshape(rows, 256), bv[...]).reshape(shape)
        W[0, j] = (own + W[0, j].astype(F32)).astype(BF)
        if j == 1:
            z_sum.relay(part.at[(z + 1) % 4, TOP], part.at[(z + 3) % 4, LOW], (v0, v1))
    start(1)
    start(2)
    end(0)
    z_sum.end()
    dn = from_pieces(
        part[z].astype(F32) + (below[...].astype(F32) + above[...].astype(F32))
    )
    back, gain_grad = rms_back(hf[...], gain[...], dn)
    total = gv[z].astype(F32) + back
    DH[...] = total
    GAIN[...] = gain_grad
    vv[z] = total.astype(BF)
    v_ring = Gather(k, q, "z", halves(vv.at[z]), ring_halves(vv))
    out_sum.end()
    OUT[...] = hf[...] + (
        outs[z].astype(F32) + (out_below[...].astype(F32) + out_above[...].astype(F32))
    )
    relay(1)
    relay(2)
    v_ring.relay()
    end(2)
    v_ring.near()
    v_ring.end()
    done.append(k.local(vv, V))
    DO[...] = nt(vv[...].reshape(rows, D), wo[...]).astype(BF)
    end(1)
    for cp in done:
        cp.wait()
    k.close()


def quarter(xt, rows):
    return (
        pl.ds(pl.multiple_of((xt // 2) * rows, rows), rows),
        pl.ds(pl.multiple_of((xt % 2) * 128, 128), 128),
    )


def tail_kernel(
    dkv, dq, cosine, sine, x, dh, gain, gain2, fa, fb, f2, wq, n1, o, dho,
    IG, G1, G3, G2, GO, GQ, GKV, gain_out, *scratch,
):
    (
        wv, nv, ov, gv, R, dm, dn, p0, p1, v0, v1, below, above, mate_o, sum_o, mate_q, sum_q,
        ob0, ob1, ob2, ob3, qb0, qb1, qb2, qb3, la, lb, l2, pa, pb, p2, t2, lo, lq, fo, fq,
        po, pq, to_, gains, s0, s1, s2, s3, s4, total,
        kv_own, kv_low, cv, sv, xv, dv, fav, fbv, f2v, ss, rs,
    ) = scratch
    q = coords()
    y, xx, xh, xl, z, c = q["y"], q["x"], q["xh"], q["xl"], q["z"], q["c"]
    zs, ys, xs = ring(q, "z"), ring(q, "y"), ring(q, "x")
    mate, other, cross = device(q, c=1 - c), device(q, x=xx ^ 1), device(q, x=3 - xx)
    other_mate = device(q, x=xx ^ 1, c=1 - c)
    steps = (1, 3, 2)
    rows_all = RING * TOK
    k = Copies(ss, rs)
    get_o, get_g = k.local(o, ov), k.local(dho, gv)
    r, cc = quarter(xx, 704)
    get_f = [k.local(fb.at[xx], fbv), k.local(fa.at[y], fav), k.local(f2.at[r, cc], f2v)]
    get_kv = [k.local(dkv.at[xl, :, c], kv_own), k.local(dkv.at[0, :, c], kv_low)]
    get_d = [
        k.local(dq, dm.at[:, :, pl.ds(0, QZ)]),
        k.local(cosine, cv),
        k.local(sine, sv),
        k.local(wq, wv),
    ]
    get_n = k.local(n1, nv)
    get_x = [k.local(x, xv), k.local(dh, dv)]
    greet(zs + ys + xs + [mate, other_mate], q)
    leg_b = [k.send(fb.at[(xx + s) % 4], lb.at[i], xs[i]) for i, s in enumerate(steps)]
    leg_a = [k.send(fa.at[(y + s) % 4], la.at[i], ys[i]) for i, s in enumerate(steps)]
    lanes = lambda cc, j: pl.ds(pl.multiple_of(1024 * cc + 256 * j, 256), 256)
    get_o.wait()
    get_g.wait()
    swaps = []
    for j in range(4):
        mate_o[j] = tn(ov[...], gv[:, lanes(1 - c, j)]).astype(BF)
        swaps.append(k.send(mate_o.at[j], sum_o.at[j], mate))
    leg_2 = []
    for i, s in enumerate(steps):
        r, cc = quarter((xx + s) % 4, 704)
        leg_2.append(k.send(f2.at[r, cc], l2.at[i], xs[i]))
    for j in range(4):
        swaps[j].wait_recv()
        sum_o[j] = (tn(ov[...], gv[:, lanes(c, j)]) + sum_o[j].astype(F32)).astype(BF)
    half = lambda ref: lambda h: ref.at[h]
    o_block = lambda j, h: sum_o.at[j, pl.ds(256 * h, 256)]
    q_block = lambda j, h: sum_q.at[j, pl.ds(2 * h, 2)]
    o_sum = Sum(k, q, "y", o_block, half(ob2), half(ob3), (ob0.at[0], ob0.at[1]))
    at = lambda zz, off, n: pl.ds(pl.multiple_of(FZ * zz + off, 128), n)
    rows = pl.ds(pl.multiple_of(128 * c + 64 * xl, 64), 64)
    pair = pl.ds(pl.multiple_of(128 * c, 128), 128)
    f1 = pl.ds(0, FZ)
    rest = SPLIT - FZ
    quarter_rows = lambda h: pl.ds(pl.multiple_of(128 * c + 64 * xl + 32 * h, 32), 32)

    def over_z(src, ref, off, n):
        return Gather(
            k, q, "z", lambda h: src.at[pl.ds(32 * h, 32)],
            lambda j, h: ref.at[quarter_rows(h), at(j, off, n)],
        )

    spans = [(G1, 0, FZ), (G3, 0, rest), (G3, rest, FZ - rest)]
    pieces = [pa.at[:, f1], pa.at[:, pl.ds(FZ, rest)], pb]
    block = lambda i, j: spans[i][0].at[rows, at(j, spans[i][1], spans[i][2])]
    rings, to_x, heres = [None] * 3, [], []

    def across(i, j):
        to_x.append(k.send(block(i, j), block(i, j), other))

    def own_across(i):
        to_x.append(k.send(pieces[i], block(i, z), other))
        heres.append(k.local(pieces[i], block(i, z)))

    def onward(i):
        rings[i].near()
        across(i, rings[i].below)
        across(i, rings[i].above)

    for cp in get_f:
        cp.wait()
    for cp in leg_b:
        cp.wait_recv()
    pb[...] = add4(fbv[...], lb[0], lb[1], lb[2])
    rings[2] = over_z(pieces[2], *spans[2])
    near = k.send(dkv.at[xl, :, 1 - c], R.at[0], mate)
    n = k.n
    k.n += 2
    pre, far = [
        pltpu.make_async_remote_copy(
            src_ref=src,
            dst_ref=dst,
            send_sem=ss.at[n + i],
            recv_sem=rs.at[n + i],
            device_id=to,
            device_id_type=MESH,
        )
        for i, (src, dst, to) in enumerate(
            ((dkv.at[0, :, 1 - c], R.at[1], mate), (R.at[2], R.at[3], other))
        )
    ]

    @pl.when(xl == 1)
    def _():
        pre.start()

    for cp in get_kv:
        cp.wait()
    rings[2].relay()
    o_sum.relay(o_block((y + 1) % 4, 0), o_block((y + 3) % 4, 1), (ob1.at[0], ob1.at[1]))

    @pl.when(xl == 1)
    def _():
        R[3] = jnp.zeros(R.shape[1:], BF)
        pre.wait()
        for i in range(RING):
            R[2, i] = (kv_low[i].astype(F32) + R[1, i].astype(F32)).astype(BF)
        far.start()

    for cp in leg_a:
        cp.wait_recv()
    pa[...] = add4(fav[...], la[0], la[1], la[2])
    rings[0] = over_z(pieces[0], *spans[0])
    rings[1] = over_z(pieces[1], *spans[1])
    for cp in leg_2:
        cp.wait_recv()
    p2[...] = add4(f2v[...], l2[0], l2[1], l2[2])
    turned = turn(k, q, [(p2, t2)])
    onward(2)
    own_across(2)

    @pl.when(xl == 1)
    def _():
        far.wait_send()

    @pl.when(xl == 0)
    def _():
        far.wait_recv()

    near.wait_recv()
    for cp in get_d:
        cp.wait()
    for i in range(RING):
        w = kv_own[i].astype(F32) + (R[0, i].astype(F32) + R[3, i].astype(F32))
        lane = lax.broadcasted_iota(jnp.int32, w.shape, 1)
        dm[i, :, QZ:] = jnp.where(
            lane < HEAD_DIM, w * cv[i] - swapped(w) * sv[i], w
        ).astype(BF)
    dmixed = dm[...].reshape(rows_all, MZ)
    dn[...] = nt(dmixed, wv[...]).astype(BF).reshape(RING, TOK, D)
    z_sum = Sum(k, q, "z", ring_halves(dn), halves(below), halves(above), (p0, p1))
    onward(0)
    rings[1].relay()
    get_n.wait()
    cols = lambda cc: pl.ds(pl.multiple_of(1024 * cc, 1024), 1024)
    shape = (4, 4, 64, MZ)
    mate_q[...] = tn(nv[:, cols(1 - c)], dmixed).astype(BF).reshape(shape)
    swap = k.send(mate_q, sum_q, mate)
    own = tn(nv[:, cols(c)], dmixed).reshape(shape)
    swap.wait_recv()
    sum_q[...] = (own + sum_q[...].astype(F32)).astype(BF)
    q_sum = Sum(k, q, "y", q_block, half(qb2), half(qb3), (qb0.at[0], qb0.at[1]))
    o_sum.end()
    for h in range(2):
        part = o_block(y, h)[...].astype(F32) + (ob2[h].astype(F32) + ob3[h].astype(F32))
        fo[pl.ds(256 * h, 256)] = part.astype(BF)
    leg_o, leg_q = [], []
    for i, s in enumerate(steps):
        r, cc = quarter((xx + s) % 4, 256)
        leg_o.append(k.send(fo.at[r, cc], lo.at[i], xs[i]))
    turned()
    col = pl.ds(pl.multiple_of(128 * (c * 8 + z * 2 + xl), 128), 128)
    down_x = k.send(t2, G2.at[:, col], other)
    down_here = k.local(t2, G2.at[:, col])
    z_sum.relay(dn.at[(z + 1) % 4, TOP], dn.at[(z + 3) % 4, LOW], (v0, v1))
    q_sum.relay(q_block((y + 1) % 4, 0), q_block((y + 3) % 4, 1), (qb1.at[0], qb1.at[1]))
    onward(1)
    for cp in leg_o:
        cp.wait_recv()
    r, cc = quarter(xx, 256)
    po[...] = add4(fo[r, cc], lo[0], lo[1], lo[2])
    o_turned = turn(k, q, [(po, to_)])
    q_sum.end()
    for h in range(2):
        part = q_block(y, h)[...].astype(F32) + (qb2[h].astype(F32) + qb3[h].astype(F32))
        fq[pl.ds(2 * h, 2)] = part.astype(BF)
    for i, s in enumerate(steps):
        leg_q.append(k.send(fq.at[(xx + s) % 4], lq.at[i], xs[i]))
    rings[1].end()
    across(1, rings[1].far)
    rings[0].relay()
    z_sum.end()
    for cp in get_x:
        cp.wait()
    back, gain1 = rms_back(
        xv[...].astype(F32),
        gain[...],
        from_pieces(dn[z].astype(F32) + (below[...].astype(F32) + above[...].astype(F32))),
    )
    IG[...] = dv[...] + back
    gains[...] = jnp.zeros_like(gains)
    for d in range(8):
        gains[d // 2, d % 2, 0:1] = gain1[:, 256 * d : 256 * d + 256]
        gains[d // 2, d % 2, 1:2] = gain2[:, 256 * d : 256 * d + 256]
    gain_y = [k.send(gains.at[(y + s) % 4], s0.at[y], ys[i]) for i, s in enumerate(steps)]
    gain_here = k.local(gains.at[y], s0.at[y])
    down_x.wait_recv()
    down_here.wait()
    down_half = lambda j, h: G2.at[
        pl.ds(352 * h, 352), pl.ds(pl.multiple_of(128 * (c * 8 + j * 2), 256), 256)
    ]
    down_ring = Gather(k, q, "z", lambda h: down_half(z, h), down_half)
    own_across(0)
    own_across(1)
    for cp in leg_q:
        cp.wait_recv()
    pq[...] = add4(fq[xx], lq[0], lq[1], lq[2])
    qc = lambda j: pl.ds(pl.multiple_of(QZ * j, 128), QZ)
    kc = lambda j: pl.ds(pl.multiple_of(128 * j, 128), 128)
    q_pieces = [
        (pq.at[:, pl.ds(0, QZ)], GQ.at[rows, qc(z)]),
        (pq.at[:, pl.ds(QZ, 128)], GKV.at[rows, kc(z)]),
    ]
    q_x = [k.send(src, dst, other) for src, dst in q_pieces]
    q_here = [k.local(src, dst) for src, dst in q_pieces]
    o_turned()
    o_x = k.send(to_, GO.at[:, col], other)
    o_here = k.local(to_, GO.at[:, col])
    for cp in gain_y:
        cp.wait_recv()
    gain_here.wait()
    s1[0] = (s0[0] + s0[1]) + (s0[2] + s0[3])
    gain_x = k.send(s1.at[0, 1 - xh], s1.at[1, 0], cross)
    gain_x.wait_recv()
    s2[z] = s1[0, xh] + s1[1, 0]
    gain_z = [k.send(s2.at[z], s2.at[z], to) for to in zs]
    down_ring.relay()
    rings[0].end()
    across(0, rings[0].far)
    o_x.wait_recv()
    o_here.wait()
    o_half = lambda j, h: GO.at[
        pl.ds(128 * h, 128), pl.ds(pl.multiple_of(128 * (c * 8 + j * 2), 256), 256)
    ]
    o_ring = Gather(k, q, "z", lambda h: o_half(z, h), o_half)
    for cp in q_x:
        cp.wait_recv()
    for cp in q_here:
        cp.wait()
    half_rows = lambda h: pl.ds(pl.multiple_of(128 * c + 64 * h, 64), 64)
    q_half = lambda j, h: GQ.at[half_rows(h), qc(j)]
    kv_half = lambda j, h: GKV.at[half_rows(h), kc(j)]
    q_rings = [
        Gather(k, q, "z", lambda h: q_half(z, h), q_half),
        Gather(k, q, "z", lambda h: kv_half(z, h), kv_half),
    ]
    rings[2].end()
    across(2, rings[2].far)
    down_ring.near()
    down_ring.end()
    last = [k.send(G2.at[:, cols(c)], G2.at[:, cols(c)], mate)]
    for cp in to_x:
        cp.wait_recv()
    for cp in heres:
        cp.wait()
    last += [k.send(ref.at[pair], ref.at[pair], mate) for ref in (G1, G3)]
    o_ring.relay()
    for cp in gain_z:
        cp.wait_recv()
    s3[0] = (s2[0] + s2[1]) + (s2[2] + s2[3])
    gain_x = k.send(s3.at[0], s3.at[1], other)
    for one in q_rings:
        one.relay()
    o_ring.near()
    o_ring.end()
    last.append(k.send(GO.at[:, cols(c)], GO.at[:, cols(c)], mate))
    gain_x.wait_recv()
    s4[0] = s3[0] + s3[1]
    gain_c = k.send(s4.at[0], s4.at[1], mate)
    for one in q_rings:
        one.near()
        one.end()
    last += [k.send(ref.at[pair], ref.at[pair], mate) for ref in (GQ, GKV)]
    gain_c.wait_recv()
    total[...] = s4[0] + s4[1]
    gain_done = k.local(total, gain_out)
    for cp in last:
        cp.wait_recv()
    gain_done.wait()
    k.close()


PARAMS = pltpu.CompilerParams(vmem_limit_bytes=VMEM_LIMIT)


def add4(a, b, c, d):
    a, b, c, d = (v.astype(F32) for v in (a, b, c, d))
    return ((a + b) + (c + d)).astype(BF)


def to_pieces(v):
    return jnp.concatenate(
        [v[:, 256 * d + 128 * c : 256 * d + 128 * c + 128] for c in range(2) for d in range(8)],
        axis=1,
    )


def from_pieces(v):
    return jnp.concatenate(
        [v[:, 1024 * c + 128 * d : 1024 * c + 128 * d + 128] for d in range(8) for c in range(2)],
        axis=1,
    )


def swapped(u):
    lane = lax.broadcasted_iota(jnp.int32, u.shape, 1)
    return jnp.where(lane % 64 < 32, pltpu.roll(u, 96, 1), pltpu.roll(u, 32, 1))


def stacked_low(tiles):
    out = []
    for pair in range(4):
        tile = tiles[:, 128 * pair : 128 * pair + 128].astype(F32)
        lane = lax.broadcasted_iota(jnp.int32, tile.shape, 1)
        out.append(jnp.where(lane < HEAD_DIM, tile, 0.0))
        out.append(jnp.where(lane < HEAD_DIM, pltpu.roll(tile, 64, 1), 0.0))
    return jnp.concatenate(out, axis=0)


def stacked_high(tiles):
    out = []
    for pair in range(4):
        tile = tiles[:, 128 * pair : 128 * pair + 128].astype(F32)
        lane = lax.broadcasted_iota(jnp.int32, tile.shape, 1)
        out.append(jnp.where(lane >= HEAD_DIM, pltpu.roll(tile, 64, 1), 0.0))
        out.append(jnp.where(lane >= HEAD_DIM, tile, 0.0))
    return jnp.concatenate(out, axis=0)


def unstacked(v):
    tiles = []
    for pair in range(4):
        both = jnp.concatenate(
            [v[:, 256 * pair : 256 * pair + 128], v[:, 256 * pair + 128 : 256 * pair + 256]],
            axis=0,
        )
        tiles.append(both.T)
    return tiles


def nt(a, b):
    return lax.dot_general(a, b, (((1,), (1,)), ((), ())), preferred_element_type=F32)


def tn(a, b):
    return lax.dot_general(a, b, (((0,), (0,)), ((), ())), preferred_element_type=F32)


def own_chunk(i):
    ctx = lax.axis_index("ctx")
    return (ctx // 8) * 8 + 2 * i + ctx % 2


def over_chunks(start, chunk, step, carry):
    first = start.astype(F32)
    low = jnp.min(first).astype(jnp.int32) // TOK
    high = jnp.minimum((jnp.max(first).astype(jnp.int32) + TOK - 1) // TOK, chunk)
    carry = lax.fori_loop(low, high, lambda kc, cr: step(kc, 1, True, cr), carry)
    pairs = (chunk - high) // 2
    carry = lax.fori_loop(0, pairs, lambda n, cr: step(high + 2 * n, 2, False, cr), carry)
    carry = lax.fori_loop(
        high + 2 * pairs, chunk, lambda kc, cr: step(kc, 1, False, cr), carry
    )
    return step(chunk, 1, True, carry)


def chunk_scores(keys, stacked, kc, chunk, starts, masked):
    raw = nt(keys, stacked)
    if not masked:
        return raw
    key = kc * TOK + lax.broadcasted_iota(jnp.int32, raw.shape, 0)
    query = chunk * TOK + lax.broadcasted_iota(jnp.int32, raw.shape, 1) % TOK
    return jnp.where((key <= query) & (key >= starts), raw, -1e30)


def attend_kernel(query, kv, start, out, logsum):
    chunk = own_chunk(pl.program_id(0))
    stacked = (stacked_low(query[0]) * (1.0 / HEAD_DIM**0.5)).astype(BF)
    starts = jnp.concatenate([start[0]] * GROUP, axis=1)

    def step(kc, size, masked, carry):
        top, summed, total = carry
        keys = kv[pl.ds(kc, size)].reshape(size * TOK, 128)
        scores = chunk_scores(keys, stacked, kc, chunk, starts, masked)
        new_top = jnp.maximum(top, jnp.max(scores, axis=0, keepdims=True))
        weights = jnp.exp(scores - new_top)
        fade = jnp.exp(top - new_top)
        summed = summed * fade + jnp.sum(weights, axis=0, keepdims=True)
        part = tn(keys, weights.astype(BF))
        return new_top, summed, total * fade + part[HEAD_DIM:]

    rows = GROUP * TOK
    carry = (jnp.full((1, rows), -1e30, F32), jnp.zeros((1, rows), F32), jnp.zeros((64, rows), F32))
    top, summed, total = over_chunks(start[0], chunk, step, carry)
    for pair, tile in enumerate(unstacked(total / summed)):
        out[0, :, 128 * pair : 128 * pair + 128] = tile.astype(BF)
    logsum[0] = top + jnp.log(summed)


def attend(query, kv, start):
    chunk = lambda r, cols: pl.BlockSpec((1, r, cols), lambda i: (i, 0, 0))
    return pl.pallas_call(
        attend_kernel,
        name="attend",
        cost_estimate=cost(12),
        grid=(RING,),
        in_specs=[
            chunk(TOK, QZ),
            pl.BlockSpec((16, TOK, 128), lambda i: (0, 0, 0)),
            chunk(1, TOK),
        ],
        out_specs=[chunk(TOK, QZ), chunk(1, GROUP * TOK)],
        out_shape=[
            jax.ShapeDtypeStruct((RING, TOK, QZ), BF),
            jax.ShapeDtypeStruct((RING, 1, GROUP * TOK), F32),
        ],
        compiler_params=PARAMS,
    )(query, kv, start)


def attend_back_kernel(
    query, kv, start, out, grad_out, logsum, cosine, sine, dquery, dkv, total
):
    i = pl.program_id(0)
    chunk = own_chunk(i)
    stacked = (stacked_low(query[0]) * (1.0 / HEAD_DIM**0.5)).astype(BF)
    grads = stacked_high(grad_out[0]).astype(BF)
    starts = jnp.concatenate([start[0]] * GROUP, axis=1)
    lse = logsum[0]
    deltas = []
    for pair in range(4):
        cols = slice(128 * pair, 128 * pair + 128)
        prod = (out[0, :, cols].astype(F32) * grad_out[0, :, cols].astype(F32)).T
        deltas.append(jnp.sum(prod[:HEAD_DIM], axis=0, keepdims=True))
        deltas.append(jnp.sum(prod[HEAD_DIM:], axis=0, keepdims=True))
    delta = jnp.concatenate(deltas, axis=1)

    @pl.when(i == 0)
    def _():
        total[...] = jnp.zeros_like(total)

    def step(kc, size, masked, dq):
        keys = kv[pl.ds(kc, size)].reshape(size * TOK, 128)
        scores = chunk_scores(keys, stacked, kc, chunk, starts, masked)
        probs = jnp.exp(scores - lse)
        grad_probs = nt(keys, grads)
        grad_scores = (probs * (grad_probs - delta)).astype(BF)
        part = dot(grad_scores, stacked) + dot(probs.astype(BF), grads)
        total[pl.ds(kc, size)] += part.reshape(size, TOK, 128)
        return dq + tn(keys, grad_scores)[:HEAD_DIM]

    dq = over_chunks(start[0], chunk, step, jnp.zeros((64, GROUP * TOK), F32))
    cos, sin = cosine[0], sine[0]
    for pair, tile in enumerate(unstacked(dq)):
        tile = tile * (1.0 / HEAD_DIM**0.5)
        dquery[0, :, 128 * pair : 128 * pair + 128] = (tile * cos - swapped(tile) * sin).astype(BF)

    @pl.when(i == RING - 1)
    def _():
        dkv[...] = total[...].astype(BF)


def attend_back(query, kv, start, out, grad_out, logsum, cosine, sine):
    chunk = lambda r, cols: pl.BlockSpec((1, r, cols), lambda i: (i, 0, 0))
    whole = pl.BlockSpec((16, TOK, 128), lambda i: (0, 0, 0))
    return pl.pallas_call(
        attend_back_kernel,
        name="attend_back",
        cost_estimate=cost(15),
        grid=(RING,),
        in_specs=[
            chunk(TOK, QZ),
            whole,
            chunk(1, TOK),
            chunk(TOK, QZ),
            chunk(TOK, QZ),
            chunk(1, GROUP * TOK),
            chunk(TOK, 128),
            chunk(TOK, 128),
        ],
        out_specs=[chunk(TOK, QZ), whole],
        scratch_shapes=[pltpu.VMEM((16, TOK, 128), F32)],
        out_shape=[
            jax.ShapeDtypeStruct((RING, TOK, QZ), BF),
            jax.ShapeDtypeStruct((16, TOK, 128), BF),
        ],
        compiler_params=PARAMS,
    )(query, kv, start, out, grad_out, logsum, cosine, sine)


def rms_back(v, gain, grad):
    scale = lax.rsqrt(jnp.mean(v * v, axis=-1, keepdims=True) + EPS)
    unit = v * scale
    gain_grad = jnp.sum(grad * unit, axis=0, keepdims=True)
    inner = grad * gain
    return scale * (inner - unit * jnp.mean(inner * unit, axis=-1, keepdims=True)), gain_grad


def finish_kernel(
    a, b, g1, g3, g2, go, gq, gkv, gains, out, grad, gate, up, down, proj, qkv, gain1, gain2
):
    gain1[...] = gains[0]
    gain2[...] = gains[1]
    out[...] = a[...]
    grad[...] = b[...]
    for src, dst in ((g1, gate), (g3, up), (g2, down), (go, proj)):
        dst[...] = src[...].astype(F32)
    qkv[:, :QDIM] = gq[...].astype(F32)
    kv = gkv[...].astype(F32)
    tiles = [kv[:, 128 * j : 128 * j + 128] for j in range(4)]
    lane = lax.broadcasted_iota(jnp.int32, tiles[0].shape, 1)
    for j in range(2):
        one, two = tiles[2 * j], tiles[2 * j + 1]
        keys = jnp.where(lane < HEAD_DIM, one, pltpu.roll(two, 64, 1))
        values = jnp.where(lane < HEAD_DIM, pltpu.roll(one, 64, 1), two)
        qkv[:, QDIM + 128 * j : QDIM + 128 * j + 128] = keys
        qkv[:, QDIM + KVDIM + 128 * j : QDIM + KVDIM + 128 * j + 128] = values


def finish(*arrays):
    steps = 4
    spec = lambda v: pl.BlockSpec((v.shape[0] // steps, v.shape[1]), lambda i: (i, 0))
    outs = [jax.ShapeDtypeStruct(v.shape, F32) for v in arrays[:-3]]
    outs.append(jax.ShapeDtypeStruct((256, QDIM + 2 * KVDIM), F32))
    gain = jax.ShapeDtypeStruct((256,), F32)
    return pl.pallas_call(
        finish_kernel,
        name="finish",
        cost_estimate=cost(12),
        grid=(steps,),
        in_specs=[spec(v) for v in arrays[:-1]] + [pl.BlockSpec((8, 256), lambda i: (0, 0))],
        out_specs=[spec(v) for v in outs] + [pl.BlockSpec((256,), lambda i: (0,))] * 2,
        out_shape=outs + [gain] * 2,
        compiler_params=PARAMS,
    )(*arrays)


def pick(v, index, axis=0):
    return lax.dynamic_index_in_dim(v, index, axis, keepdims=False)


def dot(a, b):
    return jnp.dot(a, b, preferred_element_type=F32)


def body(tokens, segments, cotangent, norm_attn, norm_ffn, wqkv, wo, w1, w3, w2):
    q = coords()
    y, xx, xl, z, c = q["y"], q["x"], q["xl"], q["z"], q["c"]
    x = tokens[0]
    g = cotangent[0]
    freq = THETA ** (-(np.arange(128) % 32) * 2.0 / HEAD_DIM)
    freq = jnp.asarray(freq[None], F32)
    table = ((RING, TOK, 128), F32)
    G, WQ, WO, W13, t2, n1, query, KV, cosine, sine, start, gain_attn, gain_ffn = talk(
        front_kernel,
        "front",
        1,
        46,
        120,
        (
            x, g, segments, norm_attn, norm_ffn, freq,
            wqkv, wo, w1, w3, w2,
        ),
        [
            ((RING, TOK, D), BF),
            ((2, 4, 2, 2, 64, MZ), BF),
            ((2, 256, D), BF),
            ((2, 4, 2, 2, 64, 2 * FZ), BF),
            ((4, 704, 128), BF),
            ((RING, TOK, D), BF),
            ((RING, TOK, QZ), BF),
            ((2, 4, 2, TOK, 128), BF),
            table,
            table,
            ((RING, 1, TOK), jnp.int32),
            ((1, D), F32),
            ((1, D), F32),
        ],
        scratch=[
            pltpu.VMEM((256, 128), BF),
            pltpu.VMEM((704, 128), BF),
            pltpu.VMEM((64, MZ), BF),
            pltpu.VMEM((64, 128), BF),
            pltpu.VMEM((64, 128), BF),
            pltpu.VMEM((64, FZ), BF),
            pltpu.VMEM((64, FZ), BF),
            pltpu.VMEM((8, TOK), jnp.int32),
            pltpu.VMEM((32, 256), BF),
            pltpu.VMEM((2, 4, 2, 8, TOK), jnp.int32),
            pltpu.VMEM((4, 2, 32, 256), BF),
            pltpu.VMEM((RING, TOK, D), BF),
            pltpu.VMEM((2, 4, 2, 2, 64, MZ), BF),
            pltpu.VMEM((RING, TOK, D), BF),
            pltpu.VMEM((RING, TOK, QZ), BF),
            pltpu.VMEM((RING, TOK, 128), BF),
        ],
        near=tuple(range(6)),
        near_out=(8, 9, 10, 11, 12),
    )
    WQ = WQ.reshape(D, MZ)
    WO = WO.reshape(QZ, D)
    KV = KV.reshape(16, TOK, 128)
    heads_out, logsum = attend(query, KV, start)
    o = heads_out.reshape(RING * TOK, QZ)
    rest = 2 * FZ - SPLIT
    buffers = []
    for shape in ((704, 256), (2, 64, SPLIT), (2, 64, rest)):
        buffers += [pltpu.VMEM((2,) + shape, BF)] * 4
    chunks = pltpu.VMEM((RING, TOK, D), BF)
    DH, fa, fb, f2, dheads, output, dh, gain2 = talk(
        core_kernel,
        "core",
        3,
        120,
        150,
        (heads_out, x, gain_ffn, t2, W13, WO, G),
        [
            ((RING, TOK, D), BF),
            ((2, 2, 64, SPLIT), BF),
            ((2, 2, 64, rest), BF),
            ((2, 704, 256), BF),
            ((RING * TOK, QZ), BF),
            ((TOK, D), F32),
            ((TOK, D), F32),
            ((1, D), F32),
        ],
        scratch=[
            pltpu.VMEM((2, 4, 2, 2, 64, 2 * FZ), BF),
            pltpu.VMEM((FZ, D), BF),
            chunks,
            chunks,
            pltpu.VMEM((RING * TOK, FZ), BF),
            pltpu.VMEM((FZ, RING * TOK), BF),
            pltpu.VMEM((RING * TOK, 2 * FZ), BF),
            chunks,
            chunks,
            pltpu.VMEM((QZ, D), BF),
            pltpu.VMEM((RING, TOK, QZ), BF),
            chunks,
            pltpu.VMEM((TOK, D), F32),
            pltpu.VMEM((TOK, D), BF),
            *[pltpu.VMEM(HALF, BF)] * 8,
            *[pltpu.VMEM((TOK, D), BF)] * 4,
            *buffers,
            pltpu.SemaphoreType.REGULAR((2,)),
        ],
        near=(2,),
        near_out=(4, 5, 6, 7),
    )
    fa, fb = fa.reshape(4, 64, SPLIT), fb.reshape(4, 64, rest)
    f2 = f2.reshape(1408, 256)
    DH = DH.reshape(RING * TOK, D)
    dquery, dkv = attend_back(
        query, KV, start, heads_out, dheads.reshape(RING, TOK, QZ), logsum, cosine, sine
    )
    small = (8, 256)
    input_grad, G1, G3, G2, GO, GQ, GKV, gain_out = talk(
        tail_kernel,
        "tail",
        6,
        75,
        170,
        (
            dkv.reshape(2, 4, 2, TOK, 128), dquery, cosine, sine, x, dh, gain_attn, gain2,
            fa, fb, f2, WQ, n1.reshape(RING * TOK, D), o, DH,
        ),
        [
            ((TOK, D), F32),
            ((256, 4 * FZ), BF),
            ((256, 4 * FZ), BF),
            ((704, D), BF),
            ((256, D), BF),
            ((256, QDIM), BF),
            ((256, 2 * KVDIM), BF),
            (small, F32),
        ],
        scratch=[
            pltpu.VMEM((D, MZ), BF),
            pltpu.VMEM((RING * TOK, D), BF),
            pltpu.VMEM((RING * TOK, QZ), BF),
            pltpu.VMEM((RING * TOK, D), BF),
            pltpu.VMEM((4, RING, TOK, 128), BF),
            pltpu.VMEM((RING, TOK, MZ), BF),
            pltpu.VMEM((RING, TOK, D), BF),
            *[pltpu.VMEM(HALF, BF)] * 4,
            *[pltpu.VMEM((TOK, D), BF)] * 2,
            *[pltpu.VMEM((4, QZ, 256), BF)] * 2,
            *[pltpu.VMEM((4, 4, 64, MZ), BF)] * 2,
            *[pltpu.VMEM((2, 256, 256), BF)] * 4,
            *[pltpu.VMEM((2, 2, 64, MZ), BF)] * 4,
            pltpu.VMEM((3, 64, SPLIT), BF),
            pltpu.VMEM((3, 64, rest), BF),
            pltpu.VMEM((3, 704, 128), BF),
            pltpu.VMEM((64, SPLIT), BF),
            pltpu.VMEM((64, rest), BF),
            pltpu.VMEM((704, 128), BF),
            pltpu.VMEM((704, 128), BF),
            pltpu.VMEM((3, 256, 128), BF),
            pltpu.VMEM((3, 64, MZ), BF),
            pltpu.VMEM((512, 256), BF),
            pltpu.VMEM((4, 64, MZ), BF),
            pltpu.VMEM((256, 128), BF),
            pltpu.VMEM((64, MZ), BF),
            pltpu.VMEM((256, 128), BF),
            pltpu.VMEM((4, 2) + small, F32),
            pltpu.VMEM((4, 2) + small, F32),
            pltpu.VMEM((2, 2) + small, F32),
            pltpu.VMEM((4,) + small, F32),
            pltpu.VMEM((2,) + small, F32),
            pltpu.VMEM((2,) + small, F32),
            pltpu.VMEM(small, F32),
            *[pltpu.VMEM((RING, TOK, 128), BF)] * 2,
            *[pltpu.VMEM((RING, TOK, 128), F32)] * 2,
            pltpu.VMEM((TOK, D), BF),
            pltpu.VMEM((TOK, D), F32),
            pltpu.VMEM((64, SPLIT), BF),
            pltpu.VMEM((64, rest), BF),
            pltpu.VMEM((704, 128), BF),
        ],
        near=(6, 7),
        near_out=(0,),
    )
    output, input_grad, gate_grad, up_grad, down_grad, out_grad, qkv_grad, gain1, gain2 = finish(
        output, input_grad, G1, G3, G2, GO, GQ, GKV, gain_out
    )
    return (
        output[None],
        input_grad[None],
        gain1,
        gain2,
        qkv_grad,
        out_grad,
        gate_grad,
        up_grad,
        down_grad,
    )


def solution(mesh):
    rows = P("dp", None)
    acts = P("dp", "ctx", None)
    return jax.shard_map(
        body,
        mesh=mesh,
        in_specs=(acts, P("dp", "ctx"), acts, P("dp"), P("dp"), rows, rows, rows, rows, rows),
        out_specs=(acts, acts, P("dp"), P("dp"), rows, rows, rows, rows, rows),
        check_vma=False,
    )
```

```python
import functools

import jax
import jax.numpy as jnp
import numpy as np
from jax import lax
from jax.experimental import pallas as pl
from jax.experimental.pallas import tpu as pltpu
from jax.sharding import PartitionSpec as P

D = 2048
HEAD_DIM = 64
TOK = 128
RING = 4
QDIM = 2048
KVDIM = 256
GROUP = 8
QZ = 512
MZ = 640
FZ = 1408
SPLIT = 1536
EPS = 1e-05
THETA = 10000.0
MESH = pl.DeviceIdType.MESH
VMEM_LIMIT = 60 << 20
BF = jnp.bfloat16
F32 = jnp.float32
ANY = pl.BlockSpec(memory_space=pl.ANY)
VMEM = pl.BlockSpec(memory_space=pltpu.VMEM)


def coords():
    dp, ctx = lax.axis_index("dp"), lax.axis_index("ctx")
    y, xh = dp // 2, dp % 2
    xl, z, c = ctx // 8, (ctx // 2) % 4, ctx % 2
    return dict(y=y, x=xh * 2 + xl, xh=xh, xl=xl, z=z, c=c)


def device(q, **change):
    r = {k: change.get(k, q[k]) for k in ("y", "x", "z", "c")}
    return (r["y"] * 2 + r["x"] // 2, (r["x"] % 2) * 8 + r["z"] * 2 + r["c"])


def ring(q, axis):
    return [device(q, **{axis: (q[axis] + s) % 4}) for s in (1, 3, 2)]


def shift_pairs(axis, by):
    size = 2 if axis == "c" else 4
    pairs = []
    for y in range(4):
        for x in range(4):
            for z in range(4):
                for c in range(2):
                    q = dict(y=y, x=x, z=z, c=c)
                    pairs.append((device(q), device(q, **{axis: (q[axis] + by) % size})))
    return [(a[0] * 16 + a[1], b[0] * 16 + b[1]) for a, b in pairs]


def swap_pairs():
    pairs = []
    for y in range(4):
        for x in range(4):
            for z in range(4):
                for c in range(2):
                    q = dict(y=y, x=x, z=z, c=c)
                    pairs.append((device(q), device(q, y=z, z=y)))
    return [(a[0] * 16 + a[1], b[0] * 16 + b[1]) for a, b in pairs]


def move(v, axis, by):
    return lax.ppermute(v, ("dp", "ctx"), shift_pairs(axis, by))


class Copies:
    def __init__(self, send_sems, recv_sems):
        self.send_sems, self.recv_sems, self.n, self.open = send_sems, recv_sems, 0, []

    def send(self, src, dst, to):
        cp = pltpu.make_async_remote_copy(
            src_ref=src,
            dst_ref=dst,
            send_sem=self.send_sems.at[self.n],
            recv_sem=self.recv_sems.at[self.n],
            device_id=to,
            device_id_type=MESH,
        )
        cp.start()
        self.n += 1
        self.open.append(cp)
        return cp

    def local(self, src, dst):
        cp = pltpu.make_async_copy(src, dst, self.send_sems.at[self.n])
        cp.start()
        self.n += 1
        return cp

    def close(self):
        for cp in self.open:
            cp.wait_send()
        self.open = []


def deal(k, q, src, col, dst):
    y, z = q["y"], q["z"]
    n = k.n
    k.n += 4
    copies = [
        pltpu.make_async_remote_copy(
            src_ref=src.at[:, col((y + s) % 4)],
            dst_ref=dst,
            send_sem=k.send_sems.at[n + i],
            recv_sem=k.recv_sems.at[n],
            device_id=to,
            device_id_type=MESH,
        )
        for i, (s, to) in enumerate(zip((1, 3, 2), ring(q, "y")))
    ]
    here = pltpu.make_async_copy(src.at[:, col(y)], dst, k.send_sems.at[n + 3])

    @pl.when(y == z)
    def _():
        for cp in copies:
            cp.start()
        here.start()

    def wait():
        @pl.when(y == z)
        def _():
            for cp in copies:
                cp.wait_send()
            here.wait()

        @pl.when(y != z)
        def _():
            copies[0].wait_recv()

    return wait


def greet(targets, q=None):
    barrier = pltpu.get_barrier_semaphore()
    for to in targets:
        pl.semaphore_signal(barrier, inc=1, device_id=to, device_id_type=MESH)
    if q is None:
        pl.semaphore_wait(barrier, len(targets))
    else:
        y, z = q["y"], q["z"]

        @pl.when(y != z)
        def _():
            to = device(q, y=z, z=y)
            pl.semaphore_signal(barrier, inc=1, device_id=to, device_id_type=MESH)

        pl.semaphore_wait(barrier, len(targets) + (y != z).astype(jnp.int32))


TOP, LOW = pl.ds(0, TOK // 2), pl.ds(TOK // 2, TOK // 2)
HALF = (TOK // 2, D)


class Gather:
    def __init__(self, k, q, axis, src, dst):
        at = q[axis]
        self.k, self.dst = k, dst
        self.above, self.below, self.far = (at + 1) % 4, (at + 3) % 4, (at + 2) % 4
        self.up, self.down = device(q, **{axis: self.above}), device(q, **{axis: self.below})
        self.low0 = k.send(src(0), dst(at, 0), self.up)
        self.top1 = k.send(src(1), dst(at, 1), self.down)
        self.low1 = k.send(src(1), dst(at, 1), self.up)
        self.top0 = k.send(src(0), dst(at, 0), self.down)

        self.waiting = {0: self.low0, 1: self.top1}

    def arrived(self, half):
        cp = self.waiting.pop(half, None)
        if cp is not None:
            cp.wait_recv()

    def relay(self):
        self.arrived(0)
        ref = self.dst(self.below, 0)
        self.far0 = self.k.send(ref, ref, self.up)
        self.arrived(1)
        ref = self.dst(self.above, 1)
        self.far1 = self.k.send(ref, ref, self.down)

    def near(self):
        self.arrived(0)
        self.arrived(1)
        self.low1.wait_recv()
        self.top0.wait_recv()

    def end(self):
        self.far0.wait_recv()
        self.far1.wait_recv()


class Sum:
    def __init__(self, k, q, axis, block, below, above, passed):
        at = q[axis]
        self.k, self.below, self.above, self.passed = k, below, above, passed
        up, down, far = (at + 1) % 4, (at + 3) % 4, (at + 2) % 4
        self.up, self.down = device(q, **{axis: up}), device(q, **{axis: down})
        self.first = k.send(block(far, 0), passed[0], self.up)
        self.second = k.send(block(far, 1), passed[1], self.down)
        self.rest = [
            k.send(block(up, 1), below(1), self.up),
            k.send(block(down, 0), above(0), self.down),
        ]

    def relay(self, own0, own1, sent):
        self.first.wait_recv()
        sent[0][...] = (self.passed[0][...].astype(F32) + own0[...].astype(F32)).astype(BF)
        self.rest.append(self.k.send(sent[0], self.below(0), self.up))
        self.second.wait_recv()
        sent[1][...] = (self.passed[1][...].astype(F32) + own1[...].astype(F32)).astype(BF)
        self.rest.append(self.k.send(sent[1], self.above(1), self.down))

    def end(self):
        for cp in self.rest:
            cp.wait_recv()


def halves(ref):
    return lambda h: ref.at[(TOP, LOW)[h]]


def ring_halves(ref):
    return lambda j, h: ref.at[j, (TOP, LOW)[h]]


def turn(k, q, moves):
    y, z = q["y"], q["z"]
    swap = device(q, y=z, z=y)
    pairs = []
    for src, dst in moves:
        n = k.n
        k.n += 1
        remote = pltpu.make_async_remote_copy(
            src_ref=src,
            dst_ref=dst,
            send_sem=k.send_sems.at[n],
            recv_sem=k.recv_sems.at[n],
            device_id=swap,
            device_id_type=MESH,
        )
        pairs.append((remote, pltpu.make_async_copy(src, dst, k.send_sems.at[n])))

    @pl.when(y != z)
    def _():
        for remote, _ in pairs:
            remote.start()

    @pl.when(y == z)
    def _():
        for _, here in pairs:
            here.start()

    def wait():
        @pl.when(y != z)
        def _():
            for remote, _ in pairs:
                remote.wait_recv()
                remote.wait_send()

        @pl.when(y == z)
        def _():
            for _, here in pairs:
                here.wait()

    return wait


def cost(us):
    return pl.CostEstimate(flops=int(us * 1e9), bytes_accessed=0, transcendentals=0)


def talk(kernel, name, cid, us, copies, ins, outs, scratch=(), near=(), near_out=(), alias={}):
    return pl.pallas_call(
        kernel,
        name=name,
        out_shape=[jax.ShapeDtypeStruct(s, t) for s, t in outs],
        in_specs=[VMEM if i in near else ANY for i in range(len(ins))],
        out_specs=[VMEM if i in near_out else ANY for i in range(len(outs))],
        scratch_shapes=[
            *scratch,
            pltpu.SemaphoreType.DMA((copies,)),
            pltpu.SemaphoreType.DMA((copies,)),
        ],
        cost_estimate=cost(us),
        input_output_aliases=alias,
        compiler_params=pltpu.CompilerParams(
            collective_id=cid, has_side_effects=True, vmem_limit_bytes=VMEM_LIMIT
        ),
    )(*ins)


def front_kernel(
    x, g, seg, na, nf, freq, wq, wo, w1, w3, w2,
    G, WQ, WO, W13, T2, N1, Q, KV, COS, SIN, START, GA, GF,
    TO, TV, QP, KT, VT, P1, P3, SG, NG, SEGS, GN, XV, WV, NV, QV, KVV, ss, rs,
):
    q = coords()
    y, xx, xh, xl, z, c = q["y"], q["x"], q["xh"], q["xl"], q["z"], q["c"]
    zs, ys, xs = ring(q, "z"), ring(q, "y"), ring(q, "x")
    mate = device(q, c=1 - c)
    other = device(q, x=xx ^ 1)
    other_mate = device(q, x=xx ^ 1, c=1 - c)
    k = Copies(ss, rs)
    rows = pl.ds(pl.multiple_of(128 * c + 64 * xl, 64), 64)
    qcols = pl.ds(pl.multiple_of(QZ * z, 128), QZ)
    tile = 128 * (z // 2)
    kcols = pl.ds(pl.multiple_of(QDIM + tile, 128), 128)
    vcols = pl.ds(pl.multiple_of(QDIM + KVDIM + tile, 128), 128)
    fcols = pl.ds(pl.multiple_of(FZ * z, 128), FZ)
    loads = [
        k.local(wq.at[rows, qcols], QP.at[:, pl.ds(0, QZ)]),
        k.local(wq.at[rows, kcols], KT),
        k.local(wq.at[rows, vcols], VT),
        k.local(w1.at[rows, fcols], P1),
        k.local(w3.at[rows, fcols], P3),
    ]
    SG[...] = jnp.broadcast_to(seg[...], (8, TOK))
    NG[0:16] = jnp.broadcast_to(na[...].astype(F32)[None], (16, 256)).astype(BF)
    NG[16:32] = jnp.broadcast_to(nf[...].astype(F32)[None], (16, 256)).astype(BF)
    greet(zs + ys + xs + [mate, other_mate])
    seg_z = [k.send(SG, SEGS.at[xl, z, c], to) for to in zs]
    x_ring = Gather(k, q, "z", halves(x), ring_halves(XV))
    lanes = lambda j, n=1: pl.ds(pl.multiple_of(128 * j, 128 * n), 128 * n)
    dealt = deal(k, q, wo, lambda j: lanes(c * 8 + j * 2 + xl), TO)
    for cp in loads:
        cp.wait()
    odd = z % 2 == 1
    kt, vt = KT[...].astype(F32), VT[...].astype(F32)
    lane = lax.broadcasted_iota(jnp.int32, kt.shape, 1)
    kt = jnp.where(odd, pltpu.roll(kt, 64, 1), kt)
    vt = jnp.where(odd, vt, pltpu.roll(vt, 64, 1))
    QP[:, QZ:] = jnp.where(lane < HEAD_DIM, kt, vt).astype(BF)
    f1, f3 = pl.ds(0, FZ), pl.ds(FZ, FZ)
    top, low = pl.ds(0, 32), pl.ds(32, 32)
    thirty = lambda h: pl.ds(32 * h, 32)
    q_top = [k.send(QP.at[top], WV.at[c, y, xh, xl, top], to) for to in xs]
    q_low = [k.send(QP.at[low], WV.at[c, y, xh, xl, low], to) for to in ys]
    gn_y = [k.send(NG, GN.at[y, xh], to) for to in ys]
    up_y = Gather(
        k, q, "y", lambda h: P3.at[thirty(h)], lambda j, h: W13.at[c, j, xh, xl, thirty(h), f3]
    )
    gate_x = Gather(
        k, q, "x", lambda h: P1.at[thirty(h)],
        lambda j, h: W13.at[c, y, j // 2, j % 2, thirty(h), f1],
    )
    q_here = k.local(QP, WV.at[c, y, xh, xl])
    seg_here = k.local(SG, SEGS.at[xl, z, c])
    gn_here = k.local(NG, GN.at[y, xh])
    x_here = k.local(x, XV.at[z])
    up_here = k.local(P3, W13.at[c, y, xh, xl, :, f3])
    heres = [k.local(P1, W13.at[c, y, xh, xl, :, f1]), k.local(g, G.at[z])]
    dealt()
    o1 = [k.send(TO, WO.at[xh, :, lanes(c * 8 + y * 2 + xl)], to) for to in xs]
    o1_here = k.local(TO, WO.at[xh, :, lanes(c * 8 + y * 2 + xl)])
    for cp in seg_z:
        cp.wait_recv()
    seg_here.wait()
    part = SEGS.at[xl, :, c]
    seg2 = [k.send(part, part, to) for to in (mate, other, other_mate)]
    q_here.wait()
    for cp in q_top:
        cp.wait_recv()
    q_y = Gather(k, q, "y", lambda h: WV.at[c, y, h, :, top], lambda j, h: WV.at[c, j, h, :, top])
    for cp in gn_y:
        cp.wait_recv()
    gn_here.wait()
    gn2 = k.send(GN.at[:, xh], GN.at[:, xh], device(q, x=3 - xx))
    gate_x.relay()
    for cp in q_low:
        cp.wait_recv()
    q_half = lambda j, h: WV.at[c, pl.ds(2 * h, 2), j // 2, j % 2, low]
    q_x = Gather(k, q, "x", lambda h: q_half(xx, h), q_half)
    x_ring.relay()
    g_ring = Gather(k, q, "z", halves(g), ring_halves(G))
    up_y.relay()
    for cp in o1:
        cp.wait_recv()
    o1_here.wait()
    o_half = lambda j, h: WO.at[h, :, lanes(c * 8 + j * 2, 2)]
    o_y = Gather(k, q, "y", lambda h: o_half(y, h), o_half)
    for cp in seg2:
        cp.wait_recv()
    docs = [SEGS[i // 8, (i // 2) % 4, i % 2, 0:1].astype(F32) for i in range(16)]
    columns = jnp.concatenate(docs + [jnp.zeros((TOK - 16, TOK), F32)], axis=0).T
    for i in range(RING):
        mine = SEGS[xl, i, c, 0:1].astype(F32)
        count = jnp.zeros((TOK, TOK), F32)
        for j in range(16):
            count = count + jnp.where(columns[:, j : j + 1] < mine, 1.0, 0.0)
        first = jnp.sum(count, axis=0, keepdims=True)
        START[i] = first.astype(jnp.int32)
        index = TOK * (8 * xl + 2 * i + c) + lax.broadcasted_iota(jnp.int32, (1, TOK), 1)
        place = index.astype(F32) - first
        angle = jnp.broadcast_to(place, (TOK, TOK)).T * freq[...]
        COS[i] = jnp.cos(angle)
        sine = jnp.sin(angle)
        lane = lax.broadcasted_iota(jnp.int32, sine.shape, 1)
        SIN[i] = jnp.where(lane % 64 < 32, -sine, sine)
    q_y.relay()
    w2_dealt = deal(k, q, w2, lambda j: lanes(c * 8 + xl * 4 + j), TV)
    q_x.relay()
    up_y.near()
    up_y.end()
    up_here.wait()
    part = W13.at[c, :, xh, xl, :, f3]
    a3 = [k.send(part, part, to) for to in xs[:2]]
    o_y.relay()
    gn2.wait_recv()
    whole = lambda r: jnp.concatenate(
        [GN[d // 2, d % 2, r : r + 1].astype(F32) for d in range(8)], axis=1
    )
    gain = whole(0)
    GA[...] = gain
    GF[...] = whole(16)
    x_ring.near()
    x_ring.end()
    x_here.wait()
    for i in range(RING):
        xv = XV[i].astype(F32)
        scale = lax.rsqrt(jnp.mean(xv * xv, axis=-1, keepdims=True) + EPS)
        NV[i] = to_pieces((xv * scale * gain).astype(BF))
    done = [k.local(NV, N1)]
    for r in (q_y, q_x):
        r.near()
        r.end()
    q3 = k.send(WV.at[c], WV.at[c], mate)
    g_ring.relay()
    q3.wait_recv()
    done.append(k.local(WV, WQ))
    mixed = dot(NV[...].reshape(RING * TOK, D), WV[...].reshape(D, MZ))
    for i in range(RING):
        cos, sin = COS[i], SIN[i]
        for j in range(5):
            u = mixed[TOK * i : TOK * i + TOK, 128 * j : 128 * j + 128]
            turned = u * cos + swapped(u) * sin
            if j < 4:
                QV[i, :, 128 * j : 128 * j + 128] = turned.astype(BF)
            else:
                lane = lax.broadcasted_iota(jnp.int32, u.shape, 1)
                KVV[i] = jnp.where(lane < HEAD_DIM, turned, u).astype(BF)
    near = k.send(KVV, KV.at[xl, :, c], mate)
    n = k.n
    k.n += 2
    far, on = [
        pltpu.make_async_remote_copy(
            src_ref=src,
            dst_ref=KV.at[0, :, c],
            send_sem=ss.at[n + i],
            recv_sem=rs.at[n + i],
            device_id=to,
            device_id_type=MESH,
        )
        for i, (src, to) in enumerate(((KVV, other), (KV.at[0, :, c], mate)))
    ]

    @pl.when(xl == 0)
    def _():
        far.start()

    done += [k.local(KVV, KV.at[xl, :, c]), k.local(QV, Q)]
    o_y.near()
    o_y.end()
    part = WO.at[:, :, pl.ds(pl.multiple_of(1024 * c, 1024), 1024)]
    o3 = k.send(part, part, mate)
    w2_dealt()
    done.append(k.local(TV, T2))

    @pl.when(xl == 0)
    def _():
        far.wait_send()

    @pl.when(xl == 1)
    def _():
        far.wait_recv()
        on.start()
        on.wait_recv()
        on.wait_send()

    near.wait_recv()
    for cp in a3 + [o3]:
        cp.wait_recv()
    for cp in heres + done:
        cp.wait()
    for r in (gate_x, g_ring):
        r.near()
        r.end()
    k.close()


def core_kernel(
    o, x, gain, t2, w13, wo_in, G, V, FA, FB, F2, DO, OUT, DH, GAIN, *scratch
):
    (
        W, W2, N2, gv, hv, hT, bv, part, outs, wo, ov, vv, hf, xb, outf, dhf,
        p0, p1, p2, p3, v0, v1, v2, v3, below, above, out_below, out_above, *rest_of,
    ) = scratch
    bufs, (used, ss, rs) = rest_of[:-3], rest_of[-3:]
    q = coords()
    y, xx, xh, xl, z, c = q["y"], q["x"], q["xh"], q["xl"], q["z"], q["c"]
    ys, xs = ring(q, "y"), ring(q, "x")
    up, down = device(q, z=(z + 1) % 4), device(q, z=(z + 3) % 4)
    mate = device(q, c=1 - c)
    k = Copies(ss, rs)
    f1, f3 = pl.ds(0, FZ), pl.ds(FZ, FZ)
    lower, higher = (xx + 3) % 4, (xx + 1) % 4
    gate_at = lambda ref, j: ref.at[c, j, :, :, :, f1]
    gate_half = lambda ref, j, h: ref.at[c, j, h, :, :, f1]
    up_at = lambda ref, j: ref.at[c, :, j // 2, j % 2, :, f3]
    up_half = lambda ref, j, h: ref.at[c, pl.ds(2 * h, 2), j // 2, j % 2, :, f3]
    get_wo, get_o = k.local(wo_in, wo), k.local(o, ov)
    loads = [k.local(x, xb), k.local(gate_at(w13, y), gate_at(W, y))]
    loads += [k.local(up_at(w13, j), up_at(W, j)) for j in (xx, lower, higher)]
    get_g = k.local(G, gv)
    greet(ys + xs + [up, down, mate])
    cols = lambda j, n: pl.ds(pl.multiple_of(128 * (8 * c + j), 128 * n), 128 * n)
    frows = lambda j, h: pl.ds(pl.multiple_of(704 * (j // 2) + 352 * h, 32), 352)
    w2_here = k.local(t2, W2.at[pl.ds(pl.multiple_of(704 * xh, 64), 704), cols(xl * 4 + y, 1)])
    w2y = Gather(
        k, q, "y", lambda h: t2.at[pl.ds(352 * h, 352)],
        lambda j, h: W2.at[frows(xx, h), cols(xl * 4 + j, 1)],
    )
    far = [
        k.send(up_half(w13, lower, 0), up_half(W, lower, 0), xs[0]),
        k.send(up_half(w13, higher, 1), up_half(W, higher, 1), xs[1]),
    ]
    sent = [k.send(up_at(w13, j), up_at(W, j), mate) for j in (xx, lower, higher)]
    get_wo.wait()
    get_o.wait()
    rows = RING * TOK
    part[...] = dot(ov[...].reshape(rows, QZ), wo[...]).astype(BF).reshape(RING, TOK, D)
    z_sum = Sum(k, q, "z", ring_halves(part), halves(below), halves(above), (p0, p1))
    w2y.relay()
    gate = Gather(
        k, q, "y", lambda h: gate_half(w13, y, h), lambda j, h: gate_half(W, j, h)
    )
    sent.append(k.send(gate_at(w13, y), gate_at(W, y), mate))
    w2_here.wait()
    w2y.near()
    w2y.end()
    down2 = lambda j: W2.at[
        pl.ds(pl.multiple_of(704 * (j // 2), 64), 704), cols((j % 2) * 4, 4)
    ]
    down_half = lambda j, h: W2.at[frows(j, h), cols((j % 2) * 4, 4)]
    down_ring = Gather(k, q, "x", lambda h: down_half(xx, h), down_half)
    sent.append(k.send(down2(xx), down2(xx), mate))
    z_sum.relay(part.at[(z + 1) % 4, TOP], part.at[(z + 3) % 4, LOW], (v0, v1))
    z_sum.end()
    for cp in loads:
        cp.wait()
    total = xb[...].astype(F32) + (
        part[z].astype(F32) + (below[...].astype(F32) + above[...].astype(F32))
    )
    hf[...] = total
    scale = lax.rsqrt(jnp.mean(total * total, axis=-1, keepdims=True) + EPS)
    N2[z] = to_pieces((total * scale * gain[...]).astype(BF))
    n2_ring = Gather(k, q, "z", halves(N2.at[z]), ring_halves(N2))
    gate.relay()
    down_ring.relay()
    for cp in far:
        cp.wait_recv()
    ref = up_at(W, (xx + 2) % 4)
    sent.append(k.send(ref, ref, mate))
    gate.near()
    for j in (gate.below, gate.above):
        sent.append(k.send(gate_at(W, j), gate_at(W, j), mate))
    down_ring.near()
    for j in (down_ring.below, down_ring.above):
        sent.append(k.send(down2(j), down2(j), mate))
    n2_ring.relay()
    gate.end()
    sent.append(k.send(gate_at(W, gate.far), gate_at(W, gate.far), mate))
    down_ring.end()
    sent.append(k.send(down2(down_ring.far), down2(down_ring.far), mate))
    get_g.wait()
    for cp in sent:
        cp.wait_recv()
    tiles = [(256 * i, min(256 * i + 256, FZ)) for i in range(6)]
    gs = gv[...].reshape(rows, D)
    for a, b in tiles:
        bv[:, a:b] = nt(gs, W2[a:b]).astype(BF)
    n2_ring.near()
    n2_ring.end()
    k.close()
    n2 = N2[...].reshape(rows, D)
    for a, b in tiles:
        gates = dot(n2, W[:, :, :, :, :, a:b].reshape(D, b - a))
        ups = dot(n2, W[:, :, :, :, :, FZ + a : FZ + b].reshape(D, b - a))
        sigma = jax.nn.sigmoid(gates)
        silu = gates * sigma
        hv[:, a:b] = (silu * ups).astype(BF)
        dhid = bv[:, a:b].astype(F32)
        bv[:, a:b] = (dhid * ups * sigma * (1.0 + gates * (1.0 - sigma))).astype(BF)
        bv[:, FZ + a : FZ + b] = (dhid * silu).astype(BF)
    for j in range(4):
        at = slice(512 * j, 512 * j + 512)
        outs[:, :, at] = dot(hv[...], W2[:, at]).astype(BF).reshape(RING, TOK, 512)
    out_sum = Sum(
        k, q, "z", ring_halves(outs), halves(out_below), halves(out_above), (p2, p3)
    )
    pl.semaphore_signal(used.at[0], inc=1, device_id=mate, device_id_type=MESH)
    half = lambda ref: lambda i: ref.at[i]
    rest = 2 * FZ - SPLIT
    jobs = [
        ("y", lambda j, i: W2.at[pl.ds(704 * i, 704), lanes(0, j)], F2),
        ("x", lambda j, i: W.at[0, pl.ds(2 * i, 2), j // 2, j % 2, :, pl.ds(0, SPLIT)], FA),
        ("y", lambda j, i: W.at[0, j, i, :, :, pl.ds(SPLIT, rest)], FB),
    ]
    sums, done = [], []
    lanes = lambda cc, j: pl.ds(pl.multiple_of(1024 * cc + 256 * j, 256), 256)

    def start(n):
        axis, block, _ = jobs[n]
        b = bufs[4 * n : 4 * n + 4]
        sums.append(Sum(k, q, axis, block, half(b[2]), half(b[3]), (b[0].at[0], b[0].at[1])))

    def relay(n):
        axis, block, _ = jobs[n]
        b = bufs[4 * n : 4 * n + 4]
        at = q[axis]
        sums[n].relay(block((at + 1) % 4, 0), block((at + 3) % 4, 1), (b[1].at[0], b[1].at[1]))

    def end(n):
        axis, block, out = jobs[n]
        b = bufs[4 * n : 4 * n + 4]
        sums[n].end()
        for i in range(2):
            total = block(q[axis], i)[...].astype(F32) + (
                b[2][i].astype(F32) + b[3][i].astype(F32)
            )
            b[2][i] = total.astype(BF)
        done.append(k.local(b[2], out))

    hT[...] = hv[...].T
    pl.semaphore_wait(used.at[0], 1)
    sent2, sent13 = [], []
    for j in range(4):
        W2[:, 1024 + 256 * j : 1280 + 256 * j] = dot(
            hT[...], gv[:, :, lanes(1 - c, j)].reshape(rows, 256)
        ).astype(BF)
        sent2.append(k.send(W2.at[:, lanes(1, j)], W2.at[:, lanes(0, j)], mate))
    for j in range(4):
        sent2[j].wait_recv()
        at = slice(256 * j, 256 * j + 256)
        own = dot(hT[...], gv[:, :, lanes(c, j)].reshape(rows, 256))
        W2[:, at] = (own + W2[:, at].astype(F32)).astype(BF)
    start(0)
    out_sum.relay(outs.at[(z + 1) % 4, TOP], outs.at[(z + 3) % 4, LOW], (v2, v3))
    for j in range(2):
        at = slice(1024 * j, 1024 * j + 1024)
        dn = nt(bv[...], W[j].reshape(1024, 2 * FZ))
        part[:, :, at] = dn.astype(BF).reshape(RING, TOK, 1024)
    z_sum = Sum(k, q, "z", ring_halves(part), halves(below), halves(above), (p0, p1))
    pl.semaphore_signal(used.at[1], inc=1, device_id=mate, device_id_type=MESH)
    pl.semaphore_wait(used.at[1], 1)
    shape = (2, 2, 64, 2 * FZ)
    for j in range(4):
        W[1, j] = tn(N2[:, :, lanes(1 - c, j)].reshape(rows, 256), bv[...]).astype(BF).reshape(shape)
        sent13.append(k.send(W.at[1, j], W.at[0, j], mate))
        if j == 0:
            relay(0)
    for j in range(4):
        sent13[j].wait_recv()
        own = tn(N2[:, :, lanes(c, j)].reshape(rows, 256), bv[...]).reshape(shape)
        W[0, j] = (own + W[0, j].astype(F32)).astype(BF)
        if j == 1:
            z_sum.relay(part.at[(z + 1) % 4, TOP], part.at[(z + 3) % 4, LOW], (v0, v1))
    start(1)
    start(2)
    end(0)
    z_sum.end()
    dn = from_pieces(
        part[z].astype(F32) + (below[...].astype(F32) + above[...].astype(F32))
    )
    back, gain_grad = rms_back(hf[...], gain[...], dn)
    total = gv[z].astype(F32) + back
    dhf[...] = total
    done.append(k.local(dhf, DH))
    GAIN[...] = gain_grad
    vv[z] = total.astype(BF)
    v_ring = Gather(k, q, "z", halves(vv.at[z]), ring_halves(vv))
    out_sum.end()
    outf[...] = hf[...] + (
        outs[z].astype(F32) + (out_below[...].astype(F32) + out_above[...].astype(F32))
    )
    done.append(k.local(outf, OUT))
    relay(1)
    relay(2)
    v_ring.relay()
    end(2)
    v_ring.near()
    v_ring.end()
    done.append(k.local(vv, V))
    DO[...] = nt(vv[...].reshape(rows, D), wo[...]).astype(BF)
    end(1)
    for cp in done:
        cp.wait()
    k.close()


def quarter(xt, rows):
    return (
        pl.ds(pl.multiple_of((xt // 2) * rows, rows), rows),
        pl.ds(pl.multiple_of((xt % 2) * 128, 128), 128),
    )


def tail_kernel(
    dkv, dq, cosine, sine, x, dh, gain, gain2, fa, fb, f2, wq, n1, o, dho,
    IG, G1, G3, G2, GO, GQ, GKV, gain_out, *scratch,
):
    (
        wv, nv, ov, gv, R, dm, dn, p0, p1, v0, v1, below, above, mate_o, sum_o, mate_q, sum_q,
        ob0, ob1, ob2, ob3, qb0, qb1, qb2, qb3, la, lb, l2, pa, pb, p2, t2, lo, lq, fo, fq,
        po, pq, to_, gains, s0, s1, s2, s3, s4, total,
        kv_own, kv_low, cv, sv, xv, dv, fav, fbv, f2v, ig, ss, rs,
    ) = scratch
    q = coords()
    y, xx, xh, xl, z, c = q["y"], q["x"], q["xh"], q["xl"], q["z"], q["c"]
    zs, ys, xs = ring(q, "z"), ring(q, "y"), ring(q, "x")
    mate, other, cross = device(q, c=1 - c), device(q, x=xx ^ 1), device(q, x=3 - xx)
    other_mate = device(q, x=xx ^ 1, c=1 - c)
    steps = (1, 3, 2)
    rows_all = RING * TOK
    k = Copies(ss, rs)
    get_o, get_g = k.local(o, ov), k.local(dho, gv)
    r, cc = quarter(xx, 704)
    get_f = [k.local(fb.at[xx], fbv), k.local(fa.at[y], fav), k.local(f2.at[r, cc], f2v)]
    get_kv = [k.local(dkv.at[xl, :, c], kv_own), k.local(dkv.at[0, :, c], kv_low)]
    get_d = [
        k.local(dq, dm.at[:, :, pl.ds(0, QZ)]),
        k.local(cosine, cv),
        k.local(sine, sv),
        k.local(wq, wv),
    ]
    get_n = k.local(n1, nv)
    get_x = [k.local(x, xv), k.local(dh, dv)]
    greet(zs + ys + xs + [mate, other_mate], q)
    leg_b = [k.send(fb.at[(xx + s) % 4], lb.at[i], xs[i]) for i, s in enumerate(steps)]
    leg_a = [k.send(fa.at[(y + s) % 4], la.at[i], ys[i]) for i, s in enumerate(steps)]
    lanes = lambda cc, j: pl.ds(pl.multiple_of(1024 * cc + 256 * j, 256), 256)
    get_o.wait()
    get_g.wait()
    swaps = []
    for j in range(4):
        mate_o[j] = tn(ov[...], gv[:, lanes(1 - c, j)]).astype(BF)
        swaps.append(k.send(mate_o.at[j], sum_o.at[j], mate))
    leg_2 = []
    for i, s in enumerate(steps):
        r, cc = quarter((xx + s) % 4, 704)
        leg_2.append(k.send(f2.at[r, cc], l2.at[i], xs[i]))
    for j in range(4):
        swaps[j].wait_recv()
        sum_o[j] = (tn(ov[...], gv[:, lanes(c, j)]) + sum_o[j].astype(F32)).astype(BF)
    half = lambda ref: lambda h: ref.at[h]
    o_block = lambda j, h: sum_o.at[j, pl.ds(256 * h, 256)]
    q_block = lambda j, h: sum_q.at[j, pl.ds(2 * h, 2)]
    o_sum = Sum(k, q, "y", o_block, half(ob2), half(ob3), (ob0.at[0], ob0.at[1]))
    at = lambda zz, off, n: pl.ds(pl.multiple_of(FZ * zz + off, 128), n)
    rows = pl.ds(pl.multiple_of(128 * c + 64 * xl, 64), 64)
    pair = pl.ds(pl.multiple_of(128 * c, 128), 128)
    f1 = pl.ds(0, FZ)
    rest = SPLIT - FZ
    quarter_rows = lambda h: pl.ds(pl.multiple_of(128 * c + 64 * xl + 32 * h, 32), 32)

    def over_z(src, ref, off, n):
        return Gather(
            k, q, "z", lambda h: src.at[pl.ds(32 * h, 32)],
            lambda j, h: ref.at[quarter_rows(h), at(j, off, n)],
        )

    spans = [(G1, 0, FZ), (G3, 0, rest), (G3, rest, FZ - rest)]
    pieces = [pa.at[:, f1], pa.at[:, pl.ds(FZ, rest)], pb]
    block = lambda i, j: spans[i][0].at[rows, at(j, spans[i][1], spans[i][2])]
    rings, to_x, heres = [None] * 3, [], []

    def across(i, j):
        to_x.append(k.send(block(i, j), block(i, j), other))

    def own_across(i):
        to_x.append(k.send(pieces[i], block(i, z), other))
        heres.append(k.local(pieces[i], block(i, z)))

    def onward(i):
        rings[i].near()
        across(i, rings[i].below)
        across(i, rings[i].above)

    for cp in get_f:
        cp.wait()
    for cp in leg_b:
        cp.wait_recv()
    pb[...] = add4(fbv[...], lb[0], lb[1], lb[2])
    rings[2] = over_z(pieces[2], *spans[2])
    near = k.send(dkv.at[xl, :, 1 - c], R.at[0], mate)
    n = k.n
    k.n += 2
    pre, far = [
        pltpu.make_async_remote_copy(
            src_ref=src,
            dst_ref=dst,
            send_sem=ss.at[n + i],
            recv_sem=rs.at[n + i],
            device_id=to,
            device_id_type=MESH,
        )
        for i, (src, dst, to) in enumerate(
            ((dkv.at[0, :, 1 - c], R.at[1], mate), (R.at[2], R.at[3], other))
        )
    ]

    @pl.when(xl == 1)
    def _():
        pre.start()

    for cp in get_kv:
        cp.wait()
    rings[2].relay()
    o_sum.relay(o_block((y + 1) % 4, 0), o_block((y + 3) % 4, 1), (ob1.at[0], ob1.at[1]))

    @pl.when(xl == 1)
    def _():
        R[3] = jnp.zeros(R.shape[1:], BF)
        pre.wait()
        for i in range(RING):
            R[2, i] = (kv_low[i].astype(F32) + R[1, i].astype(F32)).astype(BF)
        far.start()

    for cp in leg_a:
        cp.wait_recv()
    pa[...] = add4(fav[...], la[0], la[1], la[2])
    rings[0] = over_z(pieces[0], *spans[0])
    rings[1] = over_z(pieces[1], *spans[1])
    for cp in leg_2:
        cp.wait_recv()
    p2[...] = add4(f2v[...], l2[0], l2[1], l2[2])
    turned = turn(k, q, [(p2, t2)])
    onward(2)
    own_across(2)

    @pl.when(xl == 1)
    def _():
        far.wait_send()

    @pl.when(xl == 0)
    def _():
        far.wait_recv()

    near.wait_recv()
    for cp in get_d:
        cp.wait()
    for i in range(RING):
        w = kv_own[i].astype(F32) + (R[0, i].astype(F32) + R[3, i].astype(F32))
        lane = lax.broadcasted_iota(jnp.int32, w.shape, 1)
        dm[i, :, QZ:] = jnp.where(
            lane < HEAD_DIM, w * cv[i] - swapped(w) * sv[i], w
        ).astype(BF)
    dmixed = dm[...].reshape(rows_all, MZ)
    dn[...] = nt(dmixed, wv[...]).astype(BF).reshape(RING, TOK, D)
    z_sum = Sum(k, q, "z", ring_halves(dn), halves(below), halves(above), (p0, p1))
    onward(0)
    rings[1].relay()
    get_n.wait()
    cols = lambda cc: pl.ds(pl.multiple_of(1024 * cc, 1024), 1024)
    shape = (4, 4, 64, MZ)
    mate_q[...] = tn(nv[:, cols(1 - c)], dmixed).astype(BF).reshape(shape)
    swap = k.send(mate_q, sum_q, mate)
    own = tn(nv[:, cols(c)], dmixed).reshape(shape)
    swap.wait_recv()
    sum_q[...] = (own + sum_q[...].astype(F32)).astype(BF)
    q_sum = Sum(k, q, "y", q_block, half(qb2), half(qb3), (qb0.at[0], qb0.at[1]))
    o_sum.end()
    for h in range(2):
        part = o_block(y, h)[...].astype(F32) + (ob2[h].astype(F32) + ob3[h].astype(F32))
        fo[pl.ds(256 * h, 256)] = part.astype(BF)
    leg_o, leg_q = [], []
    for i, s in enumerate(steps):
        r, cc = quarter((xx + s) % 4, 256)
        leg_o.append(k.send(fo.at[r, cc], lo.at[i], xs[i]))
    turned()
    col = pl.ds(pl.multiple_of(128 * (c * 8 + z * 2 + xl), 128), 128)
    down_x = k.send(t2, G2.at[:, col], other)
    down_here = k.local(t2, G2.at[:, col])
    z_sum.relay(dn.at[(z + 1) % 4, TOP], dn.at[(z + 3) % 4, LOW], (v0, v1))
    q_sum.relay(q_block((y + 1) % 4, 0), q_block((y + 3) % 4, 1), (qb1.at[0], qb1.at[1]))
    onward(1)
    for cp in leg_o:
        cp.wait_recv()
    r, cc = quarter(xx, 256)
    po[...] = add4(fo[r, cc], lo[0], lo[1], lo[2])
    o_turned = turn(k, q, [(po, to_)])
    q_sum.end()
    for h in range(2):
        part = q_block(y, h)[...].astype(F32) + (qb2[h].astype(F32) + qb3[h].astype(F32))
        fq[pl.ds(2 * h, 2)] = part.astype(BF)
    for i, s in enumerate(steps):
        leg_q.append(k.send(fq.at[(xx + s) % 4], lq.at[i], xs[i]))
    rings[1].end()
    across(1, rings[1].far)
    rings[0].relay()
    z_sum.end()
    for cp in get_x:
        cp.wait()
    back, gain1 = rms_back(
        xv[...].astype(F32),
        gain[...],
        from_pieces(dn[z].astype(F32) + (below[...].astype(F32) + above[...].astype(F32))),
    )
    ig[...] = dv[...] + back
    ig_done = k.local(ig, IG)
    gains[...] = jnp.zeros_like(gains)
    for d in range(8):
        gains[d // 2, d % 2, 0:1] = gain1[:, 256 * d : 256 * d + 256]
        gains[d // 2, d % 2, 1:2] = gain2[:, 256 * d : 256 * d + 256]
    gain_y = [k.send(gains.at[(y + s) % 4], s0.at[y], ys[i]) for i, s in enumerate(steps)]
    gain_here = k.local(gains.at[y], s0.at[y])
    down_x.wait_recv()
    down_here.wait()
    down_half = lambda j, h: G2.at[
        pl.ds(352 * h, 352), pl.ds(pl.multiple_of(128 * (c * 8 + j * 2), 256), 256)
    ]
    down_ring = Gather(k, q, "z", lambda h: down_half(z, h), down_half)
    own_across(0)
    own_across(1)
    for cp in leg_q:
        cp.wait_recv()
    pq[...] = add4(fq[xx], lq[0], lq[1], lq[2])
    qc = lambda j: pl.ds(pl.multiple_of(QZ * j, 128), QZ)
    kc = lambda j: pl.ds(pl.multiple_of(128 * j, 128), 128)
    q_pieces = [
        (pq.at[:, pl.ds(0, QZ)], GQ.at[rows, qc(z)]),
        (pq.at[:, pl.ds(QZ, 128)], GKV.at[rows, kc(z)]),
    ]
    q_x = [k.send(src, dst, other) for src, dst in q_pieces]
    q_here = [k.local(src, dst) for src, dst in q_pieces]
    o_turned()
    o_x = k.send(to_, GO.at[:, col], other)
    o_here = k.local(to_, GO.at[:, col])
    for cp in gain_y:
        cp.wait_recv()
    gain_here.wait()
    s1[0] = (s0[0] + s0[1]) + (s0[2] + s0[3])
    gain_x = k.send(s1.at[0, 1 - xh], s1.at[1, 0], cross)
    gain_x.wait_recv()
    s2[z] = s1[0, xh] + s1[1, 0]
    gain_z = [k.send(s2.at[z], s2.at[z], to) for to in zs]
    down_ring.relay()
    rings[0].end()
    across(0, rings[0].far)
    o_x.wait_recv()
    o_here.wait()
    o_half = lambda j, h: GO.at[
        pl.ds(128 * h, 128), pl.ds(pl.multiple_of(128 * (c * 8 + j * 2), 256), 256)
    ]
    o_ring = Gather(k, q, "z", lambda h: o_half(z, h), o_half)
    for cp in q_x:
        cp.wait_recv()
    for cp in q_here:
        cp.wait()
    half_rows = lambda h: pl.ds(pl.multiple_of(128 * c + 64 * h, 64), 64)
    q_half = lambda j, h: GQ.at[half_rows(h), qc(j)]
    kv_half = lambda j, h: GKV.at[half_rows(h), kc(j)]
    q_rings = [
        Gather(k, q, "z", lambda h: q_half(z, h), q_half),
        Gather(k, q, "z", lambda h: kv_half(z, h), kv_half),
    ]
    rings[2].end()
    across(2, rings[2].far)
    down_ring.near()
    down_ring.end()
    last = [k.send(G2.at[:, cols(c)], G2.at[:, cols(c)], mate)]
    for cp in to_x:
        cp.wait_recv()
    for cp in heres:
        cp.wait()
    last += [k.send(ref.at[pair], ref.at[pair], mate) for ref in (G1, G3)]
    o_ring.relay()
    for cp in gain_z:
        cp.wait_recv()
    s3[0] = (s2[0] + s2[1]) + (s2[2] + s2[3])
    gain_x = k.send(s3.at[0], s3.at[1], other)
    for one in q_rings:
        one.relay()
    o_ring.near()
    o_ring.end()
    last.append(k.send(GO.at[:, cols(c)], GO.at[:, cols(c)], mate))
    gain_x.wait_recv()
    s4[0] = s3[0] + s3[1]
    gain_c = k.send(s4.at[0], s4.at[1], mate)
    for one in q_rings:
        one.near()
        one.end()
    last += [k.send(ref.at[pair], ref.at[pair], mate) for ref in (GQ, GKV)]
    gain_c.wait_recv()
    total[...] = s4[0] + s4[1]
    gain_done = k.local(total, gain_out)
    for cp in last:
        cp.wait_recv()
    gain_done.wait()
    ig_done.wait()
    k.close()


PARAMS = pltpu.CompilerParams(vmem_limit_bytes=VMEM_LIMIT)


def add4(a, b, c, d):
    a, b, c, d = (v.astype(F32) for v in (a, b, c, d))
    return ((a + b) + (c + d)).astype(BF)


def to_pieces(v):
    return jnp.concatenate(
        [v[:, 256 * d + 128 * c : 256 * d + 128 * c + 128] for c in range(2) for d in range(8)],
        axis=1,
    )


def from_pieces(v):
    return jnp.concatenate(
        [v[:, 1024 * c + 128 * d : 1024 * c + 128 * d + 128] for d in range(8) for c in range(2)],
        axis=1,
    )


def swapped(u):
    lane = lax.broadcasted_iota(jnp.int32, u.shape, 1)
    return jnp.where(lane % 64 < 32, pltpu.roll(u, 96, 1), pltpu.roll(u, 32, 1))


def stacked_low(tiles):
    out = []
    for pair in range(4):
        tile = tiles[:, 128 * pair : 128 * pair + 128].astype(F32)
        lane = lax.broadcasted_iota(jnp.int32, tile.shape, 1)
        out.append(jnp.where(lane < HEAD_DIM, tile, 0.0))
        out.append(jnp.where(lane < HEAD_DIM, pltpu.roll(tile, 64, 1), 0.0))
    return jnp.concatenate(out, axis=0)


def stacked_high(tiles):
    out = []
    for pair in range(4):
        tile = tiles[:, 128 * pair : 128 * pair + 128].astype(F32)
        lane = lax.broadcasted_iota(jnp.int32, tile.shape, 1)
        out.append(jnp.where(lane >= HEAD_DIM, pltpu.roll(tile, 64, 1), 0.0))
        out.append(jnp.where(lane >= HEAD_DIM, tile, 0.0))
    return jnp.concatenate(out, axis=0)


def unstacked(v):
    tiles = []
    for pair in range(4):
        both = jnp.concatenate(
            [v[:, 256 * pair : 256 * pair + 128], v[:, 256 * pair + 128 : 256 * pair + 256]],
            axis=0,
        )
        tiles.append(both.T)
    return tiles


def nt(a, b):
    return lax.dot_general(a, b, (((1,), (1,)), ((), ())), preferred_element_type=F32)


def tn(a, b):
    return lax.dot_general(a, b, (((0,), (0,)), ((), ())), preferred_element_type=F32)


def own_chunk(i):
    ctx = lax.axis_index("ctx")
    return (ctx // 8) * 8 + 2 * i + ctx % 2


def over_chunks(start, chunk, step, carry):
    first = start.astype(F32)
    low = jnp.min(first).astype(jnp.int32) // TOK
    high = jnp.minimum((jnp.max(first).astype(jnp.int32) + TOK - 1) // TOK, chunk)
    carry = lax.fori_loop(low, high, lambda kc, cr: step(kc, 1, True, cr), carry)
    pairs = (chunk - high) // 2
    carry = lax.fori_loop(0, pairs, lambda n, cr: step(high + 2 * n, 2, False, cr), carry)
    carry = lax.fori_loop(
        high + 2 * pairs, chunk, lambda kc, cr: step(kc, 1, False, cr), carry
    )
    return step(chunk, 1, True, carry)


def chunk_scores(keys, stacked, kc, chunk, starts, masked):
    raw = nt(keys, stacked)
    if not masked:
        return raw
    key = kc * TOK + lax.broadcasted_iota(jnp.int32, raw.shape, 0)
    query = chunk * TOK + lax.broadcasted_iota(jnp.int32, raw.shape, 1) % TOK
    return jnp.where((key <= query) & (key >= starts), raw, -1e30)


def attend_kernel(query, kv, start, out, logsum):
    chunk = own_chunk(pl.program_id(0))
    stacked = (stacked_low(query[0]) * (1.0 / HEAD_DIM**0.5)).astype(BF)
    starts = jnp.concatenate([start[0]] * GROUP, axis=1)

    def step(kc, size, masked, carry):
        top, summed, total = carry
        keys = kv[pl.ds(kc, size)].reshape(size * TOK, 128)
        scores = chunk_scores(keys, stacked, kc, chunk, starts, masked)
        new_top = jnp.maximum(top, jnp.max(scores, axis=0, keepdims=True))
        weights = jnp.exp(scores - new_top)
        fade = jnp.exp(top - new_top)
        summed = summed * fade + jnp.sum(weights, axis=0, keepdims=True)
        part = tn(keys, weights.astype(BF))
        return new_top, summed, total * fade + part[HEAD_DIM:]

    rows = GROUP * TOK
    carry = (jnp.full((1, rows), -1e30, F32), jnp.zeros((1, rows), F32), jnp.zeros((64, rows), F32))
    top, summed, total = over_chunks(start[0], chunk, step, carry)
    for pair, tile in enumerate(unstacked(total / summed)):
        out[0, :, 128 * pair : 128 * pair + 128] = tile.astype(BF)
    logsum[0] = top + jnp.log(summed)


def attend(query, kv, start):
    chunk = lambda r, cols: pl.BlockSpec((1, r, cols), lambda i: (i, 0, 0))
    return pl.pallas_call(
        attend_kernel,
        name="attend",
        cost_estimate=cost(12),
        grid=(RING,),
        in_specs=[
            chunk(TOK, QZ),
            pl.BlockSpec((16, TOK, 128), lambda i: (0, 0, 0)),
            chunk(1, TOK),
        ],
        out_specs=[chunk(TOK, QZ), chunk(1, GROUP * TOK)],
        out_shape=[
            jax.ShapeDtypeStruct((RING, TOK, QZ), BF),
            jax.ShapeDtypeStruct((RING, 1, GROUP * TOK), F32),
        ],
        compiler_params=PARAMS,
    )(query, kv, start)


def attend_back_kernel(
    query, kv, start, out, grad_out, logsum, cosine, sine, dquery, dkv, total
):
    i = pl.program_id(0)
    chunk = own_chunk(i)
    stacked = (stacked_low(query[0]) * (1.0 / HEAD_DIM**0.5)).astype(BF)
    grads = stacked_high(grad_out[0]).astype(BF)
    starts = jnp.concatenate([start[0]] * GROUP, axis=1)
    lse = logsum[0]
    deltas = []
    for pair in range(4):
        cols = slice(128 * pair, 128 * pair + 128)
        prod = (out[0, :, cols].astype(F32) * grad_out[0, :, cols].astype(F32)).T
        deltas.append(jnp.sum(prod[:HEAD_DIM], axis=0, keepdims=True))
        deltas.append(jnp.sum(prod[HEAD_DIM:], axis=0, keepdims=True))
    delta = jnp.concatenate(deltas, axis=1)

    @pl.when(i == 0)
    def _():
        total[...] = jnp.zeros_like(total)

    def step(kc, size, masked, dq):
        keys = kv[pl.ds(kc, size)].reshape(size * TOK, 128)
        scores = chunk_scores(keys, stacked, kc, chunk, starts, masked)
        probs = jnp.exp(scores - lse)
        grad_probs = nt(keys, grads)
        grad_scores = (probs * (grad_probs - delta)).astype(BF)
        part = dot(grad_scores, stacked) + dot(probs.astype(BF), grads)
        total[pl.ds(kc, size)] += part.reshape(size, TOK, 128)
        return dq + tn(keys, grad_scores)[:HEAD_DIM]

    dq = over_chunks(start[0], chunk, step, jnp.zeros((64, GROUP * TOK), F32))
    cos, sin = cosine[0], sine[0]
    for pair, tile in enumerate(unstacked(dq)):
        tile = tile * (1.0 / HEAD_DIM**0.5)
        dquery[0, :, 128 * pair : 128 * pair + 128] = (tile * cos - swapped(tile) * sin).astype(BF)

    @pl.when(i == RING - 1)
    def _():
        dkv[...] = total[...].astype(BF)


def attend_back(query, kv, start, out, grad_out, logsum, cosine, sine):
    chunk = lambda r, cols: pl.BlockSpec((1, r, cols), lambda i: (i, 0, 0))
    whole = pl.BlockSpec((16, TOK, 128), lambda i: (0, 0, 0))
    return pl.pallas_call(
        attend_back_kernel,
        name="attend_back",
        cost_estimate=cost(15),
        grid=(RING,),
        in_specs=[
            chunk(TOK, QZ),
            whole,
            chunk(1, TOK),
            chunk(TOK, QZ),
            chunk(TOK, QZ),
            chunk(1, GROUP * TOK),
            chunk(TOK, 128),
            chunk(TOK, 128),
        ],
        out_specs=[chunk(TOK, QZ), whole],
        scratch_shapes=[pltpu.VMEM((16, TOK, 128), F32)],
        out_shape=[
            jax.ShapeDtypeStruct((RING, TOK, QZ), BF),
            jax.ShapeDtypeStruct((16, TOK, 128), BF),
        ],
        compiler_params=PARAMS,
    )(query, kv, start, out, grad_out, logsum, cosine, sine)


def rms_back(v, gain, grad):
    scale = lax.rsqrt(jnp.mean(v * v, axis=-1, keepdims=True) + EPS)
    unit = v * scale
    gain_grad = jnp.sum(grad * unit, axis=0, keepdims=True)
    inner = grad * gain
    return scale * (inner - unit * jnp.mean(inner * unit, axis=-1, keepdims=True)), gain_grad


def finish_kernel(
    a, b, g1, g3, g2, go, gq, gkv, gains, out, grad, gate, up, down, proj, qkv, gain1, gain2
):
    gain1[...] = gains[0]
    gain2[...] = gains[1]
    out[...] = a[...]
    grad[...] = b[...]
    for src, dst in ((g1, gate), (g3, up), (g2, down), (go, proj)):
        dst[...] = src[...].astype(F32)
    qkv[:, :QDIM] = gq[...].astype(F32)
    kv = gkv[...].astype(F32)
    tiles = [kv[:, 128 * j : 128 * j + 128] for j in range(4)]
    lane = lax.broadcasted_iota(jnp.int32, tiles[0].shape, 1)
    for j in range(2):
        one, two = tiles[2 * j], tiles[2 * j + 1]
        keys = jnp.where(lane < HEAD_DIM, one, pltpu.roll(two, 64, 1))
        values = jnp.where(lane < HEAD_DIM, pltpu.roll(one, 64, 1), two)
        qkv[:, QDIM + 128 * j : QDIM + 128 * j + 128] = keys
        qkv[:, QDIM + KVDIM + 128 * j : QDIM + KVDIM + 128 * j + 128] = values


def finish(*arrays):
    steps = 4
    spec = lambda v: pl.BlockSpec((v.shape[0] // steps, v.shape[1]), lambda i: (i, 0))
    outs = [jax.ShapeDtypeStruct(v.shape, F32) for v in arrays[:-3]]
    outs.append(jax.ShapeDtypeStruct((256, QDIM + 2 * KVDIM), F32))
    gain = jax.ShapeDtypeStruct((256,), F32)
    return pl.pallas_call(
        finish_kernel,
        name="finish",
        cost_estimate=cost(12),
        grid=(steps,),
        in_specs=[spec(v) for v in arrays[:-1]] + [pl.BlockSpec((8, 256), lambda i: (0, 0))],
        out_specs=[spec(v) for v in outs] + [pl.BlockSpec((256,), lambda i: (0,))] * 2,
        out_shape=outs + [gain] * 2,
        compiler_params=PARAMS,
    )(*arrays)


def pick(v, index, axis=0):
    return lax.dynamic_index_in_dim(v, index, axis, keepdims=False)


def dot(a, b):
    return jnp.dot(a, b, preferred_element_type=F32)


def body(tokens, segments, cotangent, norm_attn, norm_ffn, wqkv, wo, w1, w3, w2):
    q = coords()
    y, xx, xl, z, c = q["y"], q["x"], q["xl"], q["z"], q["c"]
    x = tokens[0]
    g = cotangent[0]
    freq = THETA ** (-(np.arange(128) % 32) * 2.0 / HEAD_DIM)
    freq = jnp.asarray(freq[None], F32)
    table = ((RING, TOK, 128), F32)
    G, WQ, WO, W13, t2, n1, query, KV, cosine, sine, start, gain_attn, gain_ffn = talk(
        front_kernel,
        "front",
        1,
        46,
        120,
        (
            x, g, segments, norm_attn, norm_ffn, freq,
            wqkv, wo, w1, w3, w2,
        ),
        [
            ((RING, TOK, D), BF),
            ((2, 4, 2, 2, 64, MZ), BF),
            ((2, 256, D), BF),
            ((2, 4, 2, 2, 64, 2 * FZ), BF),
            ((704, 128), BF),
            ((RING, TOK, D), BF),
            ((RING, TOK, QZ), BF),
            ((2, 4, 2, TOK, 128), BF),
            table,
            table,
            ((RING, 1, TOK), jnp.int32),
            ((1, D), F32),
            ((1, D), F32),
        ],
        scratch=[
            pltpu.VMEM((256, 128), BF),
            pltpu.VMEM((704, 128), BF),
            pltpu.VMEM((64, MZ), BF),
            pltpu.VMEM((64, 128), BF),
            pltpu.VMEM((64, 128), BF),
            pltpu.VMEM((64, FZ), BF),
            pltpu.VMEM((64, FZ), BF),
            pltpu.VMEM((8, TOK), jnp.int32),
            pltpu.VMEM((32, 256), BF),
            pltpu.VMEM((2, 4, 2, 8, TOK), jnp.int32),
            pltpu.VMEM((4, 2, 32, 256), BF),
            pltpu.VMEM((RING, TOK, D), BF),
            pltpu.VMEM((2, 4, 2, 2, 64, MZ), BF),
            pltpu.VMEM((RING, TOK, D), BF),
            pltpu.VMEM((RING, TOK, QZ), BF),
            pltpu.VMEM((RING, TOK, 128), BF),
        ],
        near=tuple(range(6)),
        near_out=(8, 9, 10, 11, 12),
    )
    WQ = WQ.reshape(D, MZ)
    WO = WO.reshape(QZ, D)
    KV = KV.reshape(16, TOK, 128)
    heads_out, logsum = attend(query, KV, start)
    o = heads_out.reshape(RING * TOK, QZ)
    rest = 2 * FZ - SPLIT
    buffers = []
    for shape in ((704, 256), (2, 64, SPLIT), (2, 64, rest)):
        buffers += [pltpu.VMEM((2,) + shape, BF)] * 4
    chunks = pltpu.VMEM((RING, TOK, D), BF)
    DH, fa, fb, f2, dheads, output, dh, gain2 = talk(
        core_kernel,
        "core",
        3,
        120,
        150,
        (heads_out, x, gain_ffn, t2, W13, WO, G),
        [
            ((RING, TOK, D), BF),
            ((2, 2, 64, SPLIT), BF),
            ((2, 2, 64, rest), BF),
            ((2, 704, 256), BF),
            ((RING * TOK, QZ), BF),
            ((TOK, D), F32),
            ((TOK, D), F32),
            ((1, D), F32),
        ],
        scratch=[
            pltpu.VMEM((2, 4, 2, 2, 64, 2 * FZ), BF),
            pltpu.VMEM((FZ, D), BF),
            chunks,
            chunks,
            pltpu.VMEM((RING * TOK, FZ), BF),
            pltpu.VMEM((FZ, RING * TOK), BF),
            pltpu.VMEM((RING * TOK, 2 * FZ), BF),
            chunks,
            chunks,
            pltpu.VMEM((QZ, D), BF),
            pltpu.VMEM((RING, TOK, QZ), BF),
            chunks,
            pltpu.VMEM((TOK, D), F32),
            pltpu.VMEM((TOK, D), BF),
            *[pltpu.VMEM((TOK, D), F32)] * 2,
            *[pltpu.VMEM(HALF, BF)] * 8,
            *[pltpu.VMEM((TOK, D), BF)] * 4,
            *buffers,
            pltpu.SemaphoreType.REGULAR((2,)),
        ],
        near=(2,),
        near_out=(4, 7),
    )
    fa, fb = fa.reshape(4, 64, SPLIT), fb.reshape(4, 64, rest)
    f2 = f2.reshape(1408, 256)
    DH = DH.reshape(RING * TOK, D)
    dquery, dkv = attend_back(
        query, KV, start, heads_out, dheads.reshape(RING, TOK, QZ), logsum, cosine, sine
    )
    small = (8, 256)
    input_grad, G1, G3, G2, GO, GQ, GKV, gain_out = talk(
        tail_kernel,
        "tail",
        6,
        75,
        170,
        (
            dkv.reshape(2, 4, 2, TOK, 128), dquery, cosine, sine, x, dh, gain_attn, gain2,
            fa, fb, f2, WQ, n1.reshape(RING * TOK, D), o, DH,
        ),
        [
            ((TOK, D), F32),
            ((256, 4 * FZ), BF),
            ((256, 4 * FZ), BF),
            ((704, D), BF),
            ((256, D), BF),
            ((256, QDIM), BF),
            ((256, 2 * KVDIM), BF),
            (small, F32),
        ],
        scratch=[
            pltpu.VMEM((D, MZ), BF),
            pltpu.VMEM((RING * TOK, D), BF),
            pltpu.VMEM((RING * TOK, QZ), BF),
            pltpu.VMEM((RING * TOK, D), BF),
            pltpu.VMEM((4, RING, TOK, 128), BF),
            pltpu.VMEM((RING, TOK, MZ), BF),
            pltpu.VMEM((RING, TOK, D), BF),
            *[pltpu.VMEM(HALF, BF)] * 4,
            *[pltpu.VMEM((TOK, D), BF)] * 2,
            *[pltpu.VMEM((4, QZ, 256), BF)] * 2,
            *[pltpu.VMEM((4, 4, 64, MZ), BF)] * 2,
            *[pltpu.VMEM((2, 256, 256), BF)] * 4,
            *[pltpu.VMEM((2, 2, 64, MZ), BF)] * 4,
            pltpu.VMEM((3, 64, SPLIT), BF),
            pltpu.VMEM((3, 64, rest), BF),
            pltpu.VMEM((3, 704, 128), BF),
            pltpu.VMEM((64, SPLIT), BF),
            pltpu.VMEM((64, rest), BF),
            pltpu.VMEM((704, 128), BF),
            pltpu.VMEM((704, 128), BF),
            pltpu.VMEM((3, 256, 128), BF),
            pltpu.VMEM((3, 64, MZ), BF),
            pltpu.VMEM((512, 256), BF),
            pltpu.VMEM((4, 64, MZ), BF),
            pltpu.VMEM((256, 128), BF),
            pltpu.VMEM((64, MZ), BF),
            pltpu.VMEM((256, 128), BF),
            pltpu.VMEM((4, 2) + small, F32),
            pltpu.VMEM((4, 2) + small, F32),
            pltpu.VMEM((2, 2) + small, F32),
            pltpu.VMEM((4,) + small, F32),
            pltpu.VMEM((2,) + small, F32),
            pltpu.VMEM((2,) + small, F32),
            pltpu.VMEM(small, F32),
            *[pltpu.VMEM((RING, TOK, 128), BF)] * 2,
            *[pltpu.VMEM((RING, TOK, 128), F32)] * 2,
            pltpu.VMEM((TOK, D), BF),
            pltpu.VMEM((TOK, D), F32),
            pltpu.VMEM((64, SPLIT), BF),
            pltpu.VMEM((64, rest), BF),
            pltpu.VMEM((704, 128), BF),
            pltpu.VMEM((TOK, D), F32),
        ],
        near=(6, 7),
    )
    output, input_grad, gate_grad, up_grad, down_grad, out_grad, qkv_grad, gain1, gain2 = finish(
        output, input_grad, G1, G3, G2, GO, GQ, GKV, gain_out
    )
    return (
        output[None],
        input_grad[None],
        gain1,
        gain2,
        qkv_grad,
        out_grad,
        gate_grad,
        up_grad,
        down_grad,
    )


def solution(mesh):
    rows = P("dp", None)
    acts = P("dp", "ctx", None)
    return jax.shard_map(
        body,
        mesh=mesh,
        in_specs=(acts, P("dp", "ctx"), acts, P("dp"), P("dp"), rows, rows, rows, rows, rows),
        out_specs=(acts, acts, P("dp"), P("dp"), rows, rows, rows, rows, rows),
        check_vma=False,
    )
```
